32 devices in a mesh: section: 2 (over core), tensor: 4 (over z), dp: 4 (over y, x).
Axes of the slice: x: 2, y: 2, z: 4, core: 2. Of those that a mesh axis runs over, the one named last changes fastest.
Arguments:
- block_input: bfloat16 [2, 1024, 1024], P(None, ('dp', 'tensor')), may hold values from -6 to 6
- output_grad: bfloat16 [2, 1024, 1024], P(None, ('dp', 'tensor')), may hold values from -6 to 6
- valid_len: int32 [2], replicated, may hold values from 769 to 1024
- first_gain: bfloat16 [2, 1024], P('section'), may hold values from 0.5 to 1.5
- first_bias: bfloat16 [2, 1024], P('section'), may hold values from -1.1953125 to 1.1953125
- triple_weight: bfloat16 [2, 1024, 3, 1024], P('section', None, None, 'tensor'), may hold values from -0.1875 to 0.1875
- triple_bias: bfloat16 [2, 3, 1024], P('section', None, 'tensor'), may hold values from -1.1953125 to 1.1953125
- mixer_weight: bfloat16 [2, 1024, 1024], P('section', 'tensor'), may hold values from -1.5 to 1.5
- mixer_bias: bfloat16 [2, 1024], P('section'), may hold values from -1.1953125 to 1.1953125
- second_gain: bfloat16 [2, 1024], P('section'), may hold values from 0.5 to 1.5
- second_bias: bfloat16 [2, 1024], P('section'), may hold values from -1.1953125 to 1.1953125
- expand_weight: bfloat16 [2, 1024, 4096], P('section', None, 'tensor'), may hold values from -0.1875 to 0.1875
- expand_bias: bfloat16 [2, 4096], P('section', 'tensor'), may hold values from -3 to 3
- reduce_weight: bfloat16 [2, 4096, 1024], P('section', 'tensor'), may hold values from -0.09375 to 0.09375
- reduce_bias: bfloat16 [2, 1024], P('section'), may hold values from -1.1953125 to 1.1953125
- prefix_table: bfloat16 [10, 1024], replicated, may hold values from -6 to 6
- inner_weight: bfloat16 [1024, 512], replicated, may hold values from -0.1875 to 0.1875
- inner_bias: bfloat16 [512], replicated, may hold values from -3 to 3
- outer_weight: bfloat16 [512, 2, 2, 1024], P(None, 'section', None, 'tensor'), may hold values from -0.25 to 0.25
- outer_bias: bfloat16 [2, 2, 1024], P('section', None, 'tensor'), may hold values from -3 to 3
Outputs:
- layer_outputs: bfloat16 [2, 2, 1024, 1024], P('section', None, ('dp', 'tensor'))
- input_grads: bfloat16 [2, 2, 1024, 1024], P('section', None, ('dp', 'tensor'))
- prefix_states: bfloat16 [2, 2, 10, 1024], P('section', None, None, 'tensor')
- table_grad: float32 [10, 1024], replicated
- inner_weight_grad: float32 [1024, 512], replicated
- inner_bias_grad: float32 [512], replicated
- outer_weight_grad: float32 [512, 2, 2, 1024], P(None, 'section', None, 'tensor')
- outer_bias_grad: float32 [2, 2, 1024], P('section', None, 'tensor')
The draws below stay inside these ranges and needn't reach their ends.
Inputs may be any that keep to these rules, and one draw needn't show every extreme that they name: Positions at or after valid_len of a micro-batch are padding and are never attended to as keys.
All inputs are finite; a program needn't handle non-finite values.
Results may differ from the reference program's by a relative error of at most 0.015.
Values may be sent and summed in bfloat16 or wider, within the bound.
A program may use at most 128 MiB of HBM per device.

```python
import jax
import jax.numpy as jnp
from jax import lax

D = 1024
HEADS = 16
HD = 64
FF = 4096
P_SIZE = 10
R = 512
LAYERS = 2
MB = 2
TOK_DEV = 256
LEN = 1024


def block_levels(own_key, dims, pieces, low, high):
    def one(axis_at, blocks):
        draws = jax.random.uniform(jax.random.fold_in(jax.random.fold_in(own_key, 6), axis_at), (blocks,), jnp.float32, low / len(pieces), high / len(pieces))
        return jnp.repeat(jnp.exp(draws), dims[axis_at] // blocks).reshape((-1,) + (1,) * (len(dims) - axis_at - 1))

    level = one(*pieces[0])
    for cut in pieces[1:]:
        level = level * one(*cut)
    return level


def noise(stream_key, dims, spread, limit, split=(), kind=jnp.bfloat16):
    entries = spread * jax.random.normal(stream_key, dims, jnp.float32)
    if split:
        entries = entries * block_levels(stream_key, dims, split, -0.22, 0.18)
    return jnp.clip(entries, -limit, limit).astype(kind)


def setup_inputs(seed: int = 0) -> dict:
    splits = jax.random.split(jax.random.key(seed), 21)
    block_input = noise(splits[0], (MB, LEN, D), 1.0, 6.0, ((1, 16),))
    output_grad = noise(splits[1], (MB, LEN, D), 1.0, 6.0, ((1, 16),))
    valid_len = jax.random.randint(splits[2], (MB,), LEN - TOK_DEV + 1, LEN + 1).astype(jnp.int32)
    first_gain = jnp.clip(1.0 + 0.1 * jax.random.normal(splits[3], (LAYERS, D), jnp.float32), 0.5, 1.5).astype(jnp.bfloat16)
    first_bias = noise(splits[4], (LAYERS, D), 0.2, 1.1953125, ((0, 2),))
    triple_weight = noise(splits[5], (LAYERS, D, 3, D), D ** -0.5, 0.1875, ((0, 2), (3, 4)))
    triple_bias = noise(splits[6], (LAYERS, 3, D), 0.2, 1.1953125, ((0, 2), (2, 4)))
    mixer_weight = noise(splits[7], (LAYERS, D, D), (max(D * 16 // LEN, 1)) ** -0.5, 1.5, ((0, 2), (1, 4)))
    mixer_bias = noise(splits[8], (LAYERS, D), 0.2, 1.1953125, ((0, 2),))
    second_gain = jnp.clip(1.0 + 0.1 * jax.random.normal(splits[9], (LAYERS, D), jnp.float32), 0.5, 1.5).astype(jnp.bfloat16)
    second_bias = noise(splits[10], (LAYERS, D), 0.2, 1.1953125, ((0, 2),))
    expand_weight = noise(splits[11], (LAYERS, D, FF), D ** -0.5, 0.1875, ((0, 2), (2, 4)))
    expand_bias = noise(splits[12], (LAYERS, FF), 0.5, 3.0, ((0, 2), (1, 4)))
    reduce_weight = noise(splits[13], (LAYERS, FF, D), FF ** -0.5, 0.09375, ((0, 2), (1, 4)))
    reduce_bias = noise(splits[14], (LAYERS, D), 0.2, 1.1953125, ((0, 2),))
    prefix_table = noise(splits[15], (P_SIZE, D), 1.0, 6.0)
    inner_weight = noise(splits[16], (D, R), D ** -0.5, 0.1875)
    inner_bias = noise(splits[17], (R,), 0.5, 3.0)
    outer_weight = noise(splits[18], (R, LAYERS, 2, D), R ** -0.5, 0.25, ((1, 2), (3, 4)))
    outer_bias = noise(splits[19], (LAYERS, 2, D), 0.5, 3.0, ((0, 2), (2, 4)))
    return dict(block_input=block_input, output_grad=output_grad, valid_len=valid_len, first_gain=first_gain, first_bias=first_bias, triple_weight=triple_weight, triple_bias=triple_bias, mixer_weight=mixer_weight, mixer_bias=mixer_bias, second_gain=second_gain, second_bias=second_bias, expand_weight=expand_weight, expand_bias=expand_bias, reduce_weight=reduce_weight, reduce_bias=reduce_bias, prefix_table=prefix_table, inner_weight=inner_weight, inner_bias=inner_bias, outer_weight=outer_weight, outer_bias=outer_bias)


@jax.custom_vjp
def low(v):
    return lax.optimization_barrier(v.astype(jnp.bfloat16)).astype(jnp.float32)

@jax.custom_vjp
def low_back(v):
    return v

def low_keep(v):
    return (low(v), None)

def low_pass(kept, grad):
    return (grad,)

def back_keep(v):
    return (v, None)

def back_low(kept, grad):
    return (low(grad),)
low.defvjp(low_keep, low_pass)
low_back.defvjp(back_keep, back_low)
epsilon = 1e-05
masked_score = -1e+30
highest = lax.Precision.HIGHEST

def layer_norm(values, norm_gain, norm_bias):
    center = values - lax.optimization_barrier(jnp.mean(values, axis=-1, keepdims=True))
    variance = lax.optimization_barrier(jnp.mean(center * center, axis=-1, keepdims=True))
    return center * lax.rsqrt(variance + epsilon) * norm_gain + norm_bias

def attention(queries, seq_keys, seq_values, pre_keys, pre_values, valid):
    length = queries.shape[0]
    block_size = min(512, length)
    block_count = length // block_size
    score_scale = HD ** (-0.5)
    key_pos = jnp.arange(length, dtype=jnp.int32)[None, :]
    all_values = jnp.concatenate([pre_values, seq_values], axis=0)

    def one_block(packed):
        query_block, block_start = packed
        seq_scores = low_back(jnp.einsum('qhd,khd->hqk', query_block, seq_keys, precision=highest) * score_scale)
        pre_scores = low_back(jnp.einsum('qhd,khd->hqk', query_block, pre_keys, precision=highest) * score_scale)
        query_pos = block_start + jnp.arange(block_size, dtype=jnp.int32)[:, None]
        visible = (key_pos <= query_pos) & (key_pos < valid)
        seq_scores = jnp.where(visible[None], seq_scores, masked_score)
        joined = jnp.concatenate([pre_scores, seq_scores], axis=2)
        peak = lax.optimization_barrier(jnp.max(joined, axis=2, keepdims=True))
        expons = jnp.exp(joined - peak)
        probs = low(expons / lax.optimization_barrier(jnp.sum(expons, axis=2, keepdims=True)))
        return jnp.einsum('hqk,khd->qhd', probs, all_values, precision=highest)
    blocks = queries.reshape(block_count, block_size, HEADS, HD)
    starts = jnp.arange(block_count, dtype=jnp.int32) * block_size
    result = lax.map(jax.checkpoint(one_block), (blocks, starts))
    return result.reshape(length, HEADS, HD)

def block_layer(inputs, weights, prefix, valid):
    first_gain, first_bias, triple_weight, triple_bias, mixer_weight, mixer_bias, second_gain, second_bias, expand_weight, expand_bias, reduce_weight, reduce_bias = weights
    length = inputs.shape[0]
    normed = low(layer_norm(inputs, first_gain, first_bias))
    mixed = jnp.einsum('td,dcf->tcf', normed, triple_weight, precision=highest) + triple_bias
    mixed = low_back(low(mixed))
    queries = mixed[:, 0].reshape(length, HEADS, HD)
    seq_keys = mixed[:, 1].reshape(length, HEADS, HD)
    seq_values = mixed[:, 2].reshape(length, HEADS, HD)
    pre_keys = prefix[0].reshape(P_SIZE, HEADS, HD)
    pre_values = prefix[1].reshape(P_SIZE, HEADS, HD)
    attended = attention(queries, seq_keys, seq_values, pre_keys, pre_values, valid)
    attended = low_back(low(attended)).reshape(length, D)
    branch = low_back(jnp.dot(attended, mixer_weight, precision=highest) + mixer_bias)
    residual = inputs + branch
    middle = low(layer_norm(residual, second_gain, second_bias))
    hidden_pre = low_back(jnp.dot(middle, expand_weight, precision=highest) + expand_bias)
    active = low(jax.nn.gelu(hidden_pre, approximate=True))
    return residual + low_back(jnp.dot(active, reduce_weight, precision=highest) + reduce_bias)

def reference(block_input, output_grad, valid_len, first_gain, first_bias, triple_weight, triple_bias, mixer_weight, mixer_bias, second_gain, second_bias, expand_weight, expand_bias, reduce_weight, reduce_bias, prefix_table, inner_weight, inner_bias, outer_weight, outer_bias):
    stacked_weights = tuple((member.astype(jnp.float32) for member in (first_gain, first_bias, triple_weight, triple_bias, mixer_weight, mixer_bias, second_gain, second_bias, expand_weight, expand_bias, reduce_weight, reduce_bias)))
    inputs = block_input.astype(jnp.float32)

    def forward(probes, table, inner_matrix, inner_shift, outer_matrix, outer_shift):
        hidden = low(jnp.tanh(jnp.dot(table, inner_matrix, precision=highest) + inner_shift))
        prefix = low(jnp.einsum('pr,rlcd->lcpd', hidden, outer_matrix, precision=highest) + outer_shift[:, :, None, :])
        per_batch = []
        for number in range(MB):
            middle = inputs[number]
            outputs = []
            for layer_index in range(LAYERS):
                layer_params = tuple((member[layer_index] for member in stacked_weights))
                middle = middle + probes[layer_index, number]
                middle = low_back(low(block_layer(middle, layer_params, prefix[layer_index], valid_len[number])))
                outputs.append(middle)
            per_batch.append(jnp.stack(outputs))
        stacked = jnp.stack(per_batch, axis=1)
        return (stacked[LAYERS - 1], (stacked, prefix))
    probes = jnp.zeros((LAYERS, MB, LEN, D), jnp.float32)
    last_layer, pullback, (stacked, prefix) = jax.vjp(forward, probes, prefix_table.astype(jnp.float32), inner_weight.astype(jnp.float32), inner_bias.astype(jnp.float32), outer_weight.astype(jnp.float32), outer_bias.astype(jnp.float32), has_aux=True)
    probe_grad, table_grad, inner_weight_grad, inner_bias_grad, outer_weight_grad, outer_bias_grad = pullback(output_grad.astype(jnp.float32))
    return (stacked.astype(jnp.bfloat16), probe_grad.astype(jnp.bfloat16), prefix.astype(jnp.bfloat16), table_grad, inner_weight_grad, inner_bias_grad, outer_weight_grad, outer_bias_grad)
```

```python
from functools import partial

import jax
import jax.numpy as jnp
from jax import lax
from jax.experimental import pallas as pl
from jax.experimental.pallas import tpu as pltpu
from jax.sharding import PartitionSpec as P

HD = 64


epsilon = 1e-05
masked_score = -1e30
highest = lax.Precision.HIGHEST
MESH = pl.DeviceIdType.MESH
f32 = jnp.float32
bf16 = jnp.bfloat16


def passed_along(block, axis, distance):
    devices = range(lax.axis_size(axis))
    route = [(i - distance, i) for i in devices if i - distance in devices]
    return lax.ppermute(block, axis, route)


def layer_norm(values, norm_gain, norm_bias):
    center = values - jnp.mean(values, axis=-1, keepdims=True)
    variance = jnp.mean(center * center, axis=-1, keepdims=True)
    inverse = lax.rsqrt(variance + epsilon)
    normed = center * inverse
    return (normed * norm_gain + norm_bias, normed, inverse)


def norm_back(grad_out, normed, inverse, norm_gain):
    scaled = grad_out * norm_gain
    mean_grad = jnp.mean(scaled, axis=-1, keepdims=True)
    mean_cross = jnp.mean(scaled * normed, axis=-1, keepdims=True)
    return inverse * (scaled - mean_grad - normed * mean_cross)


def attention_scores(queries, seq_keys, pre_keys, valid, query_start):
    score_scale = HD ** (-0.5)
    seq_scores = (
        jnp.einsum("qhd,khd->hqk", queries, seq_keys, preferred_element_type=jnp.float32)
        * score_scale
    )
    pre_scores = (
        jnp.einsum("qhd,khd->hqk", queries, pre_keys, preferred_element_type=jnp.float32)
        * score_scale
    )
    query_pos = query_start + lax.broadcasted_iota(jnp.int32, (queries.shape[0], 1), 0)
    key_pos = lax.broadcasted_iota(jnp.int32, (1, seq_keys.shape[0]), 1)
    visible = (key_pos <= query_pos) & (key_pos < valid)
    seq_scores = jnp.where(visible[None], seq_scores, masked_score)
    return (seq_scores, pre_scores)


def split_prefix(prefix_full, local_width):
    local_heads = local_width // HD
    pre_keys = prefix_full[:, :local_width].reshape(-1, local_heads, HD)
    pre_values = prefix_full[:, local_width:].reshape(-1, local_heads, HD)
    return (pre_keys, pre_values)


def layer_forward(inputs, weights, prefix_full, valid, query_start):
    (
        gain_one,
        bias_one,
        triple_weight,
        triple_bias,
        mixer_weight,
        mixer_bias,
        gain_two,
        bias_two,
        expand_weight,
        expand_bias,
        reduce_weight,
        reduce_bias,
    ) = weights
    local_width = triple_weight.shape[1] // 3
    local_heads = local_width // HD
    normed_one, unit_one, inverse_one = layer_norm(inputs, gain_one, bias_one)
    mixed_rows = (
        jnp.dot(
            lax.all_gather(normed_one.astype(jnp.bfloat16), "tensor", axis=0, tiled=True),
            triple_weight,
            preferred_element_type=jnp.float32,
        )
        + triple_bias
    ).astype(jnp.bfloat16)
    tokens = mixed_rows.shape[0]
    queries = mixed_rows[:, :local_width].reshape(tokens, local_heads, HD)
    seq_keys, seq_values = (
        lax.all_gather(mixed_rows[:, local_width : 2 * local_width], "dp", axis=0, tiled=True),
        lax.all_gather(mixed_rows[:, 2 * local_width :], "dp", axis=0, tiled=True),
    )
    seq_keys = seq_keys.reshape(-1, local_heads, HD)
    seq_values = seq_values.reshape(-1, local_heads, HD)
    pre_keys, pre_values = split_prefix(prefix_full, local_width)
    seq_scores, pre_scores = attention_scores(queries, seq_keys, pre_keys, valid, query_start)
    row_max = jnp.maximum(
        jnp.max(seq_scores, axis=2, keepdims=True), jnp.max(pre_scores, axis=2, keepdims=True)
    )
    seq_exp = jnp.exp(seq_scores - row_max)
    pre_exp = jnp.exp(pre_scores - row_max)
    row_total = jnp.sum(seq_exp, axis=2, keepdims=True) + jnp.sum(pre_exp, axis=2, keepdims=True)
    log_total = row_max + jnp.log(row_total)
    seq_low = (seq_exp / row_total).astype(jnp.bfloat16)
    pre_low = (pre_exp / row_total).astype(jnp.bfloat16)
    attended = jnp.einsum("hqk,khd->qhd", seq_low, seq_values, preferred_element_type=jnp.float32)
    attended = attended + jnp.einsum(
        "hqk,khd->qhd", pre_low, pre_values, preferred_element_type=jnp.float32
    )
    attended = attended.astype(jnp.bfloat16).reshape(tokens, local_width)
    mixer_out = lax.psum_scatter(
        jnp.dot(attended, mixer_weight, preferred_element_type=jnp.float32),
        "tensor",
        scatter_dimension=0,
        tiled=True,
    )
    residual = inputs + mixer_out + mixer_bias
    normed_two, unit_two, inverse_two = layer_norm(residual, gain_two, bias_two)
    hidden_pre = (
        jnp.dot(
            lax.all_gather(normed_two.astype(jnp.bfloat16), "tensor", axis=0, tiled=True),
            expand_weight,
            preferred_element_type=jnp.float32,
        )
        + expand_bias
    )
    active = jax.nn.gelu(hidden_pre, approximate=True).astype(jnp.bfloat16)
    result = (
        residual
        + lax.psum_scatter(
            jnp.dot(active, reduce_weight, preferred_element_type=jnp.float32),
            "tensor",
            scatter_dimension=0,
            tiled=True,
        )
        + reduce_bias
    )
    saved_state = (
        unit_one,
        inverse_one,
        queries,
        seq_keys,
        seq_values,
        log_total,
        unit_two,
        inverse_two,
        hidden_pre,
    )
    return (result, saved_state)


def layer_backward(grad_out, saved_state, weights, prefix_full, valid, query_start):
    (
        gain_one,
        bias_one,
        triple_weight,
        triple_bias,
        mixer_weight,
        mixer_bias,
        gain_two,
        bias_two,
        expand_weight,
        expand_bias,
        reduce_weight,
        reduce_bias,
    ) = weights
    (
        unit_one,
        inverse_one,
        queries,
        seq_keys,
        seq_values,
        log_total,
        unit_two,
        inverse_two,
        hidden_pre,
    ) = saved_state
    tokens = queries.shape[0]
    local_heads = queries.shape[1]
    local_width = local_heads * HD
    score_scale = HD ** (-0.5)
    grad_active = jnp.dot(
        lax.all_gather(grad_out.astype(jnp.bfloat16), "tensor", axis=0, tiled=True),
        reduce_weight.T,
        preferred_element_type=jnp.float32,
    )
    gelu_pull = jax.vjp(partial(jax.nn.gelu, approximate=True), hidden_pre)[1]
    grad_pre = gelu_pull(grad_active)[0].astype(jnp.bfloat16)
    grad_two = lax.psum_scatter(
        jnp.dot(grad_pre, expand_weight.T, preferred_element_type=jnp.float32),
        "tensor",
        scatter_dimension=0,
        tiled=True,
    )
    grad_residual = grad_out + norm_back(grad_two, unit_two, inverse_two, gain_two)
    grad_heads = jnp.dot(
        lax.all_gather(grad_residual.astype(jnp.bfloat16), "tensor", axis=0, tiled=True),
        mixer_weight.T,
        preferred_element_type=jnp.float32,
    ).astype(jnp.bfloat16)
    grad_heads = grad_heads.reshape(tokens, local_heads, HD)
    pre_keys, pre_values = split_prefix(prefix_full, local_width)
    seq_scores, pre_scores = attention_scores(queries, seq_keys, pre_keys, valid, query_start)
    seq_prob = jnp.exp(seq_scores - log_total)
    pre_prob = jnp.exp(pre_scores - log_total)
    seq_dprob = jnp.einsum(
        "qhd,khd->hqk", grad_heads, seq_values, preferred_element_type=jnp.float32
    )
    pre_dprob = jnp.einsum(
        "qhd,khd->hqk", grad_heads, pre_values, preferred_element_type=jnp.float32
    )
    delta_row = jnp.sum(seq_prob * seq_dprob, axis=2, keepdims=True) + jnp.sum(
        pre_prob * pre_dprob, axis=2, keepdims=True
    )
    seq_dscore = (seq_prob * (seq_dprob - delta_row)).astype(jnp.bfloat16)
    pre_dscore = (pre_prob * (pre_dprob - delta_row)).astype(jnp.bfloat16)
    seq_low = seq_prob.astype(jnp.bfloat16)
    pre_low = pre_prob.astype(jnp.bfloat16)
    grad_queries = jnp.einsum(
        "hqk,khd->qhd", seq_dscore, seq_keys, preferred_element_type=jnp.float32
    )
    grad_queries = (
        grad_queries
        + jnp.einsum("hqk,khd->qhd", pre_dscore, pre_keys, preferred_element_type=jnp.float32)
    ) * score_scale
    key_term = (
        jnp.einsum("hqk,qhd->khd", seq_dscore, queries, preferred_element_type=jnp.float32)
        * score_scale
    )
    value_term = jnp.einsum("hqk,qhd->khd", seq_low, grad_heads, preferred_element_type=jnp.float32)
    grad_keys, grad_values = (
        lax.psum_scatter(key_term.reshape(-1, local_width), "dp", scatter_dimension=0, tiled=True),
        lax.psum_scatter(
            value_term.reshape(-1, local_width), "dp", scatter_dimension=0, tiled=True
        ),
    )
    pre_key_grad = (
        jnp.einsum("hqk,qhd->khd", pre_dscore, queries, preferred_element_type=jnp.float32)
        * score_scale
    )
    pre_value_grad = jnp.einsum(
        "hqk,qhd->khd", pre_low, grad_heads, preferred_element_type=jnp.float32
    )
    prefix_term = jnp.concatenate(
        [pre_key_grad.reshape(-1, local_width), pre_value_grad.reshape(-1, local_width)], axis=1
    )
    grad_mixed = jnp.concatenate(
        [grad_queries.reshape(tokens, local_width), grad_keys, grad_values], axis=1
    ).astype(jnp.bfloat16)
    grad_one = lax.psum_scatter(
        jnp.dot(grad_mixed, triple_weight.T, preferred_element_type=jnp.float32),
        "tensor",
        scatter_dimension=0,
        tiled=True,
    )
    grad_input = grad_residual + norm_back(grad_one, unit_one, inverse_one, gain_one)
    return (grad_input, prefix_term)


def shards(
    block_input,
    output_grad,
    valid_len,
    first_gain,
    first_bias,
    triple_weight,
    triple_bias,
    mixer_weight,
    mixer_bias,
    second_gain,
    second_bias,
    expand_weight,
    expand_bias,
    reduce_weight,
    reduce_bias,
    prefix_table,
    inner_weight,
    inner_bias,
    outer_weight,
    outer_bias,
):
    section_index = lax.axis_index("section")
    micro_count = block_input.shape[0]
    share_rows = block_input.shape[1]
    model_width = block_input.shape[2]
    local_width = triple_weight.shape[3]
    query_start = lax.axis_index("dp") * (share_rows * lax.axis_size("tensor"))
    weights = (
        first_gain[0],
        first_bias[0],
        triple_weight[0].reshape(-1, 3 * local_width),
        triple_bias[0].reshape(3 * local_width),
        mixer_weight[0],
        mixer_bias[0],
        second_gain[0],
        second_bias[0],
        expand_weight[0],
        expand_bias[0],
        reduce_weight[0],
        reduce_bias[0],
    )
    inner_pre = jnp.dot(prefix_table, inner_weight, preferred_element_type=jnp.float32) + inner_bias
    inner_act = jnp.tanh(inner_pre)
    inner_low = inner_act.astype(jnp.bfloat16)
    outer_local = outer_weight[:, 0].reshape(outer_weight.shape[0], 2 * local_width)
    prefix_full = (
        jnp.dot(inner_low, outer_local, preferred_element_type=jnp.float32)
        + outer_bias[0].reshape(2 * local_width)
    ).astype(jnp.bfloat16)
    moments = micro_count + 1
    carried = jnp.zeros((share_rows, model_width), jnp.bfloat16)
    results = []
    stored_states = []
    for moment in range(moments):
        micro_index = jnp.clip(moment - section_index, 0, micro_count - 1)
        inputs = jnp.where(
            section_index == 0, block_input[min(moment, micro_count - 1)], carried
        ).astype(jnp.float32)
        result, saved_state = layer_forward(
            inputs, weights, prefix_full, valid_len[micro_index], query_start
        )
        result_low = result.astype(jnp.bfloat16)
        results.append(result_low)
        stored_states.append(inputs)
        if moment + 1 < moments:
            carried = passed_along(result_low, "section", 1)
    grad_carried = jnp.zeros((share_rows, model_width), jnp.bfloat16)
    grad_list = []
    prefix_grad = jnp.zeros((prefix_full.shape[0], 2 * local_width), jnp.float32)
    for moment in range(moments):
        micro_index = moment - 1 + section_index
        valid_tick = (micro_index >= 0) & (micro_index < micro_count)
        clipped = jnp.clip(micro_index, 0, micro_count - 1)
        grad_in = jnp.where(
            section_index == 1, output_grad[min(moment, micro_count - 1)], grad_carried
        ).astype(jnp.float32)
        early_state = stored_states[max(moment - 1, 0)]
        late_state = stored_states[min(moment + 1, moments - 1)]
        picked = jnp.where(section_index == 0, early_state, late_state)
        picked_state = layer_forward(picked, weights, prefix_full, valid_len[clipped], query_start)[
            1
        ]
        grad_input, prefix_term = layer_backward(
            grad_in, picked_state, weights, prefix_full, valid_len[clipped], query_start
        )
        prefix_grad = prefix_grad + jnp.where(valid_tick, prefix_term, 0.0)
        grad_low = grad_input.astype(jnp.bfloat16)
        grad_list.append(grad_low)
        if moment + 1 < moments:
            grad_carried = passed_along(grad_low, "section", -1)
    layer_outputs = jnp.stack(
        [
            jnp.where(section_index == 0, results[number], results[number + 1])
            for number in range(micro_count)
        ]
    )[None]
    input_grads = jnp.stack(
        [
            jnp.where(section_index == 0, grad_list[number + 1], grad_list[number])
            for number in range(micro_count)
        ]
    )[None]
    prefix_total = lax.psum(prefix_grad, "dp")
    return (layer_outputs, input_grads) + prefix_back(
        prefix_total,
        prefix_full,
        inner_act,
        inner_low,
        outer_local,
        prefix_table,
        inner_weight,
        local_width,
    )


def dot_nn(left, right):
    return lax.dot_general(left, right, (((1,), (0,)), ((), ())), preferred_element_type=f32)


def dot_nt(left, right):
    return lax.dot_general(left, right, (((1,), (1,)), ((), ())), preferred_element_type=f32)


class Sizes:
    def __init__(self, planes, blocks, rows, width, local_width, hidden, prefix_rows):
        self.planes = planes
        self.blocks = blocks
        self.rows = rows
        self.block_rows = rows * planes
        self.width = width
        self.local_width = local_width
        self.hidden = hidden
        self.prefix_rows = prefix_rows
        self.cells = planes * blocks
        self.tile = 256


def both_layers(
    z,
    valid_ref,
    x_in,
    gy_in,
    vec_in,
    tbias_in,
    triple_in,
    mixer_in,
    expand_in,
    reduce_in,
    prefix_in,
    lo_out,
    ig_out,
    pg_out,
    vec,
    tbias,
    triple_own,
    wq,
    wm,
    we,
    wr,
    pre,
    xs,
    gys,
    qkv_send,
    qkv,
    ot_send,
    att,
    y_send,
    y_recv,
    gh_send,
    gh,
    dm_send,
    dm,
    gi_send,
    gi_recv,
    z_one,
    inv_one,
    z_two,
    inv_two,
    gelu_grad,
    probs,
    probs_pre,
    out_t,
    keys_n,
    normed,
    wide,
    total,
    grad_res,
    resid,
    dkeys,
    dvalues,
    y_last,
    gi_own,
    pg,
    pg_recv,
    pg_sum,
    pg_all,
    send_sem,
    recv_sem,
    local_sem,
):
    s = lax.axis_index("section")
    t = lax.axis_index("tensor")
    d = lax.axis_index("dp")
    nt, nb, rows, brows, tile = z.planes, z.blocks, z.rows, z.block_rows, z.tile
    cells = z.cells
    me = t * nb + d
    sib = (1 - s, t, d)
    counts = dict(send=0, recv=0, local=0)
    pending = []

    def claim(kind, number):
        first = counts[kind]
        counts[kind] += number
        return first

    def rcopy(src, dst, ss, rs, device):
        return pltpu.make_async_remote_copy(
            src_ref=src,
            dst_ref=dst,
            send_sem=send_sem.at[ss],
            recv_sem=recv_sem.at[rs],
            device_id=device,
            device_id_type=MESH,
        )

    def push(src, dst, rs, device, when=None):
        copy = rcopy(src, dst, claim("send", 1), rs, device)
        if when is None:
            copy.start()
            pending.append((copy, None))
        else:
            pl.when(when)(copy.start)
            pending.append((copy, when))

    def arrived(dst, rs, when=None):
        copy = rcopy(dst, dst, 0, rs, sib)
        if when is None:
            copy.wait_recv()
        else:
            pl.when(when)(copy.wait_recv)

    def lcopy(src, dst):
        copy = pltpu.make_async_copy(src, dst, local_sem.at[claim("local", 1)])
        copy.start()
        return copy

    def plane(k):
        return lax.rem(t + k, nt)

    def block(k):
        return lax.rem(d + k, nb)

    barrier = pltpu.get_barrier_semaphore()
    for k in range(1, cells):
        pl.semaphore_signal(
            barrier, inc=1, device_id=(s, plane(k // nb), block(k % nb)), device_id_type=MESH
        )
    pl.semaphore_signal(barrier, inc=1, device_id=sib, device_id_type=MESH)

    load_x = lcopy(x_in.at[s], xs.at[0, t])
    load_triple = lcopy(triple_in, triple_own)
    load_vec = lcopy(vec_in, vec.at[s])
    load_tbias = lcopy(tbias_in, tbias.at[s])
    load_pre = lcopy(prefix_in, pre.at[s])
    load_mixer = lcopy(mixer_in, wm.at[s, pl.ds(pl.multiple_of(t * z.local_width, 256), z.local_width)])
    load_expand = lcopy(expand_in, we.at[s])
    load_reduce = lcopy(reduce_in, wr.at[s])
    load_gy = lcopy(gy_in.at[s], gys.at[1, t])

    pl.semaphore_wait(barrier, cells)

    def spread(src, buf, layer):
        first = claim("recv", nt)
        for k in range(1, nt):
            push(src, buf.at[layer, t], first + k, (s, plane(k), d))
        return first

    def spread_wait(buf, layer, first, k):
        arrived(buf.at[layer, plane(nt - k)], first + k)

    x_first = [None, None]
    gy_first = [None, None]
    x_first[0] = spread(x_in.at[s], xs, 0)

    small = claim("recv", 3)
    push(vec_in, vec.at[s], small, sib)
    push(tbias_in, tbias.at[s], small + 1, sib)
    push(prefix_in, pre.at[s], small + 2, sib)

    mix_first = [claim("recv", nt), claim("recv", nt)]
    mix_second = [claim("recv", nt * nb), claim("recv", nt * nb)]
    mix_third = [claim("recv", 1), claim("recv", 1)]

    def piece(layer, p, q):
        return wm.at[layer, pl.ds(pl.multiple_of((p * nb + q) * (z.local_width // nb), 64), z.local_width // nb)]

    def mix_one(layer):
        part = z.local_width // nb
        for k in range(1, nt):
            push(
                mixer_in.at[pl.ds(pl.multiple_of(d * part, 64), part)],
                piece(layer, t, d),
                mix_first[layer] + k,
                (s, plane(k), d),
                s == layer,
            )

    def mix_two(layer):
        for k in range(1, nt):
            source = plane(nt - k)
            arrived(piece(layer, source, d), mix_first[layer] + k, s == layer)
            for q in range(1, nb):
                push(
                    piece(layer, source, d),
                    piece(layer, source, d),
                    mix_second[layer] + k * nb + q,
                    (s, t, block(q)),
                    s == layer,
                )

    def mix_three(layer):
        for k in range(1, nt):
            for q in range(1, nb):
                arrived(
                    piece(layer, plane(nt - k), block(nb - q)),
                    mix_second[layer] + k * nb + q,
                    s == layer,
                )
        push(wm.at[layer], wm.at[layer], mix_third[layer], sib, s == layer)

    mix_one(0)

    load_triple.wait()
    for c in range(3):
        for n in range(z.width // tile):
            turned = triple_own[c, n * tile : (n + 1) * tile, :].T
            for j in range(nb):
                wq[s, j, c * HD : (c + 1) * HD, n * tile : (n + 1) * tile] = turned[j * HD : (j + 1) * HD]
    wq_first = claim("recv", 1)
    push(wq.at[s], wq.at[s], wq_first, sib)
    load_vec.wait()
    load_tbias.wait()
    load_pre.wait()
    arrived(vec.at[1 - s], small)
    arrived(tbias.at[1 - s], small + 1)
    arrived(pre.at[1 - s], small + 2)

    def row(layer, index):
        return vec[layer, index : index + 1, :]

    step = 32

    def norm_one(layer, p):
        def some(i, _):
            at = pl.multiple_of(i * step, step)
            x = xs[layer, p, pl.ds(at, step), :].astype(f32)
            center = x - jnp.mean(x, axis=1, keepdims=True)
            inverse = lax.rsqrt(jnp.mean(center * center, axis=1, keepdims=True) + epsilon)
            unit = center * inverse
            where = pl.multiple_of(p * rows + at, step)
            z_one[layer, pl.ds(where, step), :] = unit
            inv_one[layer, pl.ds(where, step), :] = inverse
            normed[pl.ds(where, step), :] = (unit * row(layer, 0) + row(layer, 1)).astype(bf16)
            return 0

        lax.fori_loop(0, rows // step, some, 0)

    def norm_two(layer):
        def some(i, _):
            at = pl.multiple_of(i * step, step)
            x = resid[pl.ds(at, step), :]
            center = x - jnp.mean(x, axis=1, keepdims=True)
            inverse = lax.rsqrt(jnp.mean(center * center, axis=1, keepdims=True) + epsilon)
            unit = center * inverse
            z_two[layer, pl.ds(at, step), :] = unit
            inv_two[layer, pl.ds(at, step), :] = inverse
            normed[pl.ds(at, step), :] = (unit * row(layer, 3) + row(layer, 4)).astype(bf16)
            return 0

        lax.fori_loop(0, brows // step, some, 0)

    def norm_pull(i, units, inverses, gain):
        at = pl.multiple_of(i * step, step)
        unit = units[pl.ds(at, step), :]
        scaled = total[pl.ds(at, step), :] * gain
        mean_grad = jnp.mean(scaled, axis=1, keepdims=True)
        mean_cross = jnp.mean(scaled * unit, axis=1, keepdims=True)
        return at, inverses[pl.ds(at, step), :] * (scaled - mean_grad - unit * mean_cross)

    def tiles(count, body):
        def some(i, _):
            body(pl.multiple_of(i * tile, tile))
            return 0

        lax.fori_loop(0, count // tile, some, 0)

    def project(layer):
        first = claim("recv", nb)
        for k in range(1, nb + 1):
            head = block(k)
            part = dot_nt(wq[layer, head], normed[...])
            shift = tbias[layer, head].astype(f32)
            part = (part + jnp.concatenate([shift, shift], axis=1)).astype(bf16)
            if k < nb:
                qkv_send[layer, k] = part
                push(qkv_send.at[layer, k], qkv.at[layer, d], first + k, (s, t, head))
            else:
                qkv[layer, d] = part
        return first

    def attend(layer, first):
        out_first = claim("recv", cells)
        pre_keys = pre[layer, 0, d]
        pre_values = pre[layer, 1, d].T
        prefix_row = lax.broadcasted_iota(jnp.int32, (z.prefix_pad, brows), 0)
        key_at = lax.broadcasted_iota(jnp.int32, (brows, brows), 0)
        query_at = lax.broadcasted_iota(jnp.int32, (brows, brows), 1)
        valid = valid_ref[s]
        number = 0
        for b in range(nb):
            arrived(qkv.at[layer, b], first + lax.rem(d + nb - b, nb), d != b)
            keys_n[layer, b] = qkv[layer, b, HD : 2 * HD, :].T
            queries = (qkv[layer, b, 0:HD, :].astype(f32) * HD ** (-0.5)).astype(bf16)
            scores = dot_nn(pre_keys, queries)
            scores = jnp.where(prefix_row < z.prefix_rows, scores, masked_score)
            probs_pre[layer, b] = scores
            peak = jnp.max(scores, axis=0, keepdims=True)
            for kb in range(b + 1):
                scores = dot_nn(keys_n[layer, kb], queries)
                if kb == b:
                    seen = key_at <= query_at
                    if b == nb - 1:
                        seen = seen & (key_at + b * brows < valid)
                    scores = jnp.where(seen, scores, masked_score)
                probs[layer, number + kb] = scores
                peak = jnp.maximum(peak, jnp.max(scores, axis=0, keepdims=True))
            expons = jnp.exp(probs_pre[layer, b] - peak)
            probs_pre[layer, b] = expons
            denominator = jnp.sum(expons, axis=0, keepdims=True)
            for kb in range(b + 1):
                expons = jnp.exp(probs[layer, number + kb] - peak)
                probs[layer, number + kb] = expons
                denominator = denominator + jnp.sum(expons, axis=0, keepdims=True)
            scale = 1.0 / denominator
            prob = probs_pre[layer, b] * scale
            probs_pre[layer, b] = prob
            result = dot_nn(pre_values, prob.astype(bf16))
            for kb in range(b + 1):
                prob = probs[layer, number + kb] * scale
                probs[layer, number + kb] = prob
                result = result + dot_nn(qkv[layer, kb, 2 * HD : 3 * HD, :], prob.astype(bf16))
            number += b + 1
            out_t[layer, b] = result
            low = result.astype(bf16)
            ot_send[layer, b] = low
            for k in range(nt):
                if k == 0:
                    push(ot_send.at[layer, b], att.at[layer, me], out_first + me, (s, t, b), d != b)

                    @pl.when(d == b)
                    def _():
                        att[layer, me] = low
                else:
                    push(ot_send.at[layer, b], att.at[layer, me], out_first + me, (s, plane(k), b))
        return out_first

    def cells_wait(buf, layer, first):
        for cell in range(cells):
            arrived(buf.at[layer, cell], first + cell, me != cell)

    def mixer_rows(layer, first):
        cells_wait(att, layer, first)
        for p in range(nt):
            joined = att[layer, p * nb : (p + 1) * nb].reshape(nb * HD, brows)
            wide[:, p * nb * HD : (p + 1) * nb * HD] = joined.T

        def some(at):
            x = xs[layer, :, :, pl.ds(at, tile)].reshape(brows, tile).astype(f32)
            shift = vec[layer, 2:3, pl.ds(at, tile)]
            resid[:, pl.ds(at, tile)] = dot_nn(wide[...], wm[layer, :, pl.ds(at, tile)]) + x + shift

        tiles(z.width, some)

    def feed_first(layer):
        def some(at):
            v = dot_nn(normed[...], we[layer, :, pl.ds(at, tile)]) + vec[layer, 6:7, pl.ds(at, tile)]
            root = 0.7978845608028654
            square = v * v
            th = jnp.tanh(root * v * (1.0 + 0.044715 * square))
            half = 0.5 * (1.0 + th)
            wide[:, pl.ds(at, tile)] = (v * half).astype(bf16)
            gelu_grad[layer, :, pl.ds(at, tile)] = half + (0.5 * root) * v * (1.0 - th * th) * (
                1.0 + 3.0 * 0.044715 * square
            )

        tiles(z.hidden, some)

    def feed_second(layer):
        def some(at):
            part = dot_nn(wide[...], wr[layer, :, pl.ds(at, tile)])
            total[:, pl.ds(at, tile)] = part
            y_send[layer, :, :, pl.ds(at, tile)] = part.astype(bf16).reshape(nt, rows, tile)

        tiles(z.width, some)
        first = claim("recv", nt)
        for k in range(1, nt):
            push(y_send.at[layer, plane(k)], y_recv.at[layer, k], first + k, (s, plane(k), d))
        return first

    def own_rows(ref):
        return ref[pl.ds(pl.multiple_of(t * rows, rows), rows), :]

    def output_sum(layer, first, base):
        result = base
        for k in range(1, nt):
            arrived(y_recv.at[layer, k], first + k)
            result = result + y_recv[layer, k].astype(f32)
        return result.astype(bf16)

    out_sem = claim("recv", 4)
    out_loads = []

    def put(src, out, layer, index):
        push(src, out.at[0, s], out_sem + index, sib, s != layer)
        copy = pltpu.make_async_copy(src, out.at[0, s], local_sem.at[claim("local", 1)])
        pl.when(s == layer)(copy.start)
        out_loads.append((copy, s == layer))

    own_weights = [load_mixer, load_expand, load_reduce]
    feed_recv = claim("recv", 2)
    y_base = []
    out_first = None
    for layer in range(2):
        if layer == 0:
            load_x.wait()
        norm_one(layer, t)
        for k in range(1, nt):
            spread_wait(xs, layer, x_first[layer], k)
            norm_one(layer, plane(nt - k))
        if layer == 0:
            arrived(wq.at[0], wq_first, s == 1)
        else:
            arrived(wq.at[1], wq_first, s == 0)
        q_first = project(layer)
        if layer == 0:
            push(expand_in, we.at[s], feed_recv, sib)
            push(reduce_in, wr.at[s], feed_recv + 1, sib)
            mix_two(0)
            mix_one(1)
        else:
            load_gy.wait()
            gy_first[1] = spread(gys.at[1, t], gys, 1)
        out_first = attend(layer, q_first)
        if layer == 0:
            for copy in own_weights:
                copy.wait()
            arrived(we.at[1 - s], feed_recv)
            arrived(wr.at[1 - s], feed_recv + 1)
            mix_three(0)
        else:
            mix_three(1)
        arrived(wm.at[layer], mix_third[layer], s != layer)
        mixer_rows(layer, out_first)
        norm_two(layer)
        y_base.append(None)
        feed_first(layer)
        y_first = feed_second(layer)
        base = own_rows(resid) + own_rows(total) + row(layer, 5)
        if layer == 0:
            mix_two(1)
            low = output_sum(0, y_first, base)
            xs[1, t] = low
            x_first[1] = spread(xs.at[1, t], xs, 1)
            put(xs.at[1, t], lo_out, 0, 0)
        else:
            gi_own[...] = base
            last_first = y_first

    def grad_hidden(layer):
        def some(at):
            upper = gys[layer].reshape(brows, z.width)
            part = dot_nt(upper, wr[layer, pl.ds(at, tile), :])
            wide[:, pl.ds(at, tile)] = (part * gelu_grad[layer, :, pl.ds(at, tile)]).astype(bf16)

        tiles(z.hidden, some)

    def grad_mid(layer):
        def some(at):
            total[:, pl.ds(at, tile)] = dot_nt(wide[...], we[layer, pl.ds(at, tile), :])

        tiles(z.width, some)

        def pull(i, _):
            at, part = norm_pull(i, z_two.at[layer], inv_two.at[layer], row(layer, 3))
            upper = gys[layer, i // (rows // step), pl.ds(lax.rem(i, rows // step) * step, step), :]
            part = part + upper.astype(f32) * (1.0 / nt)
            grad_res[pl.ds(at, step), :] = part
            normed[pl.ds(at, step), :] = part.astype(bf16)
            return 0

        lax.fori_loop(0, brows // step, pull, 0)

    def grad_to_heads(layer):
        first = claim("recv", cells)
        for k in range(1, nt + 1):
            p = plane(k)
            here = wm[layer, pl.ds(pl.multiple_of(p * z.local_width, z.local_width), z.local_width), :]
            part = dot_nt(here, normed[...]).astype(bf16).reshape(nb, HD, brows)
            gh_send[layer, k - 1] = part
            for j in range(nb):
                away = None if k < nt else d != j
                push(gh_send.at[layer, k - 1, j], gh.at[layer, me], first + me, (s, p, j), away)
                if k == nt:

                    @pl.when(d == j)
                    def _():
                        gh[layer, me] = part[j]

        return first

    def attend_back(layer, first):
        cells_wait(gh, layer, first)
        out_first = claim("recv", nb)
        pre_values = pre[layer, 1, d]
        pre_keys = pre[layer, 0, d].T
        dkeys[...] = jnp.zeros_like(dkeys)
        dvalues[...] = jnp.zeros_like(dvalues)
        pre_dkeys = jnp.zeros((z.prefix_pad, HD), f32)
        pre_dvalues = jnp.zeros((z.prefix_pad, HD), f32)
        for b in reversed(range(nb)):
            number = b * (b + 1) // 2
            grad = gh[layer, b].astype(f32)
            for p in range(1, nt):
                grad = grad + gh[layer, p * nb + b].astype(f32)
            grad = grad.astype(bf16)
            delta = jnp.sum(grad.astype(f32) * out_t[layer, b], axis=0, keepdims=True)
            grad_n = grad.T
            queries = (qkv[layer, b, 0:HD, :].astype(f32) * HD ** (-0.5)).astype(bf16).T
            prob = probs_pre[layer, b]
            dscore = (prob * (dot_nn(pre_values, grad) - delta)).astype(bf16)
            dq = dot_nn(pre_keys, dscore)
            pre_dkeys = pre_dkeys + dot_nn(dscore, queries)
            pre_dvalues = pre_dvalues + dot_nn(prob.astype(bf16), grad_n)
            for kb in range(b + 1):
                prob = probs[layer, number + kb]
                values = qkv[layer, kb, 2 * HD : 3 * HD, :].T
                dscore = (prob * (dot_nn(values, grad) - delta)).astype(bf16)
                dq = dq + dot_nn(qkv[layer, kb, HD : 2 * HD, :], dscore)
                dkeys[kb] = dkeys[kb] + dot_nn(dscore, queries)
                dvalues[kb] = dvalues[kb] + dot_nn(prob.astype(bf16), grad_n)
            joined = jnp.concatenate(
                [dq * HD ** (-0.5), dkeys[b].T, dvalues[b].T], axis=0
            ).astype(bf16)
            dm_send[layer, b] = joined
            push(dm_send.at[layer, b], dm.at[layer, d], out_first + d, (s, t, b), d != b)

            @pl.when(d == b)
            def _():
                dm[layer, d] = joined

        pg[layer, 0] = pre_dkeys
        pg[layer, 1] = pre_dvalues
        return out_first

    def grad_rows(layer, first):
        for j in range(nb):
            arrived(dm.at[layer, j], first + j, d != j)
        for j in range(nb):
            wide[:, j * 3 * HD : (j + 1) * 3 * HD] = dm[layer, j].T
        depth = nb * 3 * HD

        def some(at):
            right = wq[layer, :, :, pl.ds(at, tile)].reshape(depth, tile)
            total[:, pl.ds(at, tile)] = dot_nn(wide[:, :depth], right)

        tiles(z.width, some)

        def pull(i, _):
            at, part = norm_pull(i, z_one.at[layer], inv_one.at[layer], row(layer, 0))
            part = part + grad_res[pl.ds(at, step), :]
            grad_res[pl.ds(at, step), :] = part
            p = i // (rows // step)
            gi_send[layer, p, pl.ds(lax.rem(i, rows // step) * step, step), :] = part.astype(bf16)
            return 0

        lax.fori_loop(0, brows // step, pull, 0)
        recv = claim("recv", nt)
        for k in range(1, nt):
            push(gi_send.at[layer, plane(k)], gi_recv.at[layer, k], recv + k, (s, plane(k), d))
        return recv

    def grad_sum(layer, first):
        result = own_rows(grad_res)
        for k in range(1, nt):
            arrived(gi_recv.at[layer, k], first + k)
            result = result + gi_recv[layer, k].astype(f32)
        return result.astype(bf16)

    for layer in (1, 0):
        for k in range(1, nt):
            spread_wait(gys, layer, gy_first[layer], k)
        grad_hidden(layer)
        grad_mid(layer)
        heads_first = grad_to_heads(layer)
        if layer == 1:
            y_last[...] = output_sum(1, last_first, gi_own[...])
            put(y_last, lo_out, 1, 1)
        rows_first = attend_back(layer, heads_first)
        grads_first = grad_rows(layer, rows_first)
        if layer == 1:
            gys[0, t] = grad_sum(1, grads_first)
            gy_first[0] = spread(gys.at[0, t], gys, 0)
            put(gys.at[0, t], ig_out, 1, 2)
        else:
            sib_sem = claim("recv", 1)
            push(pg.at[1 - s], pg_recv, sib_sem, sib)
            arrived(pg_recv, sib_sem)
            pg_sum[...] = pg[s] + pg_recv[...]
            all_first = claim("recv", nb)
            for k in range(1, nb):
                push(pg_sum, pg_all.at[d], all_first + k, (s, t, block(k)))
            pg_all[d] = pg_sum[...]
            y_last_two = grad_sum(0, grads_first)
            gi_low = y_last_two
            for k in range(1, nb):
                arrived(pg_all.at[block(nb - k)], all_first + k)
            pg_out[...] = pg_all[...]

    xs[0, t] = gi_low
    put(xs.at[0, t], ig_out, 0, 3)
    for index, (out, layer) in enumerate(((lo_out, 0), (lo_out, 1), (ig_out, 1), (ig_out, 0))):
        arrived(out.at[0, 1 - s], out_sem + index, s == layer)
    for copy, when in pending:
        if when is None:
            copy.wait_send()
        else:
            pl.when(when)(copy.wait_send)
    for copy, when in out_loads:
        pl.when(when)(copy.wait)
    z.counts = counts


def run_layers(z, valid_len, block_input, output_grad, vec, tbias, triple, mixer, expand, reduce, prefix):
    nt, nb, rows, brows = z.planes, z.blocks, z.rows, z.block_rows
    width, hidden = z.width, z.hidden
    pairs = nb * (nb + 1) // 2
    V = pltpu.VMEM
    any_space = pl.BlockSpec(memory_space=pl.ANY)
    scratch = [
        V((2, 8, width), f32),
        V((2, nb, 3 * HD, 128), bf16),
        V((3, width, z.local_width), bf16),
        V((2, nb, 3 * HD, width), bf16),
        V((2, width, width), bf16),
        V((2, width, hidden), bf16),
        V((2, hidden, width), bf16),
        V((2, 2, nb, z.prefix_pad, HD), bf16),
        V((2, nt, rows, width), bf16),
        V((2, nt, rows, width), bf16),
        V((2, nb, 3 * HD, brows), bf16),
        V((2, nb, 3 * HD, brows), bf16),
        V((2, nb, HD, brows), bf16),
        V((2, z.cells, HD, brows), bf16),
        V((2, nt, rows, width), bf16),
        V((2, nt, rows, width), bf16),
        V((2, nt, nb, HD, brows), bf16),
        V((2, z.cells, HD, brows), bf16),
        V((2, nb, 3 * HD, brows), bf16),
        V((2, nb, 3 * HD, brows), bf16),
        V((2, nt, rows, width), bf16),
        V((2, nt, rows, width), bf16),
        V((2, brows, width), f32),
        V((2, brows, 1), f32),
        V((2, brows, width), f32),
        V((2, brows, 1), f32),
        V((2, brows, hidden), f32),
        V((2, pairs, brows, brows), f32),
        V((2, nb, z.prefix_pad, brows), f32),
        V((2, nb, HD, brows), f32),
        V((2, nb, brows, HD), bf16),
        V((brows, width), bf16),
        V((brows, width), bf16),
        V((brows, width), f32),
        V((brows, width), f32),
        V((brows, width), f32),
        V((nb, brows, HD), f32),
        V((nb, brows, HD), f32),
        V((rows, width), bf16),
        V((rows, width), f32),
        V((2, 2, z.prefix_pad, HD), f32),
        V((2, z.prefix_pad, HD), f32),
        V((2, z.prefix_pad, HD), f32),
        V((nb, 2, z.prefix_pad, HD), f32),
        pltpu.SemaphoreType.DMA((200,)),
        pltpu.SemaphoreType.DMA((200,)),
        pltpu.SemaphoreType.DMA((20,)),
    ]
    return pl.pallas_call(
        partial(both_layers, z),
        out_shape=(
            jax.ShapeDtypeStruct((1, 2, rows, width), bf16),
            jax.ShapeDtypeStruct((1, 2, rows, width), bf16),
            jax.ShapeDtypeStruct((nb, 2, z.prefix_pad, HD), f32),
        ),
        in_specs=[pl.BlockSpec(memory_space=pltpu.SMEM)] + [any_space] * 9,
        out_specs=(any_space, any_space, pl.BlockSpec(memory_space=pltpu.VMEM)),
        scratch_shapes=scratch,
        compiler_params=pltpu.CompilerParams(
            collective_id=0, has_side_effects=True, vmem_limit_bytes=60 * 2**20
        ),
        cost_estimate=pl.CostEstimate(
            flops=7 * 10**9, bytes_accessed=16 * 2**20, transcendentals=4 * 10**6
        ),
    )(valid_len, block_input, output_grad, vec, tbias, triple, mixer, expand, reduce, prefix)


def head_a_device(
    block_input,
    output_grad,
    valid_len,
    first_gain,
    first_bias,
    triple_weight,
    triple_bias,
    mixer_weight,
    mixer_bias,
    second_gain,
    second_bias,
    expand_weight,
    expand_bias,
    reduce_weight,
    reduce_bias,
    prefix_table,
    inner_weight,
    inner_bias,
    outer_weight,
    outer_bias,
):
    planes, blocks = lax.axis_size("tensor"), lax.axis_size("dp")
    local_width = triple_weight.shape[3]
    prefix_rows = prefix_table.shape[0]
    z = Sizes(
        planes,
        blocks,
        block_input.shape[1],
        block_input.shape[2],
        local_width,
        expand_weight.shape[2],
        prefix_rows,
    )
    z.prefix_pad = -(-prefix_rows // 16) * 16
    inner_pre = jnp.dot(prefix_table, inner_weight, preferred_element_type=f32) + inner_bias
    inner_act = jnp.tanh(inner_pre)
    inner_low = inner_act.astype(bf16)
    outer_local = outer_weight[:, 0].reshape(outer_weight.shape[0], 2 * local_width)
    prefix_full = (
        jnp.dot(inner_low, outer_local, preferred_element_type=f32)
        + outer_bias[0].reshape(2 * local_width)
    ).astype(bf16)
    prefix_heads = prefix_full.reshape(prefix_rows, 2, blocks, HD).transpose(1, 2, 0, 3)
    prefix_heads = jnp.pad(prefix_heads, ((0, 0), (0, 0), (0, z.prefix_pad - prefix_rows), (0, 0)))
    vec = jnp.concatenate(
        [first_gain, first_bias, mixer_bias, second_gain, second_bias, reduce_bias, expand_bias, expand_bias],
        axis=0,
    ).astype(f32)
    tbias = triple_bias[0].reshape(3, blocks, HD).transpose(1, 0, 2).reshape(blocks, 3 * HD, 1)
    tbias = jnp.broadcast_to(tbias, (blocks, 3 * HD, 128))
    layer_outputs, input_grads, prefix_parts = run_layers(
        z,
        valid_len,
        block_input,
        output_grad,
        vec,
        tbias,
        triple_weight[0].transpose(1, 0, 2),
        mixer_weight[0],
        expand_weight[0],
        reduce_weight[0],
        prefix_heads,
    )
    prefix_total = (
        prefix_parts[:, :, :prefix_rows].transpose(2, 1, 0, 3).reshape(prefix_rows, 2 * local_width)
    )
    return (layer_outputs, input_grads) + prefix_back(
        prefix_total,
        prefix_full,
        inner_act,
        inner_low,
        outer_local,
        prefix_table,
        inner_weight,
        local_width,
    )


def prefix_back(
    prefix_total,
    prefix_full,
    inner_act,
    inner_low,
    outer_local,
    prefix_table,
    inner_weight,
    local_width,
):
    inner_float = inner_low.astype(f32)
    outer_float = outer_local.astype(f32)
    outer_weight_grad = jnp.dot(inner_float.T, prefix_total, precision=highest).reshape(
        -1, 1, 2, local_width
    )
    outer_bias_grad = jnp.sum(prefix_total, axis=0).reshape(1, 2, local_width)
    hidden_grad = lax.psum(
        jnp.dot(prefix_total, outer_float.T, precision=highest), ("section", "tensor")
    )
    inner_grad = hidden_grad * (1.0 - inner_act * inner_act)
    inner_weight_grad = jnp.dot(prefix_table.astype(f32).T, inner_grad, precision=highest)
    inner_bias_grad = jnp.sum(inner_grad, axis=0)
    table_grad = jnp.dot(inner_grad, inner_weight.astype(f32).T, precision=highest)
    prefix_states = prefix_full.reshape(-1, 2, local_width).transpose(1, 0, 2)[None]
    return (
        prefix_states,
        table_grad,
        inner_weight_grad,
        inner_bias_grad,
        outer_weight_grad,
        outer_bias_grad,
    )


def solution(mesh):
    def step(*args):
        triple_weight = args[5]
        micro_count, share_rows, width = args[0].shape
        fits = (
            lax.axis_size("section") == 2
            and micro_count == 2
            and triple_weight.shape[3] == HD * lax.axis_size("dp")
            and share_rows * lax.axis_size("tensor") == 256
            and triple_weight.shape[3] % 256 == 0
            and width % 256 == 0
            and args[11].shape[2] == width
        )
        return head_a_device(*args) if fits else shards(*args)

    return jax.shard_map(
        step,
        mesh=mesh,
        in_specs=(
            P(None, ("dp", "tensor"), None),
            P(None, ("dp", "tensor"), None),
            P(),
            P("section", None),
            P("section", None),
            P("section", None, None, "tensor"),
            P("section", None, "tensor"),
            P("section", "tensor", None),
            P("section", None),
            P("section", None),
            P("section", None),
            P("section", None, "tensor"),
            P("section", "tensor"),
            P("section", "tensor", None),
            P("section", None),
            P(),
            P(),
            P(),
            P(None, "section", None, "tensor"),
            P("section", None, "tensor"),
        ),
        out_specs=(
            P("section", None, ("dp", "tensor"), None),
            P("section", None, ("dp", "tensor"), None),
            P("section", None, None, "tensor"),
            P(),
            P(),
            P(),
            P(None, "section", None, "tensor"),
            P("section", None, "tensor"),
        ),
        check_vma=False,
    )
```

```python
from functools import partial

import jax
import jax.numpy as jnp
from jax import lax
from jax.experimental import pallas as pl
from jax.experimental.pallas import tpu as pltpu
from jax.sharding import PartitionSpec as P

HD = 64


epsilon = 1e-05
masked_score = -1e30
highest = lax.Precision.HIGHEST
MESH = pl.DeviceIdType.MESH
f32 = jnp.float32
bf16 = jnp.bfloat16


def passed_along(block, axis, distance):
    devices = range(lax.axis_size(axis))
    route = [(i - distance, i) for i in devices if i - distance in devices]
    return lax.ppermute(block, axis, route)


def layer_norm(values, norm_gain, norm_bias):
    center = values - jnp.mean(values, axis=-1, keepdims=True)
    variance = jnp.mean(center * center, axis=-1, keepdims=True)
    inverse = lax.rsqrt(variance + epsilon)
    normed = center * inverse
    return (normed * norm_gain + norm_bias, normed, inverse)


def norm_back(grad_out, normed, inverse, norm_gain):
    scaled = grad_out * norm_gain
    mean_grad = jnp.mean(scaled, axis=-1, keepdims=True)
    mean_cross = jnp.mean(scaled * normed, axis=-1, keepdims=True)
    return inverse * (scaled - mean_grad - normed * mean_cross)


def attention_scores(queries, seq_keys, pre_keys, valid, query_start):
    score_scale = HD ** (-0.5)
    seq_scores = (
        jnp.einsum("qhd,khd->hqk", queries, seq_keys, preferred_element_type=jnp.float32)
        * score_scale
    )
    pre_scores = (
        jnp.einsum("qhd,khd->hqk", queries, pre_keys, preferred_element_type=jnp.float32)
        * score_scale
    )
    query_pos = query_start + lax.broadcasted_iota(jnp.int32, (queries.shape[0], 1), 0)
    key_pos = lax.broadcasted_iota(jnp.int32, (1, seq_keys.shape[0]), 1)
    visible = (key_pos <= query_pos) & (key_pos < valid)
    seq_scores = jnp.where(visible[None], seq_scores, masked_score)
    return (seq_scores, pre_scores)


def split_prefix(prefix_full, local_width):
    local_heads = local_width // HD
    pre_keys = prefix_full[:, :local_width].reshape(-1, local_heads, HD)
    pre_values = prefix_full[:, local_width:].reshape(-1, local_heads, HD)
    return (pre_keys, pre_values)


def layer_forward(inputs, weights, prefix_full, valid, query_start):
    (
        gain_one,
        bias_one,
        triple_weight,
        triple_bias,
        mixer_weight,
        mixer_bias,
        gain_two,
        bias_two,
        expand_weight,
        expand_bias,
        reduce_weight,
        reduce_bias,
    ) = weights
    local_width = triple_weight.shape[1] // 3
    local_heads = local_width // HD
    normed_one, unit_one, inverse_one = layer_norm(inputs, gain_one, bias_one)
    mixed_rows = (
        jnp.dot(
            lax.all_gather(normed_one.astype(jnp.bfloat16), "tensor", axis=0, tiled=True),
            triple_weight,
            preferred_element_type=jnp.float32,
        )
        + triple_bias
    ).astype(jnp.bfloat16)
    tokens = mixed_rows.shape[0]
    queries = mixed_rows[:, :local_width].reshape(tokens, local_heads, HD)
    seq_keys, seq_values = (
        lax.all_gather(mixed_rows[:, local_width : 2 * local_width], "dp", axis=0, tiled=True),
        lax.all_gather(mixed_rows[:, 2 * local_width :], "dp", axis=0, tiled=True),
    )
    seq_keys = seq_keys.reshape(-1, local_heads, HD)
    seq_values = seq_values.reshape(-1, local_heads, HD)
    pre_keys, pre_values = split_prefix(prefix_full, local_width)
    seq_scores, pre_scores = attention_scores(queries, seq_keys, pre_keys, valid, query_start)
    row_max = jnp.maximum(
        jnp.max(seq_scores, axis=2, keepdims=True), jnp.max(pre_scores, axis=2, keepdims=True)
    )
    seq_exp = jnp.exp(seq_scores - row_max)
    pre_exp = jnp.exp(pre_scores - row_max)
    row_total = jnp.sum(seq_exp, axis=2, keepdims=True) + jnp.sum(pre_exp, axis=2, keepdims=True)
    log_total = row_max + jnp.log(row_total)
    seq_low = (seq_exp / row_total).astype(jnp.bfloat16)
    pre_low = (pre_exp / row_total).astype(jnp.bfloat16)
    attended = jnp.einsum("hqk,khd->qhd", seq_low, seq_values, preferred_element_type=jnp.float32)
    attended = attended + jnp.einsum(
        "hqk,khd->qhd", pre_low, pre_values, preferred_element_type=jnp.float32
    )
    attended = attended.astype(jnp.bfloat16).reshape(tokens, local_width)
    mixer_out = lax.psum_scatter(
        jnp.dot(attended, mixer_weight, preferred_element_type=jnp.float32),
        "tensor",
        scatter_dimension=0,
        tiled=True,
    )
    residual = inputs + mixer_out + mixer_bias
    normed_two, unit_two, inverse_two = layer_norm(residual, gain_two, bias_two)
    hidden_pre = (
        jnp.dot(
            lax.all_gather(normed_two.astype(jnp.bfloat16), "tensor", axis=0, tiled=True),
            expand_weight,
            preferred_element_type=jnp.float32,
        )
        + expand_bias
    )
    active = jax.nn.gelu(hidden_pre, approximate=True).astype(jnp.bfloat16)
    result = (
        residual
        + lax.psum_scatter(
            jnp.dot(active, reduce_weight, preferred_element_type=jnp.float32),
            "tensor",
            scatter_dimension=0,
            tiled=True,
        )
        + reduce_bias
    )
    saved_state = (
        unit_one,
        inverse_one,
        queries,
        seq_keys,
        seq_values,
        log_total,
        unit_two,
        inverse_two,
        hidden_pre,
    )
    return (result, saved_state)


def layer_backward(grad_out, saved_state, weights, prefix_full, valid, query_start):
    (
        gain_one,
        bias_one,
        triple_weight,
        triple_bias,
        mixer_weight,
        mixer_bias,
        gain_two,
        bias_two,
        expand_weight,
        expand_bias,
        reduce_weight,
        reduce_bias,
    ) = weights
    (
        unit_one,
        inverse_one,
        queries,
        seq_keys,
        seq_values,
        log_total,
        unit_two,
        inverse_two,
        hidden_pre,
    ) = saved_state
    tokens = queries.shape[0]
    local_heads = queries.shape[1]
    local_width = local_heads * HD
    score_scale = HD ** (-0.5)
    grad_active = jnp.dot(
        lax.all_gather(grad_out.astype(jnp.bfloat16), "tensor", axis=0, tiled=True),
        reduce_weight.T,
        preferred_element_type=jnp.float32,
    )
    gelu_pull = jax.vjp(partial(jax.nn.gelu, approximate=True), hidden_pre)[1]
    grad_pre = gelu_pull(grad_active)[0].astype(jnp.bfloat16)
    grad_two = lax.psum_scatter(
        jnp.dot(grad_pre, expand_weight.T, preferred_element_type=jnp.float32),
        "tensor",
        scatter_dimension=0,
        tiled=True,
    )
    grad_residual = grad_out + norm_back(grad_two, unit_two, inverse_two, gain_two)
    grad_heads = jnp.dot(
        lax.all_gather(grad_residual.astype(jnp.bfloat16), "tensor", axis=0, tiled=True),
        mixer_weight.T,
        preferred_element_type=jnp.float32,
    ).astype(jnp.bfloat16)
    grad_heads = grad_heads.reshape(tokens, local_heads, HD)
    pre_keys, pre_values = split_prefix(prefix_full, local_width)
    seq_scores, pre_scores = attention_scores(queries, seq_keys, pre_keys, valid, query_start)
    seq_prob = jnp.exp(seq_scores - log_total)
    pre_prob = jnp.exp(pre_scores - log_total)
    seq_dprob = jnp.einsum(
        "qhd,khd->hqk", grad_heads, seq_values, preferred_element_type=jnp.float32
    )
    pre_dprob = jnp.einsum(
        "qhd,khd->hqk", grad_heads, pre_values, preferred_element_type=jnp.float32
    )
    delta_row = jnp.sum(seq_prob * seq_dprob, axis=2, keepdims=True) + jnp.sum(
        pre_prob * pre_dprob, axis=2, keepdims=True
    )
    seq_dscore = (seq_prob * (seq_dprob - delta_row)).astype(jnp.bfloat16)
    pre_dscore = (pre_prob * (pre_dprob - delta_row)).astype(jnp.bfloat16)
    seq_low = seq_prob.astype(jnp.bfloat16)
    pre_low = pre_prob.astype(jnp.bfloat16)
    grad_queries = jnp.einsum(
        "hqk,khd->qhd", seq_dscore, seq_keys, preferred_element_type=jnp.float32
    )
    grad_queries = (
        grad_queries
        + jnp.einsum("hqk,khd->qhd", pre_dscore, pre_keys, preferred_element_type=jnp.float32)
    ) * score_scale
    key_term = (
        jnp.einsum("hqk,qhd->khd", seq_dscore, queries, preferred_element_type=jnp.float32)
        * score_scale
    )
    value_term = jnp.einsum("hqk,qhd->khd", seq_low, grad_heads, preferred_element_type=jnp.float32)
    grad_keys, grad_values = (
        lax.psum_scatter(key_term.reshape(-1, local_width), "dp", scatter_dimension=0, tiled=True),
        lax.psum_scatter(
            value_term.reshape(-1, local_width), "dp", scatter_dimension=0, tiled=True
        ),
    )
    pre_key_grad = (
        jnp.einsum("hqk,qhd->khd", pre_dscore, queries, preferred_element_type=jnp.float32)
        * score_scale
    )
    pre_value_grad = jnp.einsum(
        "hqk,qhd->khd", pre_low, grad_heads, preferred_element_type=jnp.float32
    )
    prefix_term = jnp.concatenate(
        [pre_key_grad.reshape(-1, local_width), pre_value_grad.reshape(-1, local_width)], axis=1
    )
    grad_mixed = jnp.concatenate(
        [grad_queries.reshape(tokens, local_width), grad_keys, grad_values], axis=1
    ).astype(jnp.bfloat16)
    grad_one = lax.psum_scatter(
        jnp.dot(grad_mixed, triple_weight.T, preferred_element_type=jnp.float32),
        "tensor",
        scatter_dimension=0,
        tiled=True,
    )
    grad_input = grad_residual + norm_back(grad_one, unit_one, inverse_one, gain_one)
    return (grad_input, prefix_term)


def shards(
    block_input,
    output_grad,
    valid_len,
    first_gain,
    first_bias,
    triple_weight,
    triple_bias,
    mixer_weight,
    mixer_bias,
    second_gain,
    second_bias,
    expand_weight,
    expand_bias,
    reduce_weight,
    reduce_bias,
    prefix_table,
    inner_weight,
    inner_bias,
    outer_weight,
    outer_bias,
):
    section_index = lax.axis_index("section")
    micro_count = block_input.shape[0]
    share_rows = block_input.shape[1]
    model_width = block_input.shape[2]
    local_width = triple_weight.shape[3]
    query_start = lax.axis_index("dp") * (share_rows * lax.axis_size("tensor"))
    weights = (
        first_gain[0],
        first_bias[0],
        triple_weight[0].reshape(-1, 3 * local_width),
        triple_bias[0].reshape(3 * local_width),
        mixer_weight[0],
        mixer_bias[0],
        second_gain[0],
        second_bias[0],
        expand_weight[0],
        expand_bias[0],
        reduce_weight[0],
        reduce_bias[0],
    )
    inner_pre = jnp.dot(prefix_table, inner_weight, preferred_element_type=jnp.float32) + inner_bias
    inner_act = jnp.tanh(inner_pre)
    inner_low = inner_act.astype(jnp.bfloat16)
    outer_local = outer_weight[:, 0].reshape(outer_weight.shape[0], 2 * local_width)
    prefix_full = (
        jnp.dot(inner_low, outer_local, preferred_element_type=jnp.float32)
        + outer_bias[0].reshape(2 * local_width)
    ).astype(jnp.bfloat16)
    moments = micro_count + 1
    carried = jnp.zeros((share_rows, model_width), jnp.bfloat16)
    results = []
    stored_states = []
    for moment in range(moments):
        micro_index = jnp.clip(moment - section_index, 0, micro_count - 1)
        inputs = jnp.where(
            section_index == 0, block_input[min(moment, micro_count - 1)], carried
        ).astype(jnp.float32)
        result, saved_state = layer_forward(
            inputs, weights, prefix_full, valid_len[micro_index], query_start
        )
        result_low = result.astype(jnp.bfloat16)
        results.append(result_low)
        stored_states.append(inputs)
        if moment + 1 < moments:
            carried = passed_along(result_low, "section", 1)
    grad_carried = jnp.zeros((share_rows, model_width), jnp.bfloat16)
    grad_list = []
    prefix_grad = jnp.zeros((prefix_full.shape[0], 2 * local_width), jnp.float32)
    for moment in range(moments):
        micro_index = moment - 1 + section_index
        valid_tick = (micro_index >= 0) & (micro_index < micro_count)
        clipped = jnp.clip(micro_index, 0, micro_count - 1)
        grad_in = jnp.where(
            section_index == 1, output_grad[min(moment, micro_count - 1)], grad_carried
        ).astype(jnp.float32)
        early_state = stored_states[max(moment - 1, 0)]
        late_state = stored_states[min(moment + 1, moments - 1)]
        picked = jnp.where(section_index == 0, early_state, late_state)
        picked_state = layer_forward(picked, weights, prefix_full, valid_len[clipped], query_start)[
            1
        ]
        grad_input, prefix_term = layer_backward(
            grad_in, picked_state, weights, prefix_full, valid_len[clipped], query_start
        )
        prefix_grad = prefix_grad + jnp.where(valid_tick, prefix_term, 0.0)
        grad_low = grad_input.astype(jnp.bfloat16)
        grad_list.append(grad_low)
        if moment + 1 < moments:
            grad_carried = passed_along(grad_low, "section", -1)
    layer_outputs = jnp.stack(
        [
            jnp.where(section_index == 0, results[number], results[number + 1])
            for number in range(micro_count)
        ]
    )[None]
    input_grads = jnp.stack(
        [
            jnp.where(section_index == 0, grad_list[number + 1], grad_list[number])
            for number in range(micro_count)
        ]
    )[None]
    prefix_total = lax.psum(prefix_grad, "dp")
    return (layer_outputs, input_grads) + prefix_back(
        prefix_total,
        prefix_full,
        inner_act,
        inner_low,
        outer_local,
        prefix_table,
        inner_weight,
        local_width,
    )


def dot_nn(left, right):
    return lax.dot_general(left, right, (((1,), (0,)), ((), ())), preferred_element_type=f32)


def dot_nt(left, right):
    return lax.dot_general(left, right, (((1,), (1,)), ((), ())), preferred_element_type=f32)


def dot_split(left, right, dot):
    high = left.astype(bf16)
    low = (left - high.astype(f32)).astype(bf16)
    return dot(high, right) + dot(low, right)


class Sizes:
    def __init__(self, planes, blocks, rows, width, local_width, hidden, prefix_rows):
        self.planes = planes
        self.blocks = blocks
        self.rows = rows
        self.block_rows = rows * planes
        self.width = width
        self.local_width = local_width
        self.hidden = hidden
        self.prefix_rows = prefix_rows
        self.cells = planes * blocks
        self.tile = 256


def both_layers(
    z,
    valid_ref,
    gain_one_in,
    bias_one_in,
    triple_bias_in,
    mixer_bias_in,
    gain_two_in,
    bias_two_in,
    expand_bias_in,
    reduce_bias_in,
    table_in,
    inner_bias_in,
    outer_bias_in,
    x_in,
    gy_in,
    triple_in,
    mixer_in,
    expand_in,
    reduce_in,
    inner_in,
    outer_in,
    lo_out,
    ig_out,
    pg_out,
    hidden_out,
    act_out,
    prefix_out,
    vec,
    tbias,
    triple_own,
    wq,
    wm,
    we,
    wr,
    pre,
    xs,
    gys,
    qkv_send,
    qkv,
    ot_send,
    att,
    y_send,
    y_recv,
    gh_send,
    gh,
    dm_send,
    dm,
    gi_send,
    gi_recv,
    z_one,
    inv_one,
    z_two,
    inv_two,
    gelu_grad,
    probs,
    probs_pre,
    out_t,
    keys_n,
    normed,
    wide,
    total,
    grad_res,
    resid,
    dkeys,
    dvalues,
    y_last,
    gi_own,
    pg,
    pg_recv,
    pg_sum,
    pg_all,
    table_pad,
    inner_w,
    outer_w,
    hid_part,
    hid_recv,
    hid_pair,
    hid_all,
    send_sem,
    recv_sem,
    local_sem,
):
    s = lax.axis_index("section")
    t = lax.axis_index("tensor")
    d = lax.axis_index("dp")
    nt, nb, rows, brows, tile = z.planes, z.blocks, z.rows, z.block_rows, z.tile
    cells = z.cells
    me = t * nb + d
    sib = (1 - s, t, d)
    counts = dict(send=0, recv=0, local=0)
    pending = []

    def claim(kind, number):
        first = counts[kind]
        counts[kind] += number
        return first

    def rcopy(src, dst, ss, rs, device):
        return pltpu.make_async_remote_copy(
            src_ref=src,
            dst_ref=dst,
            send_sem=send_sem.at[ss],
            recv_sem=recv_sem.at[rs],
            device_id=device,
            device_id_type=MESH,
        )

    def push(src, dst, rs, device, when=None):
        copy = rcopy(src, dst, claim("send", 1), rs, device)
        if when is None:
            copy.start()
            pending.append((copy, None))
        else:
            pl.when(when)(copy.start)
            pending.append((copy, when))

    def arrived(dst, rs, when=None):
        copy = rcopy(dst, dst, 0, rs, sib)
        if when is None:
            copy.wait_recv()
        else:
            pl.when(when)(copy.wait_recv)

    def lcopy(src, dst):
        copy = pltpu.make_async_copy(src, dst, local_sem.at[claim("local", 1)])
        copy.start()
        return copy

    def plane(k):
        return lax.rem(t + k, nt)

    def block(k):
        return lax.rem(d + k, nb)

    barrier = pltpu.get_barrier_semaphore()
    for k in range(1, cells):
        pl.semaphore_signal(
            barrier, inc=1, device_id=(s, plane(k // nb), block(k % nb)), device_id_type=MESH
        )
    pl.semaphore_signal(barrier, inc=1, device_id=sib, device_id_type=MESH)

    load_x = lcopy(x_in.at[s], xs.at[0, t])
    load_triple = lcopy(triple_in, triple_own)
    load_inner = lcopy(inner_in, inner_w)
    load_outer = lcopy(outer_in, outer_w)
    load_mixer = lcopy(mixer_in, wm.at[s, pl.ds(pl.multiple_of(t * z.local_width, 256), z.local_width)])
    load_expand = lcopy(expand_in, we.at[s])
    load_reduce = lcopy(reduce_in, wr.at[s])
    load_gy = lcopy(gy_in.at[s], gys.at[1, t])

    for index, ref in enumerate(
        (gain_one_in, bias_one_in, mixer_bias_in, gain_two_in, bias_two_in, reduce_bias_in, expand_bias_in)
    ):
        vec[s, index : index + 1, :] = ref[...].astype(f32)
    for c in range(3):
        shift = jnp.broadcast_to(triple_bias_in[0, c : c + 1, :].astype(f32), (128, z.local_width)).T
        for j in range(nb):
            tbias[s, j, c * HD : (c + 1) * HD, :] = shift[j * HD : (j + 1) * HD].astype(bf16)
    table_pad[...] = jnp.zeros_like(table_pad)
    table_pad[0 : z.prefix_rows, :] = table_in[...].astype(f32)

    pl.semaphore_wait(barrier, cells)

    def spread(src, buf, layer):
        first = claim("recv", nt)
        for k in range(1, nt):
            push(src, buf.at[layer, t], first + k, (s, plane(k), d))
        return first

    def spread_wait(buf, layer, first, k):
        arrived(buf.at[layer, plane(nt - k)], first + k)

    x_first = [None, None]
    gy_first = [None, None]
    x_first[0] = spread(x_in.at[s], xs, 0)

    small = claim("recv", 3)
    push(vec.at[s], vec.at[s], small, sib)
    push(tbias.at[s], tbias.at[s], small + 1, sib)

    mix_first = [claim("recv", nt), claim("recv", nt)]
    mix_second = [claim("recv", nt * nb), claim("recv", nt * nb)]
    mix_third = [claim("recv", 1), claim("recv", 1)]

    def piece(layer, p, q):
        return wm.at[layer, pl.ds(pl.multiple_of((p * nb + q) * (z.local_width // nb), 64), z.local_width // nb)]

    def mix_one(layer):
        part = z.local_width // nb
        for k in range(1, nt):
            push(
                mixer_in.at[pl.ds(pl.multiple_of(d * part, 64), part)],
                piece(layer, t, d),
                mix_first[layer] + k,
                (s, plane(k), d),
                s == layer,
            )

    def mix_two(layer):
        for k in range(1, nt):
            source = plane(nt - k)
            arrived(piece(layer, source, d), mix_first[layer] + k, s == layer)
            for q in range(1, nb):
                push(
                    piece(layer, source, d),
                    piece(layer, source, d),
                    mix_second[layer] + k * nb + q,
                    (s, t, block(q)),
                    s == layer,
                )

    def mix_three(layer):
        for k in range(1, nt):
            for q in range(1, nb):
                arrived(
                    piece(layer, plane(nt - k), block(nb - q)),
                    mix_second[layer] + k * nb + q,
                    s == layer,
                )
        push(wm.at[layer], wm.at[layer], mix_third[layer], sib, s == layer)

    mix_one(0)

    load_triple.wait()
    for c in range(3):
        for n in range(z.width // tile):
            turned = triple_own[c, n * tile : (n + 1) * tile, :].T
            for j in range(nb):
                wq[s, j, c * HD : (c + 1) * HD, n * tile : (n + 1) * tile] = turned[j * HD : (j + 1) * HD]
    wq_first = claim("recv", 1)
    push(wq.at[s], wq.at[s], wq_first, sib)
    load_inner.wait()
    inner_act = jnp.tanh(
        dot_nn(table_pad[...].astype(bf16), inner_w[...]) + inner_bias_in[...].astype(f32)
    )
    act_out[...] = inner_act
    load_outer.wait()
    prefix = (dot_nn(inner_act.astype(bf16), outer_w[...]) + outer_bias_in[...].astype(f32)).astype(bf16)
    prefix_out[...] = prefix
    for c in range(2):
        for j in range(nb):
            at = c * z.local_width + j * HD
            pre[s, c, j] = prefix[:, at : at + HD]
    push(pre.at[s], pre.at[s], small + 2, sib)
    arrived(vec.at[1 - s], small)
    arrived(tbias.at[1 - s], small + 1)
    arrived(pre.at[1 - s], small + 2)

    def row(layer, index):
        return vec[layer, index : index + 1, :]

    step = 32

    def norm_one(layer, p):
        def some(i, _):
            at = pl.multiple_of(i * step, step)
            x = xs[layer, p, pl.ds(at, step), :].astype(f32)
            center = x - jnp.mean(x, axis=1, keepdims=True)
            inverse = lax.rsqrt(jnp.mean(center * center, axis=1, keepdims=True) + epsilon)
            unit = center * inverse
            where = pl.multiple_of(p * rows + at, step)
            z_one[layer, pl.ds(where, step), :] = unit
            inv_one[layer, pl.ds(where, step), :] = inverse
            normed[pl.ds(where, step), :] = (unit * row(layer, 0) + row(layer, 1)).astype(bf16)
            return 0

        lax.fori_loop(0, rows // step, some, 0, unroll=True)

    def norm_two(layer):
        def some(i, _):
            at = pl.multiple_of(i * step, step)
            x = resid[pl.ds(at, step), :]
            center = x - jnp.mean(x, axis=1, keepdims=True)
            inverse = lax.rsqrt(jnp.mean(center * center, axis=1, keepdims=True) + epsilon)
            unit = center * inverse
            z_two[layer, pl.ds(at, step), :] = unit
            inv_two[layer, pl.ds(at, step), :] = inverse
            normed[pl.ds(at, step), :] = (unit * row(layer, 3) + row(layer, 4)).astype(bf16)
            return 0

        lax.fori_loop(0, brows // step, some, 0, unroll=True)

    def norm_pull(i, units, inverses, gain):
        at = pl.multiple_of(i * step, step)
        unit = units[pl.ds(at, step), :]
        scaled = total[pl.ds(at, step), :] * gain
        mean_grad = jnp.mean(scaled, axis=1, keepdims=True)
        mean_cross = jnp.mean(scaled * unit, axis=1, keepdims=True)
        return at, inverses[pl.ds(at, step), :] * (scaled - mean_grad - unit * mean_cross)

    def tiles(count, body):
        def some(i, _):
            body(pl.multiple_of(i * tile, tile))
            return 0

        lax.fori_loop(0, count // tile, some, 0, unroll=True)

    def project(layer):
        first = claim("recv", nb)
        for k in range(1, nb + 1):
            head = block(k)
            part = dot_nt(wq[layer, head], normed[...])
            shift = tbias[layer, head].astype(f32)
            part = (part + jnp.concatenate([shift, shift], axis=1)).astype(bf16)
            if k < nb:
                qkv_send[layer, k] = part
                push(qkv_send.at[layer, k], qkv.at[layer, d], first + k, (s, t, head))
            else:
                qkv[layer, d] = part
        return first

    def attend(layer, first):
        out_first = claim("recv", cells)
        pre_keys = pre[layer, 0, d]
        pre_values = pre[layer, 1, d].T
        prefix_row = lax.broadcasted_iota(jnp.int32, (z.prefix_pad, brows), 0)
        key_at = lax.broadcasted_iota(jnp.int32, (brows, brows), 0)
        query_at = lax.broadcasted_iota(jnp.int32, (brows, brows), 1)
        valid = valid_ref[s]
        number = 0
        for b in range(nb):
            arrived(qkv.at[layer, b], first + lax.rem(d + nb - b, nb), d != b)
            keys_n[layer, b] = qkv[layer, b, HD : 2 * HD, :].T
            queries = (qkv[layer, b, 0:HD, :].astype(f32) * HD ** (-0.5)).astype(bf16)
            scores = dot_nn(pre_keys, queries)
            scores = jnp.where(prefix_row < z.prefix_rows, scores, masked_score)
            probs_pre[layer, b] = scores
            peak = jnp.max(scores, axis=0, keepdims=True)
            for kb in range(b + 1):
                scores = dot_nn(keys_n[layer, kb], queries)
                if kb == b:
                    seen = key_at <= query_at
                    if b == nb - 1:
                        seen = seen & (key_at + b * brows < valid)
                    scores = jnp.where(seen, scores, masked_score)
                probs[layer, number + kb] = scores
                peak = jnp.maximum(peak, jnp.max(scores, axis=0, keepdims=True))
            expons = jnp.exp(probs_pre[layer, b] - peak)
            probs_pre[layer, b] = expons
            denominator = jnp.sum(expons, axis=0, keepdims=True)
            for kb in range(b + 1):
                expons = jnp.exp(probs[layer, number + kb] - peak)
                probs[layer, number + kb] = expons
                denominator = denominator + jnp.sum(expons, axis=0, keepdims=True)
            scale = 1.0 / denominator
            prob = probs_pre[layer, b] * scale
            probs_pre[layer, b] = prob
            result = dot_nn(pre_values, prob.astype(bf16))
            for kb in range(b + 1):
                prob = probs[layer, number + kb] * scale
                probs[layer, number + kb] = prob
                result = result + dot_nn(qkv[layer, kb, 2 * HD : 3 * HD, :], prob.astype(bf16))
            number += b + 1
            out_t[layer, b] = result
            low = result.astype(bf16)
            ot_send[layer, b] = low
            for k in range(nt):
                if k == 0:
                    push(ot_send.at[layer, b], att.at[layer, me], out_first + me, (s, t, b), d != b)

                    @pl.when(d == b)
                    def _():
                        att[layer, me] = low
                else:
                    push(ot_send.at[layer, b], att.at[layer, me], out_first + me, (s, plane(k), b))
        return out_first

    def cells_wait(buf, layer, first):
        for cell in range(cells):
            arrived(buf.at[layer, cell], first + cell, me != cell)

    def mixer_rows(layer, first):
        cells_wait(att, layer, first)
        for p in range(nt):
            joined = att[layer, p * nb : (p + 1) * nb].reshape(nb * HD, brows)
            wide[:, p * nb * HD : (p + 1) * nb * HD] = joined.T

        def some(at):
            x = xs[layer, :, :, pl.ds(at, tile)].reshape(brows, tile).astype(f32)
            shift = vec[layer, 2:3, pl.ds(at, tile)]
            resid[:, pl.ds(at, tile)] = dot_nn(wide[...], wm[layer, :, pl.ds(at, tile)]) + x + shift

        tiles(z.width, some)

    def feed_first(layer):
        def some(at):
            v = dot_nn(normed[...], we[layer, :, pl.ds(at, tile)]) + vec[layer, 6:7, pl.ds(at, tile)]
            root = 0.7978845608028654
            square = v * v
            th = jnp.tanh(root * v * (1.0 + 0.044715 * square))
            half = 0.5 * (1.0 + th)
            wide[:, pl.ds(at, tile)] = (v * half).astype(bf16)
            gelu_grad[layer, :, pl.ds(at, tile)] = half + (0.5 * root) * v * (1.0 - th * th) * (
                1.0 + 3.0 * 0.044715 * square
            )

        tiles(z.hidden, some)

    def feed_second(layer):
        def some(at):
            part = dot_nn(wide[...], wr[layer, :, pl.ds(at, tile)])
            total[:, pl.ds(at, tile)] = part
            y_send[layer, :, :, pl.ds(at, tile)] = part.astype(bf16).reshape(nt, rows, tile)

        tiles(z.width, some)
        first = claim("recv", nt)
        for k in range(1, nt):
            push(y_send.at[layer, plane(k)], y_recv.at[layer, k], first + k, (s, plane(k), d))
        return first

    def own_rows(ref):
        return ref[pl.ds(pl.multiple_of(t * rows, rows), rows), :]

    def output_sum(layer, first, base):
        result = base
        for k in range(1, nt):
            arrived(y_recv.at[layer, k], first + k)
            result = result + y_recv[layer, k].astype(f32)
        return result.astype(bf16)

    out_sem = claim("recv", 4)
    out_loads = []

    def put(src, out, layer, index):
        push(src, out.at[0, s], out_sem + index, sib, s != layer)
        copy = pltpu.make_async_copy(src, out.at[0, s], local_sem.at[claim("local", 1)])
        pl.when(s == layer)(copy.start)
        out_loads.append((copy, s == layer))

    own_weights = [load_mixer, load_expand, load_reduce]
    feed_recv = claim("recv", 2)
    y_base = []
    out_first = None
    for layer in range(2):
        if layer == 0:
            load_x.wait()
        norm_one(layer, t)
        for k in range(1, nt):
            spread_wait(xs, layer, x_first[layer], k)
            norm_one(layer, plane(nt - k))
        if layer == 0:
            arrived(wq.at[0], wq_first, s == 1)
        else:
            arrived(wq.at[1], wq_first, s == 0)
        q_first = project(layer)
        if layer == 0:
            push(expand_in, we.at[s], feed_recv, sib)
            push(reduce_in, wr.at[s], feed_recv + 1, sib)
            mix_two(0)
            mix_one(1)
        else:
            load_gy.wait()
            gy_first[1] = spread(gys.at[1, t], gys, 1)
        out_first = attend(layer, q_first)
        if layer == 0:
            for copy in own_weights:
                copy.wait()
            arrived(we.at[1 - s], feed_recv)
            arrived(wr.at[1 - s], feed_recv + 1)
            mix_three(0)
        else:
            mix_three(1)
        arrived(wm.at[layer], mix_third[layer], s != layer)
        mixer_rows(layer, out_first)
        norm_two(layer)
        y_base.append(None)
        feed_first(layer)
        y_first = feed_second(layer)
        base = own_rows(resid) + own_rows(total) + row(layer, 5)
        if layer == 0:
            mix_two(1)
            low = output_sum(0, y_first, base)
            xs[1, t] = low
            x_first[1] = spread(xs.at[1, t], xs, 1)
            put(xs.at[1, t], lo_out, 0, 0)
        else:
            gi_own[...] = base
            last_first = y_first

    def grad_hidden(layer):
        def some(at):
            upper = gys[layer].reshape(brows, z.width)
            part = dot_nt(upper, wr[layer, pl.ds(at, tile), :])
            wide[:, pl.ds(at, tile)] = (part * gelu_grad[layer, :, pl.ds(at, tile)]).astype(bf16)

        tiles(z.hidden, some)

    def grad_mid(layer):
        def some(at):
            total[:, pl.ds(at, tile)] = dot_nt(wide[...], we[layer, pl.ds(at, tile), :])

        tiles(z.width, some)

        def pull(i, _):
            at, part = norm_pull(i, z_two.at[layer], inv_two.at[layer], row(layer, 3))
            upper = gys[layer, i // (rows // step), pl.ds(lax.rem(i, rows // step) * step, step), :]
            part = part + upper.astype(f32) * (1.0 / nt)
            grad_res[pl.ds(at, step), :] = part
            normed[pl.ds(at, step), :] = part.astype(bf16)
            return 0

        lax.fori_loop(0, brows // step, pull, 0, unroll=True)

    def grad_to_heads(layer):
        first = claim("recv", cells)
        for k in range(1, nt + 1):
            p = plane(k)
            here = wm[layer, pl.ds(pl.multiple_of(p * z.local_width, z.local_width), z.local_width), :]
            part = dot_nt(here, normed[...]).astype(bf16).reshape(nb, HD, brows)
            gh_send[layer, k - 1] = part
            for j in range(nb):
                away = None if k < nt else d != j
                push(gh_send.at[layer, k - 1, j], gh.at[layer, me], first + me, (s, p, j), away)
                if k == nt:

                    @pl.when(d == j)
                    def _():
                        gh[layer, me] = part[j]

        return first

    def attend_back(layer, first):
        cells_wait(gh, layer, first)
        out_first = claim("recv", nb)
        pre_values = pre[layer, 1, d]
        pre_keys = pre[layer, 0, d].T
        dkeys[...] = jnp.zeros_like(dkeys)
        dvalues[...] = jnp.zeros_like(dvalues)
        pre_dkeys = jnp.zeros((z.prefix_pad, HD), f32)
        pre_dvalues = jnp.zeros((z.prefix_pad, HD), f32)
        for b in reversed(range(nb)):
            number = b * (b + 1) // 2
            grad = gh[layer, b].astype(f32)
            for p in range(1, nt):
                grad = grad + gh[layer, p * nb + b].astype(f32)
            grad = grad.astype(bf16)
            delta = jnp.sum(grad.astype(f32) * out_t[layer, b], axis=0, keepdims=True)
            grad_n = grad.T
            queries = (qkv[layer, b, 0:HD, :].astype(f32) * HD ** (-0.5)).astype(bf16).T
            prob = probs_pre[layer, b]
            dscore = (prob * (dot_nn(pre_values, grad) - delta)).astype(bf16)
            dq = dot_nn(pre_keys, dscore)
            pre_dkeys = pre_dkeys + dot_nn(dscore, queries)
            pre_dvalues = pre_dvalues + dot_nn(prob.astype(bf16), grad_n)
            for kb in range(b + 1):
                prob = probs[layer, number + kb]
                values = qkv[layer, kb, 2 * HD : 3 * HD, :].T
                dscore = (prob * (dot_nn(values, grad) - delta)).astype(bf16)
                dq = dq + dot_nn(qkv[layer, kb, HD : 2 * HD, :], dscore)
                dkeys[kb] = dkeys[kb] + dot_nn(dscore, queries)
                dvalues[kb] = dvalues[kb] + dot_nn(prob.astype(bf16), grad_n)
            joined = jnp.concatenate(
                [dq * HD ** (-0.5), dkeys[b].T, dvalues[b].T], axis=0
            ).astype(bf16)
            dm_send[layer, b] = joined
            push(dm_send.at[layer, b], dm.at[layer, d], out_first + d, (s, t, b), d != b)

            @pl.when(d == b)
            def _():
                dm[layer, d] = joined

        pg[layer, 0] = pre_dkeys
        pg[layer, 1] = pre_dvalues
        return out_first

    def grad_rows(layer, first):
        for j in range(nb):
            arrived(dm.at[layer, j], first + j, d != j)
        for j in range(nb):
            wide[:, j * 3 * HD : (j + 1) * 3 * HD] = dm[layer, j].T
        depth = nb * 3 * HD

        def some(at):
            right = wq[layer, :, :, pl.ds(at, tile)].reshape(depth, tile)
            total[:, pl.ds(at, tile)] = dot_nn(wide[:, :depth], right)

        tiles(z.width, some)

        def pull(i, _):
            at, part = norm_pull(i, z_one.at[layer], inv_one.at[layer], row(layer, 0))
            part = part + grad_res[pl.ds(at, step), :]
            grad_res[pl.ds(at, step), :] = part
            p = i // (rows // step)
            gi_send[layer, p, pl.ds(lax.rem(i, rows // step) * step, step), :] = part.astype(bf16)
            return 0

        lax.fori_loop(0, brows // step, pull, 0, unroll=True)
        recv = claim("recv", nt)
        for k in range(1, nt):
            push(gi_send.at[layer, plane(k)], gi_recv.at[layer, k], recv + k, (s, plane(k), d))
        return recv

    def grad_sum(layer, first):
        result = own_rows(grad_res)
        for k in range(1, nt):
            arrived(gi_recv.at[layer, k], first + k)
            result = result + gi_recv[layer, k].astype(f32)
        return result.astype(bf16)

    for layer in (1, 0):
        for k in range(1, nt):
            spread_wait(gys, layer, gy_first[layer], k)
        grad_hidden(layer)
        grad_mid(layer)
        heads_first = grad_to_heads(layer)
        if layer == 1:
            y_last[...] = output_sum(1, last_first, gi_own[...])
            put(y_last, lo_out, 1, 1)
        rows_first = attend_back(layer, heads_first)
        if layer == 0:
            sib_sem = claim("recv", 1)
            push(pg.at[1 - s], pg_recv, sib_sem, sib)
            arrived(pg_recv, sib_sem)
            pg_sum[...] = pg[s] + pg_recv[...]
            all_first = claim("recv", nb)
            for k in range(1, nb):
                push(pg_sum, pg_all.at[d], all_first + k, (s, t, block(k)))
            pg_all[d] = pg_sum[...]
        grads_first = grad_rows(layer, rows_first)
        if layer == 1:
            gys[0, t] = grad_sum(1, grads_first)
            gy_first[0] = spread(gys.at[0, t], gys, 0)
            put(gys.at[0, t], ig_out, 1, 2)
        else:
            for k in range(1, nb):
                arrived(pg_all.at[block(nb - k)], all_first + k)
            pg_out[...] = pg_all[...]
            part = jnp.zeros((z.prefix_pad, z.inner), f32)
            for j in range(nb):
                for c in range(2):
                    at = c * z.local_width + j * HD
                    part = part + dot_split(pg_all[j, c], outer_w[:, at : at + HD], dot_nt)
            hid_part[...] = part
            hid_sem = claim("recv", 1)
            push(hid_part, hid_recv, hid_sem, sib)
            arrived(hid_recv, hid_sem)
            hid_pair[...] = hid_part[...] + hid_recv[...]
            hid_first = claim("recv", nt)
            for k in range(1, nt):
                push(hid_pair, hid_all.at[t], hid_first + k, (s, plane(k), d))
            hid_all[t] = hid_pair[...]
            gi_low = grad_sum(0, grads_first)
            xs[0, t] = gi_low
            put(xs.at[0, t], ig_out, 0, 3)
            for k in range(1, nt):
                arrived(hid_all.at[plane(nt - k)], hid_first + k)
            part = hid_all[0]
            for p in range(1, nt):
                part = part + hid_all[p]
            hidden_out[...] = part

    for index, (out, layer) in enumerate(((lo_out, 0), (lo_out, 1), (ig_out, 1), (ig_out, 0))):
        arrived(out.at[0, 1 - s], out_sem + index, s == layer)
    for copy, when in pending:
        if when is None:
            copy.wait_send()
        else:
            pl.when(when)(copy.wait_send)
    for copy, when in out_loads:
        pl.when(when)(copy.wait)
    z.counts = counts


def run_layers(z, small, large):
    nt, nb, rows, brows = z.planes, z.blocks, z.rows, z.block_rows
    width, hidden = z.width, z.hidden
    pairs = nb * (nb + 1) // 2
    V = pltpu.VMEM
    any_space = pl.BlockSpec(memory_space=pl.ANY)
    scratch = [
        V((2, 8, width), f32),
        V((2, nb, 3 * HD, 128), bf16),
        V((3, width, z.local_width), bf16),
        V((2, nb, 3 * HD, width), bf16),
        V((2, width, width), bf16),
        V((2, width, hidden), bf16),
        V((2, hidden, width), bf16),
        V((2, 2, nb, z.prefix_pad, HD), bf16),
        V((2, nt, rows, width), bf16),
        V((2, nt, rows, width), bf16),
        V((2, nb, 3 * HD, brows), bf16),
        V((2, nb, 3 * HD, brows), bf16),
        V((2, nb, HD, brows), bf16),
        V((2, z.cells, HD, brows), bf16),
        V((2, nt, rows, width), bf16),
        V((2, nt, rows, width), bf16),
        V((2, nt, nb, HD, brows), bf16),
        V((2, z.cells, HD, brows), bf16),
        V((2, nb, 3 * HD, brows), bf16),
        V((2, nb, 3 * HD, brows), bf16),
        V((2, nt, rows, width), bf16),
        V((2, nt, rows, width), bf16),
        V((2, brows, width), f32),
        V((2, brows, 1), f32),
        V((2, brows, width), f32),
        V((2, brows, 1), f32),
        V((2, brows, hidden), f32),
        V((2, pairs, brows, brows), f32),
        V((2, nb, z.prefix_pad, brows), f32),
        V((2, nb, HD, brows), f32),
        V((2, nb, brows, HD), bf16),
        V((brows, width), bf16),
        V((brows, width), bf16),
        V((brows, width), f32),
        V((brows, width), f32),
        V((brows, width), f32),
        V((nb, brows, HD), f32),
        V((nb, brows, HD), f32),
        V((rows, width), bf16),
        V((rows, width), f32),
        V((2, 2, z.prefix_pad, HD), f32),
        V((2, z.prefix_pad, HD), f32),
        V((2, z.prefix_pad, HD), f32),
        V((nb, 2, z.prefix_pad, HD), f32),
        V((z.prefix_pad, width), f32),
        V((width, z.inner), bf16),
        V((z.inner, 2 * z.local_width), bf16),
        V((z.prefix_pad, z.inner), f32),
        V((z.prefix_pad, z.inner), f32),
        V((z.prefix_pad, z.inner), f32),
        V((nt, z.prefix_pad, z.inner), f32),
        pltpu.SemaphoreType.DMA((200,)),
        pltpu.SemaphoreType.DMA((200,)),
        pltpu.SemaphoreType.DMA((20,)),
    ]
    return pl.pallas_call(
        partial(both_layers, z),
        out_shape=(
            jax.ShapeDtypeStruct((1, 2, rows, width), bf16),
            jax.ShapeDtypeStruct((1, 2, rows, width), bf16),
            jax.ShapeDtypeStruct((nb, 2, z.prefix_pad, HD), f32),
            jax.ShapeDtypeStruct((z.prefix_pad, z.inner), f32),
            jax.ShapeDtypeStruct((z.prefix_pad, z.inner), f32),
            jax.ShapeDtypeStruct((z.prefix_pad, 2 * z.local_width), bf16),
        ),
        in_specs=[pl.BlockSpec(memory_space=pltpu.SMEM)]
        + [pl.BlockSpec(memory_space=pltpu.VMEM)] * (len(small) - 1)
        + [any_space] * len(large),
        out_specs=(any_space,) * 2 + (pl.BlockSpec(memory_space=pltpu.VMEM),) * 4,
        scratch_shapes=scratch,
        compiler_params=pltpu.CompilerParams(
            collective_id=0, has_side_effects=True, vmem_limit_bytes=60 * 2**20
        ),
        cost_estimate=pl.CostEstimate(
            flops=7 * 10**9, bytes_accessed=16 * 2**20, transcendentals=4 * 10**6
        ),
    )(*small, *large)


def prefix_end(
    z, lo_in, ig_in, pg_in, hidden_in, act_in, prefix_in, table_in, inner_in,
    lo_out, ig_out, states_out, table_out, inner_out, inner_bias_out, outer_out, outer_bias_out,
    table_pad, sems,
):
    copies = [
        pltpu.make_async_copy(lo_in, lo_out, sems.at[0]),
        pltpu.make_async_copy(ig_in, ig_out, sems.at[1]),
    ]
    for copy in copies:
        copy.start()
    count, width = z.prefix_rows, z.local_width
    act = act_in[...]
    inner_grad = hidden_in[...] * (1.0 - act * act)
    inner_bias_out[...] = jnp.sum(inner_grad, axis=0, keepdims=True)
    table_pad[...] = jnp.zeros_like(table_pad)
    table_pad[0:count, :] = table_in[...].astype(f32)
    high = inner_grad.astype(bf16)
    low = (inner_grad - high.astype(f32)).astype(bf16)
    table_turned = table_pad[...].T.astype(bf16)
    inner_out[...] = dot_nn(table_turned, high) + dot_nn(table_turned, low)
    table_out[...] = (dot_nt(high, inner_in[...]) + dot_nt(low, inner_in[...]))[0:count]
    act_turned = act.T.astype(bf16)
    for c in range(2):
        states_out[0, c] = prefix_in[0:count, c * width : (c + 1) * width]
        total = jnp.concatenate([pg_in[j, c] for j in range(z.blocks)], axis=1)
        high = total.astype(bf16)
        low = (total - high.astype(f32)).astype(bf16)
        outer_out[:, c, :] = dot_nn(act_turned, high) + dot_nn(act_turned, low)
        outer_bias_out[0, c : c + 1, :] = jnp.sum(total, axis=0, keepdims=True)
    for copy in copies:
        copy.wait()


def finish(z, layer_outputs, input_grads, parts, hidden, act, prefix, table, inner_weight):
    any_space = pl.BlockSpec(memory_space=pl.ANY)
    whole = pl.BlockSpec(memory_space=pltpu.VMEM)
    rows = jax.ShapeDtypeStruct(layer_outputs.shape, bf16)
    return pl.pallas_call(
        partial(prefix_end, z),
        out_shape=(
            rows,
            rows,
            jax.ShapeDtypeStruct((1, 2, z.prefix_rows, z.local_width), bf16),
            jax.ShapeDtypeStruct((z.prefix_rows, z.width), f32),
            jax.ShapeDtypeStruct((z.width, z.inner), f32),
            jax.ShapeDtypeStruct((1, z.inner), f32),
            jax.ShapeDtypeStruct((z.inner, 2, z.local_width), f32),
            jax.ShapeDtypeStruct((1, 2, z.local_width), f32),
        ),
        in_specs=[any_space] * 2 + [whole] * 6,
        out_specs=(any_space,) * 2 + (whole,) * 6,
        scratch_shapes=[pltpu.VMEM((z.prefix_pad, z.width), f32), pltpu.SemaphoreType.DMA((2,))],
        compiler_params=pltpu.CompilerParams(vmem_limit_bytes=32 * 2**20),
    )(layer_outputs, input_grads, parts, hidden, act, prefix, table, inner_weight)


def head_a_device(
    block_input,
    output_grad,
    valid_len,
    first_gain,
    first_bias,
    triple_weight,
    triple_bias,
    mixer_weight,
    mixer_bias,
    second_gain,
    second_bias,
    expand_weight,
    expand_bias,
    reduce_weight,
    reduce_bias,
    prefix_table,
    inner_weight,
    inner_bias,
    outer_weight,
    outer_bias,
):
    planes, blocks = lax.axis_size("tensor"), lax.axis_size("dp")
    local_width = triple_weight.shape[3]
    prefix_rows = prefix_table.shape[0]
    z = Sizes(
        planes,
        blocks,
        block_input.shape[1],
        block_input.shape[2],
        local_width,
        expand_weight.shape[2],
        prefix_rows,
    )
    z.prefix_pad = -(-prefix_rows // 16) * 16
    z.inner = inner_weight.shape[1]
    outer_local = outer_weight[:, 0].reshape(outer_weight.shape[0], 2 * local_width)
    small = (
        valid_len,
        first_gain,
        first_bias,
        triple_bias,
        mixer_bias,
        second_gain,
        second_bias,
        expand_bias,
        reduce_bias,
        prefix_table,
        inner_bias.reshape(1, -1),
        outer_bias.reshape(1, -1),
    )
    large = (
        block_input,
        output_grad,
        triple_weight[0].transpose(1, 0, 2),
        mixer_weight[0],
        expand_weight[0],
        reduce_weight[0],
        inner_weight,
        outer_local,
    )
    results = finish(z, *run_layers(z, small, large), prefix_table, inner_weight)
    (
        layer_outputs,
        input_grads,
        prefix_states,
        table_grad,
        inner_weight_grad,
        inner_bias_grad,
        outer_weight_grad,
        outer_bias_grad,
    ) = results
    return (
        layer_outputs,
        input_grads,
        prefix_states,
        table_grad,
        inner_weight_grad,
        inner_bias_grad.reshape(-1),
        outer_weight_grad.reshape(-1, 1, 2, local_width),
        outer_bias_grad,
    )


def prefix_back(
    prefix_total,
    prefix_full,
    inner_act,
    inner_low,
    outer_local,
    prefix_table,
    inner_weight,
    local_width,
):
    inner_float = inner_low.astype(f32)
    outer_float = outer_local.astype(f32)
    outer_weight_grad = jnp.dot(inner_float.T, prefix_total, precision=highest).reshape(
        -1, 1, 2, local_width
    )
    outer_bias_grad = jnp.sum(prefix_total, axis=0).reshape(1, 2, local_width)
    hidden_grad = lax.psum(
        jnp.dot(prefix_total, outer_float.T, precision=highest), ("section", "tensor")
    )
    inner_grad = hidden_grad * (1.0 - inner_act * inner_act)
    inner_weight_grad = jnp.dot(prefix_table.astype(f32).T, inner_grad, precision=highest)
    inner_bias_grad = jnp.sum(inner_grad, axis=0)
    table_grad = jnp.dot(inner_grad, inner_weight.astype(f32).T, precision=highest)
    prefix_states = prefix_full.reshape(-1, 2, local_width).transpose(1, 0, 2)[None]
    return (
        prefix_states,
        table_grad,
        inner_weight_grad,
        inner_bias_grad,
        outer_weight_grad,
        outer_bias_grad,
    )


def solution(mesh):
    def step(*args):
        triple_weight = args[5]
        micro_count, share_rows, width = args[0].shape
        fits = (
            lax.axis_size("section") == 2
            and micro_count == 2
            and triple_weight.shape[3] == HD * lax.axis_size("dp")
            and share_rows * lax.axis_size("tensor") == 256
            and triple_weight.shape[3] % 256 == 0
            and width % 256 == 0
            and args[11].shape[2] == width
        )
        return head_a_device(*args) if fits else shards(*args)

    return jax.shard_map(
        step,
        mesh=mesh,
        in_specs=(
            P(None, ("dp", "tensor"), None),
            P(None, ("dp", "tensor"), None),
            P(),
            P("section", None),
            P("section", None),
            P("section", None, None, "tensor"),
            P("section", None, "tensor"),
            P("section", "tensor", None),
            P("section", None),
            P("section", None),
            P("section", None),
            P("section", None, "tensor"),
            P("section", "tensor"),
            P("section", "tensor", None),
            P("section", None),
            P(),
            P(),
            P(),
            P(None, "section", None, "tensor"),
            P("section", None, "tensor"),
        ),
        out_specs=(
            P("section", None, ("dp", "tensor"), None),
            P("section", None, ("dp", "tensor"), None),
            P("section", None, None, "tensor"),
            P(),
            P(),
            P(),
            P(None, "section", None, "tensor"),
            P("section", None, "tensor"),
        ),
        check_vma=False,
    )
```

```python
from functools import partial

import jax
import jax.numpy as jnp
from jax import lax
from jax.experimental import pallas as pl
from jax.experimental.pallas import tpu as pltpu
from jax.sharding import PartitionSpec as P

HD = 64


epsilon = 1e-05
masked_score = -1e30
highest = lax.Precision.HIGHEST
MESH = pl.DeviceIdType.MESH
f32 = jnp.float32
bf16 = jnp.bfloat16


def passed_along(block, axis, distance):
    devices = range(lax.axis_size(axis))
    route = [(i - distance, i) for i in devices if i - distance in devices]
    return lax.ppermute(block, axis, route)


def layer_norm(values, norm_gain, norm_bias):
    center = values - jnp.mean(values, axis=-1, keepdims=True)
    variance = jnp.mean(center * center, axis=-1, keepdims=True)
    inverse = lax.rsqrt(variance + epsilon)
    normed = center * inverse
    return (normed * norm_gain + norm_bias, normed, inverse)


def norm_back(grad_out, normed, inverse, norm_gain):
    scaled = grad_out * norm_gain
    mean_grad = jnp.mean(scaled, axis=-1, keepdims=True)
    mean_cross = jnp.mean(scaled * normed, axis=-1, keepdims=True)
    return inverse * (scaled - mean_grad - normed * mean_cross)


def attention_scores(queries, seq_keys, pre_keys, valid, query_start):
    score_scale = HD ** (-0.5)
    seq_scores = (
        jnp.einsum("qhd,khd->hqk", queries, seq_keys, preferred_element_type=jnp.float32)
        * score_scale
    )
    pre_scores = (
        jnp.einsum("qhd,khd->hqk", queries, pre_keys, preferred_element_type=jnp.float32)
        * score_scale
    )
    query_pos = query_start + lax.broadcasted_iota(jnp.int32, (queries.shape[0], 1), 0)
    key_pos = lax.broadcasted_iota(jnp.int32, (1, seq_keys.shape[0]), 1)
    visible = (key_pos <= query_pos) & (key_pos < valid)
    seq_scores = jnp.where(visible[None], seq_scores, masked_score)
    return (seq_scores, pre_scores)


def split_prefix(prefix_full, local_width):
    local_heads = local_width // HD
    pre_keys = prefix_full[:, :local_width].reshape(-1, local_heads, HD)
    pre_values = prefix_full[:, local_width:].reshape(-1, local_heads, HD)
    return (pre_keys, pre_values)


def layer_forward(inputs, weights, prefix_full, valid, query_start):
    (
        gain_one,
        bias_one,
        triple_weight,
        triple_bias,
        mixer_weight,
        mixer_bias,
        gain_two,
        bias_two,
        expand_weight,
        expand_bias,
        reduce_weight,
        reduce_bias,
    ) = weights
    local_width = triple_weight.shape[1] // 3
    local_heads = local_width // HD
    normed_one, unit_one, inverse_one = layer_norm(inputs, gain_one, bias_one)
    mixed_rows = (
        jnp.dot(
            lax.all_gather(normed_one.astype(jnp.bfloat16), "tensor", axis=0, tiled=True),
            triple_weight,
            preferred_element_type=jnp.float32,
        )
        + triple_bias
    ).astype(jnp.bfloat16)
    tokens = mixed_rows.shape[0]
    queries = mixed_rows[:, :local_width].reshape(tokens, local_heads, HD)
    seq_keys, seq_values = (
        lax.all_gather(mixed_rows[:, local_width : 2 * local_width], "dp", axis=0, tiled=True),
        lax.all_gather(mixed_rows[:, 2 * local_width :], "dp", axis=0, tiled=True),
    )
    seq_keys = seq_keys.reshape(-1, local_heads, HD)
    seq_values = seq_values.reshape(-1, local_heads, HD)
    pre_keys, pre_values = split_prefix(prefix_full, local_width)
    seq_scores, pre_scores = attention_scores(queries, seq_keys, pre_keys, valid, query_start)
    row_max = jnp.maximum(
        jnp.max(seq_scores, axis=2, keepdims=True), jnp.max(pre_scores, axis=2, keepdims=True)
    )
    seq_exp = jnp.exp(seq_scores - row_max)
    pre_exp = jnp.exp(pre_scores - row_max)
    row_total = jnp.sum(seq_exp, axis=2, keepdims=True) + jnp.sum(pre_exp, axis=2, keepdims=True)
    log_total = row_max + jnp.log(row_total)
    seq_low = (seq_exp / row_total).astype(jnp.bfloat16)
    pre_low = (pre_exp / row_total).astype(jnp.bfloat16)
    attended = jnp.einsum("hqk,khd->qhd", seq_low, seq_values, preferred_element_type=jnp.float32)
    attended = attended + jnp.einsum(
        "hqk,khd->qhd", pre_low, pre_values, preferred_element_type=jnp.float32
    )
    attended = attended.astype(jnp.bfloat16).reshape(tokens, local_width)
    mixer_out = lax.psum_scatter(
        jnp.dot(attended, mixer_weight, preferred_element_type=jnp.float32),
        "tensor",
        scatter_dimension=0,
        tiled=True,
    )
    residual = inputs + mixer_out + mixer_bias
    normed_two, unit_two, inverse_two = layer_norm(residual, gain_two, bias_two)
    hidden_pre = (
        jnp.dot(
            lax.all_gather(normed_two.astype(jnp.bfloat16), "tensor", axis=0, tiled=True),
            expand_weight,
            preferred_element_type=jnp.float32,
        )
        + expand_bias
    )
    active = jax.nn.gelu(hidden_pre, approximate=True).astype(jnp.bfloat16)
    result = (
        residual
        + lax.psum_scatter(
            jnp.dot(active, reduce_weight, preferred_element_type=jnp.float32),
            "tensor",
            scatter_dimension=0,
            tiled=True,
        )
        + reduce_bias
    )
    saved_state = (
        unit_one,
        inverse_one,
        queries,
        seq_keys,
        seq_values,
        log_total,
        unit_two,
        inverse_two,
        hidden_pre,
    )
    return (result, saved_state)


def layer_backward(grad_out, saved_state, weights, prefix_full, valid, query_start):
    (
        gain_one,
        bias_one,
        triple_weight,
        triple_bias,
        mixer_weight,
        mixer_bias,
        gain_two,
        bias_two,
        expand_weight,
        expand_bias,
        reduce_weight,
        reduce_bias,
    ) = weights
    (
        unit_one,
        inverse_one,
        queries,
        seq_keys,
        seq_values,
        log_total,
        unit_two,
        inverse_two,
        hidden_pre,
    ) = saved_state
    tokens = queries.shape[0]
    local_heads = queries.shape[1]
    local_width = local_heads * HD
    score_scale = HD ** (-0.5)
    grad_active = jnp.dot(
        lax.all_gather(grad_out.astype(jnp.bfloat16), "tensor", axis=0, tiled=True),
        reduce_weight.T,
        preferred_element_type=jnp.float32,
    )
    gelu_pull = jax.vjp(partial(jax.nn.gelu, approximate=True), hidden_pre)[1]
    grad_pre = gelu_pull(grad_active)[0].astype(jnp.bfloat16)
    grad_two = lax.psum_scatter(
        jnp.dot(grad_pre, expand_weight.T, preferred_element_type=jnp.float32),
        "tensor",
        scatter_dimension=0,
        tiled=True,
    )
    grad_residual = grad_out + norm_back(grad_two, unit_two, inverse_two, gain_two)
    grad_heads = jnp.dot(
        lax.all_gather(grad_residual.astype(jnp.bfloat16), "tensor", axis=0, tiled=True),
        mixer_weight.T,
        preferred_element_type=jnp.float32,
    ).astype(jnp.bfloat16)
    grad_heads = grad_heads.reshape(tokens, local_heads, HD)
    pre_keys, pre_values = split_prefix(prefix_full, local_width)
    seq_scores, pre_scores = attention_scores(queries, seq_keys, pre_keys, valid, query_start)
    seq_prob = jnp.exp(seq_scores - log_total)
    pre_prob = jnp.exp(pre_scores - log_total)
    seq_dprob = jnp.einsum(
        "qhd,khd->hqk", grad_heads, seq_values, preferred_element_type=jnp.float32
    )
    pre_dprob = jnp.einsum(
        "qhd,khd->hqk", grad_heads, pre_values, preferred_element_type=jnp.float32
    )
    delta_row = jnp.sum(seq_prob * seq_dprob, axis=2, keepdims=True) + jnp.sum(
        pre_prob * pre_dprob, axis=2, keepdims=True
    )
    seq_dscore = (seq_prob * (seq_dprob - delta_row)).astype(jnp.bfloat16)
    pre_dscore = (pre_prob * (pre_dprob - delta_row)).astype(jnp.bfloat16)
    seq_low = seq_prob.astype(jnp.bfloat16)
    pre_low = pre_prob.astype(jnp.bfloat16)
    grad_queries = jnp.einsum(
        "hqk,khd->qhd", seq_dscore, seq_keys, preferred_element_type=jnp.float32
    )
    grad_queries = (
        grad_queries
        + jnp.einsum("hqk,khd->qhd", pre_dscore, pre_keys, preferred_element_type=jnp.float32)
    ) * score_scale
    key_term = (
        jnp.einsum("hqk,qhd->khd", seq_dscore, queries, preferred_element_type=jnp.float32)
        * score_scale
    )
    value_term = jnp.einsum("hqk,qhd->khd", seq_low, grad_heads, preferred_element_type=jnp.float32)
    grad_keys, grad_values = (
        lax.psum_scatter(key_term.reshape(-1, local_width), "dp", scatter_dimension=0, tiled=True),
        lax.psum_scatter(
            value_term.reshape(-1, local_width), "dp", scatter_dimension=0, tiled=True
        ),
    )
    pre_key_grad = (
        jnp.einsum("hqk,qhd->khd", pre_dscore, queries, preferred_element_type=jnp.float32)
        * score_scale
    )
    pre_value_grad = jnp.einsum(
        "hqk,qhd->khd", pre_low, grad_heads, preferred_element_type=jnp.float32
    )
    prefix_term = jnp.concatenate(
        [pre_key_grad.reshape(-1, local_width), pre_value_grad.reshape(-1, local_width)], axis=1
    )
    grad_mixed = jnp.concatenate(
        [grad_queries.reshape(tokens, local_width), grad_keys, grad_values], axis=1
    ).astype(jnp.bfloat16)
    grad_one = lax.psum_scatter(
        jnp.dot(grad_mixed, triple_weight.T, preferred_element_type=jnp.float32),
        "tensor",
        scatter_dimension=0,
        tiled=True,
    )
    grad_input = grad_residual + norm_back(grad_one, unit_one, inverse_one, gain_one)
    return (grad_input, prefix_term)


def shards(
    block_input,
    output_grad,
    valid_len,
    first_gain,
    first_bias,
    triple_weight,
    triple_bias,
    mixer_weight,
    mixer_bias,
    second_gain,
    second_bias,
    expand_weight,
    expand_bias,
    reduce_weight,
    reduce_bias,
    prefix_table,
    inner_weight,
    inner_bias,
    outer_weight,
    outer_bias,
):
    section_index = lax.axis_index("section")
    micro_count = block_input.shape[0]
    share_rows = block_input.shape[1]
    model_width = block_input.shape[2]
    local_width = triple_weight.shape[3]
    query_start = lax.axis_index("dp") * (share_rows * lax.axis_size("tensor"))
    weights = (
        first_gain[0],
        first_bias[0],
        triple_weight[0].reshape(-1, 3 * local_width),
        triple_bias[0].reshape(3 * local_width),
        mixer_weight[0],
        mixer_bias[0],
        second_gain[0],
        second_bias[0],
        expand_weight[0],
        expand_bias[0],
        reduce_weight[0],
        reduce_bias[0],
    )
    inner_pre = jnp.dot(prefix_table, inner_weight, preferred_element_type=jnp.float32) + inner_bias
    inner_act = jnp.tanh(inner_pre)
    inner_low = inner_act.astype(jnp.bfloat16)
    outer_local = outer_weight[:, 0].reshape(outer_weight.shape[0], 2 * local_width)
    prefix_full = (
        jnp.dot(inner_low, outer_local, preferred_element_type=jnp.float32)
        + outer_bias[0].reshape(2 * local_width)
    ).astype(jnp.bfloat16)
    moments = micro_count + 1
    carried = jnp.zeros((share_rows, model_width), jnp.bfloat16)
    results = []
    stored_states = []
    for moment in range(moments):
        micro_index = jnp.clip(moment - section_index, 0, micro_count - 1)
        inputs = jnp.where(
            section_index == 0, block_input[min(moment, micro_count - 1)], carried
        ).astype(jnp.float32)
        result, saved_state = layer_forward(
            inputs, weights, prefix_full, valid_len[micro_index], query_start
        )
        result_low = result.astype(jnp.bfloat16)
        results.append(result_low)
        stored_states.append(inputs)
        if moment + 1 < moments:
            carried = passed_along(result_low, "section", 1)
    grad_carried = jnp.zeros((share_rows, model_width), jnp.bfloat16)
    grad_list = []
    prefix_grad = jnp.zeros((prefix_full.shape[0], 2 * local_width), jnp.float32)
    for moment in range(moments):
        micro_index = moment - 1 + section_index
        valid_tick = (micro_index >= 0) & (micro_index < micro_count)
        clipped = jnp.clip(micro_index, 0, micro_count - 1)
        grad_in = jnp.where(
            section_index == 1, output_grad[min(moment, micro_count - 1)], grad_carried
        ).astype(jnp.float32)
        early_state = stored_states[max(moment - 1, 0)]
        late_state = stored_states[min(moment + 1, moments - 1)]
        picked = jnp.where(section_index == 0, early_state, late_state)
        picked_state = layer_forward(picked, weights, prefix_full, valid_len[clipped], query_start)[
            1
        ]
        grad_input, prefix_term = layer_backward(
            grad_in, picked_state, weights, prefix_full, valid_len[clipped], query_start
        )
        prefix_grad = prefix_grad + jnp.where(valid_tick, prefix_term, 0.0)
        grad_low = grad_input.astype(jnp.bfloat16)
        grad_list.append(grad_low)
        if moment + 1 < moments:
            grad_carried = passed_along(grad_low, "section", -1)
    layer_outputs = jnp.stack(
        [
            jnp.where(section_index == 0, results[number], results[number + 1])
            for number in range(micro_count)
        ]
    )[None]
    input_grads = jnp.stack(
        [
            jnp.where(section_index == 0, grad_list[number + 1], grad_list[number])
            for number in range(micro_count)
        ]
    )[None]
    prefix_total = lax.psum(prefix_grad, "dp")
    return (layer_outputs, input_grads) + prefix_back(
        prefix_total,
        prefix_full,
        inner_act,
        inner_low,
        outer_local,
        prefix_table,
        inner_weight,
        local_width,
    )


def dot_nn(left, right):
    return lax.dot_general(left, right, (((1,), (0,)), ((), ())), preferred_element_type=f32)


def dot_nt(left, right):
    return lax.dot_general(left, right, (((1,), (1,)), ((), ())), preferred_element_type=f32)


def dot_split(left, right, dot):
    high = left.astype(bf16)
    low = (left - high.astype(f32)).astype(bf16)
    return dot(high, right) + dot(low, right)


class Sizes:
    def __init__(self, planes, blocks, rows, width, local_width, hidden, prefix_rows):
        self.planes = planes
        self.blocks = blocks
        self.rows = rows
        self.block_rows = rows * planes
        self.width = width
        self.local_width = local_width
        self.hidden = hidden
        self.prefix_rows = prefix_rows
        self.cells = planes * blocks
        self.tile = 256


def both_layers(
    z,
    valid_ref,
    gain_one_in,
    bias_one_in,
    triple_bias_in,
    mixer_bias_in,
    gain_two_in,
    bias_two_in,
    expand_bias_in,
    reduce_bias_in,
    table_in,
    inner_bias_in,
    outer_bias_in,
    x_in,
    gy_in,
    triple_in,
    mixer_in,
    expand_in,
    reduce_in,
    inner_in,
    outer_in,
    rows_out,
    parts_out,
    vec,
    tbias,
    triple_own,
    wq,
    wm,
    we,
    wr,
    pre,
    xs,
    gys,
    qkv_send,
    qkv,
    ot_send,
    att,
    y_send,
    y_recv,
    gh_send,
    gh,
    dm_send,
    dm,
    gi_send,
    gi_recv,
    y_relay,
    gi_relay,
    gh_relay,
    z_one,
    inv_one,
    z_two,
    inv_two,
    gelu_grad,
    probs,
    probs_pre,
    out_t,
    keys_n,
    normed,
    wide,
    total,
    grad_res,
    resid,
    dkeys,
    dvalues,
    y_last,
    gi_own,
    pg,
    pg_recv,
    pg_sum,
    pg_all,
    table_pad,
    inner_w,
    outer_raw,
    outer_w,
    hid_part,
    hid_recv,
    hid_pair,
    hid_all,
    send_sem,
    recv_sem,
    local_sem,
    phase_sem,
):
    lo_out, ig_out = rows_out.at[0], rows_out.at[1]
    s = lax.axis_index("section")
    t = lax.axis_index("tensor")
    d = lax.axis_index("dp")
    nt, nb, rows, brows, tile = z.planes, z.blocks, z.rows, z.block_rows, z.tile
    cells = z.cells
    me = t * nb + d
    sib = (1 - s, t, d)
    counts = dict(send=0, recv=0, local=0)
    pending = []

    def claim(kind, number):
        first = counts[kind]
        counts[kind] += number
        return first

    def rcopy(src, dst, ss, rs, device):
        return pltpu.make_async_remote_copy(
            src_ref=src,
            dst_ref=dst,
            send_sem=send_sem.at[ss],
            recv_sem=recv_sem.at[rs],
            device_id=device,
            device_id_type=MESH,
        )

    def push(src, dst, rs, device, when=None):
        copy = rcopy(src, dst, claim("send", 1), rs, device)
        if when is None:
            copy.start()
            pending.append((copy, None))
        else:
            pl.when(when)(copy.start)
            pending.append((copy, when))

    def arrived(dst, rs, when=None):
        copy = rcopy(dst, dst, 0, rs, sib)
        if when is None:
            copy.wait_recv()
        else:
            pl.when(when)(copy.wait_recv)

    def lcopy(src, dst):
        copy = pltpu.make_async_copy(src, dst, local_sem.at[claim("local", 1)])
        copy.start()
        return copy

    outer = (t == 0) | (t == nt - 1)
    inner = jnp.logical_not(outer)
    across = lax.rem(t + 2, nt)
    beside = t + 1 - 2 * lax.rem(t, 2)

    def far(k):
        return ((t == 0) & (k == nt - 1)) | ((t == nt - 1) & (k == 1))

    def unheard(k):
        return ((t == 0) & (k == 1)) | ((t == nt - 1) & (k == nt - 1))

    def near(k):
        return jnp.logical_not(far(k))

    def plane(k):
        return lax.rem(t + k, nt)

    def block(k):
        return lax.rem(d + k, nb)

    barrier = pltpu.get_barrier_semaphore()
    for k in range(1, cells):
        pl.semaphore_signal(
            barrier, inc=1, device_id=(s, plane(k // nb), block(k % nb)), device_id_type=MESH
        )
    pl.semaphore_signal(barrier, inc=1, device_id=sib, device_id_type=MESH)

    load_x = lcopy(x_in.at[s], xs.at[0, t])
    load_triple = lcopy(triple_in, triple_own)
    load_inner = lcopy(inner_in, inner_w)
    load_outer = lcopy(outer_in, outer_raw)
    load_mixer = lcopy(mixer_in, wm.at[s, pl.ds(pl.multiple_of(t * z.local_width, 256), z.local_width)])
    load_expand = lcopy(expand_in, we.at[s])
    load_reduce = lcopy(reduce_in, wr.at[s])
    load_gy = lcopy(gy_in.at[s], gys.at[1, t])

    for index, ref in enumerate(
        (gain_one_in, bias_one_in, mixer_bias_in, gain_two_in, bias_two_in, reduce_bias_in, expand_bias_in)
    ):
        vec[s, index : index + 1, :] = ref[...].astype(f32)
    for c in range(3):
        shift = jnp.broadcast_to(triple_bias_in[0, c : c + 1, :].astype(f32), (128, z.local_width)).T
        for j in range(nb):
            tbias[s, j, c * HD : (c + 1) * HD, :] = shift[j * HD : (j + 1) * HD].astype(bf16)
    table_pad[...] = jnp.zeros_like(table_pad)
    table_pad[0 : z.prefix_rows, :] = table_in[...].astype(f32)

    for layer in range(2):
        for k in (1, nt - 1):

            @pl.when(unheard(k))
            def _():
                y_recv[layer, k] = jnp.zeros((rows, z.width), bf16)
                gi_recv[layer, k] = jnp.zeros((rows, z.width), bf16)

        @pl.when(outer)
        def _():
            for j in range(nb):
                gh[layer, (nt - 1 - t) * nb + j] = jnp.zeros((HD, brows), bf16)
            gh_relay[layer] = jnp.zeros((nb, HD, brows), bf16)

    pl.semaphore_wait(barrier, cells)

    def spread(src, buf, layer, first=None, when=None):
        if first is None:
            first = claim("recv", nt)
        for k in (2, 1, 3):
            go = near(k) if when is None else near(k) & when
            push(src, buf.at[layer, t], first + k, (s, plane(k), d), go)
        return first

    def spread_relay(buf, layer, first):
        arrived(buf.at[layer, across], first + 2, inner)
        push(buf.at[layer, across], buf.at[layer, across], first + 2 * t - 1, (s, beside, d), inner)

    def spread_wait(buf, layer, first, k):
        arrived(buf.at[layer, plane(nt - k)], first + k, outer if k == 2 else None)

    x_first = [None, None]
    gy_first = [None, None]
    x_first[0] = spread(x_in.at[s], xs, 0)

    small = claim("recv", 3)
    push(vec.at[s], vec.at[s], small, sib)
    push(tbias.at[s], tbias.at[s], small + 1, sib)

    mix_first = [claim("recv", nt), claim("recv", nt)]
    mix_second = [claim("recv", nt * nb), claim("recv", nt * nb)]
    mix_third = [claim("recv", 1), claim("recv", 1)]

    def piece(layer, p, q):
        return wm.at[layer, pl.ds(pl.multiple_of((p * nb + q) * (z.local_width // nb), 64), z.local_width // nb)]

    def mix_one(layer):
        part = z.local_width // nb
        for k in range(1, nt):
            push(
                mixer_in.at[pl.ds(pl.multiple_of(d * part, 64), part)],
                piece(layer, t, d),
                mix_first[layer] + k,
                (s, plane(k), d),
                s == layer,
            )

    def mix_two(layer):
        for k in range(1, nt):
            source = plane(nt - k)
            arrived(piece(layer, source, d), mix_first[layer] + k, s == layer)
            for q in range(1, nb):
                push(
                    piece(layer, source, d),
                    piece(layer, source, d),
                    mix_second[layer] + k * nb + q,
                    (s, t, block(q)),
                    s == layer,
                )

    def mix_three(layer):
        for k in range(1, nt):
            for q in range(1, nb):
                arrived(
                    piece(layer, plane(nt - k), block(nb - q)),
                    mix_second[layer] + k * nb + q,
                    s == layer,
                )
        push(wm.at[layer], wm.at[layer], mix_third[layer], sib, s == layer)

    mix_one(0)

    load_triple.wait()
    for c in range(3):
        for n in range(z.width // tile):
            turned = triple_own[c, n * tile : (n + 1) * tile, :].T
            for j in range(nb):
                wq[s, j, c * HD : (c + 1) * HD, n * tile : (n + 1) * tile] = turned[j * HD : (j + 1) * HD]
    wq_first = claim("recv", 1)
    push(wq.at[s], wq.at[s], wq_first, sib)
    load_inner.wait()
    inner_act = jnp.tanh(
        dot_nn(table_pad[...].astype(bf16), inner_w[...]) + inner_bias_in[...].reshape(1, z.inner).astype(f32)
    )
    parts_out[0] = inner_act
    load_outer.wait()
    for c in range(2):
        outer_w[:, c * z.local_width : (c + 1) * z.local_width] = outer_raw[:, c, :]
    outer_shift = jnp.concatenate([outer_bias_in[0, 0:1, :], outer_bias_in[0, 1:2, :]], axis=1)
    prefix = (dot_nn(inner_act.astype(bf16), outer_w[...]) + outer_shift.astype(f32)).astype(bf16)
    parts_out[1] = prefix.astype(f32)
    for c in range(2):
        for j in range(nb):
            at = c * z.local_width + j * HD
            pre[s, c, j] = prefix[:, at : at + HD]
    push(pre.at[s], pre.at[s], small + 2, sib)
    arrived(vec.at[1 - s], small)
    arrived(tbias.at[1 - s], small + 1)
    arrived(pre.at[1 - s], small + 2)

    def row(layer, index):
        return vec[layer, index : index + 1, :]

    step = 32

    def norm_one(layer, p):
        def some(i, _):
            at = pl.multiple_of(i * step, step)
            x = xs[layer, p, pl.ds(at, step), :].astype(f32)
            center = x - jnp.mean(x, axis=1, keepdims=True)
            inverse = lax.rsqrt(jnp.mean(center * center, axis=1, keepdims=True) + epsilon)
            unit = center * inverse
            where = pl.multiple_of(p * rows + at, step)
            z_one[layer, pl.ds(where, step), :] = unit
            inv_one[layer, pl.ds(where, step), :] = inverse
            normed[pl.ds(where, step), :] = (unit * row(layer, 0) + row(layer, 1)).astype(bf16)
            return 0

        lax.fori_loop(0, rows // step, some, 0, unroll=True)

    def norm_two(layer):
        def some(i, _):
            at = pl.multiple_of(i * step, step)
            x = resid[pl.ds(at, step), :]
            center = x - jnp.mean(x, axis=1, keepdims=True)
            inverse = lax.rsqrt(jnp.mean(center * center, axis=1, keepdims=True) + epsilon)
            unit = center * inverse
            z_two[layer, pl.ds(at, step), :] = unit
            inv_two[layer, pl.ds(at, step), :] = inverse
            normed[pl.ds(at, step), :] = (unit * row(layer, 3) + row(layer, 4)).astype(bf16)
            return 0

        lax.fori_loop(0, brows // step, some, 0, unroll=True)

    def norm_pull(i, units, inverses, gain):
        at = pl.multiple_of(i * step, step)
        unit = units[pl.ds(at, step), :]
        scaled = total[pl.ds(at, step), :] * gain
        mean_grad = jnp.mean(scaled, axis=1, keepdims=True)
        mean_cross = jnp.mean(scaled * unit, axis=1, keepdims=True)
        return at, inverses[pl.ds(at, step), :] * (scaled - mean_grad - unit * mean_cross)

    def tiles(count, body):
        def some(i, _):
            body(pl.multiple_of(i * tile, tile))
            return 0

        lax.fori_loop(0, count // tile, some, 0, unroll=True)

    def project(layer):
        first = claim("recv", nb)
        for k in range(1, nb + 1):
            head = block(k)
            part = dot_nt(wq[layer, head], normed[...])
            shift = tbias[layer, head].astype(f32)
            part = (part + jnp.concatenate([shift, shift], axis=1)).astype(bf16)
            if k < nb:
                qkv_send[layer, k] = part
                push(qkv_send.at[layer, k], qkv.at[layer, d], first + k, (s, t, head))
            else:
                qkv[layer, d] = part
        return first

    def attend(layer, first):
        out_first = claim("recv", cells)
        pre_keys = pre[layer, 0, d]
        pre_values = pre[layer, 1, d].T
        prefix_row = lax.broadcasted_iota(jnp.int32, (z.prefix_pad, brows), 0)
        key_at = lax.broadcasted_iota(jnp.int32, (brows, brows), 0)
        query_at = lax.broadcasted_iota(jnp.int32, (brows, brows), 1)
        valid = valid_ref[s]
        number = 0
        for b in range(nb):
            arrived(qkv.at[layer, b], first + lax.rem(d + nb - b, nb), d != b)
            keys_n[layer, b] = qkv[layer, b, HD : 2 * HD, :].T
            queries = (qkv[layer, b, 0:HD, :].astype(f32) * HD ** (-0.5)).astype(bf16)
            scores = dot_nn(pre_keys, queries)
            scores = jnp.where(prefix_row < z.prefix_rows, scores, masked_score)
            probs_pre[layer, b] = scores
            peak = jnp.max(scores, axis=0, keepdims=True)
            for kb in range(b + 1):
                scores = dot_nn(keys_n[layer, kb], queries)
                if kb == b:
                    seen = key_at <= query_at
                    if b == nb - 1:
                        seen = seen & (key_at + b * brows < valid)
                    scores = jnp.where(seen, scores, masked_score)
                probs[layer, number + kb] = scores
                peak = jnp.maximum(peak, jnp.max(scores, axis=0, keepdims=True))
            expons = jnp.exp(probs_pre[layer, b] - peak)
            probs_pre[layer, b] = expons
            denominator = jnp.sum(expons, axis=0, keepdims=True)
            for kb in range(b + 1):
                expons = jnp.exp(probs[layer, number + kb] - peak)
                probs[layer, number + kb] = expons
                denominator = denominator + jnp.sum(expons, axis=0, keepdims=True)
            scale = 1.0 / denominator
            prob = probs_pre[layer, b] * scale
            probs_pre[layer, b] = prob
            result = dot_nn(pre_values, prob.astype(bf16))
            for kb in range(b + 1):
                prob = probs[layer, number + kb] * scale
                probs[layer, number + kb] = prob
                result = result + dot_nn(qkv[layer, kb, 2 * HD : 3 * HD, :], prob.astype(bf16))
            number += b + 1
            out_t[layer, b] = result
            low = result.astype(bf16)
            ot_send[layer, b] = low
            for k in (2, 1, 3, 0):
                if k == 0:
                    push(ot_send.at[layer, b], att.at[layer, me], out_first + me, (s, t, b), d != b)

                    @pl.when(d == b)
                    def _():
                        att[layer, me] = low
                else:
                    push(
                        ot_send.at[layer, b], att.at[layer, me], out_first + me, (s, plane(k), b), near(k)
                    )
        return out_first

    def att_relay(layer, first):
        for j in range(nb):
            cell = across * nb + j
            arrived(att.at[layer, cell], first + cell, inner)
            push(att.at[layer, cell], att.at[layer, cell], first + cell, (s, beside, d), inner)

    def mixer_rows(layer, first):
        att_relay(layer, first)
        for cell in range(cells):
            seen = inner & (across == cell // nb)
            arrived(att.at[layer, cell], first + cell, (me != cell) & jnp.logical_not(seen))
        for p in range(nt):
            joined = att[layer, p * nb : (p + 1) * nb].reshape(nb * HD, brows)
            wide[:, p * nb * HD : (p + 1) * nb * HD] = joined.T

        def some(at):
            x = xs[layer, :, :, pl.ds(at, tile)].reshape(brows, tile).astype(f32)
            shift = vec[layer, 2:3, pl.ds(at, tile)]
            resid[:, pl.ds(at, tile)] = dot_nn(wide[...], wm[layer, :, pl.ds(at, tile)]) + x + shift

        tiles(z.width, some)

    def feed_first(layer):
        def some(at):
            v = dot_nn(normed[...], we[layer, :, pl.ds(at, tile)]) + vec[layer, 6:7, pl.ds(at, tile)]
            root = 0.7978845608028654
            square = v * v
            th = jnp.tanh(root * v * (1.0 + 0.044715 * square))
            half = 0.5 * (1.0 + th)
            wide[:, pl.ds(at, tile)] = (v * half).astype(bf16)
            gelu_grad[layer, :, pl.ds(at, tile)] = half + (0.5 * root) * v * (1.0 - th * th) * (
                1.0 + 3.0 * 0.044715 * square
            )

        tiles(z.hidden, some)

    def feed_second(layer):
        def some(at):
            part = dot_nn(wide[...], wr[layer, :, pl.ds(at, tile)])
            total[:, pl.ds(at, tile)] = part
            y_send[layer, :, :, pl.ds(at, tile)] = part.astype(bf16).reshape(nt, rows, tile)

        tiles(z.width, some)
        return scatter(layer, y_send, y_recv, y_relay, total)

    def scatter(layer, out, back, relay, full):
        first = claim("recv", nt + 1)
        push(out.at[layer, nt - 1 - t], relay.at[layer], first + nt, (s, beside, d), outer)
        for k in (2, 1, 3):
            go = near(k) if k != 2 else outer
            push(out.at[layer, plane(k)], back.at[layer, k], first + k, (s, plane(k), d), go)
        arrived(relay.at[layer], first + nt, inner)

        @pl.when(inner)
        def _():
            where = pl.ds(pl.multiple_of(across * rows, rows), rows)
            out[layer, across] = (full[where, :] + relay[layer].astype(f32)).astype(bf16)

        push(out.at[layer, across], back.at[layer, 2], first + 2, (s, across, d), inner)
        return first

    def scatter_wait(layer, back, first, result):
        for k in (1, 3, 2):
            arrived(back.at[layer, k], first + k, jnp.logical_not(unheard(k)))
            result = result + back[layer, k].astype(f32)
        return result

    def own_rows(ref):
        return ref[pl.ds(pl.multiple_of(t * rows, rows), rows), :]

    def output_sum(layer, first, base):
        return scatter_wait(layer, y_recv, first, base).astype(bf16)

    out_sem = claim("recv", 4)
    out_loads = []

    def put(src, out, layer, index):
        push(src, out.at[0, s], out_sem + index, sib, s != layer)
        copy = pltpu.make_async_copy(src, out.at[0, s], local_sem.at[claim("local", 1)])
        pl.when(s == layer)(copy.start)
        out_loads.append((copy, s == layer))

    own_weights = [load_mixer, load_expand, load_reduce]
    feed_recv = claim("recv", 2)
    y_base = []
    out_first = None
    for layer in range(2):
        if layer == 0:
            load_x.wait()

        norm_one(layer, t)
        spread_relay(xs, layer, x_first[layer])
        for k in (2, 1, 3):
            spread_wait(xs, layer, x_first[layer], k)
            norm_one(layer, plane(nt - k))
        if layer == 0:
            arrived(wq.at[0], wq_first, s == 1)
        else:
            arrived(wq.at[1], wq_first, s == 0)
        q_first = project(layer)
        if layer == 0:
            push(expand_in, we.at[s], feed_recv, sib)
            push(reduce_in, wr.at[s], feed_recv + 1, sib)
            mix_two(0)
            mix_one(1)
        else:
            load_gy.wait()
            gy_first[1] = spread(gys.at[1, t], gys, 1)
        out_first = attend(layer, q_first)
        if layer == 0:
            for copy in own_weights:
                copy.wait()
            arrived(we.at[1 - s], feed_recv)
            arrived(wr.at[1 - s], feed_recv + 1)
            mix_three(0)
        else:
            mix_three(1)
        arrived(wm.at[layer], mix_third[layer], s != layer)
        mixer_rows(layer, out_first)
        norm_two(layer)
        y_base.append(None)
        feed_first(layer)
        y_first = feed_second(layer)
        base = own_rows(resid) + own_rows(total) + row(layer, 5)
        if layer == 0:
            mix_two(1)
            low = output_sum(0, y_first, base)
            xs[1, t] = low
            x_first[1] = spread(xs.at[1, t], xs, 1)
            put(xs.at[1, t], lo_out, 0, 0)
        else:
            gi_own[...] = base
            last_first = y_first

    def grad_hidden(layer):
        def some(at):
            upper = gys[layer].reshape(brows, z.width)
            part = dot_nt(upper, wr[layer, pl.ds(at, tile), :])
            wide[:, pl.ds(at, tile)] = (part * gelu_grad[layer, :, pl.ds(at, tile)]).astype(bf16)

        tiles(z.hidden, some)

    def grad_mid(layer):
        def some(at):
            total[:, pl.ds(at, tile)] = dot_nt(wide[...], we[layer, pl.ds(at, tile), :])

        tiles(z.width, some)

        def pull(i, _):
            at, part = norm_pull(i, z_two.at[layer], inv_two.at[layer], row(layer, 3))
            upper = gys[layer, i // (rows // step), pl.ds(lax.rem(i, rows // step) * step, step), :]
            part = part + upper.astype(f32) * (1.0 / nt)
            grad_res[pl.ds(at, step), :] = part
            normed[pl.ds(at, step), :] = part.astype(bf16)
            return 0

        lax.fori_loop(0, brows // step, pull, 0, unroll=True)

    def grad_to_heads(layer):
        first = claim("recv", cells)
        relay_sem = claim("recv", 1)
        for k in (3, 1, 2, 4):
            p = plane(k)
            here = wm[layer, pl.ds(pl.multiple_of(p * z.local_width, z.local_width), z.local_width), :]
            part = dot_nt(here, normed[...]).astype(bf16).reshape(nb, HD, brows)
            if k == 2:
                arrived(gh_relay.at[layer], relay_sem, inner)
                met = jnp.where(inner, gh_relay[layer].astype(f32), 0.0)
                part = (part.astype(f32) + met).astype(bf16)
            gh_send[layer, k - 1] = part
            if k != 2 and k < nt:
                push(gh_send.at[layer, k - 1], gh_relay.at[layer], relay_sem, (s, beside, d), far(k))
            for j in range(nb):
                away = near(k) if k < nt else d != j
                push(gh_send.at[layer, k - 1, j], gh.at[layer, me], first + me, (s, p, j), away)
                if k == nt:

                    @pl.when(d == j)
                    def _():
                        gh[layer, me] = part[j]

        return first

    def attend_back(layer, first):
        for cell in range(cells):
            seen = outer & (t + cell // nb == nt - 1)
            arrived(gh.at[layer, cell], first + cell, (me != cell) & jnp.logical_not(seen))
        out_first = claim("recv", nb)
        pre_values = pre[layer, 1, d]
        pre_keys = pre[layer, 0, d].T
        dkeys[...] = jnp.zeros_like(dkeys)
        dvalues[...] = jnp.zeros_like(dvalues)
        pre_dkeys = jnp.zeros((z.prefix_pad, HD), f32)
        pre_dvalues = jnp.zeros((z.prefix_pad, HD), f32)
        for b in reversed(range(nb)):
            number = b * (b + 1) // 2
            grad = gh[layer, b].astype(f32)
            for p in range(1, nt):
                grad = grad + gh[layer, p * nb + b].astype(f32)
            grad = grad.astype(bf16)
            delta = jnp.sum(grad.astype(f32) * out_t[layer, b], axis=0, keepdims=True)
            grad_n = grad.T
            queries = (qkv[layer, b, 0:HD, :].astype(f32) * HD ** (-0.5)).astype(bf16).T
            prob = probs_pre[layer, b]
            dscore = (prob * (dot_nn(pre_values, grad) - delta)).astype(bf16)
            dq = dot_nn(pre_keys, dscore)
            pre_dkeys = pre_dkeys + dot_nn(dscore, queries)
            pre_dvalues = pre_dvalues + dot_nn(prob.astype(bf16), grad_n)
            for kb in range(b + 1):
                prob = probs[layer, number + kb]
                values = qkv[layer, kb, 2 * HD : 3 * HD, :].T
                dscore = (prob * (dot_nn(values, grad) - delta)).astype(bf16)
                dq = dq + dot_nn(qkv[layer, kb, HD : 2 * HD, :], dscore)
                dkeys[kb] = dkeys[kb] + dot_nn(dscore, queries)
                dvalues[kb] = dvalues[kb] + dot_nn(prob.astype(bf16), grad_n)
            joined = jnp.concatenate(
                [dq * HD ** (-0.5), dkeys[b].T, dvalues[b].T], axis=0
            ).astype(bf16)
            dm_send[layer, b] = joined
            push(dm_send.at[layer, b], dm.at[layer, d], out_first + d, (s, t, b), d != b)

            @pl.when(d == b)
            def _():
                dm[layer, d] = joined

        pg[layer, 0] = pre_dkeys
        pg[layer, 1] = pre_dvalues
        return out_first

    def grad_rows(layer, first):
        for j in range(nb):
            arrived(dm.at[layer, j], first + j, d != j)
        for j in range(nb):
            wide[:, j * 3 * HD : (j + 1) * 3 * HD] = dm[layer, j].T
        depth = nb * 3 * HD

        def some(at):
            right = wq[layer, :, :, pl.ds(at, tile)].reshape(depth, tile)
            total[:, pl.ds(at, tile)] = dot_nn(wide[:, :depth], right)

        tiles(z.width, some)

        def pull(i, _):
            at, part = norm_pull(i, z_one.at[layer], inv_one.at[layer], row(layer, 0))
            part = part + grad_res[pl.ds(at, step), :]
            grad_res[pl.ds(at, step), :] = part
            p = i // (rows // step)
            gi_send[layer, p, pl.ds(lax.rem(i, rows // step) * step, step), :] = part.astype(bf16)
            return 0

        lax.fori_loop(0, brows // step, pull, 0, unroll=True)
        return scatter(layer, gi_send, gi_recv, gi_relay, grad_res)

    def grad_sum(layer, first):
        return scatter_wait(layer, gi_recv, first, own_rows(grad_res)).astype(bf16)

    for layer in (1, 0):
        spread_relay(gys, layer, gy_first[layer])
        for k in range(1, nt):
            spread_wait(gys, layer, gy_first[layer], k)
        grad_hidden(layer)
        grad_mid(layer)
        heads_first = grad_to_heads(layer)
        if layer == 1:
            y_last[...] = output_sum(1, last_first, gi_own[...])
            put(y_last, lo_out, 1, 1)
        rows_first = attend_back(layer, heads_first)
        if layer == 0:
            sib_sem = claim("recv", 1)
            push(pg.at[1 - s], pg_recv, sib_sem, sib)
            arrived(pg_recv, sib_sem)
            pg_sum[...] = pg[s] + pg_recv[...]
            all_first = claim("recv", nb)
            for k in range(1, nb):
                push(pg_sum, pg_all.at[d], all_first + k, (s, t, block(k)))
            pg_all[d] = pg_sum[...]
        grads_first = grad_rows(layer, rows_first)
        if layer == 1:
            gys[0, t] = grad_sum(1, grads_first)
            gy_first[0] = spread(gys.at[0, t], gys, 0)
            put(gys.at[0, t], ig_out, 1, 2)
        else:
            for k in range(1, nb):
                arrived(pg_all.at[block(nb - k)], all_first + k)
            for c in range(2):
                joined = jnp.concatenate([pg_all[j, c] for j in range(nb)], axis=1)
                parts_out[2, :, c * z.local_width : (c + 1) * z.local_width] = joined
            part = jnp.zeros((z.prefix_pad, z.inner), f32)
            for j in range(nb):
                for c in range(2):
                    at = c * z.local_width + j * HD
                    part = part + dot_split(pg_all[j, c], outer_w[:, at : at + HD], dot_nt)
            hid_part[...] = part
            hid_sem = claim("recv", 1)
            push(hid_part, hid_recv, hid_sem, sib)
            arrived(hid_recv, hid_sem)
            hid_pair[...] = hid_part[...] + hid_recv[...]
            hid_first = claim("recv", nt)
            for k in range(1, nt):
                push(hid_pair, hid_all.at[t], hid_first + k, (s, plane(k), d))
            hid_all[t] = hid_pair[...]
            gi_low = grad_sum(0, grads_first)
            xs[0, t] = gi_low
            put(xs.at[0, t], ig_out, 0, 3)
            for k in range(1, nt):
                arrived(hid_all.at[plane(nt - k)], hid_first + k)
            part = hid_all[0]
            for p in range(1, nt):
                part = part + hid_all[p]
            parts_out[3] = part

    for index, (out, layer) in enumerate(((lo_out, 0), (lo_out, 1), (ig_out, 1), (ig_out, 0))):
        arrived(out.at[0, 1 - s], out_sem + index, s == layer)
    for copy, when in pending:
        if when is None:
            copy.wait_send()
        else:
            pl.when(when)(copy.wait_send)
    for copy, when in out_loads:
        pl.when(when)(copy.wait)
    z.counts = counts


def run_layers(z, small, large):
    nt, nb, rows, brows = z.planes, z.blocks, z.rows, z.block_rows
    width, hidden = z.width, z.hidden
    pairs = nb * (nb + 1) // 2
    V = pltpu.VMEM
    any_space = pl.BlockSpec(memory_space=pl.ANY)
    scratch = [
        V((2, 8, width), f32),
        V((2, nb, 3 * HD, 128), bf16),
        V((3, width, z.local_width), bf16),
        V((2, nb, 3 * HD, width), bf16),
        V((2, width, width), bf16),
        V((2, width, hidden), bf16),
        V((2, hidden, width), bf16),
        V((2, 2, nb, z.prefix_pad, HD), bf16),
        V((2, nt, rows, width), bf16),
        V((2, nt, rows, width), bf16),
        V((2, nb, 3 * HD, brows), bf16),
        V((2, nb, 3 * HD, brows), bf16),
        V((2, nb, HD, brows), bf16),
        V((2, z.cells, HD, brows), bf16),
        V((2, nt, rows, width), bf16),
        V((2, nt, rows, width), bf16),
        V((2, nt, nb, HD, brows), bf16),
        V((2, z.cells, HD, brows), bf16),
        V((2, nb, 3 * HD, brows), bf16),
        V((2, nb, 3 * HD, brows), bf16),
        V((2, nt, rows, width), bf16),
        V((2, nt, rows, width), bf16),
        V((2, rows, width), bf16),
        V((2, rows, width), bf16),
        V((2, nb, HD, brows), bf16),
        V((2, brows, width), f32),
        V((2, brows, 1), f32),
        V((2, brows, width), f32),
        V((2, brows, 1), f32),
        V((2, brows, hidden), f32),
        V((2, pairs, brows, brows), f32),
        V((2, nb, z.prefix_pad, brows), f32),
        V((2, nb, HD, brows), f32),
        V((2, nb, brows, HD), bf16),
        V((brows, width), bf16),
        V((brows, width), bf16),
        V((brows, width), f32),
        V((brows, width), f32),
        V((brows, width), f32),
        V((nb, brows, HD), f32),
        V((nb, brows, HD), f32),
        V((rows, width), bf16),
        V((rows, width), f32),
        V((2, 2, z.prefix_pad, HD), f32),
        V((2, z.prefix_pad, HD), f32),
        V((2, z.prefix_pad, HD), f32),
        V((nb, 2, z.prefix_pad, HD), f32),
        V((z.prefix_pad, width), f32),
        V((width, z.inner), bf16),
        V((z.inner, 2, z.local_width), bf16),
        V((z.inner, 2 * z.local_width), bf16),
        V((z.prefix_pad, z.inner), f32),
        V((z.prefix_pad, z.inner), f32),
        V((z.prefix_pad, z.inner), f32),
        V((nt, z.prefix_pad, z.inner), f32),
        pltpu.SemaphoreType.DMA((200,)),
        pltpu.SemaphoreType.DMA((200,)),
        pltpu.SemaphoreType.DMA((20,)),
        pltpu.SemaphoreType.REGULAR,
    ]
    return pl.pallas_call(
        partial(both_layers, z),
        out_shape=(
            jax.ShapeDtypeStruct((2, 1, 2, rows, width), bf16),
            jax.ShapeDtypeStruct((4, z.prefix_pad, z.inner), f32),
        ),
        in_specs=[pl.BlockSpec(memory_space=pltpu.SMEM)]
        + [pl.BlockSpec(memory_space=pltpu.VMEM)] * (len(small) - 1)
        + [any_space] * len(large),
        out_specs=(any_space, pl.BlockSpec(memory_space=pltpu.VMEM)),
        scratch_shapes=scratch,
        compiler_params=pltpu.CompilerParams(
            collective_id=0, has_side_effects=True, vmem_limit_bytes=60 * 2**20
        ),
        cost_estimate=pl.CostEstimate(
            flops=7 * 10**9, bytes_accessed=16 * 2**20, transcendentals=4 * 10**6
        ),
    )(*small, *large)


def prefix_end(
    z, rows_in, parts_in, table_in, inner_in,
    lo_out, ig_out, states_out, table_out, inner_out, inner_bias_out, outer_out, outer_bias_out,
    table_pad, sems,
):
    copies = [
        pltpu.make_async_copy(rows_in.at[0], lo_out, sems.at[0]),
        pltpu.make_async_copy(rows_in.at[1], ig_out, sems.at[1]),
    ]
    for copy in copies:
        copy.start()
    count, width = z.prefix_rows, z.local_width
    act = parts_in[0]
    inner_grad = parts_in[3] * (1.0 - act * act)
    inner_bias_out[...] = jnp.sum(inner_grad, axis=0, keepdims=True)
    table_pad[...] = jnp.zeros_like(table_pad)
    table_pad[0:count, :] = table_in[...].astype(f32)
    high = inner_grad.astype(bf16)
    low = (inner_grad - high.astype(f32)).astype(bf16)
    table_turned = table_pad[...].T.astype(bf16)
    inner_out[...] = dot_nn(table_turned, high) + dot_nn(table_turned, low)
    table_out[...] = (dot_nt(high, inner_in[...]) + dot_nt(low, inner_in[...]))[0:count]
    act_turned = act.T.astype(bf16)
    for c in range(2):
        at = slice(c * width, (c + 1) * width)
        states_out[:, c, :] = parts_in[1, 0:count, at].astype(bf16)
        total = parts_in[2, :, at]
        high = total.astype(bf16)
        low = (total - high.astype(f32)).astype(bf16)
        outer_out[:, c, :] = dot_nn(act_turned, high) + dot_nn(act_turned, low)
        outer_bias_out[0, c : c + 1, :] = jnp.sum(total, axis=0, keepdims=True)
    for copy in copies:
        copy.wait()


def finish(z, both_rows, parts, table, inner_weight):
    any_space = pl.BlockSpec(memory_space=pl.ANY)
    whole = pl.BlockSpec(memory_space=pltpu.VMEM)
    rows = jax.ShapeDtypeStruct(both_rows.shape[1:], bf16)
    return pl.pallas_call(
        partial(prefix_end, z),
        out_shape=(
            rows,
            rows,
            jax.ShapeDtypeStruct((z.prefix_rows, 2, z.local_width), bf16),
            jax.ShapeDtypeStruct((z.prefix_rows, z.width), f32),
            jax.ShapeDtypeStruct((z.width, z.inner), f32),
            jax.ShapeDtypeStruct((1, z.inner), f32),
            jax.ShapeDtypeStruct((z.inner, 2, z.local_width), f32),
            jax.ShapeDtypeStruct((1, 2, z.local_width), f32),
        ),
        in_specs=[any_space] + [whole] * 3,
        out_specs=(any_space,) * 2 + (whole,) * 6,
        scratch_shapes=[pltpu.VMEM((z.prefix_pad, z.width), f32), pltpu.SemaphoreType.DMA((2,))],
        compiler_params=pltpu.CompilerParams(vmem_limit_bytes=32 * 2**20),
    )(both_rows, parts, table, inner_weight)


def head_a_device(
    block_input,
    output_grad,
    valid_len,
    first_gain,
    first_bias,
    triple_weight,
    triple_bias,
    mixer_weight,
    mixer_bias,
    second_gain,
    second_bias,
    expand_weight,
    expand_bias,
    reduce_weight,
    reduce_bias,
    prefix_table,
    inner_weight,
    inner_bias,
    outer_weight,
    outer_bias,
):
    planes, blocks = lax.axis_size("tensor"), lax.axis_size("dp")
    local_width = triple_weight.shape[3]
    prefix_rows = prefix_table.shape[0]
    z = Sizes(
        planes,
        blocks,
        block_input.shape[1],
        block_input.shape[2],
        local_width,
        expand_weight.shape[2],
        prefix_rows,
    )
    z.prefix_pad = -(-prefix_rows // 16) * 16
    z.inner = inner_weight.shape[1]
    small = (
        valid_len,
        first_gain,
        first_bias,
        triple_bias,
        mixer_bias,
        second_gain,
        second_bias,
        expand_bias,
        reduce_bias,
        prefix_table,
        inner_bias,
        outer_bias,
    )
    large = (
        block_input,
        output_grad,
        triple_weight[0].transpose(1, 0, 2),
        mixer_weight[0],
        expand_weight[0],
        reduce_weight[0],
        inner_weight,
        outer_weight[:, 0],
    )
    results = finish(z, *run_layers(z, small, large), prefix_table, inner_weight)
    (
        layer_outputs,
        input_grads,
        prefix_states,
        table_grad,
        inner_weight_grad,
        inner_bias_grad,
        outer_weight_grad,
        outer_bias_grad,
    ) = results
    return (
        layer_outputs,
        input_grads,
        prefix_states.transpose(1, 0, 2)[None],
        table_grad,
        inner_weight_grad,
        inner_bias_grad.reshape(-1),
        outer_weight_grad.reshape(-1, 1, 2, local_width),
        outer_bias_grad,
    )


def prefix_back(
    prefix_total,
    prefix_full,
    inner_act,
    inner_low,
    outer_local,
    prefix_table,
    inner_weight,
    local_width,
):
    inner_float = inner_low.astype(f32)
    outer_float = outer_local.astype(f32)
    outer_weight_grad = jnp.dot(inner_float.T, prefix_total, precision=highest).reshape(
        -1, 1, 2, local_width
    )
    outer_bias_grad = jnp.sum(prefix_total, axis=0).reshape(1, 2, local_width)
    hidden_grad = lax.psum(
        jnp.dot(prefix_total, outer_float.T, precision=highest), ("section", "tensor")
    )
    inner_grad = hidden_grad * (1.0 - inner_act * inner_act)
    inner_weight_grad = jnp.dot(prefix_table.astype(f32).T, inner_grad, precision=highest)
    inner_bias_grad = jnp.sum(inner_grad, axis=0)
    table_grad = jnp.dot(inner_grad, inner_weight.astype(f32).T, precision=highest)
    prefix_states = prefix_full.reshape(-1, 2, local_width).transpose(1, 0, 2)[None]
    return (
        prefix_states,
        table_grad,
        inner_weight_grad,
        inner_bias_grad,
        outer_weight_grad,
        outer_bias_grad,
    )


def solution(mesh):
    def step(*args):
        triple_weight = args[5]
        micro_count, share_rows, width = args[0].shape
        fits = (
            lax.axis_size("section") == 2
            and micro_count == 2
            and triple_weight.shape[3] == HD * lax.axis_size("dp")
            and share_rows * lax.axis_size("tensor") == 256
            and triple_weight.shape[3] % 256 == 0
            and width % 256 == 0
            and args[11].shape[2] == width
        )
        return head_a_device(*args) if fits else shards(*args)

    return jax.shard_map(
        step,
        mesh=mesh,
        in_specs=(
            P(None, ("dp", "tensor"), None),
            P(None, ("dp", "tensor"), None),
            P(),
            P("section", None),
            P("section", None),
            P("section", None, None, "tensor"),
            P("section", None, "tensor"),
            P("section", "tensor", None),
            P("section", None),
            P("section", None),
            P("section", None),
            P("section", None, "tensor"),
            P("section", "tensor"),
            P("section", "tensor", None),
            P("section", None),
            P(),
            P(),
            P(),
            P(None, "section", None, "tensor"),
            P("section", None, "tensor"),
        ),
        out_specs=(
            P("section", None, ("dp", "tensor"), None),
            P("section", None, ("dp", "tensor"), None),
            P("section", None, None, "tensor"),
            P(),
            P(),
            P(),
            P(None, "section", None, "tensor"),
            P("section", None, "tensor"),
        ),
        check_vma=False,
    )
```

```python
from functools import partial

import jax
import jax.numpy as jnp
from jax import lax
from jax.experimental import pallas as pl
from jax.experimental.pallas import tpu as pltpu
from jax.sharding import PartitionSpec as P

HD = 64


epsilon = 1e-05
masked_score = -1e30
highest = lax.Precision.HIGHEST
MESH = pl.DeviceIdType.MESH
f32 = jnp.float32
bf16 = jnp.bfloat16


def passed_along(block, axis, distance):
    devices = range(lax.axis_size(axis))
    route = [(i - distance, i) for i in devices if i - distance in devices]
    return lax.ppermute(block, axis, route)


def layer_norm(values, norm_gain, norm_bias):
    center = values - jnp.mean(values, axis=-1, keepdims=True)
    variance = jnp.mean(center * center, axis=-1, keepdims=True)
    inverse = lax.rsqrt(variance + epsilon)
    normed = center * inverse
    return (normed * norm_gain + norm_bias, normed, inverse)


def norm_back(grad_out, normed, inverse, norm_gain):
    scaled = grad_out * norm_gain
    mean_grad = jnp.mean(scaled, axis=-1, keepdims=True)
    mean_cross = jnp.mean(scaled * normed, axis=-1, keepdims=True)
    return inverse * (scaled - mean_grad - normed * mean_cross)


def attention_scores(queries, seq_keys, pre_keys, valid, query_start):
    score_scale = HD ** (-0.5)
    seq_scores = (
        jnp.einsum("qhd,khd->hqk", queries, seq_keys, preferred_element_type=jnp.float32)
        * score_scale
    )
    pre_scores = (
        jnp.einsum("qhd,khd->hqk", queries, pre_keys, preferred_element_type=jnp.float32)
        * score_scale
    )
    query_pos = query_start + lax.broadcasted_iota(jnp.int32, (queries.shape[0], 1), 0)
    key_pos = lax.broadcasted_iota(jnp.int32, (1, seq_keys.shape[0]), 1)
    visible = (key_pos <= query_pos) & (key_pos < valid)
    seq_scores = jnp.where(visible[None], seq_scores, masked_score)
    return (seq_scores, pre_scores)


def split_prefix(prefix_full, local_width):
    local_heads = local_width // HD
    pre_keys = prefix_full[:, :local_width].reshape(-1, local_heads, HD)
    pre_values = prefix_full[:, local_width:].reshape(-1, local_heads, HD)
    return (pre_keys, pre_values)


def layer_forward(inputs, weights, prefix_full, valid, query_start):
    (
        gain_one,
        bias_one,
        triple_weight,
        triple_bias,
        mixer_weight,
        mixer_bias,
        gain_two,
        bias_two,
        expand_weight,
        expand_bias,
        reduce_weight,
        reduce_bias,
    ) = weights
    local_width = triple_weight.shape[1] // 3
    local_heads = local_width // HD
    normed_one, unit_one, inverse_one = layer_norm(inputs, gain_one, bias_one)
    mixed_rows = (
        jnp.dot(
            lax.all_gather(normed_one.astype(jnp.bfloat16), "tensor", axis=0, tiled=True),
            triple_weight,
            preferred_element_type=jnp.float32,
        )
        + triple_bias
    ).astype(jnp.bfloat16)
    tokens = mixed_rows.shape[0]
    queries = mixed_rows[:, :local_width].reshape(tokens, local_heads, HD)
    seq_keys, seq_values = (
        lax.all_gather(mixed_rows[:, local_width : 2 * local_width], "dp", axis=0, tiled=True),
        lax.all_gather(mixed_rows[:, 2 * local_width :], "dp", axis=0, tiled=True),
    )
    seq_keys = seq_keys.reshape(-1, local_heads, HD)
    seq_values = seq_values.reshape(-1, local_heads, HD)
    pre_keys, pre_values = split_prefix(prefix_full, local_width)
    seq_scores, pre_scores = attention_scores(queries, seq_keys, pre_keys, valid, query_start)
    row_max = jnp.maximum(
        jnp.max(seq_scores, axis=2, keepdims=True), jnp.max(pre_scores, axis=2, keepdims=True)
    )
    seq_exp = jnp.exp(seq_scores - row_max)
    pre_exp = jnp.exp(pre_scores - row_max)
    row_total = jnp.sum(seq_exp, axis=2, keepdims=True) + jnp.sum(pre_exp, axis=2, keepdims=True)
    log_total = row_max + jnp.log(row_total)
    seq_low = (seq_exp / row_total).astype(jnp.bfloat16)
    pre_low = (pre_exp / row_total).astype(jnp.bfloat16)
    attended = jnp.einsum("hqk,khd->qhd", seq_low, seq_values, preferred_element_type=jnp.float32)
    attended = attended + jnp.einsum(
        "hqk,khd->qhd", pre_low, pre_values, preferred_element_type=jnp.float32
    )
    attended = attended.astype(jnp.bfloat16).reshape(tokens, local_width)
    mixer_out = lax.psum_scatter(
        jnp.dot(attended, mixer_weight, preferred_element_type=jnp.float32),
        "tensor",
        scatter_dimension=0,
        tiled=True,
    )
    residual = inputs + mixer_out + mixer_bias
    normed_two, unit_two, inverse_two = layer_norm(residual, gain_two, bias_two)
    hidden_pre = (
        jnp.dot(
            lax.all_gather(normed_two.astype(jnp.bfloat16), "tensor", axis=0, tiled=True),
            expand_weight,
            preferred_element_type=jnp.float32,
        )
        + expand_bias
    )
    active = jax.nn.gelu(hidden_pre, approximate=True).astype(jnp.bfloat16)
    result = (
        residual
        + lax.psum_scatter(
            jnp.dot(active, reduce_weight, preferred_element_type=jnp.float32),
            "tensor",
            scatter_dimension=0,
            tiled=True,
        )
        + reduce_bias
    )
    saved_state = (
        unit_one,
        inverse_one,
        queries,
        seq_keys,
        seq_values,
        log_total,
        unit_two,
        inverse_two,
        hidden_pre,
    )
    return (result, saved_state)


def layer_backward(grad_out, saved_state, weights, prefix_full, valid, query_start):
    (
        gain_one,
        bias_one,
        triple_weight,
        triple_bias,
        mixer_weight,
        mixer_bias,
        gain_two,
        bias_two,
        expand_weight,
        expand_bias,
        reduce_weight,
        reduce_bias,
    ) = weights
    (
        unit_one,
        inverse_one,
        queries,
        seq_keys,
        seq_values,
        log_total,
        unit_two,
        inverse_two,
        hidden_pre,
    ) = saved_state
    tokens = queries.shape[0]
    local_heads = queries.shape[1]
    local_width = local_heads * HD
    score_scale = HD ** (-0.5)
    grad_active = jnp.dot(
        lax.all_gather(grad_out.astype(jnp.bfloat16), "tensor", axis=0, tiled=True),
        reduce_weight.T,
        preferred_element_type=jnp.float32,
    )
    gelu_pull = jax.vjp(partial(jax.nn.gelu, approximate=True), hidden_pre)[1]
    grad_pre = gelu_pull(grad_active)[0].astype(jnp.bfloat16)
    grad_two = lax.psum_scatter(
        jnp.dot(grad_pre, expand_weight.T, preferred_element_type=jnp.float32),
        "tensor",
        scatter_dimension=0,
        tiled=True,
    )
    grad_residual = grad_out + norm_back(grad_two, unit_two, inverse_two, gain_two)
    grad_heads = jnp.dot(
        lax.all_gather(grad_residual.astype(jnp.bfloat16), "tensor", axis=0, tiled=True),
        mixer_weight.T,
        preferred_element_type=jnp.float32,
    ).astype(jnp.bfloat16)
    grad_heads = grad_heads.reshape(tokens, local_heads, HD)
    pre_keys, pre_values = split_prefix(prefix_full, local_width)
    seq_scores, pre_scores = attention_scores(queries, seq_keys, pre_keys, valid, query_start)
    seq_prob = jnp.exp(seq_scores - log_total)
    pre_prob = jnp.exp(pre_scores - log_total)
    seq_dprob = jnp.einsum(
        "qhd,khd->hqk", grad_heads, seq_values, preferred_element_type=jnp.float32
    )
    pre_dprob = jnp.einsum(
        "qhd,khd->hqk", grad_heads, pre_values, preferred_element_type=jnp.float32
    )
    delta_row = jnp.sum(seq_prob * seq_dprob, axis=2, keepdims=True) + jnp.sum(
        pre_prob * pre_dprob, axis=2, keepdims=True
    )
    seq_dscore = (seq_prob * (seq_dprob - delta_row)).astype(jnp.bfloat16)
    pre_dscore = (pre_prob * (pre_dprob - delta_row)).astype(jnp.bfloat16)
    seq_low = seq_prob.astype(jnp.bfloat16)
    pre_low = pre_prob.astype(jnp.bfloat16)
    grad_queries = jnp.einsum(
        "hqk,khd->qhd", seq_dscore, seq_keys, preferred_element_type=jnp.float32
    )
    grad_queries = (
        grad_queries
        + jnp.einsum("hqk,khd->qhd", pre_dscore, pre_keys, preferred_element_type=jnp.float32)
    ) * score_scale
    key_term = (
        jnp.einsum("hqk,qhd->khd", seq_dscore, queries, preferred_element_type=jnp.float32)
        * score_scale
    )
    value_term = jnp.einsum("hqk,qhd->khd", seq_low, grad_heads, preferred_element_type=jnp.float32)
    grad_keys, grad_values = (
        lax.psum_scatter(key_term.reshape(-1, local_width), "dp", scatter_dimension=0, tiled=True),
        lax.psum_scatter(
            value_term.reshape(-1, local_width), "dp", scatter_dimension=0, tiled=True
        ),
    )
    pre_key_grad = (
        jnp.einsum("hqk,qhd->khd", pre_dscore, queries, preferred_element_type=jnp.float32)
        * score_scale
    )
    pre_value_grad = jnp.einsum(
        "hqk,qhd->khd", pre_low, grad_heads, preferred_element_type=jnp.float32
    )
    prefix_term = jnp.concatenate(
        [pre_key_grad.reshape(-1, local_width), pre_value_grad.reshape(-1, local_width)], axis=1
    )
    grad_mixed = jnp.concatenate(
        [grad_queries.reshape(tokens, local_width), grad_keys, grad_values], axis=1
    ).astype(jnp.bfloat16)
    grad_one = lax.psum_scatter(
        jnp.dot(grad_mixed, triple_weight.T, preferred_element_type=jnp.float32),
        "tensor",
        scatter_dimension=0,
        tiled=True,
    )
    grad_input = grad_residual + norm_back(grad_one, unit_one, inverse_one, gain_one)
    return (grad_input, prefix_term)


def shards(
    block_input,
    output_grad,
    valid_len,
    first_gain,
    first_bias,
    triple_weight,
    triple_bias,
    mixer_weight,
    mixer_bias,
    second_gain,
    second_bias,
    expand_weight,
    expand_bias,
    reduce_weight,
    reduce_bias,
    prefix_table,
    inner_weight,
    inner_bias,
    outer_weight,
    outer_bias,
):
    section_index = lax.axis_index("section")
    micro_count = block_input.shape[0]
    share_rows = block_input.shape[1]
    model_width = block_input.shape[2]
    local_width = triple_weight.shape[3]
    query_start = lax.axis_index("dp") * (share_rows * lax.axis_size("tensor"))
    weights = (
        first_gain[0],
        first_bias[0],
        triple_weight[0].reshape(-1, 3 * local_width),
        triple_bias[0].reshape(3 * local_width),
        mixer_weight[0],
        mixer_bias[0],
        second_gain[0],
        second_bias[0],
        expand_weight[0],
        expand_bias[0],
        reduce_weight[0],
        reduce_bias[0],
    )
    inner_pre = jnp.dot(prefix_table, inner_weight, preferred_element_type=jnp.float32) + inner_bias
    inner_act = jnp.tanh(inner_pre)
    inner_low = inner_act.astype(jnp.bfloat16)
    outer_local = outer_weight[:, 0].reshape(outer_weight.shape[0], 2 * local_width)
    prefix_full = (
        jnp.dot(inner_low, outer_local, preferred_element_type=jnp.float32)
        + outer_bias[0].reshape(2 * local_width)
    ).astype(jnp.bfloat16)
    moments = micro_count + 1
    carried = jnp.zeros((share_rows, model_width), jnp.bfloat16)
    results = []
    stored_states = []
    for moment in range(moments):
        micro_index = jnp.clip(moment - section_index, 0, micro_count - 1)
        inputs = jnp.where(
            section_index == 0, block_input[min(moment, micro_count - 1)], carried
        ).astype(jnp.float32)
        result, saved_state = layer_forward(
            inputs, weights, prefix_full, valid_len[micro_index], query_start
        )
        result_low = result.astype(jnp.bfloat16)
        results.append(result_low)
        stored_states.append(inputs)
        if moment + 1 < moments:
            carried = passed_along(result_low, "section", 1)
    grad_carried = jnp.zeros((share_rows, model_width), jnp.bfloat16)
    grad_list = []
    prefix_grad = jnp.zeros((prefix_full.shape[0], 2 * local_width), jnp.float32)
    for moment in range(moments):
        micro_index = moment - 1 + section_index
        valid_tick = (micro_index >= 0) & (micro_index < micro_count)
        clipped = jnp.clip(micro_index, 0, micro_count - 1)
        grad_in = jnp.where(
            section_index == 1, output_grad[min(moment, micro_count - 1)], grad_carried
        ).astype(jnp.float32)
        early_state = stored_states[max(moment - 1, 0)]
        late_state = stored_states[min(moment + 1, moments - 1)]
        picked = jnp.where(section_index == 0, early_state, late_state)
        picked_state = layer_forward(picked, weights, prefix_full, valid_len[clipped], query_start)[
            1
        ]
        grad_input, prefix_term = layer_backward(
            grad_in, picked_state, weights, prefix_full, valid_len[clipped], query_start
        )
        prefix_grad = prefix_grad + jnp.where(valid_tick, prefix_term, 0.0)
        grad_low = grad_input.astype(jnp.bfloat16)
        grad_list.append(grad_low)
        if moment + 1 < moments:
            grad_carried = passed_along(grad_low, "section", -1)
    layer_outputs = jnp.stack(
        [
            jnp.where(section_index == 0, results[number], results[number + 1])
            for number in range(micro_count)
        ]
    )[None]
    input_grads = jnp.stack(
        [
            jnp.where(section_index == 0, grad_list[number + 1], grad_list[number])
            for number in range(micro_count)
        ]
    )[None]
    prefix_total = lax.psum(prefix_grad, "dp")
    return (layer_outputs, input_grads) + prefix_back(
        prefix_total,
        prefix_full,
        inner_act,
        inner_low,
        outer_local,
        prefix_table,
        inner_weight,
        local_width,
    )


def dot_nn(left, right):
    return lax.dot_general(left, right, (((1,), (0,)), ((), ())), preferred_element_type=f32)


def dot_nt(left, right):
    return lax.dot_general(left, right, (((1,), (1,)), ((), ())), preferred_element_type=f32)


def dot_split(left, right, dot):
    high = left.astype(bf16)
    low = (left - high.astype(f32)).astype(bf16)
    return dot(high, right) + dot(low, right)


class Sizes:
    def __init__(self, planes, blocks, rows, width, local_width, hidden, prefix_rows):
        self.planes = planes
        self.blocks = blocks
        self.rows = rows
        self.block_rows = rows * planes
        self.width = width
        self.local_width = local_width
        self.hidden = hidden
        self.prefix_rows = prefix_rows
        self.cells = planes * blocks
        self.tile = 256


def both_layers(
    z,
    valid_ref,
    gain_one_in,
    bias_one_in,
    triple_bias_in,
    mixer_bias_in,
    gain_two_in,
    bias_two_in,
    expand_bias_in,
    reduce_bias_in,
    table_in,
    inner_bias_in,
    outer_bias_in,
    x_in,
    gy_in,
    triple_in,
    mixer_in,
    expand_in,
    reduce_in,
    inner_in,
    outer_in,
    rows_out,
    parts_out,
    vec,
    tbias,
    triple_own,
    wq,
    wm,
    we,
    wr,
    pre,
    xs,
    gys,
    qkv_send,
    qkv,
    ot_send,
    att,
    y_send,
    y_recv,
    gh_send,
    gh,
    dm_send,
    dm,
    gi_send,
    gi_recv,
    y_relay,
    gi_relay,
    gh_relay,
    z_one,
    inv_one,
    z_two,
    inv_two,
    gelu_grad,
    upper,
    expons_low,
    expons_pre,
    scales,
    dscores,
    dscores_pre,
    values_n,
    queries_n,
    grads_n,
    out_t,
    keys_n,
    normed,
    wide,
    total,
    grad_res,
    resid,
    y_last,
    active_last,
    gi_own,
    pg,
    pg_recv,
    pg_sum,
    pg_all,
    table_pad,
    inner_w,
    outer_raw,
    outer_w,
    hid_part,
    hid_recv,
    hid_pair,
    hid_all,
    send_sem,
    recv_sem,
    local_sem,
    phase_sem,
):
    lo_out, ig_out = rows_out.at[0], rows_out.at[1]
    s = lax.axis_index("section")
    t = lax.axis_index("tensor")
    d = lax.axis_index("dp")
    nt, nb, rows, brows, tile = z.planes, z.blocks, z.rows, z.block_rows, z.tile
    cells = z.cells
    me = t * nb + d
    sib = (1 - s, t, d)
    counts = dict(send=0, recv=0, local=0)
    pending = []

    def claim(kind, number):
        first = counts[kind]
        counts[kind] += number
        return first

    def rcopy(src, dst, ss, rs, device):
        return pltpu.make_async_remote_copy(
            src_ref=src,
            dst_ref=dst,
            send_sem=send_sem.at[ss],
            recv_sem=recv_sem.at[rs],
            device_id=device,
            device_id_type=MESH,
        )

    def push(src, dst, rs, device, when=None):
        copy = rcopy(src, dst, claim("send", 1), rs, device)
        if when is None:
            copy.start()
            pending.append((copy, None))
        else:
            pl.when(when)(copy.start)
            pending.append((copy, when))

    def arrived(dst, rs, when=None):
        copy = rcopy(dst, dst, 0, rs, sib)
        if when is None:
            copy.wait_recv()
        else:
            pl.when(when)(copy.wait_recv)

    def lcopy(src, dst):
        copy = pltpu.make_async_copy(src, dst, local_sem.at[claim("local", 1)])
        copy.start()
        return copy

    outer = (t == 0) | (t == nt - 1)
    inner = jnp.logical_not(outer)
    across = lax.rem(t + 2, nt)
    beside = t + 1 - 2 * lax.rem(t, 2)

    def far(k):
        return ((t == 0) & (k == nt - 1)) | ((t == nt - 1) & (k == 1))

    def unheard(k):
        return ((t == 0) & (k == 1)) | ((t == nt - 1) & (k == nt - 1))

    def near(k):
        return jnp.logical_not(far(k))

    def plane(k):
        return lax.rem(t + k, nt)

    def block(k):
        return lax.rem(d + k, nb)

    barrier = pltpu.get_barrier_semaphore()
    for k in range(1, cells):
        pl.semaphore_signal(
            barrier, inc=1, device_id=(s, plane(k // nb), block(k % nb)), device_id_type=MESH
        )
    pl.semaphore_signal(barrier, inc=1, device_id=sib, device_id_type=MESH)

    load_x = lcopy(x_in.at[s], xs.at[0, t])
    load_triple = lcopy(triple_in, triple_own)
    load_inner = lcopy(inner_in, inner_w)
    load_outer = lcopy(outer_in, outer_raw)
    load_mixer = lcopy(mixer_in, wm.at[s, pl.ds(pl.multiple_of(t * z.local_width, 256), z.local_width)])
    load_expand = lcopy(expand_in, we.at[s])
    load_reduce = lcopy(reduce_in, wr.at[s])
    load_gy = lcopy(gy_in.at[s], gys.at[1, t])

    for layer in range(2):
        for k in (1, nt - 1):

            @pl.when(unheard(k))
            def _():
                y_recv[layer, k] = jnp.zeros((rows, z.width), bf16)
                gi_recv[layer, k] = jnp.zeros((rows, z.width), bf16)

        @pl.when(outer)
        def _():
            for j in range(nb):
                gh[layer, (nt - 1 - t) * nb + j] = jnp.zeros((HD, brows), bf16)

    pl.semaphore_wait(barrier, cells)

    half = rows // 2

    def parts_of(ref):
        return ref.at[pl.ds(0, half)], ref.at[pl.ds(half, half)]

    def spread(src, buf, layer):
        first = claim("recv", nt + 2)
        for i, (one, goal) in enumerate(zip(parts_of(src), parts_of(buf.at[layer, t]))):
            push(one, goal, first + (2, nt)[i], (s, across, d), outer)
        push(src, buf.at[layer, t], first + 2, (s, across, d), inner)
        for k in (1, 3):
            push(src, buf.at[layer, t], first + k, (s, plane(k), d), near(k))
        return first

    def spread_relay(buf, layer, first):
        for i, one in enumerate(parts_of(buf.at[layer, across])):
            arrived(one, first + (2, nt)[i], inner)
            push(one, one, first + (2 * t - 1, nt + 1)[i], (s, beside, d), inner)

    def spread_wait(buf, layer, first, k):
        unit = buf.at[layer, plane(nt - k)]
        if k == 2:
            arrived(unit, first + k, outer)
        else:
            arrived(unit, first + k, jnp.logical_not(unheard(k)))
            for i, one in enumerate(parts_of(unit)):
                arrived(one, first + (k, nt + 1)[i], unheard(k))

    x_first = [None, None]
    gy_first = [None, None]
    x_first[0] = spread(x_in.at[s], xs, 0)

    for index, ref in enumerate(
        (gain_one_in, bias_one_in, mixer_bias_in, gain_two_in, bias_two_in, reduce_bias_in, expand_bias_in)
    ):
        vec[s, index : index + 1, :] = ref[...].astype(f32)
    for c in range(3):
        shift = jnp.broadcast_to(triple_bias_in[0, c : c + 1, :].astype(f32), (128, z.local_width)).T
        for j in range(nb):
            tbias[s, j, c * HD : (c + 1) * HD, :] = shift[j * HD : (j + 1) * HD].astype(bf16)
    table_pad[...] = jnp.zeros_like(table_pad)
    table_pad[0 : z.prefix_rows, :] = table_in[...].astype(f32)


    small = claim("recv", 3)
    push(vec.at[s], vec.at[s], small, sib)
    push(tbias.at[s], tbias.at[s], small + 1, sib)

    mix_first = [claim("recv", nt), claim("recv", nt)]
    mix_second = [claim("recv", nt * nb), claim("recv", nt * nb)]
    mix_third = [claim("recv", 1), claim("recv", 1)]

    def piece(layer, p, q):
        return wm.at[layer, pl.ds(pl.multiple_of((p * nb + q) * (z.local_width // nb), 64), z.local_width // nb)]

    def mix_one(layer):
        part = z.local_width // nb
        for k in range(1, nt):
            push(
                mixer_in.at[pl.ds(pl.multiple_of(d * part, 64), part)],
                piece(layer, t, d),
                mix_first[layer] + k,
                (s, plane(k), d),
                s == layer,
            )

    def mix_two(layer):
        for k in range(1, nt):
            source = plane(nt - k)
            arrived(piece(layer, source, d), mix_first[layer] + k, s == layer)
            for q in range(1, nb):
                push(
                    piece(layer, source, d),
                    piece(layer, source, d),
                    mix_second[layer] + k * nb + q,
                    (s, t, block(q)),
                    s == layer,
                )

    def mix_three(layer):
        for k in range(1, nt):
            for q in range(1, nb):
                arrived(
                    piece(layer, plane(nt - k), block(nb - q)),
                    mix_second[layer] + k * nb + q,
                    s == layer,
                )
        push(wm.at[layer], wm.at[layer], mix_third[layer], sib, s == layer)

    mix_one(0)

    load_triple.wait()
    for c in range(3):
        for n in range(z.width // tile):
            turned = triple_own[c, n * tile : (n + 1) * tile, :].T
            for j in range(nb):
                wq[s, j, c * HD : (c + 1) * HD, n * tile : (n + 1) * tile] = turned[j * HD : (j + 1) * HD]
    wq_first = claim("recv", 1)
    push(wq.at[s], wq.at[s], wq_first, sib)
    load_inner.wait()
    inner_act = jnp.tanh(
        dot_nn(table_pad[...].astype(bf16), inner_w[...]) + inner_bias_in[...].reshape(1, z.inner).astype(f32)
    )
    parts_out[0] = inner_act
    load_outer.wait()
    for c in range(2):
        outer_w[:, c * z.local_width : (c + 1) * z.local_width] = outer_raw[:, c, :]
    outer_shift = jnp.concatenate([outer_bias_in[0, 0:1, :], outer_bias_in[0, 1:2, :]], axis=1)
    prefix = (dot_nn(inner_act.astype(bf16), outer_w[...]) + outer_shift.astype(f32)).astype(bf16)
    parts_out[1] = prefix.astype(f32)
    for c in range(2):
        for j in range(nb):
            at = c * z.local_width + j * HD
            pre[s, c, j] = prefix[:, at : at + HD]
    push(pre.at[s], pre.at[s], small + 2, sib)
    arrived(vec.at[1 - s], small)
    arrived(tbias.at[1 - s], small + 1)
    arrived(pre.at[1 - s], small + 2)

    def row(layer, index):
        return vec[layer, index : index + 1, :]

    step = 32

    def norm_one(layer, p):
        def some(i, _):
            at = pl.multiple_of(i * step, step)
            x = xs[layer, p, pl.ds(at, step), :].astype(f32)
            center = x - jnp.mean(x, axis=1, keepdims=True)
            inverse = lax.rsqrt(jnp.mean(center * center, axis=1, keepdims=True) + epsilon)
            unit = center * inverse
            where = pl.multiple_of(p * rows + at, step)
            z_one[layer, pl.ds(where, step), :] = unit
            inv_one[layer, pl.ds(where, step), :] = inverse
            normed[pl.ds(where, step), :] = (unit * row(layer, 0) + row(layer, 1)).astype(bf16)
            return 0

        lax.fori_loop(0, rows // step, some, 0, unroll=True)

    def norm_two(layer):
        def some(i, _):
            at = pl.multiple_of(i * step, step)
            x = resid[pl.ds(at, step), :]
            center = x - jnp.mean(x, axis=1, keepdims=True)
            inverse = lax.rsqrt(jnp.mean(center * center, axis=1, keepdims=True) + epsilon)
            unit = center * inverse
            z_two[layer, pl.ds(at, step), :] = unit
            inv_two[layer, pl.ds(at, step), :] = inverse
            normed[pl.ds(at, step), :] = (unit * row(layer, 3) + row(layer, 4)).astype(bf16)
            return 0

        lax.fori_loop(0, brows // step, some, 0, unroll=True)

    def norm_pull(i, units, inverses, gain):
        at = pl.multiple_of(i * step, step)
        unit = units[pl.ds(at, step), :]
        scaled = total[pl.ds(at, step), :] * gain
        mean_grad = jnp.mean(scaled, axis=1, keepdims=True)
        mean_cross = jnp.mean(scaled * unit, axis=1, keepdims=True)
        return at, inverses[pl.ds(at, step), :] * (scaled - mean_grad - unit * mean_cross)

    def tiles(count, body):
        def some(i, _):
            body(pl.multiple_of(i * tile, tile))
            return 0

        lax.fori_loop(0, count // tile, some, 0, unroll=True)

    def positions(ref, b):
        return ref.at[:, pl.ds(pl.multiple_of(b * brows, brows), brows)]

    def project(layer):
        first = claim("recv", nb)
        for k in range(1, nb + 1):
            head = block(k)
            part = dot_nt(wq[layer, head], normed[...])
            shift = tbias[layer, head].astype(f32)
            part = (part + jnp.concatenate([shift, shift], axis=1)).astype(bf16)
            if k < nb:
                qkv_send[layer, k] = part
                push(qkv_send.at[layer, k], positions(qkv.at[layer], d), first + k, (s, t, head))
            else:
                qkv[layer, :, pl.ds(pl.multiple_of(d * brows, brows), brows)] = part
        return first

    def attend(layer, first):
        out_first = claim("recv", cells)
        pre_keys = pre[layer, 0, d]
        pre_values = pre[layer, 1, d].T
        prefix_row = lax.broadcasted_iota(jnp.int32, (z.prefix_pad, brows), 0)
        key_at = lax.broadcasted_iota(jnp.int32, (brows, brows), 0)
        query_at = lax.broadcasted_iota(jnp.int32, (brows, brows), 1)
        valid = valid_ref[s]
        for b in range(nb):
            here = slice(b * brows, (b + 1) * brows)
            arrived(positions(qkv.at[layer], b), first + lax.rem(d + nb - b, nb), d != b)
            keys_n[layer, here] = qkv[layer, HD : 2 * HD, here].T
            queries = (qkv[layer, 0:HD, here].astype(f32) * HD ** (-0.5)).astype(bf16)

            def scores_of(kb):
                scores = dot_nn(keys_n[layer, kb * brows : (kb + 1) * brows], queries)
                if kb == b:
                    seen = key_at <= query_at
                    if b == nb - 1:
                        seen = seen & (key_at + b * brows < valid)
                    scores = jnp.where(seen, scores, masked_score)
                return scores

            pre_scores = dot_nn(pre_keys, queries)
            pre_scores = jnp.where(prefix_row < z.prefix_rows, pre_scores, masked_score)
            peak = jnp.max(pre_scores, axis=0, keepdims=True)
            for kb in range(b + 1):
                peak = jnp.maximum(peak, jnp.max(scores_of(kb), axis=0, keepdims=True))
            expons = jnp.exp(pre_scores - peak)
            expons_pre[layer, :, here] = expons
            denominator = jnp.sum(expons, axis=0, keepdims=True)
            for kb in range(b + 1):
                expons = jnp.exp(scores_of(kb) - peak)
                denominator = denominator + jnp.sum(expons, axis=0, keepdims=True)
                expons_low[layer, kb * brows : (kb + 1) * brows, here] = expons.astype(bf16)
            scale = 1.0 / denominator
            scales[layer, b] = scale
            seen_keys = (b + 1) * brows
            result = dot_nn(
                qkv[layer, 2 * HD : 3 * HD, :seen_keys], expons_low[layer, :seen_keys, here]
            )
            result = result + dot_nn(pre_values, expons_pre[layer, :, here].astype(bf16))
            result = result * scale
            out_t[layer, b] = result
            low = result.astype(bf16)
            ot_send[layer, b] = low
            for k in (2, 1, 3, 0):
                if k == 0:
                    push(ot_send.at[layer, b], att.at[layer, me], out_first + me, (s, t, b), d != b)

                    @pl.when(d == b)
                    def _():
                        att[layer, me] = low
                else:
                    push(
                        ot_send.at[layer, b], att.at[layer, me], out_first + me, (s, plane(k), b), near(k)
                    )
        return out_first

    def att_relay(layer, first):
        for j in range(nb):
            cell = across * nb + j
            arrived(att.at[layer, cell], first + cell, inner)
            push(att.at[layer, cell], att.at[layer, cell], first + cell, (s, beside, d), inner)

    def mixer_rows(layer, first):
        att_relay(layer, first)
        for cell in range(cells):
            seen = inner & (across == cell // nb)
            arrived(att.at[layer, cell], first + cell, (me != cell) & jnp.logical_not(seen))
        if layer == 0:
            mix_three(0)
        arrived(wm.at[layer], mix_third[layer], s != layer)
        for p in range(nt):
            joined = att[layer, p * nb : (p + 1) * nb].reshape(nb * HD, brows)
            wide[:, p * nb * HD : (p + 1) * nb * HD] = joined.T

        def some(at):
            x = xs[layer, :, :, pl.ds(at, tile)].reshape(brows, tile).astype(f32)
            shift = vec[layer, 2:3, pl.ds(at, tile)]
            resid[:, pl.ds(at, tile)] = dot_nn(wide[...], wm[layer, :, pl.ds(at, tile)]) + x + shift

        tiles(z.width, some)

    def grad_active():
        def some(at):
            last = gys[1].reshape(brows, z.width)
            upper[:, pl.ds(at, tile)] = dot_nt(last, wr[1, pl.ds(at, tile), :])

        tiles(z.hidden, some)

    def feed_first(layer, active):
        def some(at):
            v = dot_nn(normed[...], we[layer, :, pl.ds(at, tile)]) + vec[layer, 6:7, pl.ds(at, tile)]
            root = 0.7978845608028654
            square = v * v
            th = jnp.tanh(root * v * (1.0 + 0.044715 * square))
            half = 0.5 * (1.0 + th)
            active[:, pl.ds(at, tile)] = (v * half).astype(bf16)
            slope = half + (0.5 * root) * v * (1.0 - th * th) * (1.0 + 3.0 * 0.044715 * square)
            if layer == 0:
                gelu_grad[:, pl.ds(at, tile)] = slope
            else:
                wide[:, pl.ds(at, tile)] = (upper[:, pl.ds(at, tile)] * slope).astype(bf16)

        tiles(z.hidden, some)

    def feed_second(layer, active):
        def some(at):
            part = dot_nn(active[...], wr[layer, :, pl.ds(at, tile)])
            total[:, pl.ds(at, tile)] = part
            y_send[layer, :, :, pl.ds(at, tile)] = part.astype(bf16).reshape(nt, rows, tile)

        tiles(z.width, some)
        return scatter(layer, y_send, y_recv, y_relay)

    def scatter(layer, out, back, relay):
        first = claim("recv", nt + 3)
        for i, (one, goal) in enumerate(zip(parts_of(out.at[layer, nt - 1 - t]), parts_of(relay.at[layer]))):
            push(one, goal, first + nt + i, (s, beside, d), outer)
        for k in (2, 1, 3):
            go = near(k) if k != 2 else outer
            push(out.at[layer, plane(k)], back.at[layer, k], first + k, (s, plane(k), d), go)
        return first

    def scatter_relay(layer, out, back, relay, full, first):
        for i in range(2):
            arrived(parts_of(relay.at[layer])[i], first + nt + i, inner)

            @pl.when(inner)
            def _():
                at = pl.ds(i * half, half)
                where = pl.ds(pl.multiple_of(across * rows + i * half, half), half)
                out[layer, across, at] = (full[where, :] + relay[layer, at].astype(f32)).astype(bf16)

            one, goal = parts_of(out.at[layer, across])[i], parts_of(back.at[layer, 2])[i]
            push(one, goal, first + (2, nt + 2)[i], (s, across, d), inner)

    def scatter_wait(layer, back, first, result):
        for k in (1, 3, 2):
            if k == 2:
                arrived(back.at[layer, k], first + k, inner)
                for i, one in enumerate(parts_of(back.at[layer, k])):
                    arrived(one, first + (2, nt + 2)[i], outer)
            else:
                arrived(back.at[layer, k], first + k, jnp.logical_not(unheard(k)))
            result = result + back[layer, k].astype(f32)
        return result

    def own_rows(ref):
        return ref[pl.ds(pl.multiple_of(t * rows, rows), rows), :]

    def output_sum(layer, first, base):
        return scatter_wait(layer, y_recv, first, base).astype(bf16)

    out_sem = claim("recv", 4)
    out_loads = []

    def put(src, out, layer, index):
        push(src, out.at[0, s], out_sem + index, sib, s != layer)
        copy = pltpu.make_async_copy(src, out.at[0, s], local_sem.at[claim("local", 1)])
        pl.when(s == layer)(copy.start)
        out_loads.append((copy, s == layer))

    own_weights = [load_mixer, load_expand, load_reduce]
    feed_recv = claim("recv", 2)
    y_base = []
    out_first = None
    for layer in range(2):
        if layer == 0:
            load_x.wait()

        norm_one(layer, t)
        spread_relay(xs, layer, x_first[layer])
        for k in (2, 1, 3):
            spread_wait(xs, layer, x_first[layer], k)
            norm_one(layer, plane(nt - k))
        if layer == 0:
            arrived(wq.at[0], wq_first, s == 1)
        else:
            arrived(wq.at[1], wq_first, s == 0)
        q_first = project(layer)
        if layer == 0:
            push(expand_in, we.at[s], feed_recv, sib)
            push(reduce_in, wr.at[s], feed_recv + 1, sib)
            mix_two(0)
            mix_one(1)
        else:
            mix_three(1)
            load_gy.wait()
            gy_first[1] = spread(gys.at[1, t], gys, 1)
        out_first = attend(layer, q_first)
        if layer == 0:
            for copy in own_weights:
                copy.wait()
            arrived(we.at[1 - s], feed_recv)
            arrived(wr.at[1 - s], feed_recv + 1)
        if layer == 1:
            spread_relay(gys, 1, gy_first[1])
            for k in range(1, nt):
                spread_wait(gys, 1, gy_first[1], k)
            grad_active()
        mixer_rows(layer, out_first)
        norm_two(layer)
        y_base.append(None)
        feed_first(layer, wide if layer == 0 else active_last)
        if layer == 0:
            y_first = feed_second(layer, wide)
            scatter_relay(0, y_send, y_recv, y_relay, total, y_first)
            base = own_rows(resid) + own_rows(total) + row(layer, 5)
            mix_two(1)
            low = output_sum(0, y_first, base)
            xs[1, t] = low
            x_first[1] = spread(xs.at[1, t], xs, 1)
            put(xs.at[1, t], lo_out, 0, 0)

    def grad_hidden(layer):
        def some(at):
            part = dot_nt(gys[layer].reshape(brows, z.width), wr[layer, pl.ds(at, tile), :])
            wide[:, pl.ds(at, tile)] = (part * gelu_grad[:, pl.ds(at, tile)]).astype(bf16)

        tiles(z.hidden, some)

    def grad_mid(layer):
        def some(at):
            total[:, pl.ds(at, tile)] = dot_nt(wide[...], we[layer, pl.ds(at, tile), :])

        tiles(z.width, some)

        def pull(i, _):
            at, part = norm_pull(i, z_two.at[layer], inv_two.at[layer], row(layer, 3))
            above = gys[layer, i // (rows // step), pl.ds(lax.rem(i, rows // step) * step, step), :]
            part = part + above.astype(f32) * (1.0 / nt)
            grad_res[pl.ds(at, step), :] = part
            normed[pl.ds(at, step), :] = part.astype(bf16)
            return 0

        lax.fori_loop(0, brows // step, pull, 0, unroll=True)

    def grad_to_heads(layer):
        first = claim("recv", cells)
        relay_sem = claim("recv", 2)
        pairs = [pl.ds(0, nb // 2), pl.ds(nb // 2, nb - nb // 2)]

        def share(p, index):
            here = wm[layer, pl.ds(pl.multiple_of(p * z.local_width, z.local_width), z.local_width), :]
            part = dot_nt(here, normed[...]).astype(bf16).reshape(nb, HD, brows)
            gh_send[layer, index] = part
            return part

        def pass_on(p, index, when):
            for j in range(nb):
                push(gh_send.at[layer, index, j], gh.at[layer, me], first + me, (s, p, j), when)

        share(nt - 1 - t, 0)
        for i, two in enumerate(pairs):
            push(gh_send.at[layer, 0, two], gh_relay.at[layer, two], relay_sem + i, (s, beside, d), outer)
        pass_on(nt - 1 - t, 0, inner)
        share(across, 1)
        pass_on(across, 1, outer)
        share(beside, 2)
        pass_on(beside, 2, None)
        part = share(t, 3)
        for j in range(nb):
            push(gh_send.at[layer, 3, j], gh.at[layer, me], first + me, (s, t, j), d != j)

            @pl.when(d == j)
            def _():
                gh[layer, me] = part[j]

        for i, two in enumerate(pairs):
            arrived(gh_relay.at[layer, two], relay_sem + i, inner)

            @pl.when(inner)
            def _():
                met = gh_send[layer, 1, two].astype(f32) + gh_relay[layer, two].astype(f32)
                gh_send[layer, 1, two] = met.astype(bf16)

            for j in range(two.start, two.start + two.size):
                push(gh_send.at[layer, 1, j], gh.at[layer, me], first + me, (s, across, j), inner)

        return first

    def attend_back(layer, first):
        for b in range(nb):
            here = slice(b * brows, (b + 1) * brows)
            values_n[here] = qkv[layer, 2 * HD : 3 * HD, here].T
            queries = (qkv[layer, 0:HD, here].astype(f32) * HD ** (-0.5)).astype(bf16)
            queries_n[here] = queries.T
        for cell in range(cells):
            seen = outer & (t + cell // nb == nt - 1)
            arrived(gh.at[layer, cell], first + cell, (me != cell) & jnp.logical_not(seen))
        out_first = claim("recv", nb)
        pre_values = pre[layer, 1, d]
        pre_keys = pre[layer, 0, d].T
        for b in reversed(range(nb)):
            here = slice(b * brows, (b + 1) * brows)
            grad = gh[layer, b].astype(f32)
            for p in range(1, nt):
                grad = grad + gh[layer, p * nb + b].astype(f32)
            grad = grad.astype(bf16)
            scale = scales[layer, b]
            wide_grad = grad.astype(f32)
            delta = jnp.sum(wide_grad * out_t[layer, b], axis=0, keepdims=True)
            grads_n[here] = (wide_grad * scale).astype(bf16).T
            prob = expons_pre[layer, :, here] * scale
            dscores_pre[:, here] = (prob * (dot_nn(pre_values, grad) - delta)).astype(bf16)
            for kb in range(b + 1):
                rows_k = slice(kb * brows, (kb + 1) * brows)
                prob = expons_low[layer, rows_k, here].astype(f32) * scale
                dprob = dot_nn(values_n[rows_k], grad)
                dscores[rows_k, here] = (prob * (dprob - delta)).astype(bf16)
            seen_keys = (b + 1) * brows
            dq = dot_nn(qkv[layer, HD : 2 * HD, :seen_keys], dscores[:seen_keys, here])
            dq = dq + dot_nn(pre_keys, dscores_pre[:, here])
            dkey = dot_nn(dscores[here, b * brows :], queries_n[b * brows :])
            dvalue = dot_nn(expons_low[layer, here, b * brows :], grads_n[b * brows :])
            joined = jnp.concatenate(
                [dq * HD ** (-0.5), dkey.T, dvalue.T], axis=0
            ).astype(bf16)
            dm_send[layer, b] = joined
            push(dm_send.at[layer, b], dm.at[layer, d], out_first + d, (s, t, b), d != b)

            @pl.when(d == b)
            def _():
                dm[layer, d] = joined

        pg[layer, 0] = dot_nn(dscores_pre[...], queries_n[...])
        pg[layer, 1] = dot_nn(expons_pre[layer].astype(bf16), grads_n[...])
        return out_first

    def grad_rows(layer, first):
        for j in range(nb):
            arrived(dm.at[layer, j], first + j, d != j)
        for j in range(nb):
            wide[:, j * 3 * HD : (j + 1) * 3 * HD] = dm[layer, j].T
        depth = nb * 3 * HD

        def some(at):
            right = wq[layer, :, :, pl.ds(at, tile)].reshape(depth, tile)
            total[:, pl.ds(at, tile)] = dot_nn(wide[:, :depth], right)

        tiles(z.width, some)

        def pull(i, _):
            at, part = norm_pull(i, z_one.at[layer], inv_one.at[layer], row(layer, 0))
            part = part + grad_res[pl.ds(at, step), :]
            grad_res[pl.ds(at, step), :] = part
            p = i // (rows // step)
            gi_send[layer, p, pl.ds(lax.rem(i, rows // step) * step, step), :] = part.astype(bf16)
            return 0

        lax.fori_loop(0, brows // step, pull, 0, unroll=True)
        return scatter(layer, gi_send, gi_recv, gi_relay)

    def grad_sum(layer, first):
        return scatter_wait(layer, gi_recv, first, own_rows(grad_res)).astype(bf16)

    for layer in (1, 0):
        if layer == 0:
            spread_relay(gys, 0, gy_first[0])
            for k in range(1, nt):
                spread_wait(gys, 0, gy_first[0], k)
            grad_hidden(0)
        grad_mid(layer)
        heads_first = grad_to_heads(layer)
        if layer == 1:
            y_first = feed_second(1, active_last)
            gi_own[...] = own_rows(resid) + own_rows(total) + row(1, 5)
        rows_first = attend_back(layer, heads_first)
        if layer == 1:
            scatter_relay(1, y_send, y_recv, y_relay, total, y_first)
        if layer == 0:
            sib_sem = claim("recv", 1)
            push(pg.at[1 - s], pg_recv, sib_sem, sib)
            arrived(pg_recv, sib_sem)
            pg_sum[...] = pg[s] + pg_recv[...]
            all_first = claim("recv", nb)
            for k in range(1, nb):
                push(pg_sum, pg_all.at[d], all_first + k, (s, t, block(k)))
            pg_all[d] = pg_sum[...]
        grads_first = grad_rows(layer, rows_first)
        if layer == 1:
            scatter_relay(1, gi_send, gi_recv, gi_relay, grad_res, grads_first)
            y_last[...] = output_sum(1, y_first, gi_own[...])
            put(y_last, lo_out, 1, 1)
            gys[0, t] = grad_sum(1, grads_first)
            gy_first[0] = spread(gys.at[0, t], gys, 0)
            put(gys.at[0, t], ig_out, 1, 2)
        else:
            for k in range(1, nb):
                arrived(pg_all.at[block(nb - k)], all_first + k)
            for c in range(2):
                joined = jnp.concatenate([pg_all[j, c] for j in range(nb)], axis=1)
                parts_out[2, :, c * z.local_width : (c + 1) * z.local_width] = joined
            part = jnp.zeros((z.prefix_pad, z.inner), f32)
            for j in range(nb):
                for c in range(2):
                    at = c * z.local_width + j * HD
                    part = part + dot_split(pg_all[j, c], outer_w[:, at : at + HD], dot_nt)
            hid_part[...] = part
            hid_sem = claim("recv", 1)
            push(hid_part, hid_recv, hid_sem, sib)
            arrived(hid_recv, hid_sem)
            hid_pair[...] = hid_part[...] + hid_recv[...]
            hid_first = claim("recv", nt)
            for k in range(1, nt):
                push(hid_pair, hid_all.at[t], hid_first + k, (s, plane(k), d))
            hid_all[t] = hid_pair[...]
            scatter_relay(0, gi_send, gi_recv, gi_relay, grad_res, grads_first)
            gi_low = grad_sum(0, grads_first)
            xs[0, t] = gi_low
            put(xs.at[0, t], ig_out, 0, 3)
            for k in range(1, nt):
                arrived(hid_all.at[plane(nt - k)], hid_first + k)
            part = hid_all[0]
            for p in range(1, nt):
                part = part + hid_all[p]
            parts_out[3] = part

    for index, (out, layer) in enumerate(((lo_out, 0), (lo_out, 1), (ig_out, 1), (ig_out, 0))):
        arrived(out.at[0, 1 - s], out_sem + index, s == layer)
    for copy, when in pending:
        if when is None:
            copy.wait_send()
        else:
            pl.when(when)(copy.wait_send)
    for copy, when in out_loads:
        pl.when(when)(copy.wait)
    z.counts = counts


def run_layers(z, small, large):
    nt, nb, rows, brows = z.planes, z.blocks, z.rows, z.block_rows
    width, hidden = z.width, z.hidden
    length = nb * brows
    V = pltpu.VMEM
    any_space = pl.BlockSpec(memory_space=pl.ANY)
    scratch = [
        V((2, 8, width), f32),
        V((2, nb, 3 * HD, 128), bf16),
        V((3, width, z.local_width), bf16),
        V((2, nb, 3 * HD, width), bf16),
        V((2, width, width), bf16),
        V((2, width, hidden), bf16),
        V((2, hidden, width), bf16),
        V((2, 2, nb, z.prefix_pad, HD), bf16),
        V((2, nt, rows, width), bf16),
        V((2, nt, rows, width), bf16),
        V((2, nb, 3 * HD, brows), bf16),
        V((2, 3 * HD, length), bf16),
        V((2, nb, HD, brows), bf16),
        V((2, z.cells, HD, brows), bf16),
        V((2, nt, rows, width), bf16),
        V((2, nt, rows, width), bf16),
        V((2, nt, nb, HD, brows), bf16),
        V((2, z.cells, HD, brows), bf16),
        V((2, nb, 3 * HD, brows), bf16),
        V((2, nb, 3 * HD, brows), bf16),
        V((2, nt, rows, width), bf16),
        V((2, nt, rows, width), bf16),
        V((2, rows, width), bf16),
        V((2, rows, width), bf16),
        V((2, nb, HD, brows), bf16),
        V((2, brows, width), f32),
        V((2, brows, 1), f32),
        V((2, brows, width), f32),
        V((2, brows, 1), f32),
        V((brows, hidden), f32),
        V((brows, hidden), f32),
        V((2, length, length), bf16),
        V((2, z.prefix_pad, length), f32),
        V((2, nb, 1, brows), f32),
        V((length, length), bf16),
        V((z.prefix_pad, length), bf16),
        V((length, HD), bf16),
        V((length, HD), bf16),
        V((length, HD), bf16),
        V((2, nb, HD, brows), f32),
        V((2, length, HD), bf16),
        V((brows, width), bf16),
        V((brows, width), bf16),
        V((brows, width), f32),
        V((brows, width), f32),
        V((brows, width), f32),
        V((rows, width), bf16),
        V((brows, width), bf16),
        V((rows, width), f32),
        V((2, 2, z.prefix_pad, HD), f32),
        V((2, z.prefix_pad, HD), f32),
        V((2, z.prefix_pad, HD), f32),
        V((nb, 2, z.prefix_pad, HD), f32),
        V((z.prefix_pad, width), f32),
        V((width, z.inner), bf16),
        V((z.inner, 2, z.local_width), bf16),
        V((z.inner, 2 * z.local_width), bf16),
        V((z.prefix_pad, z.inner), f32),
        V((z.prefix_pad, z.inner), f32),
        V((z.prefix_pad, z.inner), f32),
        V((nt, z.prefix_pad, z.inner), f32),
        pltpu.SemaphoreType.DMA((256,)),
        pltpu.SemaphoreType.DMA((256,)),
        pltpu.SemaphoreType.DMA((20,)),
        pltpu.SemaphoreType.REGULAR,
    ]
    return pl.pallas_call(
        partial(both_layers, z),
        out_shape=(
            jax.ShapeDtypeStruct((2, 1, 2, rows, width), bf16),
            jax.ShapeDtypeStruct((4, z.prefix_pad, z.inner), f32),
        ),
        in_specs=[pl.BlockSpec(memory_space=pltpu.SMEM)]
        + [pl.BlockSpec(memory_space=pltpu.VMEM)] * (len(small) - 1)
        + [any_space] * len(large),
        out_specs=(any_space, pl.BlockSpec(memory_space=pltpu.VMEM)),
        scratch_shapes=scratch,
        compiler_params=pltpu.CompilerParams(
            collective_id=0, has_side_effects=True, vmem_limit_bytes=60 * 2**20
        ),
        cost_estimate=pl.CostEstimate(
            flops=7 * 10**9, bytes_accessed=16 * 2**20, transcendentals=4 * 10**6
        ),
    )(*small, *large)


def prefix_end(
    z, rows_in, parts_in, table_in, inner_in,
    lo_out, ig_out, states_out, table_out, inner_out, inner_bias_out, outer_out, outer_bias_out,
    table_pad, sems,
):
    copies = [
        pltpu.make_async_copy(rows_in.at[0], lo_out, sems.at[0]),
        pltpu.make_async_copy(rows_in.at[1], ig_out, sems.at[1]),
    ]
    for copy in copies:
        copy.start()
    count, width = z.prefix_rows, z.local_width
    act = parts_in[0]
    inner_grad = parts_in[3] * (1.0 - act * act)
    inner_bias_out[...] = jnp.sum(inner_grad, axis=0, keepdims=True)
    table_pad[...] = jnp.zeros_like(table_pad)
    table_pad[0:count, :] = table_in[...].astype(f32)
    high = inner_grad.astype(bf16)
    low = (inner_grad - high.astype(f32)).astype(bf16)
    table_turned = table_pad[...].T.astype(bf16)
    inner_out[...] = dot_nn(table_turned, high) + dot_nn(table_turned, low)
    table_out[...] = (dot_nt(high, inner_in[...]) + dot_nt(low, inner_in[...]))[0:count]
    act_turned = act.T.astype(bf16)
    for c in range(2):
        at = slice(c * width, (c + 1) * width)
        states_out[:, c, :] = parts_in[1, 0:count, at].astype(bf16)
        total = parts_in[2, :, at]
        high = total.astype(bf16)
        low = (total - high.astype(f32)).astype(bf16)
        outer_out[:, c, :] = dot_nn(act_turned, high) + dot_nn(act_turned, low)
        outer_bias_out[0, c : c + 1, :] = jnp.sum(total, axis=0, keepdims=True)
    for copy in copies:
        copy.wait()


def finish(z, both_rows, parts, table, inner_weight):
    any_space = pl.BlockSpec(memory_space=pl.ANY)
    whole = pl.BlockSpec(memory_space=pltpu.VMEM)
    rows = jax.ShapeDtypeStruct(both_rows.shape[1:], bf16)
    return pl.pallas_call(
        partial(prefix_end, z),
        out_shape=(
            rows,
            rows,
            jax.ShapeDtypeStruct((z.prefix_rows, 2, z.local_width), bf16),
            jax.ShapeDtypeStruct((z.prefix_rows, z.width), f32),
            jax.ShapeDtypeStruct((z.width, z.inner), f32),
            jax.ShapeDtypeStruct((1, z.inner), f32),
            jax.ShapeDtypeStruct((z.inner, 2, z.local_width), f32),
            jax.ShapeDtypeStruct((1, 2, z.local_width), f32),
        ),
        in_specs=[any_space] + [whole] * 3,
        out_specs=(any_space,) * 2 + (whole,) * 6,
        scratch_shapes=[pltpu.VMEM((z.prefix_pad, z.width), f32), pltpu.SemaphoreType.DMA((2,))],
        compiler_params=pltpu.CompilerParams(vmem_limit_bytes=32 * 2**20),
    )(both_rows, parts, table, inner_weight)


def head_a_device(
    block_input,
    output_grad,
    valid_len,
    first_gain,
    first_bias,
    triple_weight,
    triple_bias,
    mixer_weight,
    mixer_bias,
    second_gain,
    second_bias,
    expand_weight,
    expand_bias,
    reduce_weight,
    reduce_bias,
    prefix_table,
    inner_weight,
    inner_bias,
    outer_weight,
    outer_bias,
):
    planes, blocks = lax.axis_size("tensor"), lax.axis_size("dp")
    local_width = triple_weight.shape[3]
    prefix_rows = prefix_table.shape[0]
    z = Sizes(
        planes,
        blocks,
        block_input.shape[1],
        block_input.shape[2],
        local_width,
        expand_weight.shape[2],
        prefix_rows,
    )
    z.prefix_pad = -(-prefix_rows // 16) * 16
    z.inner = inner_weight.shape[1]
    small = (
        valid_len,
        first_gain,
        first_bias,
        triple_bias,
        mixer_bias,
        second_gain,
        second_bias,
        expand_bias,
        reduce_bias,
        prefix_table,
        inner_bias,
        outer_bias,
    )
    large = (
        block_input,
        output_grad,
        triple_weight[0].transpose(1, 0, 2),
        mixer_weight[0],
        expand_weight[0],
        reduce_weight[0],
        inner_weight,
        outer_weight[:, 0],
    )
    results = finish(z, *run_layers(z, small, large), prefix_table, inner_weight)
    (
        layer_outputs,
        input_grads,
        prefix_states,
        table_grad,
        inner_weight_grad,
        inner_bias_grad,
        outer_weight_grad,
        outer_bias_grad,
    ) = results
    return (
        layer_outputs,
        input_grads,
        prefix_states.transpose(1, 0, 2)[None],
        table_grad,
        inner_weight_grad,
        inner_bias_grad.reshape(-1),
        outer_weight_grad.reshape(-1, 1, 2, local_width),
        outer_bias_grad,
    )


def prefix_back(
    prefix_total,
    prefix_full,
    inner_act,
    inner_low,
    outer_local,
    prefix_table,
    inner_weight,
    local_width,
):
    inner_float = inner_low.astype(f32)
    outer_float = outer_local.astype(f32)
    outer_weight_grad = jnp.dot(inner_float.T, prefix_total, precision=highest).reshape(
        -1, 1, 2, local_width
    )
    outer_bias_grad = jnp.sum(prefix_total, axis=0).reshape(1, 2, local_width)
    hidden_grad = lax.psum(
        jnp.dot(prefix_total, outer_float.T, precision=highest), ("section", "tensor")
    )
    inner_grad = hidden_grad * (1.0 - inner_act * inner_act)
    inner_weight_grad = jnp.dot(prefix_table.astype(f32).T, inner_grad, precision=highest)
    inner_bias_grad = jnp.sum(inner_grad, axis=0)
    table_grad = jnp.dot(inner_grad, inner_weight.astype(f32).T, precision=highest)
    prefix_states = prefix_full.reshape(-1, 2, local_width).transpose(1, 0, 2)[None]
    return (
        prefix_states,
        table_grad,
        inner_weight_grad,
        inner_bias_grad,
        outer_weight_grad,
        outer_bias_grad,
    )


def solution(mesh):
    def step(*args):
        triple_weight = args[5]
        micro_count, share_rows, width = args[0].shape
        fits = (
            lax.axis_size("section") == 2
            and micro_count == 2
            and triple_weight.shape[3] == HD * lax.axis_size("dp")
            and share_rows * lax.axis_size("tensor") == 256
            and triple_weight.shape[3] % 256 == 0
            and width % 256 == 0
            and args[11].shape[2] == width
        )
        return head_a_device(*args) if fits else shards(*args)

    return jax.shard_map(
        step,
        mesh=mesh,
        in_specs=(
            P(None, ("dp", "tensor"), None),
            P(None, ("dp", "tensor"), None),
            P(),
            P("section", None),
            P("section", None),
            P("section", None, None, "tensor"),
            P("section", None, "tensor"),
            P("section", "tensor", None),
            P("section", None),
            P("section", None),
            P("section", None),
            P("section", None, "tensor"),
            P("section", "tensor"),
            P("section", "tensor", None),
            P("section", None),
            P(),
            P(),
            P(),
            P(None, "section", None, "tensor"),
            P("section", None, "tensor"),
        ),
        out_specs=(
            P("section", None, ("dp", "tensor"), None),
            P("section", None, ("dp", "tensor"), None),
            P("section", None, None, "tensor"),
            P(),
            P(),
            P(),
            P(None, "section", None, "tensor"),
            P("section", None, "tensor"),
        ),
        check_vma=False,
    )
```

```python
from functools import partial

import jax
import jax.numpy as jnp
from jax import lax
from jax.experimental import pallas as pl
from jax.experimental.pallas import tpu as pltpu
from jax.sharding import PartitionSpec as P

HD = 64


epsilon = 1e-05
masked_score = -1e30
highest = lax.Precision.HIGHEST
MESH = pl.DeviceIdType.MESH
f32 = jnp.float32
bf16 = jnp.bfloat16


def passed_along(block, axis, distance):
    devices = range(lax.axis_size(axis))
    route = [(i - distance, i) for i in devices if i - distance in devices]
    return lax.ppermute(block, axis, route)


def layer_norm(values, norm_gain, norm_bias):
    center = values - jnp.mean(values, axis=-1, keepdims=True)
    variance = jnp.mean(center * center, axis=-1, keepdims=True)
    inverse = lax.rsqrt(variance + epsilon)
    normed = center * inverse
    return (normed * norm_gain + norm_bias, normed, inverse)


def norm_back(grad_out, normed, inverse, norm_gain):
    scaled = grad_out * norm_gain
    mean_grad = jnp.mean(scaled, axis=-1, keepdims=True)
    mean_cross = jnp.mean(scaled * normed, axis=-1, keepdims=True)
    return inverse * (scaled - mean_grad - normed * mean_cross)


def attention_scores(queries, seq_keys, pre_keys, valid, query_start):
    score_scale = HD ** (-0.5)
    seq_scores = (
        jnp.einsum("qhd,khd->hqk", queries, seq_keys, preferred_element_type=jnp.float32)
        * score_scale
    )
    pre_scores = (
        jnp.einsum("qhd,khd->hqk", queries, pre_keys, preferred_element_type=jnp.float32)
        * score_scale
    )
    query_pos = query_start + lax.broadcasted_iota(jnp.int32, (queries.shape[0], 1), 0)
    key_pos = lax.broadcasted_iota(jnp.int32, (1, seq_keys.shape[0]), 1)
    visible = (key_pos <= query_pos) & (key_pos < valid)
    seq_scores = jnp.where(visible[None], seq_scores, masked_score)
    return (seq_scores, pre_scores)


def split_prefix(prefix_full, local_width):
    local_heads = local_width // HD
    pre_keys = prefix_full[:, :local_width].reshape(-1, local_heads, HD)
    pre_values = prefix_full[:, local_width:].reshape(-1, local_heads, HD)
    return (pre_keys, pre_values)


def layer_forward(inputs, weights, prefix_full, valid, query_start):
    (
        gain_one,
        bias_one,
        triple_weight,
        triple_bias,
        mixer_weight,
        mixer_bias,
        gain_two,
        bias_two,
        expand_weight,
        expand_bias,
        reduce_weight,
        reduce_bias,
    ) = weights
    local_width = triple_weight.shape[1] // 3
    local_heads = local_width // HD
    normed_one, unit_one, inverse_one = layer_norm(inputs, gain_one, bias_one)
    mixed_rows = (
        jnp.dot(
            lax.all_gather(normed_one.astype(jnp.bfloat16), "tensor", axis=0, tiled=True),
            triple_weight,
            preferred_element_type=jnp.float32,
        )
        + triple_bias
    ).astype(jnp.bfloat16)
    tokens = mixed_rows.shape[0]
    queries = mixed_rows[:, :local_width].reshape(tokens, local_heads, HD)
    seq_keys, seq_values = (
        lax.all_gather(mixed_rows[:, local_width : 2 * local_width], "dp", axis=0, tiled=True),
        lax.all_gather(mixed_rows[:, 2 * local_width :], "dp", axis=0, tiled=True),
    )
    seq_keys = seq_keys.reshape(-1, local_heads, HD)
    seq_values = seq_values.reshape(-1, local_heads, HD)
    pre_keys, pre_values = split_prefix(prefix_full, local_width)
    seq_scores, pre_scores = attention_scores(queries, seq_keys, pre_keys, valid, query_start)
    row_max = jnp.maximum(
        jnp.max(seq_scores, axis=2, keepdims=True), jnp.max(pre_scores, axis=2, keepdims=True)
    )
    seq_exp = jnp.exp(seq_scores - row_max)
    pre_exp = jnp.exp(pre_scores - row_max)
    row_total = jnp.sum(seq_exp, axis=2, keepdims=True) + jnp.sum(pre_exp, axis=2, keepdims=True)
    log_total = row_max + jnp.log(row_total)
    seq_low = (seq_exp / row_total).astype(jnp.bfloat16)
    pre_low = (pre_exp / row_total).astype(jnp.bfloat16)
    attended = jnp.einsum("hqk,khd->qhd", seq_low, seq_values, preferred_element_type=jnp.float32)
    attended = attended + jnp.einsum(
        "hqk,khd->qhd", pre_low, pre_values, preferred_element_type=jnp.float32
    )
    attended = attended.astype(jnp.bfloat16).reshape(tokens, local_width)
    mixer_out = lax.psum_scatter(
        jnp.dot(attended, mixer_weight, preferred_element_type=jnp.float32),
        "tensor",
        scatter_dimension=0,
        tiled=True,
    )
    residual = inputs + mixer_out + mixer_bias
    normed_two, unit_two, inverse_two = layer_norm(residual, gain_two, bias_two)
    hidden_pre = (
        jnp.dot(
            lax.all_gather(normed_two.astype(jnp.bfloat16), "tensor", axis=0, tiled=True),
            expand_weight,
            preferred_element_type=jnp.float32,
        )
        + expand_bias
    )
    active = jax.nn.gelu(hidden_pre, approximate=True).astype(jnp.bfloat16)
    result = (
        residual
        + lax.psum_scatter(
            jnp.dot(active, reduce_weight, preferred_element_type=jnp.float32),
            "tensor",
            scatter_dimension=0,
            tiled=True,
        )
        + reduce_bias
    )
    saved_state = (
        unit_one,
        inverse_one,
        queries,
        seq_keys,
        seq_values,
        log_total,
        unit_two,
        inverse_two,
        hidden_pre,
    )
    return (result, saved_state)


def layer_backward(grad_out, saved_state, weights, prefix_full, valid, query_start):
    (
        gain_one,
        bias_one,
        triple_weight,
        triple_bias,
        mixer_weight,
        mixer_bias,
        gain_two,
        bias_two,
        expand_weight,
        expand_bias,
        reduce_weight,
        reduce_bias,
    ) = weights
    (
        unit_one,
        inverse_one,
        queries,
        seq_keys,
        seq_values,
        log_total,
        unit_two,
        inverse_two,
        hidden_pre,
    ) = saved_state
    tokens = queries.shape[0]
    local_heads = queries.shape[1]
    local_width = local_heads * HD
    score_scale = HD ** (-0.5)
    grad_active = jnp.dot(
        lax.all_gather(grad_out.astype(jnp.bfloat16), "tensor", axis=0, tiled=True),
        reduce_weight.T,
        preferred_element_type=jnp.float32,
    )
    gelu_pull = jax.vjp(partial(jax.nn.gelu, approximate=True), hidden_pre)[1]
    grad_pre = gelu_pull(grad_active)[0].astype(jnp.bfloat16)
    grad_two = lax.psum_scatter(
        jnp.dot(grad_pre, expand_weight.T, preferred_element_type=jnp.float32),
        "tensor",
        scatter_dimension=0,
        tiled=True,
    )
    grad_residual = grad_out + norm_back(grad_two, unit_two, inverse_two, gain_two)
    grad_heads = jnp.dot(
        lax.all_gather(grad_residual.astype(jnp.bfloat16), "tensor", axis=0, tiled=True),
        mixer_weight.T,
        preferred_element_type=jnp.float32,
    ).astype(jnp.bfloat16)
    grad_heads = grad_heads.reshape(tokens, local_heads, HD)
    pre_keys, pre_values = split_prefix(prefix_full, local_width)
    seq_scores, pre_scores = attention_scores(queries, seq_keys, pre_keys, valid, query_start)
    seq_prob = jnp.exp(seq_scores - log_total)
    pre_prob = jnp.exp(pre_scores - log_total)
    seq_dprob = jnp.einsum(
        "qhd,khd->hqk", grad_heads, seq_values, preferred_element_type=jnp.float32
    )
    pre_dprob = jnp.einsum(
        "qhd,khd->hqk", grad_heads, pre_values, preferred_element_type=jnp.float32
    )
    delta_row = jnp.sum(seq_prob * seq_dprob, axis=2, keepdims=True) + jnp.sum(
        pre_prob * pre_dprob, axis=2, keepdims=True
    )
    seq_dscore = (seq_prob * (seq_dprob - delta_row)).astype(jnp.bfloat16)
    pre_dscore = (pre_prob * (pre_dprob - delta_row)).astype(jnp.bfloat16)
    seq_low = seq_prob.astype(jnp.bfloat16)
    pre_low = pre_prob.astype(jnp.bfloat16)
    grad_queries = jnp.einsum(
        "hqk,khd->qhd", seq_dscore, seq_keys, preferred_element_type=jnp.float32
    )
    grad_queries = (
        grad_queries
        + jnp.einsum("hqk,khd->qhd", pre_dscore, pre_keys, preferred_element_type=jnp.float32)
    ) * score_scale
    key_term = (
        jnp.einsum("hqk,qhd->khd", seq_dscore, queries, preferred_element_type=jnp.float32)
        * score_scale
    )
    value_term = jnp.einsum("hqk,qhd->khd", seq_low, grad_heads, preferred_element_type=jnp.float32)
    grad_keys, grad_values = (
        lax.psum_scatter(key_term.reshape(-1, local_width), "dp", scatter_dimension=0, tiled=True),
        lax.psum_scatter(
            value_term.reshape(-1, local_width), "dp", scatter_dimension=0, tiled=True
        ),
    )
    pre_key_grad = (
        jnp.einsum("hqk,qhd->khd", pre_dscore, queries, preferred_element_type=jnp.float32)
        * score_scale
    )
    pre_value_grad = jnp.einsum(
        "hqk,qhd->khd", pre_low, grad_heads, preferred_element_type=jnp.float32
    )
    prefix_term = jnp.concatenate(
        [pre_key_grad.reshape(-1, local_width), pre_value_grad.reshape(-1, local_width)], axis=1
    )
    grad_mixed = jnp.concatenate(
        [grad_queries.reshape(tokens, local_width), grad_keys, grad_values], axis=1
    ).astype(jnp.bfloat16)
    grad_one = lax.psum_scatter(
        jnp.dot(grad_mixed, triple_weight.T, preferred_element_type=jnp.float32),
        "tensor",
        scatter_dimension=0,
        tiled=True,
    )
    grad_input = grad_residual + norm_back(grad_one, unit_one, inverse_one, gain_one)
    return (grad_input, prefix_term)


def shards(
    block_input,
    output_grad,
    valid_len,
    first_gain,
    first_bias,
    triple_weight,
    triple_bias,
    mixer_weight,
    mixer_bias,
    second_gain,
    second_bias,
    expand_weight,
    expand_bias,
    reduce_weight,
    reduce_bias,
    prefix_table,
    inner_weight,
    inner_bias,
    outer_weight,
    outer_bias,
):
    section_index = lax.axis_index("section")
    micro_count = block_input.shape[0]
    share_rows = block_input.shape[1]
    model_width = block_input.shape[2]
    local_width = triple_weight.shape[3]
    query_start = lax.axis_index("dp") * (share_rows * lax.axis_size("tensor"))
    weights = (
        first_gain[0],
        first_bias[0],
        triple_weight[0].reshape(-1, 3 * local_width),
        triple_bias[0].reshape(3 * local_width),
        mixer_weight[0],
        mixer_bias[0],
        second_gain[0],
        second_bias[0],
        expand_weight[0],
        expand_bias[0],
        reduce_weight[0],
        reduce_bias[0],
    )
    inner_pre = jnp.dot(prefix_table, inner_weight, preferred_element_type=jnp.float32) + inner_bias
    inner_act = jnp.tanh(inner_pre)
    inner_low = inner_act.astype(jnp.bfloat16)
    outer_local = outer_weight[:, 0].reshape(outer_weight.shape[0], 2 * local_width)
    prefix_full = (
        jnp.dot(inner_low, outer_local, preferred_element_type=jnp.float32)
        + outer_bias[0].reshape(2 * local_width)
    ).astype(jnp.bfloat16)
    moments = micro_count + 1
    carried = jnp.zeros((share_rows, model_width), jnp.bfloat16)
    results = []
    stored_states = []
    for moment in range(moments):
        micro_index = jnp.clip(moment - section_index, 0, micro_count - 1)
        inputs = jnp.where(
            section_index == 0, block_input[min(moment, micro_count - 1)], carried
        ).astype(jnp.float32)
        result, saved_state = layer_forward(
            inputs, weights, prefix_full, valid_len[micro_index], query_start
        )
        result_low = result.astype(jnp.bfloat16)
        results.append(result_low)
        stored_states.append(inputs)
        if moment + 1 < moments:
            carried = passed_along(result_low, "section", 1)
    grad_carried = jnp.zeros((share_rows, model_width), jnp.bfloat16)
    grad_list = []
    prefix_grad = jnp.zeros((prefix_full.shape[0], 2 * local_width), jnp.float32)
    for moment in range(moments):
        micro_index = moment - 1 + section_index
        valid_tick = (micro_index >= 0) & (micro_index < micro_count)
        clipped = jnp.clip(micro_index, 0, micro_count - 1)
        grad_in = jnp.where(
            section_index == 1, output_grad[min(moment, micro_count - 1)], grad_carried
        ).astype(jnp.float32)
        early_state = stored_states[max(moment - 1, 0)]
        late_state = stored_states[min(moment + 1, moments - 1)]
        picked = jnp.where(section_index == 0, early_state, late_state)
        picked_state = layer_forward(picked, weights, prefix_full, valid_len[clipped], query_start)[
            1
        ]
        grad_input, prefix_term = layer_backward(
            grad_in, picked_state, weights, prefix_full, valid_len[clipped], query_start
        )
        prefix_grad = prefix_grad + jnp.where(valid_tick, prefix_term, 0.0)
        grad_low = grad_input.astype(jnp.bfloat16)
        grad_list.append(grad_low)
        if moment + 1 < moments:
            grad_carried = passed_along(grad_low, "section", -1)
    layer_outputs = jnp.stack(
        [
            jnp.where(section_index == 0, results[number], results[number + 1])
            for number in range(micro_count)
        ]
    )[None]
    input_grads = jnp.stack(
        [
            jnp.where(section_index == 0, grad_list[number + 1], grad_list[number])
            for number in range(micro_count)
        ]
    )[None]
    prefix_total = lax.psum(prefix_grad, "dp")
    return (layer_outputs, input_grads) + prefix_back(
        prefix_total,
        prefix_full,
        inner_act,
        inner_low,
        outer_local,
        prefix_table,
        inner_weight,
        local_width,
    )


def dot_nn(left, right):
    return lax.dot_general(left, right, (((1,), (0,)), ((), ())), preferred_element_type=f32)


def dot_nt(left, right):
    return lax.dot_general(left, right, (((1,), (1,)), ((), ())), preferred_element_type=f32)


def dot_split(left, right, dot):
    high = left.astype(bf16)
    low = (left - high.astype(f32)).astype(bf16)
    return dot(high, right) + dot(low, right)


class Sizes:
    def __init__(self, planes, blocks, rows, width, local_width, hidden, prefix_rows):
        self.planes = planes
        self.blocks = blocks
        self.rows = rows
        self.block_rows = rows * planes
        self.width = width
        self.local_width = local_width
        self.hidden = hidden
        self.prefix_rows = prefix_rows
        self.cells = planes * blocks
        self.tile = 256
        self.sends = 48


def both_layers(
    z,
    valid_ref,
    gain_one_in,
    bias_one_in,
    triple_bias_in,
    mixer_bias_in,
    gain_two_in,
    bias_two_in,
    expand_bias_in,
    reduce_bias_in,
    table_in,
    inner_bias_in,
    outer_bias_in,
    x_in,
    gy_in,
    triple_in,
    mixer_in,
    expand_in,
    reduce_in,
    inner_in,
    outer_in,
    rows_out,
    vec,
    tbias,
    triple_own,
    wq,
    wm,
    we,
    wr,
    pre,
    xs,
    gys,
    qkv_send,
    qkv,
    ot_send,
    att,
    y_send,
    y_recv,
    gh_send,
    gh,
    dm_send,
    dm,
    gi_send,
    gi_recv,
    y_relay,
    gi_relay,
    gh_relay,
    z_one,
    inv_one,
    z_two,
    inv_two,
    gelu_grad,
    upper,
    expons_low,
    expons_pre,
    scales,
    dscores,
    dscores_pre,
    values_n,
    queries_n,
    grads_n,
    out_t,
    keys_n,
    normed,
    wide,
    total,
    grad_res,
    resid,
    y_last,
    active_last,
    gi_own,
    pg,
    pg_recv,
    pg_sum,
    pg_all,
    table_pad,
    inner_w,
    outer_raw,
    outer_w,
    hid_part,
    hid_recv,
    parts_low,
    hid_all,
    send_sem,
    recv_sem,
    local_sem,
    phase_sem,
):
    lo_out, ig_out = rows_out.at[0], rows_out.at[1]
    s = lax.axis_index("section")
    t = lax.axis_index("tensor")
    d = lax.axis_index("dp")
    nt, nb, rows, brows, tile = z.planes, z.blocks, z.rows, z.block_rows, z.tile
    cells = z.cells
    me = t * nb + d
    sib = (1 - s, t, d)
    counts = dict(send=0, recv=0, local=0)
    pending = []
    shared = {}

    def claim(kind, number, name=None):
        if name in shared:
            return shared[name]
        first = counts[kind]
        counts[kind] += number
        if name is not None:
            shared[name] = first
        return first

    def rcopy(src, dst, ss, rs, device):
        return pltpu.make_async_remote_copy(
            src_ref=src,
            dst_ref=dst,
            send_sem=send_sem.at[ss],
            recv_sem=recv_sem.at[rs],
            device_id=device,
            device_id_type=MESH,
        )

    def push(src, dst, rs, device, when=None):
        if len(pending) >= z.sends:
            sent(*pending[len(pending) - z.sends])
        copy = rcopy(src, dst, len(pending) % z.sends, rs, device)
        if when is None:
            copy.start()
        else:
            pl.when(when)(copy.start)
        pending.append((copy, when))

    def sent(copy, when):
        if when is None:
            copy.wait_send()
        else:
            pl.when(when)(copy.wait_send)

    def arrived(dst, rs, when=None):
        copy = rcopy(dst, dst, 0, rs, sib)
        if when is None:
            copy.wait_recv()
        else:
            pl.when(when)(copy.wait_recv)

    def lcopy(src, dst):
        copy = pltpu.make_async_copy(src, dst, local_sem.at[claim("local", 1)])
        copy.start()
        return copy

    outer = (t == 0) | (t == nt - 1)
    inner = jnp.logical_not(outer)
    across = lax.rem(t + 2, nt)
    beside = t + 1 - 2 * lax.rem(t, 2)

    def far(k):
        return ((t == 0) & (k == nt - 1)) | ((t == nt - 1) & (k == 1))

    def unheard(k):
        return ((t == 0) & (k == 1)) | ((t == nt - 1) & (k == nt - 1))

    def near(k):
        return jnp.logical_not(far(k))

    def keep(index, value):
        high = value.astype(bf16)
        low = (value - high.astype(f32)).astype(bf16)
        at, columns = index // 2 * z.prefix_pad, slice(index % 2 * z.inner, (index % 2 + 1) * z.inner)
        parts_low[at : at + z.prefix_pad, columns] = high
        at += 2 * z.prefix_pad
        parts_low[at : at + z.prefix_pad, columns] = low

    def plane(k):
        return lax.rem(t + k, nt)

    def block(k):
        return lax.rem(d + k, nb)

    barrier = pltpu.get_barrier_semaphore()
    for k in range(1, cells):
        pl.semaphore_signal(
            barrier, inc=1, device_id=(s, plane(k // nb), block(k % nb)), device_id_type=MESH
        )
    pl.semaphore_signal(barrier, inc=1, device_id=sib, device_id_type=MESH)

    load_x = lcopy(x_in.at[s], xs.at[0, t])
    load_triple = lcopy(triple_in, triple_own)
    load_inner = lcopy(inner_in, inner_w)
    load_outer = lcopy(outer_in, outer_raw)
    load_mixer = lcopy(mixer_in, wm.at[s, pl.ds(pl.multiple_of(t * z.local_width, 256), z.local_width)])
    load_expand = lcopy(expand_in, we.at[s])
    load_reduce = lcopy(reduce_in, wr.at[s])
    load_gy = lcopy(gy_in.at[s], gys.at[1, t])

    for layer in range(2):
        for k in (1, nt - 1):

            @pl.when(unheard(k))
            def _():
                y_recv[layer, k] = jnp.zeros((rows, z.width), bf16)
                gi_recv[layer, k] = jnp.zeros((rows, z.width), bf16)

        @pl.when(outer)
        def _():
            for j in range(nb):
                gh[layer, (nt - 1 - t) * nb + j] = jnp.zeros((HD, brows), bf16)

    pl.semaphore_wait(barrier, cells)

    half = rows // 2

    def parts_of(ref):
        return ref.at[pl.ds(0, half)], ref.at[pl.ds(half, half)]

    def spread(src, buf, layer, when=True):
        first = claim("recv", nt + 2, "rows" if buf is xs else "grads")
        for i, (one, goal) in enumerate(zip(parts_of(src), parts_of(buf.at[layer, t]))):
            push(one, goal, first + (2, nt)[i], (s, across, d), outer & when)
        push(src, buf.at[layer, t], first + 2, (s, across, d), inner & when)
        for k in (1, 3):
            push(src, buf.at[layer, t], first + k, (s, plane(k), d), near(k) & when)
        return first

    def spread_relay(buf, layer, first):
        for i, one in enumerate(parts_of(buf.at[layer, across])):
            arrived(one, first + (2, nt)[i], inner)
            push(one, one, first + (2 * t - 1, nt + 1)[i], (s, beside, d), inner)

    def spread_wait(buf, layer, first, k):
        unit = buf.at[layer, plane(nt - k)]
        if k == 2:
            arrived(unit, first + k, outer)
        else:
            arrived(unit, first + k, jnp.logical_not(unheard(k)))
            for i, one in enumerate(parts_of(unit)):
                arrived(one, first + (k, nt + 1)[i], unheard(k))

    x_first = [None, None]
    gy_first = [None, None]
    x_first[0] = spread(x_in.at[s], xs, 0, s == 0)

    for index, ref in enumerate(
        (gain_one_in, bias_one_in, mixer_bias_in, gain_two_in, bias_two_in, reduce_bias_in, expand_bias_in)
    ):
        vec[s, index : index + 1, :] = ref[...].astype(f32)
    for c in range(3):
        shift = jnp.broadcast_to(triple_bias_in[0, c : c + 1, :].astype(f32), (128, z.local_width)).T
        for j in range(nb):
            tbias[s, j, c * HD : (c + 1) * HD, :] = shift[j * HD : (j + 1) * HD].astype(bf16)
    table_pad[...] = jnp.zeros_like(table_pad)
    table_pad[0 : z.prefix_rows, :] = table_in[...].astype(f32)


    small = claim("recv", 3)
    push(vec.at[s], vec.at[s], small, sib)
    push(tbias.at[s], tbias.at[s], small + 1, sib)

    mix_first = claim("recv", nt)
    mix_second = claim("recv", nt * nb)
    mix_third = claim("recv", 1)

    def piece(layer, p, q):
        return wm.at[layer, pl.ds(pl.multiple_of((p * nb + q) * (z.local_width // nb), 64), z.local_width // nb)]

    def mix_one(layer):
        part = z.local_width // nb
        for k in range(1, nt):
            push(
                mixer_in.at[pl.ds(pl.multiple_of(d * part, 64), part)],
                piece(layer, t, d),
                mix_first + k,
                (s, plane(k), d),
                s == layer,
            )

    def mix_two(layer):
        for k in range(1, nt):
            source = plane(nt - k)
            arrived(piece(layer, source, d), mix_first + k, s == layer)
            for q in range(1, nb):
                push(
                    piece(layer, source, d),
                    piece(layer, source, d),
                    mix_second + k * nb + q,
                    (s, t, block(q)),
                    s == layer,
                )

    def mix_three(layer):
        for k in range(1, nt):
            for q in range(1, nb):
                arrived(
                    piece(layer, plane(nt - k), block(nb - q)),
                    mix_second + k * nb + q,
                    s == layer,
                )
        push(wm.at[layer], wm.at[layer], mix_third, sib, s == layer)

    mix_one(0)

    load_triple.wait()
    for c in range(3):
        for n in range(z.width // tile):
            turned = triple_own[c, n * tile : (n + 1) * tile, :].T
            for j in range(nb):
                wq[s, j, c * HD : (c + 1) * HD, n * tile : (n + 1) * tile] = turned[j * HD : (j + 1) * HD]
    wq_first = claim("recv", 1)
    push(wq.at[s], wq.at[s], wq_first, sib)
    load_inner.wait()
    inner_act = jnp.tanh(
        dot_nn(table_pad[...].astype(bf16), inner_w[...]) + inner_bias_in[...].reshape(1, z.inner).astype(f32)
    )
    keep(0, inner_act)
    load_outer.wait()
    for c in range(2):
        outer_w[:, c * z.local_width : (c + 1) * z.local_width] = outer_raw[:, c, :]
    outer_shift = jnp.concatenate([outer_bias_in[0, 0:1, :], outer_bias_in[0, 1:2, :]], axis=1)
    prefix = (dot_nn(inner_act.astype(bf16), outer_w[...]) + outer_shift.astype(f32)).astype(bf16)
    keep(1, prefix.astype(f32))
    for c in range(2):
        for j in range(nb):
            at = c * z.local_width + j * HD
            pre[s, c, j] = prefix[:, at : at + HD]
    push(pre.at[s], pre.at[s], small + 2, sib)
    arrived(vec.at[1 - s], small)
    arrived(tbias.at[1 - s], small + 1)
    arrived(pre.at[1 - s], small + 2)

    def row(layer, index):
        return vec[layer, index : index + 1, :]

    step = 32

    def norm_one(layer, p):
        def some(i, _):
            at = pl.multiple_of(i * step, step)
            x = xs[layer, p, pl.ds(at, step), :].astype(f32)
            center = x - jnp.mean(x, axis=1, keepdims=True)
            inverse = lax.rsqrt(jnp.mean(center * center, axis=1, keepdims=True) + epsilon)
            unit = center * inverse
            where = pl.multiple_of(p * rows + at, step)
            z_one[layer, pl.ds(where, step), :] = unit
            inv_one[layer, pl.ds(where, step), :] = inverse
            normed[pl.ds(where, step), :] = (unit * row(layer, 0) + row(layer, 1)).astype(bf16)
            return 0

        lax.fori_loop(0, rows // step, some, 0, unroll=True)

    def norm_two(layer):
        def some(i, _):
            at = pl.multiple_of(i * step, step)
            x = resid[pl.ds(at, step), :]
            center = x - jnp.mean(x, axis=1, keepdims=True)
            inverse = lax.rsqrt(jnp.mean(center * center, axis=1, keepdims=True) + epsilon)
            unit = center * inverse
            z_two[layer, pl.ds(at, step), :] = unit
            inv_two[layer, pl.ds(at, step), :] = inverse
            normed[pl.ds(at, step), :] = (unit * row(layer, 3) + row(layer, 4)).astype(bf16)
            return 0

        lax.fori_loop(0, brows // step, some, 0, unroll=True)

    def norm_pull(i, units, inverses, gain):
        at = pl.multiple_of(i * step, step)
        unit = units[pl.ds(at, step), :]
        scaled = total[pl.ds(at, step), :] * gain
        mean_grad = jnp.mean(scaled, axis=1, keepdims=True)
        mean_cross = jnp.mean(scaled * unit, axis=1, keepdims=True)
        return at, inverses[pl.ds(at, step), :] * (scaled - mean_grad - unit * mean_cross)

    def tiles(count, body):
        def some(i, _):
            body(pl.multiple_of(i * tile, tile))
            return 0

        lax.fori_loop(0, count // tile, some, 0, unroll=True)

    def positions(ref, b):
        return ref.at[:, pl.ds(pl.multiple_of(b * brows, brows), brows)]

    def project(layer):
        first = claim("recv", nb, "project")
        for k in range(1, nb + 1):
            head = block(k)
            part = dot_nt(wq[layer, head], normed[...])
            shift = tbias[layer, head].astype(f32)
            part = (part + jnp.concatenate([shift, shift], axis=1)).astype(bf16)
            if k < nb:
                qkv_send[layer, k] = part
                push(qkv_send.at[layer, k], positions(qkv.at[layer], d), first + k, (s, t, head))
            else:
                qkv[layer, :, pl.ds(pl.multiple_of(d * brows, brows), brows)] = part
        return first

    def attend(layer, first):
        out_first = claim("recv", cells, "attend")
        pre_keys = pre[layer, 0, d]
        pre_values = pre[layer, 1, d].T
        prefix_row = lax.broadcasted_iota(jnp.int32, (z.prefix_pad, brows), 0)
        key_at = lax.broadcasted_iota(jnp.int32, (brows, brows), 0)
        query_at = lax.broadcasted_iota(jnp.int32, (brows, brows), 1)
        valid = valid_ref[s]
        for b in range(nb):
            here = slice(b * brows, (b + 1) * brows)
            arrived(positions(qkv.at[layer], b), first + lax.rem(d + nb - b, nb), d != b)
            keys_n[layer, here] = qkv[layer, HD : 2 * HD, here].T
            queries = (qkv[layer, 0:HD, here].astype(f32) * HD ** (-0.5)).astype(bf16)

            def scores_of(kb):
                scores = dot_nn(keys_n[layer, kb * brows : (kb + 1) * brows], queries)
                if kb == b:
                    seen = key_at <= query_at
                    if b == nb - 1:
                        seen = seen & (key_at + b * brows < valid)
                    scores = jnp.where(seen, scores, masked_score)
                return scores

            pre_scores = dot_nn(pre_keys, queries)
            pre_scores = jnp.where(prefix_row < z.prefix_rows, pre_scores, masked_score)
            peak = jnp.max(pre_scores, axis=0, keepdims=True)
            for kb in range(b + 1):
                peak = jnp.maximum(peak, jnp.max(scores_of(kb), axis=0, keepdims=True))
            expons = jnp.exp(pre_scores - peak)
            expons_pre[layer, :, here] = expons
            denominator = jnp.sum(expons, axis=0, keepdims=True)
            for kb in range(b + 1):
                expons = jnp.exp(scores_of(kb) - peak)
                denominator = denominator + jnp.sum(expons, axis=0, keepdims=True)
                expons_low[layer, kb * brows : (kb + 1) * brows, here] = expons.astype(bf16)
            scale = 1.0 / denominator
            scales[layer, b] = scale
            seen_keys = (b + 1) * brows
            result = dot_nn(
                qkv[layer, 2 * HD : 3 * HD, :seen_keys], expons_low[layer, :seen_keys, here]
            )
            result = result + dot_nn(pre_values, expons_pre[layer, :, here].astype(bf16))
            result = result * scale
            out_t[layer, b] = result
            low = result.astype(bf16)
            ot_send[layer, b] = low
            for k in (2, 1, 3, 0):
                if k == 0:
                    push(ot_send.at[layer, b], att.at[layer, me], out_first + me, (s, t, b), d != b)

                    @pl.when(d == b)
                    def _():
                        att[layer, me] = low
                else:
                    push(
                        ot_send.at[layer, b], att.at[layer, me], out_first + me, (s, plane(k), b), near(k)
                    )
        return out_first

    def att_relay(layer, first):
        for j in range(nb):
            cell = across * nb + j
            arrived(att.at[layer, cell], first + cell, inner)
            push(att.at[layer, cell], att.at[layer, cell], first + cell, (s, beside, d), inner)

    def mixer_rows(layer, first):
        att_relay(layer, first)
        if layer == 0:
            mix_three(0)
        for at in range(0, z.width, tile):
            at = slice(at, at + tile)
            resid[:, at] = xs[layer, :, :, at].reshape(brows, tile).astype(f32) + vec[layer, 2:3, at]
        arrived(wm.at[layer], mix_third, s != layer)
        for p, seen in ((t, None), (beside, None), (across, inner), (nt - 1 - t, None)):
            for j in range(nb):
                cell = p * nb + j
                if seen is None:
                    arrived(att.at[layer, cell], first + cell, me != cell)
                else:
                    arrived(att.at[layer, cell], first + cell, jnp.logical_not(seen))
            joined = att[layer, pl.ds(p * nb, nb)].reshape(nb * HD, brows).T
            some_rows = pl.ds(pl.multiple_of(p * z.local_width, z.local_width), z.local_width)
            for at in range(0, z.width, tile):
                at = slice(at, at + tile)
                resid[:, at] += dot_nn(joined, wm[layer, some_rows, at])

    def grad_active():
        def some(at):
            last = gys[1].reshape(brows, z.width)
            upper[:, pl.ds(at, tile)] = dot_nt(last, wr[1, pl.ds(at, tile), :])

        tiles(z.hidden, some)

    def feed_first(layer, active):
        def some(at):
            v = dot_nn(normed[...], we[layer, :, pl.ds(at, tile)]) + vec[layer, 6:7, pl.ds(at, tile)]
            root = 0.7978845608028654
            square = v * v
            th = jnp.tanh(root * v * (1.0 + 0.044715 * square))
            half = 0.5 * (1.0 + th)
            active[:, pl.ds(at, tile)] = (v * half).astype(bf16)
            slope = half + (0.5 * root) * v * (1.0 - th * th) * (1.0 + 3.0 * 0.044715 * square)
            if layer == 0:
                gelu_grad[:, pl.ds(at, tile)] = slope
            else:
                wide[:, pl.ds(at, tile)] = (upper[:, pl.ds(at, tile)] * slope).astype(bf16)

        tiles(z.hidden, some)

    def feed_second(layer, active):
        def some(at):
            part = dot_nn(active[...], wr[layer, :, pl.ds(at, tile)])
            total[:, pl.ds(at, tile)] = part
            y_send[layer, :, :, pl.ds(at, tile)] = part.astype(bf16).reshape(nt, rows, tile)

        tiles(z.width, some)
        return scatter(layer, y_send, y_recv, y_relay)

    def scatter(layer, out, back, relay):
        first = claim("recv", nt + 3, "output" if out is y_send else "input")
        for i, (one, goal) in enumerate(zip(parts_of(out.at[layer, nt - 1 - t]), parts_of(relay.at[layer]))):
            push(one, goal, first + nt + i, (s, beside, d), outer)
        for k in (2, 1, 3):
            go = near(k) if k != 2 else outer
            push(out.at[layer, plane(k)], back.at[layer, k], first + k, (s, plane(k), d), go)
        return first

    def scatter_relay(layer, out, back, relay, full, first):
        for i in range(2):
            arrived(parts_of(relay.at[layer])[i], first + nt + i, inner)

            @pl.when(inner)
            def _():
                at = pl.ds(i * half, half)
                where = pl.ds(pl.multiple_of(across * rows + i * half, half), half)
                out[layer, across, at] = (full[where, :] + relay[layer, at].astype(f32)).astype(bf16)

            one, goal = parts_of(out.at[layer, across])[i], parts_of(back.at[layer, 2])[i]
            push(one, goal, first + (2, nt + 2)[i], (s, across, d), inner)

    def scatter_wait(layer, back, first, result):
        for k in (1, 3, 2):
            if k == 2:
                arrived(back.at[layer, k], first + k, inner)
                for i, one in enumerate(parts_of(back.at[layer, k])):
                    arrived(one, first + (2, nt + 2)[i], outer)
            else:
                arrived(back.at[layer, k], first + k, jnp.logical_not(unheard(k)))
            result = result + back[layer, k].astype(f32)
        return result

    def own_rows(ref):
        return ref[pl.ds(pl.multiple_of(t * rows, rows), rows), :]

    def output_sum(layer, first, base):
        return scatter_wait(layer, y_recv, first, base).astype(bf16)

    out_sem = claim("recv", 4)
    out_loads = []

    def put(src, out, layer, index):
        push(src, out.at[0, s], out_sem + index, sib, s != layer)
        copy = pltpu.make_async_copy(src, out.at[0, s], local_sem.at[claim("local", 1)])
        pl.when(s == layer)(copy.start)
        out_loads.append((copy, s == layer))

    own_weights = [load_mixer, load_expand, load_reduce]
    feed_recv = claim("recv", 2)
    out_first = None
    for layer in range(2):
        if layer == 0:
            load_x.wait()

            @pl.when(s == 1)
            def _():
                pl.semaphore_wait(phase_sem, 1)

            spread(x_in.at[s], xs, 0, s == 1)

        norm_one(layer, t)
        spread_relay(xs, layer, x_first[layer])
        for k in (2, 1, 3):
            spread_wait(xs, layer, x_first[layer], k)
            norm_one(layer, plane(nt - k))
            if layer == 0 and k == 3:

                @pl.when(s == 0)
                def _():
                    pl.semaphore_signal(phase_sem, inc=1, device_id=sib, device_id_type=MESH)

        if layer == 0:
            arrived(wq.at[0], wq_first, s == 1)
        else:
            arrived(wq.at[1], wq_first, s == 0)
        q_first = project(layer)
        if layer == 0:
            push(expand_in, we.at[s], feed_recv, sib)
            push(reduce_in, wr.at[s], feed_recv + 1, sib)
            mix_two(0)
            mix_one(1)
        else:
            mix_three(1)
            load_gy.wait()
            gy_first[1] = spread(gys.at[1, t], gys, 1)
        out_first = attend(layer, q_first)
        if layer == 0:
            for copy in own_weights:
                copy.wait()
        if layer == 1:
            arrived(we.at[1], feed_recv, s == 0)
            arrived(wr.at[1], feed_recv + 1, s == 0)
            spread_relay(gys, 1, gy_first[1])
            for k in range(1, nt):
                spread_wait(gys, 1, gy_first[1], k)
            grad_active()
        mixer_rows(layer, out_first)
        norm_two(layer)
        if layer == 0:
            arrived(we.at[0], feed_recv, s == 1)
            arrived(wr.at[0], feed_recv + 1, s == 1)
        feed_first(layer, wide if layer == 0 else active_last)
        if layer == 0:
            y_first = feed_second(layer, wide)
            scatter_relay(0, y_send, y_recv, y_relay, total, y_first)
            base = own_rows(resid) + own_rows(total) + row(layer, 5)
            mix_two(1)
            low = output_sum(0, y_first, base)
            xs[1, t] = low
            x_first[1] = spread(xs.at[1, t], xs, 1)
            put(xs.at[1, t], lo_out, 0, 0)

    def grad_hidden(layer):
        def some(at):
            part = dot_nt(gys[layer].reshape(brows, z.width), wr[layer, pl.ds(at, tile), :])
            wide[:, pl.ds(at, tile)] = (part * gelu_grad[:, pl.ds(at, tile)]).astype(bf16)

        tiles(z.hidden, some)

    def grad_mid(layer):
        def some(at):
            total[:, pl.ds(at, tile)] = dot_nt(wide[...], we[layer, pl.ds(at, tile), :])

        tiles(z.width, some)

        def pull(i, _):
            at, part = norm_pull(i, z_two.at[layer], inv_two.at[layer], row(layer, 3))
            above = gys[layer, i // (rows // step), pl.ds(lax.rem(i, rows // step) * step, step), :]
            part = part + above.astype(f32) * (1.0 / nt)
            grad_res[pl.ds(at, step), :] = part
            normed[pl.ds(at, step), :] = part.astype(bf16)
            return 0

        lax.fori_loop(0, brows // step, pull, 0, unroll=True)

    def grad_to_heads(layer):
        first = claim("recv", cells, "heads")
        relay_sem = claim("recv", 2, "heads beside")
        pairs = [pl.ds(0, nb // 2), pl.ds(nb // 2, nb - nb // 2)]

        def share(p, index):
            here = wm[layer, pl.ds(pl.multiple_of(p * z.local_width, z.local_width), z.local_width), :]
            part = dot_nt(here, normed[...]).astype(bf16).reshape(nb, HD, brows)
            gh_send[layer, index] = part
            return part

        def pass_on(p, index, when):
            for j in range(nb):
                push(gh_send.at[layer, index, j], gh.at[layer, me], first + me, (s, p, j), when)

        share(nt - 1 - t, 0)
        for i, two in enumerate(pairs):
            push(gh_send.at[layer, 0, two], gh_relay.at[layer, two], relay_sem + i, (s, beside, d), outer)
        pass_on(nt - 1 - t, 0, inner)
        share(across, 1)
        pass_on(across, 1, outer)
        share(beside, 2)
        pass_on(beside, 2, None)
        part = share(t, 3)
        for j in range(nb):
            push(gh_send.at[layer, 3, j], gh.at[layer, me], first + me, (s, t, j), d != j)

            @pl.when(d == j)
            def _():
                gh[layer, me] = part[j]

        for i, two in enumerate(pairs):
            arrived(gh_relay.at[layer, two], relay_sem + i, inner)

            @pl.when(inner)
            def _():
                met = gh_send[layer, 1, two].astype(f32) + gh_relay[layer, two].astype(f32)
                gh_send[layer, 1, two] = met.astype(bf16)

            for j in range(two.start, two.start + two.size):
                push(gh_send.at[layer, 1, j], gh.at[layer, me], first + me, (s, across, j), inner)

        return first

    def attend_back(layer, first):
        for b in range(nb):
            here = slice(b * brows, (b + 1) * brows)
            values_n[here] = qkv[layer, 2 * HD : 3 * HD, here].T
            queries = (qkv[layer, 0:HD, here].astype(f32) * HD ** (-0.5)).astype(bf16)
            queries_n[here] = queries.T
        for cell in range(cells):
            seen = outer & (t + cell // nb == nt - 1)
            arrived(gh.at[layer, cell], first + cell, (me != cell) & jnp.logical_not(seen))
        out_first = claim("recv", nb, "mixed")
        pre_values = pre[layer, 1, d]
        pre_keys = pre[layer, 0, d].T
        for b in reversed(range(nb)):
            here = slice(b * brows, (b + 1) * brows)
            grad = gh[layer, b].astype(f32)
            for p in range(1, nt):
                grad = grad + gh[layer, p * nb + b].astype(f32)
            grad = grad.astype(bf16)
            scale = scales[layer, b]
            wide_grad = grad.astype(f32)
            delta = jnp.sum(wide_grad * out_t[layer, b], axis=0, keepdims=True)
            grads_n[here] = (wide_grad * scale).astype(bf16).T
            prob = expons_pre[layer, :, here] * scale
            dscores_pre[:, here] = (prob * (dot_nn(pre_values, grad) - delta)).astype(bf16)
            for kb in range(b + 1):
                rows_k = slice(kb * brows, (kb + 1) * brows)
                prob = expons_low[layer, rows_k, here].astype(f32) * scale
                dprob = dot_nn(values_n[rows_k], grad)
                dscores[rows_k, here] = (prob * (dprob - delta)).astype(bf16)
            seen_keys = (b + 1) * brows
            dq = dot_nn(qkv[layer, HD : 2 * HD, :seen_keys], dscores[:seen_keys, here])
            dq = dq + dot_nn(pre_keys, dscores_pre[:, here])
            dkey = dot_nn(dscores[here, b * brows :], queries_n[b * brows :])
            dvalue = dot_nn(expons_low[layer, here, b * brows :], grads_n[b * brows :])
            joined = jnp.concatenate(
                [dq * HD ** (-0.5), dkey.T, dvalue.T], axis=0
            ).astype(bf16)
            dm_send[layer, b] = joined
            push(dm_send.at[layer, b], dm.at[layer, d], out_first + d, (s, t, b), d != b)

            @pl.when(d == b)
            def _():
                dm[layer, d] = joined

        pg[layer, 0] = dot_nn(dscores_pre[...], queries_n[...])
        pg[layer, 1] = dot_nn(expons_pre[layer].astype(bf16), grads_n[...])
        return out_first

    def grad_rows(layer, first):
        for j in range(nb):
            arrived(dm.at[layer, j], first + j, d != j)
        for j in range(nb):
            wide[:, j * 3 * HD : (j + 1) * 3 * HD] = dm[layer, j].T
        depth = nb * 3 * HD

        def some(at):
            right = wq[layer, :, :, pl.ds(at, tile)].reshape(depth, tile)
            total[:, pl.ds(at, tile)] = dot_nn(wide[:, :depth], right)

        tiles(z.width, some)

        def pull(i, _):
            at, part = norm_pull(i, z_one.at[layer], inv_one.at[layer], row(layer, 0))
            part = part + grad_res[pl.ds(at, step), :]
            grad_res[pl.ds(at, step), :] = part
            p = i // (rows // step)
            gi_send[layer, p, pl.ds(lax.rem(i, rows // step) * step, step), :] = part.astype(bf16)
            return 0

        lax.fori_loop(0, brows // step, pull, 0, unroll=True)
        return scatter(layer, gi_send, gi_recv, gi_relay)

    def grad_sum(layer, first):
        return scatter_wait(layer, gi_recv, first, own_rows(grad_res)).astype(bf16)

    for layer in (1, 0):
        if layer == 0:
            spread_relay(gys, 0, gy_first[0])
            for k in range(1, nt):
                spread_wait(gys, 0, gy_first[0], k)
            grad_hidden(0)
        grad_mid(layer)
        heads_first = grad_to_heads(layer)
        if layer == 1:
            y_first = feed_second(1, active_last)
            gi_own[...] = own_rows(resid) + own_rows(total) + row(1, 5)
        rows_first = attend_back(layer, heads_first)
        if layer == 1:
            scatter_relay(1, y_send, y_recv, y_relay, total, y_first)
        if layer == 0:
            sib_sem = claim("recv", 1)
            push(pg.at[1 - s], pg_recv, sib_sem, sib)
        grads_first = grad_rows(layer, rows_first)
        if layer == 0:
            arrived(pg_recv, sib_sem)
            pg_sum[...] = pg[s] + pg_recv[...]
            all_first = claim("recv", nb)
            for k in range(1, nb):
                push(pg_sum, pg_all.at[d], all_first + k, (s, t, block(k)))
            pg_all[d] = pg_sum[...]
        if layer == 1:
            scatter_relay(1, gi_send, gi_recv, gi_relay, grad_res, grads_first)
            y_last[...] = output_sum(1, y_first, gi_own[...])
            put(y_last, lo_out, 1, 1)
            gys[0, t] = grad_sum(1, grads_first)
            gy_first[0] = spread(gys.at[0, t], gys, 0)
            put(gys.at[0, t], ig_out, 1, 2)
        else:
            scatter_relay(0, gi_send, gi_recv, gi_relay, grad_res, grads_first)
            for k in range(1, nb):
                arrived(pg_all.at[block(nb - k)], all_first + k)
            keep(2, jnp.concatenate([pg_all[j, c] for c in range(2) for j in range(nb)], axis=1))
            part = jnp.zeros((z.prefix_pad, z.inner), f32)
            for j in range(nb):
                for c in range(2):
                    at = c * z.local_width + j * HD
                    part = part + dot_split(pg_all[j, c], outer_w[:, at : at + HD], dot_nt)
            hid_all[t] = part
            hid_first = claim("recv", nt)
            for k in range(1, nt):
                push(hid_all.at[t], hid_all.at[t], hid_first + k, (s, plane(k), d))
            xs[0, t] = grad_sum(0, grads_first)
            put(xs.at[0, t], ig_out, 0, 3)
            for k in range(1, nt):
                arrived(hid_all.at[plane(nt - k)], hid_first + k)
            part = hid_all[0]
            for p in range(1, nt):
                part = part + hid_all[p]
            hid_part[...] = part
            hid_sem = claim("recv", 1)
            push(hid_part, hid_recv, hid_sem, sib)
            arrived(hid_recv, hid_sem)
            keep(3, hid_part[...] + hid_recv[...])
            load_parts = lcopy(parts_low, rows_out.at[2, 0, 0])

    for index, (out, layer) in enumerate(((lo_out, 0), (lo_out, 1), (ig_out, 1), (ig_out, 0))):
        arrived(out.at[0, 1 - s], out_sem + index, s == layer)
    for copy, when in pending[-z.sends :]:
        sent(copy, when)
    for copy, when in out_loads:
        pl.when(when)(copy.wait)
    load_parts.wait()


def run_layers(z, small, large):
    nt, nb, rows, brows = z.planes, z.blocks, z.rows, z.block_rows
    width, hidden = z.width, z.hidden
    length = nb * brows
    V = pltpu.VMEM
    any_space = pl.BlockSpec(memory_space=pl.ANY)
    scratch = [
        V((2, 8, width), f32),
        V((2, nb, 3 * HD, 128), bf16),
        V((3, width, z.local_width), bf16),
        V((2, nb, 3 * HD, width), bf16),
        V((2, width, width), bf16),
        V((2, width, hidden), bf16),
        V((2, hidden, width), bf16),
        V((2, 2, nb, z.prefix_pad, HD), bf16),
        V((2, nt, rows, width), bf16),
        V((2, nt, rows, width), bf16),
        V((2, nb, 3 * HD, brows), bf16),
        V((2, 3 * HD, length), bf16),
        V((2, nb, HD, brows), bf16),
        V((2, z.cells, HD, brows), bf16),
        V((2, nt, rows, width), bf16),
        V((2, nt, rows, width), bf16),
        V((2, nt, nb, HD, brows), bf16),
        V((2, z.cells, HD, brows), bf16),
        V((2, nb, 3 * HD, brows), bf16),
        V((2, nb, 3 * HD, brows), bf16),
        V((2, nt, rows, width), bf16),
        V((2, nt, rows, width), bf16),
        V((2, rows, width), bf16),
        V((2, rows, width), bf16),
        V((2, nb, HD, brows), bf16),
        V((2, brows, width), f32),
        V((2, brows, 1), f32),
        V((2, brows, width), f32),
        V((2, brows, 1), f32),
        V((brows, hidden), f32),
        V((brows, hidden), f32),
        V((2, length, length), bf16),
        V((2, z.prefix_pad, length), f32),
        V((2, nb, 1, brows), f32),
        V((length, length), bf16),
        V((z.prefix_pad, length), bf16),
        V((length, HD), bf16),
        V((length, HD), bf16),
        V((length, HD), bf16),
        V((2, nb, HD, brows), f32),
        V((2, length, HD), bf16),
        V((brows, width), bf16),
        V((brows, width), bf16),
        V((brows, width), f32),
        V((brows, width), f32),
        V((brows, width), f32),
        V((rows, width), bf16),
        V((brows, width), bf16),
        V((rows, width), f32),
        V((2, 2, z.prefix_pad, HD), f32),
        V((2, z.prefix_pad, HD), f32),
        V((2, z.prefix_pad, HD), f32),
        V((nb, 2, z.prefix_pad, HD), f32),
        V((z.prefix_pad, width), f32),
        V((width, z.inner), bf16),
        V((z.inner, 2, z.local_width), bf16),
        V((z.inner, 2 * z.local_width), bf16),
        V((z.prefix_pad, z.inner), f32),
        V((z.prefix_pad, z.inner), f32),
        V((rows, width), bf16),
        V((nt, z.prefix_pad, z.inner), f32),
        pltpu.SemaphoreType.DMA((z.sends,)),
        pltpu.SemaphoreType.DMA((109,)),
        pltpu.SemaphoreType.DMA((13,)),
        pltpu.SemaphoreType.REGULAR,
    ]
    return pl.pallas_call(
        partial(both_layers, z),
        out_shape=(
            jax.ShapeDtypeStruct((3, 1, 2, rows, width), bf16),
        ),
        in_specs=[pl.BlockSpec(memory_space=pltpu.SMEM)]
        + [pl.BlockSpec(memory_space=pltpu.VMEM)] * (len(small) - 1)
        + [any_space] * len(large),
        out_specs=(any_space,),
        scratch_shapes=scratch,
        compiler_params=pltpu.CompilerParams(
            collective_id=0, has_side_effects=True, vmem_limit_bytes=60 * 2**20
        ),
        cost_estimate=pl.CostEstimate(
            flops=7 * 10**9, bytes_accessed=16 * 2**20, transcendentals=4 * 10**6
        ),
    )(*small, *large)


def prefix_end(
    z, rows_in, table_in, inner_in,
    lo_out, ig_out, states_out, table_out, inner_out, inner_bias_out, outer_out, outer_bias_out,
    table_pad, parts, inner_full, outer_full, sems,
):
    copies = []

    def start(src, dst):
        copies.append(pltpu.make_async_copy(src, dst, sems.at[len(copies)]))
        copies[-1].start()

    start(rows_in.at[2, 0, 0], parts)
    start(rows_in.at[0], lo_out)
    start(rows_in.at[1], ig_out)
    count, width = z.prefix_rows, z.local_width
    table_pad[...] = jnp.zeros_like(table_pad)
    table_pad[0:count, :] = table_in[...].astype(f32)
    table_turned = table_pad[...].T.astype(bf16)
    copies[0].wait()

    def halves(index):
        at, columns = index // 2 * z.prefix_pad, slice(index % 2 * z.inner, (index % 2 + 1) * z.inner)
        high = parts[at : at + z.prefix_pad, columns]
        at += 2 * z.prefix_pad
        return high, parts[at : at + z.prefix_pad, columns]

    act = halves(0)[0].astype(f32) + halves(0)[1].astype(f32)
    hidden = halves(3)[0].astype(f32) + halves(3)[1].astype(f32)
    inner_grad = hidden * (1.0 - act * act)
    high = inner_grad.astype(bf16)
    low = (inner_grad - high.astype(f32)).astype(bf16)
    some = z.width // 2
    for i in range(2):
        at = slice(i * some, (i + 1) * some)
        inner_full[at] = dot_nn(table_turned[at], high) + dot_nn(table_turned[at], low)
        start(inner_full.at[at], inner_out.at[at])
    act_turned = act.T.astype(bf16)
    total = halves(2)
    for c in range(2):
        at = slice(c * width, (c + 1) * width)
        outer_full[:, c, :] = dot_nn(act_turned, total[0][:, at]) + dot_nn(act_turned, total[1][:, at])
    start(outer_full, outer_out)
    whole = total[0].astype(f32) + total[1].astype(f32)
    for c in range(2):
        at = slice(c * width, (c + 1) * width)
        states_out[:, c, :] = halves(1)[0][0:count, at]
        outer_bias_out[0, c : c + 1, :] = jnp.sum(whole[:, at], axis=0, keepdims=True)
    inner_bias_out[...] = jnp.sum(inner_grad, axis=0, keepdims=True)
    table_out[...] = (dot_nt(high, inner_in[...]) + dot_nt(low, inner_in[...]))[0:count]
    for copy in copies[1:]:
        copy.wait()


def finish(z, both_rows, table, inner_weight):
    any_space = pl.BlockSpec(memory_space=pl.ANY)
    whole = pl.BlockSpec(memory_space=pltpu.VMEM)
    rows = jax.ShapeDtypeStruct(both_rows.shape[1:], bf16)
    return pl.pallas_call(
        partial(prefix_end, z),
        out_shape=(
            rows,
            rows,
            jax.ShapeDtypeStruct((z.prefix_rows, 2, z.local_width), bf16),
            jax.ShapeDtypeStruct((z.prefix_rows, z.width), f32),
            jax.ShapeDtypeStruct((z.width, z.inner), f32),
            jax.ShapeDtypeStruct((1, z.inner), f32),
            jax.ShapeDtypeStruct((z.inner, 2, z.local_width), f32),
            jax.ShapeDtypeStruct((1, 2, z.local_width), f32),
        ),
        in_specs=[any_space] + [whole] * 2,
        out_specs=(any_space,) * 2 + (whole,) * 2 + (any_space, whole, any_space, whole),
        scratch_shapes=[
            pltpu.VMEM((z.prefix_pad, z.width), f32),
            pltpu.VMEM(both_rows.shape[3:], bf16),
            pltpu.VMEM((z.width, z.inner), f32),
            pltpu.VMEM((z.inner, 2, z.local_width), f32),
            pltpu.SemaphoreType.DMA((6,)),
        ],
        compiler_params=pltpu.CompilerParams(vmem_limit_bytes=32 * 2**20),
    )(both_rows, table, inner_weight)


def head_a_device(
    block_input,
    output_grad,
    valid_len,
    first_gain,
    first_bias,
    triple_weight,
    triple_bias,
    mixer_weight,
    mixer_bias,
    second_gain,
    second_bias,
    expand_weight,
    expand_bias,
    reduce_weight,
    reduce_bias,
    prefix_table,
    inner_weight,
    inner_bias,
    outer_weight,
    outer_bias,
):
    planes, blocks = lax.axis_size("tensor"), lax.axis_size("dp")
    local_width = triple_weight.shape[3]
    prefix_rows = prefix_table.shape[0]
    z = Sizes(
        planes,
        blocks,
        block_input.shape[1],
        block_input.shape[2],
        local_width,
        expand_weight.shape[2],
        prefix_rows,
    )
    z.prefix_pad = -(-prefix_rows // 16) * 16
    z.inner = inner_weight.shape[1]
    small = (
        valid_len,
        first_gain,
        first_bias,
        triple_bias,
        mixer_bias,
        second_gain,
        second_bias,
        expand_bias,
        reduce_bias,
        prefix_table,
        inner_bias,
        outer_bias,
    )
    large = (
        block_input,
        output_grad,
        triple_weight[0].transpose(1, 0, 2),
        mixer_weight[0],
        expand_weight[0],
        reduce_weight[0],
        inner_weight,
        outer_weight[:, 0],
    )
    results = finish(z, *run_layers(z, small, large), prefix_table, inner_weight)
    (
        layer_outputs,
        input_grads,
        prefix_states,
        table_grad,
        inner_weight_grad,
        inner_bias_grad,
        outer_weight_grad,
        outer_bias_grad,
    ) = results
    return (
        layer_outputs,
        input_grads,
        prefix_states.transpose(1, 0, 2)[None],
        table_grad,
        inner_weight_grad,
        inner_bias_grad.reshape(-1),
        outer_weight_grad.reshape(-1, 1, 2, local_width),
        outer_bias_grad,
    )


def prefix_back(
    prefix_total,
    prefix_full,
    inner_act,
    inner_low,
    outer_local,
    prefix_table,
    inner_weight,
    local_width,
):
    inner_float = inner_low.astype(f32)
    outer_float = outer_local.astype(f32)
    outer_weight_grad = jnp.dot(inner_float.T, prefix_total, precision=highest).reshape(
        -1, 1, 2, local_width
    )
    outer_bias_grad = jnp.sum(prefix_total, axis=0).reshape(1, 2, local_width)
    hidden_grad = lax.psum(
        jnp.dot(prefix_total, outer_float.T, precision=highest), ("section", "tensor")
    )
    inner_grad = hidden_grad * (1.0 - inner_act * inner_act)
    inner_weight_grad = jnp.dot(prefix_table.astype(f32).T, inner_grad, precision=highest)
    inner_bias_grad = jnp.sum(inner_grad, axis=0)
    table_grad = jnp.dot(inner_grad, inner_weight.astype(f32).T, precision=highest)
    prefix_states = prefix_full.reshape(-1, 2, local_width).transpose(1, 0, 2)[None]
    return (
        prefix_states,
        table_grad,
        inner_weight_grad,
        inner_bias_grad,
        outer_weight_grad,
        outer_bias_grad,
    )


def solution(mesh):
    def step(*args):
        triple_weight = args[5]
        micro_count, share_rows, width = args[0].shape
        fits = (
            lax.axis_size("section") == 2
            and micro_count == 2
            and triple_weight.shape[3] == HD * lax.axis_size("dp")
            and share_rows * lax.axis_size("tensor") == 256
            and triple_weight.shape[3] % 256 == 0
            and width % 256 == 0
            and args[11].shape[2] == width
            and args[16].shape[1] * 2 == width
            and args[15].shape[0] <= 16
            and share_rows == 64
        )
        return head_a_device(*args) if fits else shards(*args)

    return jax.shard_map(
        step,
        mesh=mesh,
        in_specs=(
            P(None, ("dp", "tensor"), None),
            P(None, ("dp", "tensor"), None),
            P(),
            P("section", None),
            P("section", None),
            P("section", None, None, "tensor"),
            P("section", None, "tensor"),
            P("section", "tensor", None),
            P("section", None),
            P("section", None),
            P("section", None),
            P("section", None, "tensor"),
            P("section", "tensor"),
            P("section", "tensor", None),
            P("section", None),
            P(),
            P(),
            P(),
            P(None, "section", None, "tensor"),
            P("section", None, "tensor"),
        ),
        out_specs=(
            P("section", None, ("dp", "tensor"), None),
            P("section", None, ("dp", "tensor"), None),
            P("section", None, None, "tensor"),
            P(),
            P(),
            P(),
            P(None, "section", None, "tensor"),
            P("section", None, "tensor"),
        ),
        check_vma=False,
    )
```

```python
from functools import partial

import jax
import jax.numpy as jnp
from jax import lax
from jax.experimental import pallas as pl
from jax.experimental.pallas import tpu as pltpu
from jax.sharding import PartitionSpec as P

HD = 64


epsilon = 1e-05
masked_score = -1e30
highest = lax.Precision.HIGHEST
MESH = pl.DeviceIdType.MESH
f32 = jnp.float32
bf16 = jnp.bfloat16


def passed_along(block, axis, distance):
    devices = range(lax.axis_size(axis))
    route = [(i - distance, i) for i in devices if i - distance in devices]
    return lax.ppermute(block, axis, route)


def layer_norm(values, norm_gain, norm_bias):
    center = values - jnp.mean(values, axis=-1, keepdims=True)
    variance = jnp.mean(center * center, axis=-1, keepdims=True)
    inverse = lax.rsqrt(variance + epsilon)
    normed = center * inverse
    return (normed * norm_gain + norm_bias, normed, inverse)


def norm_back(grad_out, normed, inverse, norm_gain):
    scaled = grad_out * norm_gain
    mean_grad = jnp.mean(scaled, axis=-1, keepdims=True)
    mean_cross = jnp.mean(scaled * normed, axis=-1, keepdims=True)
    return inverse * (scaled - mean_grad - normed * mean_cross)


def attention_scores(queries, seq_keys, pre_keys, valid, query_start):
    score_scale = HD ** (-0.5)
    seq_scores = (
        jnp.einsum("qhd,khd->hqk", queries, seq_keys, preferred_element_type=jnp.float32)
        * score_scale
    )
    pre_scores = (
        jnp.einsum("qhd,khd->hqk", queries, pre_keys, preferred_element_type=jnp.float32)
        * score_scale
    )
    query_pos = query_start + lax.broadcasted_iota(jnp.int32, (queries.shape[0], 1), 0)
    key_pos = lax.broadcasted_iota(jnp.int32, (1, seq_keys.shape[0]), 1)
    visible = (key_pos <= query_pos) & (key_pos < valid)
    seq_scores = jnp.where(visible[None], seq_scores, masked_score)
    return (seq_scores, pre_scores)


def split_prefix(prefix_full, local_width):
    local_heads = local_width // HD
    pre_keys = prefix_full[:, :local_width].reshape(-1, local_heads, HD)
    pre_values = prefix_full[:, local_width:].reshape(-1, local_heads, HD)
    return (pre_keys, pre_values)


def layer_forward(inputs, weights, prefix_full, valid, query_start):
    (
        gain_one,
        bias_one,
        triple_weight,
        triple_bias,
        mixer_weight,
        mixer_bias,
        gain_two,
        bias_two,
        expand_weight,
        expand_bias,
        reduce_weight,
        reduce_bias,
    ) = weights
    local_width = triple_weight.shape[1] // 3
    local_heads = local_width // HD
    normed_one, unit_one, inverse_one = layer_norm(inputs, gain_one, bias_one)
    mixed_rows = (
        jnp.dot(
            lax.all_gather(normed_one.astype(jnp.bfloat16), "tensor", axis=0, tiled=True),
            triple_weight,
            preferred_element_type=jnp.float32,
        )
        + triple_bias
    ).astype(jnp.bfloat16)
    tokens = mixed_rows.shape[0]
    queries = mixed_rows[:, :local_width].reshape(tokens, local_heads, HD)
    seq_keys, seq_values = (
        lax.all_gather(mixed_rows[:, local_width : 2 * local_width], "dp", axis=0, tiled=True),
        lax.all_gather(mixed_rows[:, 2 * local_width :], "dp", axis=0, tiled=True),
    )
    seq_keys = seq_keys.reshape(-1, local_heads, HD)
    seq_values = seq_values.reshape(-1, local_heads, HD)
    pre_keys, pre_values = split_prefix(prefix_full, local_width)
    seq_scores, pre_scores = attention_scores(queries, seq_keys, pre_keys, valid, query_start)
    row_max = jnp.maximum(
        jnp.max(seq_scores, axis=2, keepdims=True), jnp.max(pre_scores, axis=2, keepdims=True)
    )
    seq_exp = jnp.exp(seq_scores - row_max)
    pre_exp = jnp.exp(pre_scores - row_max)
    row_total = jnp.sum(seq_exp, axis=2, keepdims=True) + jnp.sum(pre_exp, axis=2, keepdims=True)
    log_total = row_max + jnp.log(row_total)
    seq_low = (seq_exp / row_total).astype(jnp.bfloat16)
    pre_low = (pre_exp / row_total).astype(jnp.bfloat16)
    attended = jnp.einsum("hqk,khd->qhd", seq_low, seq_values, preferred_element_type=jnp.float32)
    attended = attended + jnp.einsum(
        "hqk,khd->qhd", pre_low, pre_values, preferred_element_type=jnp.float32
    )
    attended = attended.astype(jnp.bfloat16).reshape(tokens, local_width)
    mixer_out = lax.psum_scatter(
        jnp.dot(attended, mixer_weight, preferred_element_type=jnp.float32),
        "tensor",
        scatter_dimension=0,
        tiled=True,
    )
    residual = inputs + mixer_out + mixer_bias
    normed_two, unit_two, inverse_two = layer_norm(residual, gain_two, bias_two)
    hidden_pre = (
        jnp.dot(
            lax.all_gather(normed_two.astype(jnp.bfloat16), "tensor", axis=0, tiled=True),
            expand_weight,
            preferred_element_type=jnp.float32,
        )
        + expand_bias
    )
    active = jax.nn.gelu(hidden_pre, approximate=True).astype(jnp.bfloat16)
    result = (
        residual
        + lax.psum_scatter(
            jnp.dot(active, reduce_weight, preferred_element_type=jnp.float32),
            "tensor",
            scatter_dimension=0,
            tiled=True,
        )
        + reduce_bias
    )
    saved_state = (
        unit_one,
        inverse_one,
        queries,
        seq_keys,
        seq_values,
        log_total,
        unit_two,
        inverse_two,
        hidden_pre,
    )
    return (result, saved_state)


def layer_backward(grad_out, saved_state, weights, prefix_full, valid, query_start):
    (
        gain_one,
        bias_one,
        triple_weight,
        triple_bias,
        mixer_weight,
        mixer_bias,
        gain_two,
        bias_two,
        expand_weight,
        expand_bias,
        reduce_weight,
        reduce_bias,
    ) = weights
    (
        unit_one,
        inverse_one,
        queries,
        seq_keys,
        seq_values,
        log_total,
        unit_two,
        inverse_two,
        hidden_pre,
    ) = saved_state
    tokens = queries.shape[0]
    local_heads = queries.shape[1]
    local_width = local_heads * HD
    score_scale = HD ** (-0.5)
    grad_active = jnp.dot(
        lax.all_gather(grad_out.astype(jnp.bfloat16), "tensor", axis=0, tiled=True),
        reduce_weight.T,
        preferred_element_type=jnp.float32,
    )
    gelu_pull = jax.vjp(partial(jax.nn.gelu, approximate=True), hidden_pre)[1]
    grad_pre = gelu_pull(grad_active)[0].astype(jnp.bfloat16)
    grad_two = lax.psum_scatter(
        jnp.dot(grad_pre, expand_weight.T, preferred_element_type=jnp.float32),
        "tensor",
        scatter_dimension=0,
        tiled=True,
    )
    grad_residual = grad_out + norm_back(grad_two, unit_two, inverse_two, gain_two)
    grad_heads = jnp.dot(
        lax.all_gather(grad_residual.astype(jnp.bfloat16), "tensor", axis=0, tiled=True),
        mixer_weight.T,
        preferred_element_type=jnp.float32,
    ).astype(jnp.bfloat16)
    grad_heads = grad_heads.reshape(tokens, local_heads, HD)
    pre_keys, pre_values = split_prefix(prefix_full, local_width)
    seq_scores, pre_scores = attention_scores(queries, seq_keys, pre_keys, valid, query_start)
    seq_prob = jnp.exp(seq_scores - log_total)
    pre_prob = jnp.exp(pre_scores - log_total)
    seq_dprob = jnp.einsum(
        "qhd,khd->hqk", grad_heads, seq_values, preferred_element_type=jnp.float32
    )
    pre_dprob = jnp.einsum(
        "qhd,khd->hqk", grad_heads, pre_values, preferred_element_type=jnp.float32
    )
    delta_row = jnp.sum(seq_prob * seq_dprob, axis=2, keepdims=True) + jnp.sum(
        pre_prob * pre_dprob, axis=2, keepdims=True
    )
    seq_dscore = (seq_prob * (seq_dprob - delta_row)).astype(jnp.bfloat16)
    pre_dscore = (pre_prob * (pre_dprob - delta_row)).astype(jnp.bfloat16)
    seq_low = seq_prob.astype(jnp.bfloat16)
    pre_low = pre_prob.astype(jnp.bfloat16)
    grad_queries = jnp.einsum(
        "hqk,khd->qhd", seq_dscore, seq_keys, preferred_element_type=jnp.float32
    )
    grad_queries = (
        grad_queries
        + jnp.einsum("hqk,khd->qhd", pre_dscore, pre_keys, preferred_element_type=jnp.float32)
    ) * score_scale
    key_term = (
        jnp.einsum("hqk,qhd->khd", seq_dscore, queries, preferred_element_type=jnp.float32)
        * score_scale
    )
    value_term = jnp.einsum("hqk,qhd->khd", seq_low, grad_heads, preferred_element_type=jnp.float32)
    grad_keys, grad_values = (
        lax.psum_scatter(key_term.reshape(-1, local_width), "dp", scatter_dimension=0, tiled=True),
        lax.psum_scatter(
            value_term.reshape(-1, local_width), "dp", scatter_dimension=0, tiled=True
        ),
    )
    pre_key_grad = (
        jnp.einsum("hqk,qhd->khd", pre_dscore, queries, preferred_element_type=jnp.float32)
        * score_scale
    )
    pre_value_grad = jnp.einsum(
        "hqk,qhd->khd", pre_low, grad_heads, preferred_element_type=jnp.float32
    )
    prefix_term = jnp.concatenate(
        [pre_key_grad.reshape(-1, local_width), pre_value_grad.reshape(-1, local_width)], axis=1
    )
    grad_mixed = jnp.concatenate(
        [grad_queries.reshape(tokens, local_width), grad_keys, grad_values], axis=1
    ).astype(jnp.bfloat16)
    grad_one = lax.psum_scatter(
        jnp.dot(grad_mixed, triple_weight.T, preferred_element_type=jnp.float32),
        "tensor",
        scatter_dimension=0,
        tiled=True,
    )
    grad_input = grad_residual + norm_back(grad_one, unit_one, inverse_one, gain_one)
    return (grad_input, prefix_term)


def shards(
    block_input,
    output_grad,
    valid_len,
    first_gain,
    first_bias,
    triple_weight,
    triple_bias,
    mixer_weight,
    mixer_bias,
    second_gain,
    second_bias,
    expand_weight,
    expand_bias,
    reduce_weight,
    reduce_bias,
    prefix_table,
    inner_weight,
    inner_bias,
    outer_weight,
    outer_bias,
):
    section_index = lax.axis_index("section")
    micro_count = block_input.shape[0]
    share_rows = block_input.shape[1]
    model_width = block_input.shape[2]
    local_width = triple_weight.shape[3]
    query_start = lax.axis_index("dp") * (share_rows * lax.axis_size("tensor"))
    weights = (
        first_gain[0],
        first_bias[0],
        triple_weight[0].reshape(-1, 3 * local_width),
        triple_bias[0].reshape(3 * local_width),
        mixer_weight[0],
        mixer_bias[0],
        second_gain[0],
        second_bias[0],
        expand_weight[0],
        expand_bias[0],
        reduce_weight[0],
        reduce_bias[0],
    )
    inner_pre = jnp.dot(prefix_table, inner_weight, preferred_element_type=jnp.float32) + inner_bias
    inner_act = jnp.tanh(inner_pre)
    inner_low = inner_act.astype(jnp.bfloat16)
    outer_local = outer_weight[:, 0].reshape(outer_weight.shape[0], 2 * local_width)
    prefix_full = (
        jnp.dot(inner_low, outer_local, preferred_element_type=jnp.float32)
        + outer_bias[0].reshape(2 * local_width)
    ).astype(jnp.bfloat16)
    moments = micro_count + 1
    carried = jnp.zeros((share_rows, model_width), jnp.bfloat16)
    results = []
    stored_states = []
    for moment in range(moments):
        micro_index = jnp.clip(moment - section_index, 0, micro_count - 1)
        inputs = jnp.where(
            section_index == 0, block_input[min(moment, micro_count - 1)], carried
        ).astype(jnp.float32)
        result, saved_state = layer_forward(
            inputs, weights, prefix_full, valid_len[micro_index], query_start
        )
        result_low = result.astype(jnp.bfloat16)
        results.append(result_low)
        stored_states.append(inputs)
        if moment + 1 < moments:
            carried = passed_along(result_low, "section", 1)
    grad_carried = jnp.zeros((share_rows, model_width), jnp.bfloat16)
    grad_list = []
    prefix_grad = jnp.zeros((prefix_full.shape[0], 2 * local_width), jnp.float32)
    for moment in range(moments):
        micro_index = moment - 1 + section_index
        valid_tick = (micro_index >= 0) & (micro_index < micro_count)
        clipped = jnp.clip(micro_index, 0, micro_count - 1)
        grad_in = jnp.where(
            section_index == 1, output_grad[min(moment, micro_count - 1)], grad_carried
        ).astype(jnp.float32)
        early_state = stored_states[max(moment - 1, 0)]
        late_state = stored_states[min(moment + 1, moments - 1)]
        picked = jnp.where(section_index == 0, early_state, late_state)
        picked_state = layer_forward(picked, weights, prefix_full, valid_len[clipped], query_start)[
            1
        ]
        grad_input, prefix_term = layer_backward(
            grad_in, picked_state, weights, prefix_full, valid_len[clipped], query_start
        )
        prefix_grad = prefix_grad + jnp.where(valid_tick, prefix_term, 0.0)
        grad_low = grad_input.astype(jnp.bfloat16)
        grad_list.append(grad_low)
        if moment + 1 < moments:
            grad_carried = passed_along(grad_low, "section", -1)
    layer_outputs = jnp.stack(
        [
            jnp.where(section_index == 0, results[number], results[number + 1])
            for number in range(micro_count)
        ]
    )[None]
    input_grads = jnp.stack(
        [
            jnp.where(section_index == 0, grad_list[number + 1], grad_list[number])
            for number in range(micro_count)
        ]
    )[None]
    prefix_total = lax.psum(prefix_grad, "dp")
    return (layer_outputs, input_grads) + prefix_back(
        prefix_total,
        prefix_full,
        inner_act,
        inner_low,
        outer_local,
        prefix_table,
        inner_weight,
        local_width,
    )


def dot_nn(left, right):
    return lax.dot_general(left, right, (((1,), (0,)), ((), ())), preferred_element_type=f32)


def dot_nt(left, right):
    return lax.dot_general(left, right, (((1,), (1,)), ((), ())), preferred_element_type=f32)


def dot_split(left, right, dot):
    high = left.astype(bf16)
    low = (left - high.astype(f32)).astype(bf16)
    return dot(high, right) + dot(low, right)


class Sizes:
    def __init__(self, planes, blocks, rows, width, local_width, hidden, prefix_rows):
        self.planes = planes
        self.blocks = blocks
        self.rows = rows
        self.block_rows = rows * planes
        self.width = width
        self.local_width = local_width
        self.hidden = hidden
        self.prefix_rows = prefix_rows
        self.cells = planes * blocks
        self.tile = 256
        self.sends = 48


def both_layers(
    z,
    valid_ref,
    gain_one_in,
    bias_one_in,
    triple_bias_in,
    mixer_bias_in,
    gain_two_in,
    bias_two_in,
    expand_bias_in,
    reduce_bias_in,
    table_in,
    inner_bias_in,
    outer_bias_in,
    x_in,
    gy_in,
    triple_in,
    mixer_in,
    expand_in,
    reduce_in,
    inner_in,
    outer_in,
    rows_out,
    vec,
    tbias,
    triple_own,
    wq,
    wm,
    we,
    wr,
    pre,
    xs,
    gys,
    qkv_send,
    qkv,
    ot_send,
    att,
    y_send,
    y_recv,
    gh_send,
    gh,
    dm_send,
    dm,
    gi_send,
    gi_recv,
    y_relay,
    gi_relay,
    gh_relay,
    z_one,
    inv_one,
    z_two,
    inv_two,
    gelu_grad,
    upper,
    expons_low,
    expons_pre,
    scales,
    dscores,
    dscores_pre,
    values_n,
    queries_n,
    grads_n,
    out_t,
    keys_n,
    normed,
    wide,
    total,
    grad_res,
    resid,
    y_last,
    active_last,
    gi_own,
    pg,
    pg_recv,
    pg_sum,
    pg_all,
    table_pad,
    inner_w,
    outer_raw,
    outer_w,
    hid_part,
    hid_recv,
    parts_low,
    hid_all,
    send_sem,
    recv_sem,
    local_sem,
):
    lo_out, ig_out = rows_out.at[0], rows_out.at[1]
    s = lax.axis_index("section")
    t = lax.axis_index("tensor")
    d = lax.axis_index("dp")
    nt, nb, rows, brows, tile = z.planes, z.blocks, z.rows, z.block_rows, z.tile
    cells = z.cells
    me = t * nb + d
    sib = (1 - s, t, d)
    counts = dict(send=0, recv=0, local=0)
    pending = []
    shared = {}

    def claim(kind, number, name=None):
        if name in shared:
            return shared[name]
        first = counts[kind]
        counts[kind] += number
        if name is not None:
            shared[name] = first
        return first

    def rcopy(src, dst, ss, rs, device):
        return pltpu.make_async_remote_copy(
            src_ref=src,
            dst_ref=dst,
            send_sem=send_sem.at[ss],
            recv_sem=recv_sem.at[rs],
            device_id=device,
            device_id_type=MESH,
        )

    def push(src, dst, rs, device, when=None):
        if len(pending) >= z.sends:
            sent(*pending[len(pending) - z.sends])
        copy = rcopy(src, dst, len(pending) % z.sends, rs, device)
        if when is None:
            copy.start()
        else:
            pl.when(when)(copy.start)
        pending.append((copy, when))

    def sent(copy, when):
        if when is None:
            copy.wait_send()
        else:
            pl.when(when)(copy.wait_send)

    def arrived(dst, rs, when=None):
        copy = rcopy(dst, dst, 0, rs, sib)
        if when is None:
            copy.wait_recv()
        else:
            pl.when(when)(copy.wait_recv)

    def lcopy(src, dst):
        copy = pltpu.make_async_copy(src, dst, local_sem.at[claim("local", 1)])
        copy.start()
        return copy

    outer = (t == 0) | (t == nt - 1)
    inner = jnp.logical_not(outer)
    across = lax.rem(t + 2, nt)
    beside = t + 1 - 2 * lax.rem(t, 2)

    def far(k):
        return ((t == 0) & (k == nt - 1)) | ((t == nt - 1) & (k == 1))

    def unheard(k):
        return ((t == 0) & (k == 1)) | ((t == nt - 1) & (k == nt - 1))

    def near(k):
        return jnp.logical_not(far(k))

    def keep(index, value):
        high = value.astype(bf16)
        low = (value - high.astype(f32)).astype(bf16)
        at, columns = index // 2 * z.prefix_pad, slice(index % 2 * z.inner, (index % 2 + 1) * z.inner)
        parts_low[at : at + z.prefix_pad, columns] = high
        at += 2 * z.prefix_pad
        parts_low[at : at + z.prefix_pad, columns] = low

    def plane(k):
        return lax.rem(t + k, nt)

    def block(k):
        return lax.rem(d + k, nb)

    barrier = pltpu.get_barrier_semaphore()
    for k in range(1, cells):
        pl.semaphore_signal(
            barrier, inc=1, device_id=(s, plane(k // nb), block(k % nb)), device_id_type=MESH
        )
    pl.semaphore_signal(barrier, inc=1, device_id=sib, device_id_type=MESH)

    load_x = lcopy(x_in.at[s], xs.at[0, t])
    load_triple = lcopy(triple_in, triple_own)
    load_inner = lcopy(inner_in, inner_w)
    load_outer = lcopy(outer_in, outer_raw)
    load_mixer = lcopy(mixer_in, wm.at[s, pl.ds(pl.multiple_of(t * z.local_width, 256), z.local_width)])
    load_expand = lcopy(expand_in, we.at[s])
    load_reduce = lcopy(reduce_in, wr.at[s])
    load_gy = lcopy(gy_in.at[s], gys.at[1, t])

    for layer in range(2):
        for k in (1, nt - 1):

            @pl.when(unheard(k))
            def _():
                y_recv[layer, k] = jnp.zeros((rows, z.width), bf16)
                gi_recv[layer, k] = jnp.zeros((rows, z.width), bf16)

        @pl.when(outer)
        def _():
            for j in range(nb):
                gh[layer, (nt - 1 - t) * nb + j] = jnp.zeros((HD, brows), bf16)

    pl.semaphore_wait(barrier, cells)

    half = rows // 2

    def parts_of(ref):
        return ref.at[pl.ds(0, half)], ref.at[pl.ds(half, half)]

    def spread(src, buf, layer, when=True):
        first = claim("recv", nt + 2, "rows" if buf is xs else "grads")
        for i, (one, goal) in enumerate(zip(parts_of(src), parts_of(buf.at[layer, t]))):
            push(one, goal, first + (2, nt)[i], (s, across, d), outer & when)
        push(src, buf.at[layer, t], first + 2, (s, across, d), inner & when)
        for k in (1, 3):
            push(src, buf.at[layer, t], first + k, (s, plane(k), d), near(k) & when)
        return first

    def spread_relay(buf, layer, first):
        for i, one in enumerate(parts_of(buf.at[layer, across])):
            arrived(one, first + (2, nt)[i], inner)
            push(one, one, first + (2 * t - 1, nt + 1)[i], (s, beside, d), inner)

    def spread_wait(buf, layer, first, k):
        unit = buf.at[layer, plane(nt - k)]
        if k == 2:
            arrived(unit, first + k, outer)
        else:
            arrived(unit, first + k, jnp.logical_not(unheard(k)))
            for i, one in enumerate(parts_of(unit)):
                arrived(one, first + (k, nt + 1)[i], unheard(k))

    x_first = [None, None]
    gy_first = [None, None]
    mix_first = claim("recv", nt)
    mix_second = claim("recv", nt * nb)
    mix_third = claim("recv", 1)

    def piece(layer, p, q):
        return wm.at[layer, pl.ds(pl.multiple_of((p * nb + q) * (z.local_width // nb), 64), z.local_width // nb)]

    def mix_one(layer):
        part = z.local_width // nb
        for k in range(1, nt):
            push(
                mixer_in.at[pl.ds(pl.multiple_of(d * part, 64), part)],
                piece(layer, t, d),
                mix_first + k,
                (s, plane(k), d),
                s == layer,
            )

    def mix_two(layer):
        for k in range(1, nt):
            source = plane(nt - k)
            arrived(piece(layer, source, d), mix_first + k, s == layer)
            for q in range(1, nb):
                push(
                    piece(layer, source, d),
                    piece(layer, source, d),
                    mix_second + k * nb + q,
                    (s, t, block(q)),
                    s == layer,
                )

    def mix_three(layer):
        for k in range(1, nt):
            for q in range(1, nb):
                arrived(
                    piece(layer, plane(nt - k), block(nb - q)),
                    mix_second + k * nb + q,
                    s == layer,
                )
        push(wm.at[layer], wm.at[layer], mix_third, sib, s == layer)

    mix_one(0)

    x_first[0] = spread(x_in.at[s], xs, 0, s == 1)

    for index, ref in enumerate(
        (gain_one_in, bias_one_in, mixer_bias_in, gain_two_in, bias_two_in, reduce_bias_in, expand_bias_in)
    ):
        vec[s, index : index + 1, :] = ref[...].astype(f32)
    for c in range(3):
        shift = jnp.broadcast_to(triple_bias_in[0, c : c + 1, :].astype(f32), (128, z.local_width)).T
        for j in range(nb):
            tbias[s, j, c * HD : (c + 1) * HD, :] = shift[j * HD : (j + 1) * HD].astype(bf16)
    table_pad[...] = jnp.zeros_like(table_pad)
    table_pad[0 : z.prefix_rows, :] = table_in[...].astype(f32)


    small = claim("recv", 3)
    push(vec.at[s], vec.at[s], small, sib)
    push(tbias.at[s], tbias.at[s], small + 1, sib)

    load_triple.wait()
    for c in range(3):
        for n in range(z.width // tile):
            turned = triple_own[c, n * tile : (n + 1) * tile, :].T
            for j in range(nb):
                wq[s, j, c * HD : (c + 1) * HD, n * tile : (n + 1) * tile] = turned[j * HD : (j + 1) * HD]
    wq_first = claim("recv", 1)
    push(wq.at[s], wq.at[s], wq_first, sib)
    load_inner.wait()
    inner_act = jnp.tanh(
        dot_nn(table_pad[...].astype(bf16), inner_w[...]) + inner_bias_in[...].reshape(1, z.inner).astype(f32)
    )
    keep(0, inner_act)
    load_outer.wait()
    for c in range(2):
        outer_w[:, c * z.local_width : (c + 1) * z.local_width] = outer_raw[:, c, :]
    outer_shift = jnp.concatenate([outer_bias_in[0, 0:1, :], outer_bias_in[0, 1:2, :]], axis=1)
    prefix = (dot_nn(inner_act.astype(bf16), outer_w[...]) + outer_shift.astype(f32)).astype(bf16)
    keep(1, prefix.astype(f32))
    for c in range(2):
        for j in range(nb):
            at = c * z.local_width + j * HD
            pre[s, c, j] = prefix[:, at : at + HD]
    push(pre.at[s], pre.at[s], small + 2, sib)
    arrived(vec.at[1 - s], small)
    arrived(tbias.at[1 - s], small + 1)
    arrived(pre.at[1 - s], small + 2)

    def row(layer, index):
        return vec[layer, index : index + 1, :]

    step = 32

    def norm_one(layer, p):
        def some(i, _):
            at = pl.multiple_of(i * step, step)
            x = xs[layer, p, pl.ds(at, step), :].astype(f32)
            center = x - jnp.mean(x, axis=1, keepdims=True)
            inverse = lax.rsqrt(jnp.mean(center * center, axis=1, keepdims=True) + epsilon)
            unit = center * inverse
            where = pl.multiple_of(p * rows + at, step)
            z_one[layer, pl.ds(where, step), :] = unit
            inv_one[layer, pl.ds(where, step), :] = inverse
            normed[pl.ds(where, step), :] = (unit * row(layer, 0) + row(layer, 1)).astype(bf16)
            return 0

        lax.fori_loop(0, rows // step, some, 0, unroll=True)

    def norm_two(layer):
        def some(i, _):
            at = pl.multiple_of(i * step, step)
            x = resid[pl.ds(at, step), :]
            center = x - jnp.mean(x, axis=1, keepdims=True)
            inverse = lax.rsqrt(jnp.mean(center * center, axis=1, keepdims=True) + epsilon)
            unit = center * inverse
            z_two[layer, pl.ds(at, step), :] = unit
            inv_two[layer, pl.ds(at, step), :] = inverse
            normed[pl.ds(at, step), :] = (unit * row(layer, 3) + row(layer, 4)).astype(bf16)
            return 0

        lax.fori_loop(0, brows // step, some, 0, unroll=True)

    def norm_pull(i, units, inverses, gain):
        at = pl.multiple_of(i * step, step)
        unit = units[pl.ds(at, step), :]
        scaled = total[pl.ds(at, step), :] * gain
        mean_grad = jnp.mean(scaled, axis=1, keepdims=True)
        mean_cross = jnp.mean(scaled * unit, axis=1, keepdims=True)
        return at, inverses[pl.ds(at, step), :] * (scaled - mean_grad - unit * mean_cross)

    def tiles(count, body):
        def some(i, _):
            body(pl.multiple_of(i * tile, tile))
            return 0

        lax.fori_loop(0, count // tile, some, 0, unroll=True)

    def positions(ref, b):
        return ref.at[:, pl.ds(pl.multiple_of(b * brows, brows), brows)]

    def project(layer):
        first = claim("recv", nb, "project")
        for k in range(1, nb + 1):
            head = block(k)
            part = dot_nt(wq[layer, head], normed[...])
            shift = tbias[layer, head].astype(f32)
            part = (part + jnp.concatenate([shift, shift], axis=1)).astype(bf16)
            if k < nb:
                qkv_send[layer, k] = part
                push(qkv_send.at[layer, k], positions(qkv.at[layer], d), first + k, (s, t, head))
            else:
                qkv[layer, :, pl.ds(pl.multiple_of(d * brows, brows), brows)] = part
        return first

    def attend(layer, first):
        out_first = claim("recv", cells, "attend")
        pre_keys = pre[layer, 0, d]
        pre_values = pre[layer, 1, d].T
        prefix_row = lax.broadcasted_iota(jnp.int32, (z.prefix_pad, brows), 0)
        key_at = lax.broadcasted_iota(jnp.int32, (brows, brows), 0)
        query_at = lax.broadcasted_iota(jnp.int32, (brows, brows), 1)
        valid = valid_ref[s]
        for b in range(nb):
            here = slice(b * brows, (b + 1) * brows)
            arrived(positions(qkv.at[layer], b), first + lax.rem(d + nb - b, nb), d != b)
            keys_n[layer, here] = qkv[layer, HD : 2 * HD, here].T
            queries = (qkv[layer, 0:HD, here].astype(f32) * HD ** (-0.5)).astype(bf16)

            def scores_of(kb):
                scores = dot_nn(keys_n[layer, kb * brows : (kb + 1) * brows], queries)
                if kb == b:
                    seen = key_at <= query_at
                    if b == nb - 1:
                        seen = seen & (key_at + b * brows < valid)
                    scores = jnp.where(seen, scores, masked_score)
                return scores

            pre_scores = dot_nn(pre_keys, queries)
            pre_scores = jnp.where(prefix_row < z.prefix_rows, pre_scores, masked_score)
            peak = jnp.max(pre_scores, axis=0, keepdims=True)
            for kb in range(b + 1):
                peak = jnp.maximum(peak, jnp.max(scores_of(kb), axis=0, keepdims=True))
            expons = jnp.exp(pre_scores - peak)
            expons_pre[layer, :, here] = expons
            denominator = jnp.sum(expons, axis=0, keepdims=True)
            for kb in range(b + 1):
                expons = jnp.exp(scores_of(kb) - peak)
                denominator = denominator + jnp.sum(expons, axis=0, keepdims=True)
                expons_low[layer, kb * brows : (kb + 1) * brows, here] = expons.astype(bf16)
            scale = 1.0 / denominator
            scales[layer, b] = scale
            seen_keys = (b + 1) * brows
            result = dot_nn(
                qkv[layer, 2 * HD : 3 * HD, :seen_keys], expons_low[layer, :seen_keys, here]
            )
            result = result + dot_nn(pre_values, expons_pre[layer, :, here].astype(bf16))
            result = result * scale
            out_t[layer, b] = result
            low = result.astype(bf16)
            ot_send[layer, b] = low
            for k in (2, 1, 3, 0):
                if k == 0:
                    push(ot_send.at[layer, b], att.at[layer, me], out_first + me, (s, t, b), d != b)

                    @pl.when(d == b)
                    def _():
                        att[layer, me] = low
                else:
                    push(
                        ot_send.at[layer, b], att.at[layer, me], out_first + me, (s, plane(k), b), near(k)
                    )
        return out_first

    def att_relay(layer, first):
        for j in range(nb):
            cell = across * nb + j
            arrived(att.at[layer, cell], first + cell, inner)
            push(att.at[layer, cell], att.at[layer, cell], first + cell, (s, beside, d), inner)

    def mixer_rows(layer, first):
        att_relay(layer, first)
        for at in range(0, z.width, tile):
            at = slice(at, at + tile)
            resid[:, at] = xs[layer, :, :, at].reshape(brows, tile).astype(f32) + vec[layer, 2:3, at]
        arrived(wm.at[layer], mix_third, s != layer)
        for p, seen in ((t, None), (beside, None), (across, inner), (nt - 1 - t, None)):
            for j in range(nb):
                cell = p * nb + j
                if seen is None:
                    arrived(att.at[layer, cell], first + cell, me != cell)
                else:
                    arrived(att.at[layer, cell], first + cell, jnp.logical_not(seen))
            joined = att[layer, pl.ds(p * nb, nb)].reshape(nb * HD, brows).T
            some_rows = pl.ds(pl.multiple_of(p * z.local_width, z.local_width), z.local_width)
            for at in range(0, z.width, tile):
                at = slice(at, at + tile)
                resid[:, at] += dot_nn(joined, wm[layer, some_rows, at])

    def grad_active():
        def some(at):
            last = gys[1].reshape(brows, z.width)
            upper[:, pl.ds(at, tile)] = dot_nt(last, wr[1, pl.ds(at, tile), :])

        tiles(z.hidden, some)

    def feed_first(layer, active):
        def some(at):
            v = dot_nn(normed[...], we[layer, :, pl.ds(at, tile)]) + vec[layer, 6:7, pl.ds(at, tile)]
            root = 0.7978845608028654
            square = v * v
            th = jnp.tanh(root * v * (1.0 + 0.044715 * square))
            half = 0.5 * (1.0 + th)
            active[:, pl.ds(at, tile)] = (v * half).astype(bf16)
            slope = half + (0.5 * root) * v * (1.0 - th * th) * (1.0 + 3.0 * 0.044715 * square)
            if layer == 0:
                gelu_grad[:, pl.ds(at, tile)] = slope
            else:
                wide[:, pl.ds(at, tile)] = (upper[:, pl.ds(at, tile)] * slope).astype(bf16)

        tiles(z.hidden, some)

    def feed_second(layer, active):
        def some(at):
            part = dot_nn(active[...], wr[layer, :, pl.ds(at, tile)])
            total[:, pl.ds(at, tile)] = part
            y_send[layer, :, :, pl.ds(at, tile)] = part.astype(bf16).reshape(nt, rows, tile)

        tiles(z.width, some)
        return scatter(layer, y_send, y_recv, y_relay)

    def scatter(layer, out, back, relay):
        first = claim("recv", nt + 3, "output" if out is y_send else "input")
        for i, (one, goal) in enumerate(zip(parts_of(out.at[layer, nt - 1 - t]), parts_of(relay.at[layer]))):
            push(one, goal, first + nt + i, (s, beside, d), outer)
        for k in (2, 1, 3):
            go = near(k) if k != 2 else outer
            push(out.at[layer, plane(k)], back.at[layer, k], first + k, (s, plane(k), d), go)
        return first

    def scatter_relay(layer, out, back, relay, full, first):
        for i in range(2):
            arrived(parts_of(relay.at[layer])[i], first + nt + i, inner)

            @pl.when(inner)
            def _():
                at = pl.ds(i * half, half)
                where = pl.ds(pl.multiple_of(across * rows + i * half, half), half)
                out[layer, across, at] = (full[where, :] + relay[layer, at].astype(f32)).astype(bf16)

            one, goal = parts_of(out.at[layer, across])[i], parts_of(back.at[layer, 2])[i]
            push(one, goal, first + (2, nt + 2)[i], (s, across, d), inner)

    def scatter_wait(layer, back, first, result):
        for k in (1, 3, 2):
            if k == 2:
                arrived(back.at[layer, k], first + k, inner)
                for i, one in enumerate(parts_of(back.at[layer, k])):
                    arrived(one, first + (2, nt + 2)[i], outer)
            else:
                arrived(back.at[layer, k], first + k, jnp.logical_not(unheard(k)))
            result = result + back[layer, k].astype(f32)
        return result

    def own_rows(ref):
        return ref[pl.ds(pl.multiple_of(t * rows, rows), rows), :]

    def output_sum(layer, first, base):
        return scatter_wait(layer, y_recv, first, base).astype(bf16)

    out_sem = claim("recv", 4)
    out_loads = []

    def put(src, out, layer, index):
        push(src, out.at[0, s], out_sem + index, sib, s != layer)
        copy = pltpu.make_async_copy(src, out.at[0, s], local_sem.at[claim("local", 1)])
        pl.when(s == layer)(copy.start)
        out_loads.append((copy, s == layer))

    own_weights = [load_mixer, load_expand, load_reduce]
    feed_recv = claim("recv", 2)
    out_first = None
    for layer in range(2):
        if layer == 0:
            load_x.wait()

            spread(x_in.at[s], xs, 0, s == 0)
            mix_two(0)

        norm_one(layer, t)
        spread_relay(xs, layer, x_first[layer])
        for k in (2, 1, 3):
            spread_wait(xs, layer, x_first[layer], k)
            norm_one(layer, plane(nt - k))
        if layer == 0:
            arrived(wq.at[0], wq_first, s == 1)
        else:
            arrived(wq.at[1], wq_first, s == 0)
        q_first = project(layer)
        if layer == 0:
            push(expand_in, we.at[s], feed_recv, sib)
            push(reduce_in, wr.at[s], feed_recv + 1, sib)
            mix_one(1)
        else:
            mix_three(1)
            load_gy.wait()
            gy_first[1] = spread(gys.at[1, t], gys, 1)
        out_first = attend(layer, q_first)
        if layer == 0:
            for copy in own_weights:
                copy.wait()
            mix_three(0)
        if layer == 1:
            arrived(we.at[1], feed_recv, s == 0)
            arrived(wr.at[1], feed_recv + 1, s == 0)
            spread_relay(gys, 1, gy_first[1])
            for k in range(1, nt):
                spread_wait(gys, 1, gy_first[1], k)
            grad_active()
        mixer_rows(layer, out_first)
        norm_two(layer)
        if layer == 0:
            arrived(we.at[0], feed_recv, s == 1)
            arrived(wr.at[0], feed_recv + 1, s == 1)
        feed_first(layer, wide if layer == 0 else active_last)
        if layer == 0:
            y_first = feed_second(layer, wide)
            scatter_relay(0, y_send, y_recv, y_relay, total, y_first)
            base = own_rows(resid) + own_rows(total) + row(layer, 5)
            mix_two(1)
            low = output_sum(0, y_first, base)
            xs[1, t] = low
            x_first[1] = spread(xs.at[1, t], xs, 1)
            put(xs.at[1, t], lo_out, 0, 0)

    def grad_hidden(layer):
        def some(at):
            part = dot_nt(gys[layer].reshape(brows, z.width), wr[layer, pl.ds(at, tile), :])
            wide[:, pl.ds(at, tile)] = (part * gelu_grad[:, pl.ds(at, tile)]).astype(bf16)

        tiles(z.hidden, some)

    def grad_mid(layer):
        def some(at):
            total[:, pl.ds(at, tile)] = dot_nt(wide[...], we[layer, pl.ds(at, tile), :])

        tiles(z.width, some)

        def pull(i, _):
            at, part = norm_pull(i, z_two.at[layer], inv_two.at[layer], row(layer, 3))
            above = gys[layer, i // (rows // step), pl.ds(lax.rem(i, rows // step) * step, step), :]
            part = part + above.astype(f32) * (1.0 / nt)
            grad_res[pl.ds(at, step), :] = part
            normed[pl.ds(at, step), :] = part.astype(bf16)
            return 0

        lax.fori_loop(0, brows // step, pull, 0, unroll=True)

    def grad_to_heads(layer):
        first = claim("recv", cells, "heads")
        relay_sem = claim("recv", 2, "heads beside")
        pairs = [pl.ds(0, nb // 2), pl.ds(nb // 2, nb - nb // 2)]

        def share(p, index):
            here = wm[layer, pl.ds(pl.multiple_of(p * z.local_width, z.local_width), z.local_width), :]
            part = dot_nt(here, normed[...]).astype(bf16).reshape(nb, HD, brows)
            gh_send[layer, index] = part
            return part

        def pass_on(p, index, when):
            for j in range(nb):
                push(gh_send.at[layer, index, j], gh.at[layer, me], first + me, (s, p, j), when)

        share(nt - 1 - t, 0)
        for i, two in enumerate(pairs):
            push(gh_send.at[layer, 0, two], gh_relay.at[layer, two], relay_sem + i, (s, beside, d), outer)
        pass_on(nt - 1 - t, 0, inner)
        share(across, 1)
        pass_on(across, 1, outer)
        share(beside, 2)
        pass_on(beside, 2, None)
        part = share(t, 3)
        for j in range(nb):
            push(gh_send.at[layer, 3, j], gh.at[layer, me], first + me, (s, t, j), d != j)

            @pl.when(d == j)
            def _():
                gh[layer, me] = part[j]

        for i, two in enumerate(pairs):
            arrived(gh_relay.at[layer, two], relay_sem + i, inner)

            @pl.when(inner)
            def _():
                met = gh_send[layer, 1, two].astype(f32) + gh_relay[layer, two].astype(f32)
                gh_send[layer, 1, two] = met.astype(bf16)

            for j in range(two.start, two.start + two.size):
                push(gh_send.at[layer, 1, j], gh.at[layer, me], first + me, (s, across, j), inner)

        return first

    def attend_back(layer, first):
        for b in range(nb):
            here = slice(b * brows, (b + 1) * brows)
            values_n[here] = qkv[layer, 2 * HD : 3 * HD, here].T
            queries = (qkv[layer, 0:HD, here].astype(f32) * HD ** (-0.5)).astype(bf16)
            queries_n[here] = queries.T
        out_first = claim("recv", nb, "mixed")
        pre_values = pre[layer, 1, d]
        pre_keys = pre[layer, 0, d].T
        for b in reversed(range(nb)):
            here = slice(b * brows, (b + 1) * brows)
            for p in range(nt):
                cell = p * nb + b
                heard = (me != cell) & jnp.logical_not(outer & (t + p == nt - 1))
                arrived(gh.at[layer, cell], first + cell, heard)
            grad = gh[layer, b].astype(f32)
            for p in range(1, nt):
                grad = grad + gh[layer, p * nb + b].astype(f32)
            grad = grad.astype(bf16)
            scale = scales[layer, b]
            wide_grad = grad.astype(f32)
            delta = jnp.sum(wide_grad * out_t[layer, b], axis=0, keepdims=True)
            grads_n[here] = (wide_grad * scale).astype(bf16).T
            prob = expons_pre[layer, :, here] * scale
            dscores_pre[:, here] = (prob * (dot_nn(pre_values, grad) - delta)).astype(bf16)
            for kb in range(b + 1):
                rows_k = slice(kb * brows, (kb + 1) * brows)
                prob = expons_low[layer, rows_k, here].astype(f32) * scale
                dprob = dot_nn(values_n[rows_k], grad)
                dscores[rows_k, here] = (prob * (dprob - delta)).astype(bf16)
            seen_keys = (b + 1) * brows
            dq = dot_nn(qkv[layer, HD : 2 * HD, :seen_keys], dscores[:seen_keys, here])
            dq = dq + dot_nn(pre_keys, dscores_pre[:, here])
            dkey = dot_nn(dscores[here, b * brows :], queries_n[b * brows :])
            dvalue = dot_nn(expons_low[layer, here, b * brows :], grads_n[b * brows :])
            joined = jnp.concatenate(
                [dq * HD ** (-0.5), dkey.T, dvalue.T], axis=0
            ).astype(bf16)
            dm_send[layer, b] = joined
            push(dm_send.at[layer, b], dm.at[layer, d], out_first + d, (s, t, b), d != b)

            @pl.when(d == b)
            def _():
                dm[layer, d] = joined

        pg[layer, 0] = dot_nn(dscores_pre[...], queries_n[...])
        pg[layer, 1] = dot_nn(expons_pre[layer].astype(bf16), grads_n[...])
        return out_first

    def grad_rows(layer, first):
        for j in range(nb):
            arrived(dm.at[layer, j], first + j, d != j)
        for j in range(nb):
            wide[:, j * 3 * HD : (j + 1) * 3 * HD] = dm[layer, j].T
        depth = nb * 3 * HD

        def some(at):
            right = wq[layer, :, :, pl.ds(at, tile)].reshape(depth, tile)
            total[:, pl.ds(at, tile)] = dot_nn(wide[:, :depth], right)

        tiles(z.width, some)

        def pull(i, _):
            at, part = norm_pull(i, z_one.at[layer], inv_one.at[layer], row(layer, 0))
            part = part + grad_res[pl.ds(at, step), :]
            grad_res[pl.ds(at, step), :] = part
            p = i // (rows // step)
            gi_send[layer, p, pl.ds(lax.rem(i, rows // step) * step, step), :] = part.astype(bf16)
            return 0

        lax.fori_loop(0, brows // step, pull, 0, unroll=True)
        return scatter(layer, gi_send, gi_recv, gi_relay)

    def grad_sum(layer, first):
        return scatter_wait(layer, gi_recv, first, own_rows(grad_res)).astype(bf16)

    for layer in (1, 0):
        if layer == 0:
            spread_relay(gys, 0, gy_first[0])
            for k in range(1, nt):
                spread_wait(gys, 0, gy_first[0], k)
            grad_hidden(0)
        grad_mid(layer)
        heads_first = grad_to_heads(layer)
        if layer == 1:
            y_first = feed_second(1, active_last)
            gi_own[...] = own_rows(resid) + own_rows(total) + row(1, 5)
        rows_first = attend_back(layer, heads_first)
        if layer == 1:
            scatter_relay(1, y_send, y_recv, y_relay, total, y_first)
        if layer == 0:
            sib_sem = claim("recv", 1)
            push(pg.at[1 - s], pg_recv, sib_sem, sib)
        grads_first = grad_rows(layer, rows_first)
        if layer == 0:
            arrived(pg_recv, sib_sem)
            pg_sum[...] = pg[s] + pg_recv[...]
            all_first = claim("recv", nb)
            for k in range(1, nb):
                push(pg_sum, pg_all.at[d], all_first + k, (s, t, block(k)))
            pg_all[d] = pg_sum[...]
        if layer == 1:
            scatter_relay(1, gi_send, gi_recv, gi_relay, grad_res, grads_first)
            y_last[...] = output_sum(1, y_first, gi_own[...])
            put(y_last, lo_out, 1, 1)
            gys[0, t] = grad_sum(1, grads_first)
            gy_first[0] = spread(gys.at[0, t], gys, 0)
            put(gys.at[0, t], ig_out, 1, 2)
        else:
            scatter_relay(0, gi_send, gi_recv, gi_relay, grad_res, grads_first)
            for k in range(1, nb):
                arrived(pg_all.at[block(nb - k)], all_first + k)
            keep(2, jnp.concatenate([pg_all[j, c] for c in range(2) for j in range(nb)], axis=1))
            part = jnp.zeros((z.prefix_pad, z.inner), f32)
            for j in range(nb):
                for c in range(2):
                    at = c * z.local_width + j * HD
                    part = part + dot_split(pg_all[j, c], outer_w[:, at : at + HD], dot_nt)
            hid_all[t] = part
            hid_first = claim("recv", nt)
            for k in range(1, nt):
                push(hid_all.at[t], hid_all.at[t], hid_first + k, (s, plane(k), d))
            xs[0, t] = grad_sum(0, grads_first)
            put(xs.at[0, t], ig_out, 0, 3)
            for k in range(1, nt):
                arrived(hid_all.at[plane(nt - k)], hid_first + k)
            part = hid_all[0]
            for p in range(1, nt):
                part = part + hid_all[p]
            hid_part[...] = part
            hid_sem = claim("recv", 1)
            push(hid_part, hid_recv, hid_sem, sib)
            arrived(hid_recv, hid_sem)
            keep(3, hid_part[...] + hid_recv[...])
            load_parts = lcopy(parts_low, rows_out.at[2, 0, 0])

    for index, (out, layer) in enumerate(((lo_out, 0), (lo_out, 1), (ig_out, 1), (ig_out, 0))):
        arrived(out.at[0, 1 - s], out_sem + index, s == layer)
    for copy, when in pending[-z.sends :]:
        sent(copy, when)
    for copy, when in out_loads:
        pl.when(when)(copy.wait)
    load_parts.wait()


def run_layers(z, small, large):
    nt, nb, rows, brows = z.planes, z.blocks, z.rows, z.block_rows
    width, hidden = z.width, z.hidden
    length = nb * brows
    V = pltpu.VMEM
    any_space = pl.BlockSpec(memory_space=pl.ANY)
    scratch = [
        V((2, 8, width), f32),
        V((2, nb, 3 * HD, 128), bf16),
        V((3, width, z.local_width), bf16),
        V((2, nb, 3 * HD, width), bf16),
        V((2, width, width), bf16),
        V((2, width, hidden), bf16),
        V((2, hidden, width), bf16),
        V((2, 2, nb, z.prefix_pad, HD), bf16),
        V((2, nt, rows, width), bf16),
        V((2, nt, rows, width), bf16),
        V((2, nb, 3 * HD, brows), bf16),
        V((2, 3 * HD, length), bf16),
        V((2, nb, HD, brows), bf16),
        V((2, z.cells, HD, brows), bf16),
        V((2, nt, rows, width), bf16),
        V((2, nt, rows, width), bf16),
        V((2, nt, nb, HD, brows), bf16),
        V((2, z.cells, HD, brows), bf16),
        V((2, nb, 3 * HD, brows), bf16),
        V((2, nb, 3 * HD, brows), bf16),
        V((2, nt, rows, width), bf16),
        V((2, nt, rows, width), bf16),
        V((2, rows, width), bf16),
        V((2, rows, width), bf16),
        V((2, nb, HD, brows), bf16),
        V((2, brows, width), f32),
        V((2, brows, 1), f32),
        V((2, brows, width), f32),
        V((2, brows, 1), f32),
        V((brows, hidden), f32),
        V((brows, hidden), f32),
        V((2, length, length), bf16),
        V((2, z.prefix_pad, length), f32),
        V((2, nb, 1, brows), f32),
        V((length, length), bf16),
        V((z.prefix_pad, length), bf16),
        V((length, HD), bf16),
        V((length, HD), bf16),
        V((length, HD), bf16),
        V((2, nb, HD, brows), f32),
        V((2, length, HD), bf16),
        V((brows, width), bf16),
        V((brows, width), bf16),
        V((brows, width), f32),
        V((brows, width), f32),
        V((brows, width), f32),
        V((rows, width), bf16),
        V((brows, width), bf16),
        V((rows, width), f32),
        V((2, 2, z.prefix_pad, HD), f32),
        V((2, z.prefix_pad, HD), f32),
        V((2, z.prefix_pad, HD), f32),
        V((nb, 2, z.prefix_pad, HD), f32),
        V((z.prefix_pad, width), f32),
        V((width, z.inner), bf16),
        V((z.inner, 2, z.local_width), bf16),
        V((z.inner, 2 * z.local_width), bf16),
        V((z.prefix_pad, z.inner), f32),
        V((z.prefix_pad, z.inner), f32),
        V((rows, width), bf16),
        V((nt, z.prefix_pad, z.inner), f32),
        pltpu.SemaphoreType.DMA((z.sends,)),
        pltpu.SemaphoreType.DMA((109,)),
        pltpu.SemaphoreType.DMA((13,)),
    ]
    return pl.pallas_call(
        partial(both_layers, z),
        out_shape=(
            jax.ShapeDtypeStruct((3, 1, 2, rows, width), bf16),
        ),
        in_specs=[pl.BlockSpec(memory_space=pltpu.SMEM)]
        + [pl.BlockSpec(memory_space=pltpu.VMEM)] * (len(small) - 1)
        + [any_space] * len(large),
        out_specs=(any_space,),
        scratch_shapes=scratch,
        compiler_params=pltpu.CompilerParams(
            collective_id=0, has_side_effects=True, vmem_limit_bytes=60 * 2**20
        ),
        cost_estimate=pl.CostEstimate(
            flops=7 * 10**9, bytes_accessed=16 * 2**20, transcendentals=4 * 10**6
        ),
    )(*small, *large)


def prefix_end(
    z, rows_in, table_in, inner_in,
    lo_out, ig_out, states_out, table_out, inner_out, inner_bias_out, outer_out, outer_bias_out,
    table_pad, parts, inner_full, outer_full, sems,
):
    copies = []

    def start(src, dst):
        copies.append(pltpu.make_async_copy(src, dst, sems.at[len(copies)]))
        copies[-1].start()

    start(rows_in.at[2, 0, 0], parts)
    start(rows_in.at[0], lo_out)
    start(rows_in.at[1], ig_out)
    count, width = z.prefix_rows, z.local_width
    table_pad[...] = jnp.zeros_like(table_pad)
    table_pad[0:count, :] = table_in[...].astype(f32)
    table_turned = table_pad[...].T.astype(bf16)
    copies[0].wait()

    def halves(index):
        at, columns = index // 2 * z.prefix_pad, slice(index % 2 * z.inner, (index % 2 + 1) * z.inner)
        high = parts[at : at + z.prefix_pad, columns]
        at += 2 * z.prefix_pad
        return high, parts[at : at + z.prefix_pad, columns]

    act = halves(0)[0].astype(f32) + halves(0)[1].astype(f32)
    hidden = halves(3)[0].astype(f32) + halves(3)[1].astype(f32)
    inner_grad = hidden * (1.0 - act * act)
    high = inner_grad.astype(bf16)
    low = (inner_grad - high.astype(f32)).astype(bf16)
    some = z.width // 2
    for i in range(2):
        at = slice(i * some, (i + 1) * some)
        inner_full[at] = dot_nn(table_turned[at], high) + dot_nn(table_turned[at], low)
        start(inner_full.at[at], inner_out.at[at])
    act_turned = act.T.astype(bf16)
    total = halves(2)
    for c in range(2):
        at = slice(c * width, (c + 1) * width)
        outer_full[:, c, :] = dot_nn(act_turned, total[0][:, at]) + dot_nn(act_turned, total[1][:, at])
    start(outer_full, outer_out)
    whole = total[0].astype(f32) + total[1].astype(f32)
    for c in range(2):
        at = slice(c * width, (c + 1) * width)
        states_out[:, c, :] = halves(1)[0][0:count, at]
        outer_bias_out[0, c : c + 1, :] = jnp.sum(whole[:, at], axis=0, keepdims=True)
    inner_bias_out[...] = jnp.sum(inner_grad, axis=0, keepdims=True)
    table_out[...] = (dot_nt(high, inner_in[...]) + dot_nt(low, inner_in[...]))[0:count]
    for copy in copies[1:]:
        copy.wait()


def finish(z, both_rows, table, inner_weight):
    any_space = pl.BlockSpec(memory_space=pl.ANY)
    whole = pl.BlockSpec(memory_space=pltpu.VMEM)
    rows = jax.ShapeDtypeStruct(both_rows.shape[1:], bf16)
    return pl.pallas_call(
        partial(prefix_end, z),
        out_shape=(
            rows,
            rows,
            jax.ShapeDtypeStruct((z.prefix_rows, 2, z.local_width), bf16),
            jax.ShapeDtypeStruct((z.prefix_rows, z.width), f32),
            jax.ShapeDtypeStruct((z.width, z.inner), f32),
            jax.ShapeDtypeStruct((1, z.inner), f32),
            jax.ShapeDtypeStruct((z.inner, 2, z.local_width), f32),
            jax.ShapeDtypeStruct((1, 2, z.local_width), f32),
        ),
        in_specs=[any_space] + [whole] * 2,
        out_specs=(any_space,) * 2 + (whole,) * 2 + (any_space, whole, any_space, whole),
        scratch_shapes=[
            pltpu.VMEM((z.prefix_pad, z.width), f32),
            pltpu.VMEM(both_rows.shape[3:], bf16),
            pltpu.VMEM((z.width, z.inner), f32),
            pltpu.VMEM((z.inner, 2, z.local_width), f32),
            pltpu.SemaphoreType.DMA((6,)),
        ],
        compiler_params=pltpu.CompilerParams(vmem_limit_bytes=32 * 2**20),
    )(both_rows, table, inner_weight)


def head_a_device(
    block_input,
    output_grad,
    valid_len,
    first_gain,
    first_bias,
    triple_weight,
    triple_bias,
    mixer_weight,
    mixer_bias,
    second_gain,
    second_bias,
    expand_weight,
    expand_bias,
    reduce_weight,
    reduce_bias,
    prefix_table,
    inner_weight,
    inner_bias,
    outer_weight,
    outer_bias,
):
    planes, blocks = lax.axis_size("tensor"), lax.axis_size("dp")
    local_width = triple_weight.shape[3]
    prefix_rows = prefix_table.shape[0]
    z = Sizes(
        planes,
        blocks,
        block_input.shape[1],
        block_input.shape[2],
        local_width,
        expand_weight.shape[2],
        prefix_rows,
    )
    z.prefix_pad = -(-prefix_rows // 16) * 16
    z.inner = inner_weight.shape[1]
    small = (
        valid_len,
        first_gain,
        first_bias,
        triple_bias,
        mixer_bias,
        second_gain,
        second_bias,
        expand_bias,
        reduce_bias,
        prefix_table,
        inner_bias,
        outer_bias,
    )
    large = (
        block_input,
        output_grad,
        triple_weight[0].transpose(1, 0, 2),
        mixer_weight[0],
        expand_weight[0],
        reduce_weight[0],
        inner_weight,
        outer_weight[:, 0],
    )
    results = finish(z, *run_layers(z, small, large), prefix_table, inner_weight)
    (
        layer_outputs,
        input_grads,
        prefix_states,
        table_grad,
        inner_weight_grad,
        inner_bias_grad,
        outer_weight_grad,
        outer_bias_grad,
    ) = results
    return (
        layer_outputs,
        input_grads,
        prefix_states.transpose(1, 0, 2)[None],
        table_grad,
        inner_weight_grad,
        inner_bias_grad.reshape(-1),
        outer_weight_grad.reshape(-1, 1, 2, local_width),
        outer_bias_grad,
    )


def prefix_back(
    prefix_total,
    prefix_full,
    inner_act,
    inner_low,
    outer_local,
    prefix_table,
    inner_weight,
    local_width,
):
    inner_float = inner_low.astype(f32)
    outer_float = outer_local.astype(f32)
    outer_weight_grad = jnp.dot(inner_float.T, prefix_total, precision=highest).reshape(
        -1, 1, 2, local_width
    )
    outer_bias_grad = jnp.sum(prefix_total, axis=0).reshape(1, 2, local_width)
    hidden_grad = lax.psum(
        jnp.dot(prefix_total, outer_float.T, precision=highest), ("section", "tensor")
    )
    inner_grad = hidden_grad * (1.0 - inner_act * inner_act)
    inner_weight_grad = jnp.dot(prefix_table.astype(f32).T, inner_grad, precision=highest)
    inner_bias_grad = jnp.sum(inner_grad, axis=0)
    table_grad = jnp.dot(inner_grad, inner_weight.astype(f32).T, precision=highest)
    prefix_states = prefix_full.reshape(-1, 2, local_width).transpose(1, 0, 2)[None]
    return (
        prefix_states,
        table_grad,
        inner_weight_grad,
        inner_bias_grad,
        outer_weight_grad,
        outer_bias_grad,
    )


def solution(mesh):
    def step(*args):
        triple_weight = args[5]
        micro_count, share_rows, width = args[0].shape
        fits = (
            lax.axis_size("section") == 2
            and micro_count == 2
            and triple_weight.shape[3] == HD * lax.axis_size("dp")
            and share_rows * lax.axis_size("tensor") == 256
            and triple_weight.shape[3] % 256 == 0
            and width % 256 == 0
            and args[11].shape[2] == width
            and args[16].shape[1] * 2 == width
            and args[15].shape[0] <= 16
            and share_rows == 64
        )
        return head_a_device(*args) if fits else shards(*args)

    return jax.shard_map(
        step,
        mesh=mesh,
        in_specs=(
            P(None, ("dp", "tensor"), None),
            P(None, ("dp", "tensor"), None),
            P(),
            P("section", None),
            P("section", None),
            P("section", None, None, "tensor"),
            P("section", None, "tensor"),
            P("section", "tensor", None),
            P("section", None),
            P("section", None),
            P("section", None),
            P("section", None, "tensor"),
            P("section", "tensor"),
            P("section", "tensor", None),
            P("section", None),
            P(),
            P(),
            P(),
            P(None, "section", None, "tensor"),
            P("section", None, "tensor"),
        ),
        out_specs=(
            P("section", None, ("dp", "tensor"), None),
            P("section", None, ("dp", "tensor"), None),
            P("section", None, None, "tensor"),
            P(),
            P(),
            P(),
            P(None, "section", None, "tensor"),
            P("section", None, "tensor"),
        ),
        check_vma=False,
    )
```

```python
from functools import partial

import jax
import jax.numpy as jnp
from jax import lax
from jax.experimental import pallas as pl
from jax.experimental.pallas import tpu as pltpu
from jax.sharding import PartitionSpec as P

HD = 64


epsilon = 1e-05
masked_score = -1e30
highest = lax.Precision.HIGHEST
MESH = pl.DeviceIdType.MESH
f32 = jnp.float32
bf16 = jnp.bfloat16


def passed_along(block, axis, distance):
    devices = range(lax.axis_size(axis))
    route = [(i - distance, i) for i in devices if i - distance in devices]
    return lax.ppermute(block, axis, route)


def layer_norm(values, norm_gain, norm_bias):
    center = values - jnp.mean(values, axis=-1, keepdims=True)
    variance = jnp.mean(center * center, axis=-1, keepdims=True)
    inverse = lax.rsqrt(variance + epsilon)
    normed = center * inverse
    return (normed * norm_gain + norm_bias, normed, inverse)


def norm_back(grad_out, normed, inverse, norm_gain):
    scaled = grad_out * norm_gain
    mean_grad = jnp.mean(scaled, axis=-1, keepdims=True)
    mean_cross = jnp.mean(scaled * normed, axis=-1, keepdims=True)
    return inverse * (scaled - mean_grad - normed * mean_cross)


def attention_scores(queries, seq_keys, pre_keys, valid, query_start):
    score_scale = HD ** (-0.5)
    seq_scores = (
        jnp.einsum("qhd,khd->hqk", queries, seq_keys, preferred_element_type=jnp.float32)
        * score_scale
    )
    pre_scores = (
        jnp.einsum("qhd,khd->hqk", queries, pre_keys, preferred_element_type=jnp.float32)
        * score_scale
    )
    query_pos = query_start + lax.broadcasted_iota(jnp.int32, (queries.shape[0], 1), 0)
    key_pos = lax.broadcasted_iota(jnp.int32, (1, seq_keys.shape[0]), 1)
    visible = (key_pos <= query_pos) & (key_pos < valid)
    seq_scores = jnp.where(visible[None], seq_scores, masked_score)
    return (seq_scores, pre_scores)


def split_prefix(prefix_full, local_width):
    local_heads = local_width // HD
    pre_keys = prefix_full[:, :local_width].reshape(-1, local_heads, HD)
    pre_values = prefix_full[:, local_width:].reshape(-1, local_heads, HD)
    return (pre_keys, pre_values)


def layer_forward(inputs, weights, prefix_full, valid, query_start):
    (
        gain_one,
        bias_one,
        triple_weight,
        triple_bias,
        mixer_weight,
        mixer_bias,
        gain_two,
        bias_two,
        expand_weight,
        expand_bias,
        reduce_weight,
        reduce_bias,
    ) = weights
    local_width = triple_weight.shape[1] // 3
    local_heads = local_width // HD
    normed_one, unit_one, inverse_one = layer_norm(inputs, gain_one, bias_one)
    mixed_rows = (
        jnp.dot(
            lax.all_gather(normed_one.astype(jnp.bfloat16), "tensor", axis=0, tiled=True),
            triple_weight,
            preferred_element_type=jnp.float32,
        )
        + triple_bias
    ).astype(jnp.bfloat16)
    tokens = mixed_rows.shape[0]
    queries = mixed_rows[:, :local_width].reshape(tokens, local_heads, HD)
    seq_keys, seq_values = (
        lax.all_gather(mixed_rows[:, local_width : 2 * local_width], "dp", axis=0, tiled=True),
        lax.all_gather(mixed_rows[:, 2 * local_width :], "dp", axis=0, tiled=True),
    )
    seq_keys = seq_keys.reshape(-1, local_heads, HD)
    seq_values = seq_values.reshape(-1, local_heads, HD)
    pre_keys, pre_values = split_prefix(prefix_full, local_width)
    seq_scores, pre_scores = attention_scores(queries, seq_keys, pre_keys, valid, query_start)
    row_max = jnp.maximum(
        jnp.max(seq_scores, axis=2, keepdims=True), jnp.max(pre_scores, axis=2, keepdims=True)
    )
    seq_exp = jnp.exp(seq_scores - row_max)
    pre_exp = jnp.exp(pre_scores - row_max)
    row_total = jnp.sum(seq_exp, axis=2, keepdims=True) + jnp.sum(pre_exp, axis=2, keepdims=True)
    log_total = row_max + jnp.log(row_total)
    seq_low = (seq_exp / row_total).astype(jnp.bfloat16)
    pre_low = (pre_exp / row_total).astype(jnp.bfloat16)
    attended = jnp.einsum("hqk,khd->qhd", seq_low, seq_values, preferred_element_type=jnp.float32)
    attended = attended + jnp.einsum(
        "hqk,khd->qhd", pre_low, pre_values, preferred_element_type=jnp.float32
    )
    attended = attended.astype(jnp.bfloat16).reshape(tokens, local_width)
    mixer_out = lax.psum_scatter(
        jnp.dot(attended, mixer_weight, preferred_element_type=jnp.float32),
        "tensor",
        scatter_dimension=0,
        tiled=True,
    )
    residual = inputs + mixer_out + mixer_bias
    normed_two, unit_two, inverse_two = layer_norm(residual, gain_two, bias_two)
    hidden_pre = (
        jnp.dot(
            lax.all_gather(normed_two.astype(jnp.bfloat16), "tensor", axis=0, tiled=True),
            expand_weight,
            preferred_element_type=jnp.float32,
        )
        + expand_bias
    )
    active = jax.nn.gelu(hidden_pre, approximate=True).astype(jnp.bfloat16)
    result = (
        residual
        + lax.psum_scatter(
            jnp.dot(active, reduce_weight, preferred_element_type=jnp.float32),
            "tensor",
            scatter_dimension=0,
            tiled=True,
        )
        + reduce_bias
    )
    saved_state = (
        unit_one,
        inverse_one,
        queries,
        seq_keys,
        seq_values,
        log_total,
        unit_two,
        inverse_two,
        hidden_pre,
    )
    return (result, saved_state)


def layer_backward(grad_out, saved_state, weights, prefix_full, valid, query_start):
    (
        gain_one,
        bias_one,
        triple_weight,
        triple_bias,
        mixer_weight,
        mixer_bias,
        gain_two,
        bias_two,
        expand_weight,
        expand_bias,
        reduce_weight,
        reduce_bias,
    ) = weights
    (
        unit_one,
        inverse_one,
        queries,
        seq_keys,
        seq_values,
        log_total,
        unit_two,
        inverse_two,
        hidden_pre,
    ) = saved_state
    tokens = queries.shape[0]
    local_heads = queries.shape[1]
    local_width = local_heads * HD
    score_scale = HD ** (-0.5)
    grad_active = jnp.dot(
        lax.all_gather(grad_out.astype(jnp.bfloat16), "tensor", axis=0, tiled=True),
        reduce_weight.T,
        preferred_element_type=jnp.float32,
    )
    gelu_pull = jax.vjp(partial(jax.nn.gelu, approximate=True), hidden_pre)[1]
    grad_pre = gelu_pull(grad_active)[0].astype(jnp.bfloat16)
    grad_two = lax.psum_scatter(
        jnp.dot(grad_pre, expand_weight.T, preferred_element_type=jnp.float32),
        "tensor",
        scatter_dimension=0,
        tiled=True,
    )
    grad_residual = grad_out + norm_back(grad_two, unit_two, inverse_two, gain_two)
    grad_heads = jnp.dot(
        lax.all_gather(grad_residual.astype(jnp.bfloat16), "tensor", axis=0, tiled=True),
        mixer_weight.T,
        preferred_element_type=jnp.float32,
    ).astype(jnp.bfloat16)
    grad_heads = grad_heads.reshape(tokens, local_heads, HD)
    pre_keys, pre_values = split_prefix(prefix_full, local_width)
    seq_scores, pre_scores = attention_scores(queries, seq_keys, pre_keys, valid, query_start)
    seq_prob = jnp.exp(seq_scores - log_total)
    pre_prob = jnp.exp(pre_scores - log_total)
    seq_dprob = jnp.einsum(
        "qhd,khd->hqk", grad_heads, seq_values, preferred_element_type=jnp.float32
    )
    pre_dprob = jnp.einsum(
        "qhd,khd->hqk", grad_heads, pre_values, preferred_element_type=jnp.float32
    )
    delta_row = jnp.sum(seq_prob * seq_dprob, axis=2, keepdims=True) + jnp.sum(
        pre_prob * pre_dprob, axis=2, keepdims=True
    )
    seq_dscore = (seq_prob * (seq_dprob - delta_row)).astype(jnp.bfloat16)
    pre_dscore = (pre_prob * (pre_dprob - delta_row)).astype(jnp.bfloat16)
    seq_low = seq_prob.astype(jnp.bfloat16)
    pre_low = pre_prob.astype(jnp.bfloat16)
    grad_queries = jnp.einsum(
        "hqk,khd->qhd", seq_dscore, seq_keys, preferred_element_type=jnp.float32
    )
    grad_queries = (
        grad_queries
        + jnp.einsum("hqk,khd->qhd", pre_dscore, pre_keys, preferred_element_type=jnp.float32)
    ) * score_scale
    key_term = (
        jnp.einsum("hqk,qhd->khd", seq_dscore, queries, preferred_element_type=jnp.float32)
        * score_scale
    )
    value_term = jnp.einsum("hqk,qhd->khd", seq_low, grad_heads, preferred_element_type=jnp.float32)
    grad_keys, grad_values = (
        lax.psum_scatter(key_term.reshape(-1, local_width), "dp", scatter_dimension=0, tiled=True),
        lax.psum_scatter(
            value_term.reshape(-1, local_width), "dp", scatter_dimension=0, tiled=True
        ),
    )
    pre_key_grad = (
        jnp.einsum("hqk,qhd->khd", pre_dscore, queries, preferred_element_type=jnp.float32)
        * score_scale
    )
    pre_value_grad = jnp.einsum(
        "hqk,qhd->khd", pre_low, grad_heads, preferred_element_type=jnp.float32
    )
    prefix_term = jnp.concatenate(
        [pre_key_grad.reshape(-1, local_width), pre_value_grad.reshape(-1, local_width)], axis=1
    )
    grad_mixed = jnp.concatenate(
        [grad_queries.reshape(tokens, local_width), grad_keys, grad_values], axis=1
    ).astype(jnp.bfloat16)
    grad_one = lax.psum_scatter(
        jnp.dot(grad_mixed, triple_weight.T, preferred_element_type=jnp.float32),
        "tensor",
        scatter_dimension=0,
        tiled=True,
    )
    grad_input = grad_residual + norm_back(grad_one, unit_one, inverse_one, gain_one)
    return (grad_input, prefix_term)


def shards(
    block_input,
    output_grad,
    valid_len,
    first_gain,
    first_bias,
    triple_weight,
    triple_bias,
    mixer_weight,
    mixer_bias,
    second_gain,
    second_bias,
    expand_weight,
    expand_bias,
    reduce_weight,
    reduce_bias,
    prefix_table,
    inner_weight,
    inner_bias,
    outer_weight,
    outer_bias,
):
    section_index = lax.axis_index("section")
    micro_count = block_input.shape[0]
    share_rows = block_input.shape[1]
    model_width = block_input.shape[2]
    local_width = triple_weight.shape[3]
    query_start = lax.axis_index("dp") * (share_rows * lax.axis_size("tensor"))
    weights = (
        first_gain[0],
        first_bias[0],
        triple_weight[0].reshape(-1, 3 * local_width),
        triple_bias[0].reshape(3 * local_width),
        mixer_weight[0],
        mixer_bias[0],
        second_gain[0],
        second_bias[0],
        expand_weight[0],
        expand_bias[0],
        reduce_weight[0],
        reduce_bias[0],
    )
    inner_pre = jnp.dot(prefix_table, inner_weight, preferred_element_type=jnp.float32) + inner_bias
    inner_act = jnp.tanh(inner_pre)
    inner_low = inner_act.astype(jnp.bfloat16)
    outer_local = outer_weight[:, 0].reshape(outer_weight.shape[0], 2 * local_width)
    prefix_full = (
        jnp.dot(inner_low, outer_local, preferred_element_type=jnp.float32)
        + outer_bias[0].reshape(2 * local_width)
    ).astype(jnp.bfloat16)
    moments = micro_count + 1
    carried = jnp.zeros((share_rows, model_width), jnp.bfloat16)
    results = []
    stored_states = []
    for moment in range(moments):
        micro_index = jnp.clip(moment - section_index, 0, micro_count - 1)
        inputs = jnp.where(
            section_index == 0, block_input[min(moment, micro_count - 1)], carried
        ).astype(jnp.float32)
        result, saved_state = layer_forward(
            inputs, weights, prefix_full, valid_len[micro_index], query_start
        )
        result_low = result.astype(jnp.bfloat16)
        results.append(result_low)
        stored_states.append(inputs)
        if moment + 1 < moments:
            carried = passed_along(result_low, "section", 1)
    grad_carried = jnp.zeros((share_rows, model_width), jnp.bfloat16)
    grad_list = []
    prefix_grad = jnp.zeros((prefix_full.shape[0], 2 * local_width), jnp.float32)
    for moment in range(moments):
        micro_index = moment - 1 + section_index
        valid_tick = (micro_index >= 0) & (micro_index < micro_count)
        clipped = jnp.clip(micro_index, 0, micro_count - 1)
        grad_in = jnp.where(
            section_index == 1, output_grad[min(moment, micro_count - 1)], grad_carried
        ).astype(jnp.float32)
        early_state = stored_states[max(moment - 1, 0)]
        late_state = stored_states[min(moment + 1, moments - 1)]
        picked = jnp.where(section_index == 0, early_state, late_state)
        picked_state = layer_forward(picked, weights, prefix_full, valid_len[clipped], query_start)[
            1
        ]
        grad_input, prefix_term = layer_backward(
            grad_in, picked_state, weights, prefix_full, valid_len[clipped], query_start
        )
        prefix_grad = prefix_grad + jnp.where(valid_tick, prefix_term, 0.0)
        grad_low = grad_input.astype(jnp.bfloat16)
        grad_list.append(grad_low)
        if moment + 1 < moments:
            grad_carried = passed_along(grad_low, "section", -1)
    layer_outputs = jnp.stack(
        [
            jnp.where(section_index == 0, results[number], results[number + 1])
            for number in range(micro_count)
        ]
    )[None]
    input_grads = jnp.stack(
        [
            jnp.where(section_index == 0, grad_list[number + 1], grad_list[number])
            for number in range(micro_count)
        ]
    )[None]
    prefix_total = lax.psum(prefix_grad, "dp")
    return (layer_outputs, input_grads) + prefix_back(
        prefix_total,
        prefix_full,
        inner_act,
        inner_low,
        outer_local,
        prefix_table,
        inner_weight,
        local_width,
    )


def dot_nn(left, right):
    return lax.dot_general(left, right, (((1,), (0,)), ((), ())), preferred_element_type=f32)


def dot_nt(left, right):
    return lax.dot_general(left, right, (((1,), (1,)), ((), ())), preferred_element_type=f32)


def dot_split(left, right, dot):
    high = left.astype(bf16)
    low = (left - high.astype(f32)).astype(bf16)
    return dot(high, right) + dot(low, right)


class Sizes:
    def __init__(self, planes, blocks, rows, width, local_width, hidden, prefix_rows):
        self.planes = planes
        self.blocks = blocks
        self.rows = rows
        self.block_rows = rows * planes
        self.width = width
        self.local_width = local_width
        self.hidden = hidden
        self.prefix_rows = prefix_rows
        self.cells = planes * blocks
        self.tile = 256
        self.sends = 48


def both_layers(
    z,
    valid_ref,
    gain_one_in,
    bias_one_in,
    triple_bias_in,
    mixer_bias_in,
    gain_two_in,
    bias_two_in,
    expand_bias_in,
    reduce_bias_in,
    table_in,
    inner_bias_in,
    outer_bias_in,
    x_in,
    gy_in,
    triple_in,
    mixer_in,
    expand_in,
    reduce_in,
    inner_in,
    outer_in,
    rows_out,
    vec,
    tbias,
    triple_own,
    wq,
    wm,
    we,
    wr,
    pre,
    xs,
    gys,
    qkv_send,
    qkv,
    ot_send,
    att,
    y_send,
    y_recv,
    gh_send,
    gh,
    dm_send,
    dm,
    gi_send,
    gi_recv,
    y_relay,
    gi_relay,
    gh_relay,
    z_one,
    inv_one,
    z_two,
    inv_two,
    gelu_grad,
    upper,
    expons_low,
    expons_pre,
    scales,
    dscores,
    dscores_pre,
    values_n,
    queries_n,
    grads_n,
    out_t,
    keys_n,
    normed,
    wide,
    total,
    grad_res,
    resid,
    y_last,
    active_last,
    gi_own,
    pg,
    pg_recv,
    pg_sum,
    pg_all,
    table_pad,
    inner_w,
    outer_raw,
    outer_w,
    hid_part,
    hid_recv,
    parts_low,
    hid_all,
    send_sem,
    recv_sem,
    local_sem,
):
    lo_out, ig_out = rows_out.at[0], rows_out.at[1]
    s = lax.axis_index("section")
    t = lax.axis_index("tensor")
    d = lax.axis_index("dp")
    nt, nb, rows, brows, tile = z.planes, z.blocks, z.rows, z.block_rows, z.tile
    cells = z.cells
    me = t * nb + d
    sib = (1 - s, t, d)
    counts = dict(send=0, recv=0, local=0)
    pending = []
    shared = {}

    def claim(kind, number, name=None):
        if name in shared:
            return shared[name]
        first = counts[kind]
        counts[kind] += number
        if name is not None:
            shared[name] = first
        return first

    def rcopy(src, dst, ss, rs, device):
        return pltpu.make_async_remote_copy(
            src_ref=src,
            dst_ref=dst,
            send_sem=send_sem.at[ss],
            recv_sem=recv_sem.at[rs],
            device_id=device,
            device_id_type=MESH,
        )

    def push(src, dst, rs, device, when=None):
        if len(pending) >= z.sends:
            sent(*pending[len(pending) - z.sends])
        copy = rcopy(src, dst, len(pending) % z.sends, rs, device)
        if when is None:
            copy.start()
        else:
            pl.when(when)(copy.start)
        pending.append((copy, when))

    def sent(copy, when):
        if when is None:
            copy.wait_send()
        else:
            pl.when(when)(copy.wait_send)

    def arrived(dst, rs, when=None):
        copy = rcopy(dst, dst, 0, rs, sib)
        if when is None:
            copy.wait_recv()
        else:
            pl.when(when)(copy.wait_recv)

    def lcopy(src, dst):
        copy = pltpu.make_async_copy(src, dst, local_sem.at[claim("local", 1)])
        copy.start()
        return copy

    outer = (t == 0) | (t == nt - 1)
    inner = jnp.logical_not(outer)
    across = lax.rem(t + 2, nt)
    beside = t + 1 - 2 * lax.rem(t, 2)

    def far(k):
        return ((t == 0) & (k == nt - 1)) | ((t == nt - 1) & (k == 1))

    def unheard(k):
        return ((t == 0) & (k == 1)) | ((t == nt - 1) & (k == nt - 1))

    def near(k):
        return jnp.logical_not(far(k))

    def keep(index, value):
        high = value.astype(bf16)
        low = (value - high.astype(f32)).astype(bf16)
        at, columns = index // 2 * z.prefix_pad, slice(index % 2 * z.inner, (index % 2 + 1) * z.inner)
        parts_low[at : at + z.prefix_pad, columns] = high
        at += 2 * z.prefix_pad
        parts_low[at : at + z.prefix_pad, columns] = low

    def plane(k):
        return lax.rem(t + k, nt)

    def block(k):
        return lax.rem(d + k, nb)

    barrier = pltpu.get_barrier_semaphore()
    for k in range(1, cells):
        pl.semaphore_signal(
            barrier, inc=1, device_id=(s, plane(k // nb), block(k % nb)), device_id_type=MESH
        )
    pl.semaphore_signal(barrier, inc=1, device_id=sib, device_id_type=MESH)

    load_x = lcopy(x_in.at[s], xs.at[0, t])
    load_triple = lcopy(triple_in, triple_own)
    load_inner = lcopy(inner_in, inner_w)
    load_outer = lcopy(outer_in, outer_raw)
    load_mixer = lcopy(mixer_in, wm.at[s, pl.ds(pl.multiple_of(t * z.local_width, 256), z.local_width)])
    load_expand = lcopy(expand_in, we.at[s])
    load_reduce = lcopy(reduce_in, wr.at[s])
    load_gy = lcopy(gy_in.at[s], gys.at[1, t])

    for layer in range(2):
        for k in (1, nt - 1):

            @pl.when(unheard(k))
            def _():
                y_recv[layer, k] = jnp.zeros((rows, z.width), bf16)
                gi_recv[layer, k] = jnp.zeros((rows, z.width), bf16)

        @pl.when(outer)
        def _():
            for j in range(nb):
                gh[layer, (nt - 1 - t) * nb + j] = jnp.zeros((HD, brows), bf16)

    pl.semaphore_wait(barrier, cells)

    half = rows // 2

    def parts_of(ref):
        return ref.at[pl.ds(0, half)], ref.at[pl.ds(half, half)]

    def spread(src, buf, layer, when=True):
        first = claim("recv", nt + 2, "rows" if buf is xs else "grads")
        for i, (one, goal) in enumerate(zip(parts_of(src), parts_of(buf.at[layer, t]))):
            push(one, goal, first + (2, nt)[i], (s, across, d), outer & when)
        push(src, buf.at[layer, t], first + 2, (s, across, d), inner & when)
        for k in (1, 3):
            push(src, buf.at[layer, t], first + k, (s, plane(k), d), near(k) & when)
        return first

    def spread_relay(buf, layer, first):
        for i, one in enumerate(parts_of(buf.at[layer, across])):
            arrived(one, first + (2, nt)[i], inner)
            push(one, one, first + (2 * t - 1, nt + 1)[i], (s, beside, d), inner)

    def spread_wait(buf, layer, first, k):
        unit = buf.at[layer, plane(nt - k)]
        if k == 2:
            arrived(unit, first + k, outer)
        else:
            arrived(unit, first + k, jnp.logical_not(unheard(k)))
            for i, one in enumerate(parts_of(unit)):
                arrived(one, first + (k, nt + 1)[i], unheard(k))

    x_first = [None, None]
    gy_first = [None, None]
    mix_first = claim("recv", nt)
    mix_second = claim("recv", nt * nb)
    mix_third = claim("recv", 1)

    def piece(layer, p, q):
        return wm.at[layer, pl.ds(pl.multiple_of((p * nb + q) * (z.local_width // nb), 64), z.local_width // nb)]

    def mix_one(layer):
        part = z.local_width // nb
        for k in range(1, nt):
            push(
                mixer_in.at[pl.ds(pl.multiple_of(d * part, 64), part)],
                piece(layer, t, d),
                mix_first + k,
                (s, plane(k), d),
                s == layer,
            )

    def mix_two(layer):
        for k in range(1, nt):
            source = plane(nt - k)
            arrived(piece(layer, source, d), mix_first + k, s == layer)
            for q in range(1, nb):
                push(
                    piece(layer, source, d),
                    piece(layer, source, d),
                    mix_second + k * nb + q,
                    (s, t, block(q)),
                    s == layer,
                )

    def mix_three(layer):
        for k in range(1, nt):
            for q in range(1, nb):
                arrived(
                    piece(layer, plane(nt - k), block(nb - q)),
                    mix_second + k * nb + q,
                    s == layer,
                )
        push(wm.at[layer], wm.at[layer], mix_third, sib, s == layer)

    mix_one(0)

    x_first[0] = spread(x_in.at[s], xs, 0, s == 1)

    for index, ref in enumerate(
        (gain_one_in, bias_one_in, mixer_bias_in, gain_two_in, bias_two_in, reduce_bias_in, expand_bias_in)
    ):
        vec[s, index : index + 1, :] = ref[...].astype(f32)
    for c in range(3):
        shift = jnp.broadcast_to(triple_bias_in[0, c : c + 1, :].astype(f32), (128, z.local_width)).T
        for j in range(nb):
            tbias[s, j, c * HD : (c + 1) * HD, :] = shift[j * HD : (j + 1) * HD].astype(bf16)
    table_pad[...] = jnp.zeros_like(table_pad)
    table_pad[0 : z.prefix_rows, :] = table_in[...].astype(f32)


    small = claim("recv", 3)
    push(vec.at[s], vec.at[s], small, sib)
    push(tbias.at[s], tbias.at[s], small + 1, sib)

    load_triple.wait()
    for c in range(3):
        for n in range(z.width // tile):
            turned = triple_own[c, n * tile : (n + 1) * tile, :].T
            for j in range(nb):
                wq[s, j, c * HD : (c + 1) * HD, n * tile : (n + 1) * tile] = turned[j * HD : (j + 1) * HD]
    wq_first = claim("recv", 1)
    push(wq.at[s], wq.at[s], wq_first, sib)
    load_inner.wait()
    inner_act = jnp.tanh(
        dot_nn(table_pad[...].astype(bf16), inner_w[...]) + inner_bias_in[...].reshape(1, z.inner).astype(f32)
    )
    keep(0, inner_act)
    load_outer.wait()
    for c in range(2):
        outer_w[:, c * z.local_width : (c + 1) * z.local_width] = outer_raw[:, c, :]
    outer_shift = jnp.concatenate([outer_bias_in[0, 0:1, :], outer_bias_in[0, 1:2, :]], axis=1)
    prefix = (dot_nn(inner_act.astype(bf16), outer_w[...]) + outer_shift.astype(f32)).astype(bf16)
    keep(1, prefix.astype(f32))
    for c in range(2):
        for j in range(nb):
            at = c * z.local_width + j * HD
            pre[s, c, j] = prefix[:, at : at + HD]
    push(pre.at[s], pre.at[s], small + 2, sib)
    arrived(vec.at[1 - s], small)
    arrived(tbias.at[1 - s], small + 1)
    arrived(pre.at[1 - s], small + 2)

    def row(layer, index):
        return vec[layer, index : index + 1, :]

    step = 32

    def norm_one(layer, p):
        def some(i, _):
            at = pl.multiple_of(i * step, step)
            x = xs[layer, p, pl.ds(at, step), :].astype(f32)
            center = x - jnp.mean(x, axis=1, keepdims=True)
            inverse = lax.rsqrt(jnp.mean(center * center, axis=1, keepdims=True) + epsilon)
            unit = center * inverse
            where = pl.multiple_of(p * rows + at, step)
            z_one[layer, pl.ds(where, step), :] = unit
            inv_one[layer, pl.ds(where, step), :] = inverse
            normed[pl.ds(where, step), :] = (unit * row(layer, 0) + row(layer, 1)).astype(bf16)
            return 0

        lax.fori_loop(0, rows // step, some, 0, unroll=True)

    def norm_two(layer):
        def some(i, _):
            at = pl.multiple_of(i * step, step)
            x = resid[pl.ds(at, step), :]
            center = x - jnp.mean(x, axis=1, keepdims=True)
            inverse = lax.rsqrt(jnp.mean(center * center, axis=1, keepdims=True) + epsilon)
            unit = center * inverse
            z_two[layer, pl.ds(at, step), :] = unit
            inv_two[layer, pl.ds(at, step), :] = inverse
            normed[pl.ds(at, step), :] = (unit * row(layer, 3) + row(layer, 4)).astype(bf16)
            return 0

        lax.fori_loop(0, brows // step, some, 0, unroll=True)

    def norm_pull(i, units, inverses, gain):
        at = pl.multiple_of(i * step, step)
        unit = units[pl.ds(at, step), :]
        scaled = total[pl.ds(at, step), :] * gain
        mean_grad = jnp.mean(scaled, axis=1, keepdims=True)
        mean_cross = jnp.mean(scaled * unit, axis=1, keepdims=True)
        return at, inverses[pl.ds(at, step), :] * (scaled - mean_grad - unit * mean_cross)

    def tiles(count, body):
        def some(i, _):
            body(pl.multiple_of(i * tile, tile))
            return 0

        lax.fori_loop(0, count // tile, some, 0, unroll=True)

    def positions(ref, b):
        return ref.at[:, pl.ds(pl.multiple_of(b * brows, brows), brows)]

    def project(layer):
        first = claim("recv", nb, "project")
        for k in range(1, nb + 1):
            head = block(k)
            part = dot_nt(wq[layer, head], normed[...])
            shift = tbias[layer, head].astype(f32)
            part = (part + jnp.concatenate([shift, shift], axis=1)).astype(bf16)
            if k < nb:
                qkv_send[layer, k] = part
                push(qkv_send.at[layer, k], positions(qkv.at[layer], d), first + k, (s, t, head))
            else:
                qkv[layer, :, pl.ds(pl.multiple_of(d * brows, brows), brows)] = part
        return first

    def attend(layer, first):
        out_first = claim("recv", cells, "attend")
        pre_keys = pre[layer, 0, d]
        pre_values = pre[layer, 1, d].T
        prefix_row = lax.broadcasted_iota(jnp.int32, (z.prefix_pad, brows), 0)
        key_at = lax.broadcasted_iota(jnp.int32, (brows, brows), 0)
        query_at = lax.broadcasted_iota(jnp.int32, (brows, brows), 1)
        valid = valid_ref[s]
        for b in range(nb):
            here = slice(b * brows, (b + 1) * brows)
            arrived(positions(qkv.at[layer], b), first + lax.rem(d + nb - b, nb), d != b)
            keys_n[layer, here] = qkv[layer, HD : 2 * HD, here].T
            queries = (qkv[layer, 0:HD, here].astype(f32) * HD ** (-0.5)).astype(bf16)

            def scores_of(kb):
                scores = dot_nn(keys_n[layer, kb * brows : (kb + 1) * brows], queries)
                if kb == b:
                    seen = key_at <= query_at
                    if b == nb - 1:
                        seen = seen & (key_at + b * brows < valid)
                    scores = jnp.where(seen, scores, masked_score)
                return scores

            pre_scores = dot_nn(pre_keys, queries)
            pre_scores = jnp.where(prefix_row < z.prefix_rows, pre_scores, masked_score)
            peak = jnp.max(pre_scores, axis=0, keepdims=True)
            for kb in range(b + 1):
                peak = jnp.maximum(peak, jnp.max(scores_of(kb), axis=0, keepdims=True))
            expons = jnp.exp(pre_scores - peak)
            expons_pre[layer, :, here] = expons
            denominator = jnp.sum(expons, axis=0, keepdims=True)
            for kb in range(b + 1):
                expons = jnp.exp(scores_of(kb) - peak)
                denominator = denominator + jnp.sum(expons, axis=0, keepdims=True)
                expons_low[layer, kb * brows : (kb + 1) * brows, here] = expons.astype(bf16)
            scale = 1.0 / denominator
            scales[layer, b] = scale
            seen_keys = (b + 1) * brows
            result = dot_nn(
                qkv[layer, 2 * HD : 3 * HD, :seen_keys], expons_low[layer, :seen_keys, here]
            )
            result = result + dot_nn(pre_values, expons_pre[layer, :, here].astype(bf16))
            result = result * scale
            out_t[layer, b] = result
            low = result.astype(bf16)
            ot_send[layer, b] = low
            for k in (2, 1, 3, 0):
                if k == 0:
                    push(ot_send.at[layer, b], att.at[layer, me], out_first + me, (s, t, b), d != b)

                    @pl.when(d == b)
                    def _():
                        att[layer, me] = low
                else:
                    push(
                        ot_send.at[layer, b], att.at[layer, me], out_first + me, (s, plane(k), b), near(k)
                    )
        return out_first

    def att_relay(layer, first):
        for j in range(nb):
            cell = across * nb + j
            arrived(att.at[layer, cell], first + cell, inner)
            push(att.at[layer, cell], att.at[layer, cell], first + cell, (s, beside, d), inner)

    def mixer_rows(layer, first):
        att_relay(layer, first)
        for at in range(0, z.width, tile):
            at = slice(at, at + tile)
            resid[:, at] = xs[layer, :, :, at].reshape(brows, tile).astype(f32) + vec[layer, 2:3, at]
        arrived(wm.at[layer], mix_third, s != layer)
        for p, seen in ((t, None), (beside, None), (across, inner), (nt - 1 - t, None)):
            for j in range(nb):
                cell = p * nb + j
                if seen is None:
                    arrived(att.at[layer, cell], first + cell, me != cell)
                else:
                    arrived(att.at[layer, cell], first + cell, jnp.logical_not(seen))
            joined = att[layer, pl.ds(p * nb, nb)].reshape(nb * HD, brows).T
            some_rows = pl.ds(pl.multiple_of(p * z.local_width, z.local_width), z.local_width)
            for at in range(0, z.width, tile):
                at = slice(at, at + tile)
                resid[:, at] += dot_nn(joined, wm[layer, some_rows, at])

    def grad_active():
        def some(at):
            last = gys[1].reshape(brows, z.width)
            upper[:, pl.ds(at, tile)] = dot_nt(last, wr[1, pl.ds(at, tile), :])

        tiles(z.hidden, some)

    def feed_first(layer, active):
        def some(at):
            v = dot_nn(normed[...], we[layer, :, pl.ds(at, tile)]) + vec[layer, 6:7, pl.ds(at, tile)]
            root = 0.7978845608028654
            square = v * v
            th = jnp.tanh(root * v * (1.0 + 0.044715 * square))
            half = 0.5 * (1.0 + th)
            active[:, pl.ds(at, tile)] = (v * half).astype(bf16)
            slope = half + (0.5 * root) * v * (1.0 - th * th) * (1.0 + 3.0 * 0.044715 * square)
            if layer == 0:
                gelu_grad[:, pl.ds(at, tile)] = slope
            else:
                wide[:, pl.ds(at, tile)] = (upper[:, pl.ds(at, tile)] * slope).astype(bf16)

        tiles(z.hidden, some)

    def feed_second(layer, active):
        def some(at):
            part = dot_nn(active[...], wr[layer, :, pl.ds(at, tile)])
            total[:, pl.ds(at, tile)] = part
            y_send[layer, :, :, pl.ds(at, tile)] = part.astype(bf16).reshape(nt, rows, tile)

        tiles(z.width, some)
        return scatter(layer, y_send, y_recv, y_relay)

    def scatter(layer, out, back, relay):
        first = claim("recv", nt + 3, "output" if out is y_send else "input")
        for i, (one, goal) in enumerate(zip(parts_of(out.at[layer, nt - 1 - t]), parts_of(relay.at[layer]))):
            push(one, goal, first + nt + i, (s, beside, d), outer)
        for k in (2, 1, 3):
            go = near(k) if k != 2 else outer
            push(out.at[layer, plane(k)], back.at[layer, k], first + k, (s, plane(k), d), go)
        return first

    def scatter_relay(layer, out, back, relay, full, first):
        for i in range(2):
            arrived(parts_of(relay.at[layer])[i], first + nt + i, inner)

            @pl.when(inner)
            def _():
                at = pl.ds(i * half, half)
                where = pl.ds(pl.multiple_of(across * rows + i * half, half), half)
                out[layer, across, at] = (full[where, :] + relay[layer, at].astype(f32)).astype(bf16)

            one, goal = parts_of(out.at[layer, across])[i], parts_of(back.at[layer, 2])[i]
            push(one, goal, first + (2, nt + 2)[i], (s, across, d), inner)

    def scatter_wait(layer, back, first, result):
        for k in (1, 3, 2):
            if k == 2:
                arrived(back.at[layer, k], first + k, inner)
                for i, one in enumerate(parts_of(back.at[layer, k])):
                    arrived(one, first + (2, nt + 2)[i], outer)
            else:
                arrived(back.at[layer, k], first + k, jnp.logical_not(unheard(k)))
            result = result + back[layer, k].astype(f32)
        return result

    def own_rows(ref):
        return ref[pl.ds(pl.multiple_of(t * rows, rows), rows), :]

    def output_sum(layer, first, base):
        return scatter_wait(layer, y_recv, first, base).astype(bf16)

    out_sem = claim("recv", 4)
    out_loads = []

    def put(src, out, layer, index):
        push(src, out.at[0, s], out_sem + index, sib, s != layer)
        copy = pltpu.make_async_copy(src, out.at[0, s], local_sem.at[claim("local", 1)])
        pl.when(s == layer)(copy.start)
        out_loads.append((copy, s == layer))

    own_weights = [load_mixer, load_expand, load_reduce]
    feed_recv = claim("recv", 2)
    out_first = None
    for layer in range(2):
        if layer == 0:
            load_x.wait()

            spread(x_in.at[s], xs, 0, s == 0)
            mix_two(0)

        norm_one(layer, t)
        spread_relay(xs, layer, x_first[layer])
        for k in (2, 1, 3):
            spread_wait(xs, layer, x_first[layer], k)
            norm_one(layer, plane(nt - k))
        if layer == 0:
            arrived(wq.at[0], wq_first, s == 1)
        else:
            arrived(wq.at[1], wq_first, s == 0)
        q_first = project(layer)
        if layer == 0:
            push(expand_in, we.at[s], feed_recv, sib)
            push(reduce_in, wr.at[s], feed_recv + 1, sib)
        else:
            mix_three(1)
            load_gy.wait()
            gy_first[1] = spread(gys.at[1, t], gys, 1)
        out_first = attend(layer, q_first)
        if layer == 0:
            for copy in own_weights:
                copy.wait()
            mix_three(0)
            mix_one(1)
        if layer == 1:
            arrived(we.at[1], feed_recv, s == 0)
            arrived(wr.at[1], feed_recv + 1, s == 0)
            spread_relay(gys, 1, gy_first[1])
            for k in range(1, nt):
                spread_wait(gys, 1, gy_first[1], k)
            grad_active()
        mixer_rows(layer, out_first)
        norm_two(layer)
        if layer == 0:
            arrived(we.at[0], feed_recv, s == 1)
            arrived(wr.at[0], feed_recv + 1, s == 1)
        feed_first(layer, wide if layer == 0 else active_last)
        if layer == 0:
            y_first = feed_second(layer, wide)
            scatter_relay(0, y_send, y_recv, y_relay, total, y_first)
            base = own_rows(resid) + own_rows(total) + row(layer, 5)
            mix_two(1)
            low = output_sum(0, y_first, base)
            xs[1, t] = low
            x_first[1] = spread(xs.at[1, t], xs, 1)
            put(xs.at[1, t], lo_out, 0, 0)

    def grad_hidden(layer):
        def some(at):
            part = dot_nt(gys[layer].reshape(brows, z.width), wr[layer, pl.ds(at, tile), :])
            wide[:, pl.ds(at, tile)] = (part * gelu_grad[:, pl.ds(at, tile)]).astype(bf16)

        tiles(z.hidden, some)

    def grad_mid(layer):
        def some(at):
            total[:, pl.ds(at, tile)] = dot_nt(wide[...], we[layer, pl.ds(at, tile), :])

        tiles(z.width, some)

        def pull(i, _):
            at, part = norm_pull(i, z_two.at[layer], inv_two.at[layer], row(layer, 3))
            above = gys[layer, i // (rows // step), pl.ds(lax.rem(i, rows // step) * step, step), :]
            part = part + above.astype(f32) * (1.0 / nt)
            grad_res[pl.ds(at, step), :] = part
            normed[pl.ds(at, step), :] = part.astype(bf16)
            return 0

        lax.fori_loop(0, brows // step, pull, 0, unroll=True)

    def grad_to_heads(layer):
        first = claim("recv", cells, "heads")
        relay_sem = claim("recv", 2, "heads beside")
        pairs = [pl.ds(0, nb // 2), pl.ds(nb // 2, nb - nb // 2)]

        def share(p, index):
            here = wm[layer, pl.ds(pl.multiple_of(p * z.local_width, z.local_width), z.local_width), :]
            part = dot_nt(here, normed[...]).astype(bf16).reshape(nb, HD, brows)
            gh_send[layer, index] = part
            return part

        def pass_on(p, index, when):
            for j in range(nb):
                push(gh_send.at[layer, index, j], gh.at[layer, me], first + me, (s, p, j), when)

        share(nt - 1 - t, 0)
        for i, two in enumerate(pairs):
            push(gh_send.at[layer, 0, two], gh_relay.at[layer, two], relay_sem + i, (s, beside, d), outer)
        pass_on(nt - 1 - t, 0, inner)
        share(across, 1)
        pass_on(across, 1, outer)
        share(beside, 2)
        pass_on(beside, 2, None)
        part = share(t, 3)
        for j in range(nb):
            push(gh_send.at[layer, 3, j], gh.at[layer, me], first + me, (s, t, j), d != j)

            @pl.when(d == j)
            def _():
                gh[layer, me] = part[j]

        for i, two in enumerate(pairs):
            arrived(gh_relay.at[layer, two], relay_sem + i, inner)

            @pl.when(inner)
            def _():
                met = gh_send[layer, 1, two].astype(f32) + gh_relay[layer, two].astype(f32)
                gh_send[layer, 1, two] = met.astype(bf16)

            for j in range(two.start, two.start + two.size):
                push(gh_send.at[layer, 1, j], gh.at[layer, me], first + me, (s, across, j), inner)

        return first

    def attend_back(layer, first):
        for b in range(nb):
            here = slice(b * brows, (b + 1) * brows)
            values_n[here] = qkv[layer, 2 * HD : 3 * HD, here].T
            queries = (qkv[layer, 0:HD, here].astype(f32) * HD ** (-0.5)).astype(bf16)
            queries_n[here] = queries.T
        out_first = claim("recv", nb, "mixed")
        pre_values = pre[layer, 1, d]
        pre_keys = pre[layer, 0, d].T
        for b in reversed(range(nb)):
            here = slice(b * brows, (b + 1) * brows)
            for p in range(nt):
                cell = p * nb + b
                heard = (me != cell) & jnp.logical_not(outer & (t + p == nt - 1))
                arrived(gh.at[layer, cell], first + cell, heard)
            grad = gh[layer, b].astype(f32)
            for p in range(1, nt):
                grad = grad + gh[layer, p * nb + b].astype(f32)
            grad = grad.astype(bf16)
            scale = scales[layer, b]
            wide_grad = grad.astype(f32)
            delta = jnp.sum(wide_grad * out_t[layer, b], axis=0, keepdims=True)
            grads_n[here] = (wide_grad * scale).astype(bf16).T
            prob = expons_pre[layer, :, here] * scale
            dscores_pre[:, here] = (prob * (dot_nn(pre_values, grad) - delta)).astype(bf16)
            for kb in range(b + 1):
                rows_k = slice(kb * brows, (kb + 1) * brows)
                prob = expons_low[layer, rows_k, here].astype(f32) * scale
                dprob = dot_nn(values_n[rows_k], grad)
                dscores[rows_k, here] = (prob * (dprob - delta)).astype(bf16)
            seen_keys = (b + 1) * brows
            dq = dot_nn(qkv[layer, HD : 2 * HD, :seen_keys], dscores[:seen_keys, here])
            dq = dq + dot_nn(pre_keys, dscores_pre[:, here])
            dkey = dot_nn(dscores[here, b * brows :], queries_n[b * brows :])
            dvalue = dot_nn(expons_low[layer, here, b * brows :], grads_n[b * brows :])
            joined = jnp.concatenate(
                [dq * HD ** (-0.5), dkey.T, dvalue.T], axis=0
            ).astype(bf16)
            dm_send[layer, b] = joined
            push(dm_send.at[layer, b], dm.at[layer, d], out_first + d, (s, t, b), d != b)

            @pl.when(d == b)
            def _():
                dm[layer, d] = joined

        pg[layer, 0] = dot_nn(dscores_pre[...], queries_n[...])
        pg[layer, 1] = dot_nn(expons_pre[layer].astype(bf16), grads_n[...])
        return out_first

    def grad_rows(layer, first):
        for j in range(nb):
            arrived(dm.at[layer, j], first + j, d != j)
        for j in range(nb):
            wide[:, j * 3 * HD : (j + 1) * 3 * HD] = dm[layer, j].T
        depth = nb * 3 * HD

        def some(at):
            right = wq[layer, :, :, pl.ds(at, tile)].reshape(depth, tile)
            total[:, pl.ds(at, tile)] = dot_nn(wide[:, :depth], right)

        tiles(z.width, some)

        def pull(i, _):
            at, part = norm_pull(i, z_one.at[layer], inv_one.at[layer], row(layer, 0))
            part = part + grad_res[pl.ds(at, step), :]
            grad_res[pl.ds(at, step), :] = part
            p = i // (rows // step)
            gi_send[layer, p, pl.ds(lax.rem(i, rows // step) * step, step), :] = part.astype(bf16)
            return 0

        lax.fori_loop(0, brows // step, pull, 0, unroll=True)
        return scatter(layer, gi_send, gi_recv, gi_relay)

    def grad_sum(layer, first):
        return scatter_wait(layer, gi_recv, first, own_rows(grad_res)).astype(bf16)

    for layer in (1, 0):
        if layer == 0:
            spread_relay(gys, 0, gy_first[0])
            for k in range(1, nt):
                spread_wait(gys, 0, gy_first[0], k)
            grad_hidden(0)
        grad_mid(layer)
        heads_first = grad_to_heads(layer)
        if layer == 1:
            y_first = feed_second(1, active_last)
            gi_own[...] = own_rows(resid) + own_rows(total) + row(1, 5)
        rows_first = attend_back(layer, heads_first)
        if layer == 1:
            scatter_relay(1, y_send, y_recv, y_relay, total, y_first)
        if layer == 0:
            sib_sem = claim("recv", 1)
            push(pg.at[1 - s], pg_recv, sib_sem, sib)
        grads_first = grad_rows(layer, rows_first)
        if layer == 0:
            arrived(pg_recv, sib_sem)
            pg_sum[...] = pg[s] + pg_recv[...]
            all_first = claim("recv", nb)
            for k in range(1, nb):
                push(pg_sum, pg_all.at[d], all_first + k, (s, t, block(k)))
            pg_all[d] = pg_sum[...]
        if layer == 1:
            scatter_relay(1, gi_send, gi_recv, gi_relay, grad_res, grads_first)
            y_last[...] = output_sum(1, y_first, gi_own[...])
            put(y_last, lo_out, 1, 1)
            gys[0, t] = grad_sum(1, grads_first)
            gy_first[0] = spread(gys.at[0, t], gys, 0)
            put(gys.at[0, t], ig_out, 1, 2)
        else:
            scatter_relay(0, gi_send, gi_recv, gi_relay, grad_res, grads_first)
            for k in range(1, nb):
                arrived(pg_all.at[block(nb - k)], all_first + k)
            keep(2, jnp.concatenate([pg_all[j, c] for c in range(2) for j in range(nb)], axis=1))
            part = jnp.zeros((z.prefix_pad, z.inner), f32)
            for j in range(nb):
                for c in range(2):
                    at = c * z.local_width + j * HD
                    part = part + dot_split(pg_all[j, c], outer_w[:, at : at + HD], dot_nt)
            hid_all[t] = part
            hid_first = claim("recv", nt)
            for k in range(1, nt):
                push(hid_all.at[t], hid_all.at[t], hid_first + k, (s, plane(k), d))
            xs[0, t] = grad_sum(0, grads_first)
            put(xs.at[0, t], ig_out, 0, 3)
            for k in range(1, nt):
                arrived(hid_all.at[plane(nt - k)], hid_first + k)
            part = hid_all[0]
            for p in range(1, nt):
                part = part + hid_all[p]
            hid_part[...] = part
            hid_sem = claim("recv", 1)
            push(hid_part, hid_recv, hid_sem, sib)
            arrived(hid_recv, hid_sem)
            keep(3, hid_part[...] + hid_recv[...])
            load_parts = lcopy(parts_low, rows_out.at[2, 0, 0])

    for index, (out, layer) in enumerate(((lo_out, 0), (lo_out, 1), (ig_out, 1), (ig_out, 0))):
        arrived(out.at[0, 1 - s], out_sem + index, s == layer)
    for copy, when in pending[-z.sends :]:
        sent(copy, when)
    for copy, when in out_loads:
        pl.when(when)(copy.wait)
    load_parts.wait()


def run_layers(z, small, large):
    nt, nb, rows, brows = z.planes, z.blocks, z.rows, z.block_rows
    width, hidden = z.width, z.hidden
    length = nb * brows
    V = pltpu.VMEM
    any_space = pl.BlockSpec(memory_space=pl.ANY)
    scratch = [
        V((2, 8, width), f32),
        V((2, nb, 3 * HD, 128), bf16),
        V((3, width, z.local_width), bf16),
        V((2, nb, 3 * HD, width), bf16),
        V((2, width, width), bf16),
        V((2, width, hidden), bf16),
        V((2, hidden, width), bf16),
        V((2, 2, nb, z.prefix_pad, HD), bf16),
        V((2, nt, rows, width), bf16),
        V((2, nt, rows, width), bf16),
        V((2, nb, 3 * HD, brows), bf16),
        V((2, 3 * HD, length), bf16),
        V((2, nb, HD, brows), bf16),
        V((2, z.cells, HD, brows), bf16),
        V((2, nt, rows, width), bf16),
        V((2, nt, rows, width), bf16),
        V((2, nt, nb, HD, brows), bf16),
        V((2, z.cells, HD, brows), bf16),
        V((2, nb, 3 * HD, brows), bf16),
        V((2, nb, 3 * HD, brows), bf16),
        V((2, nt, rows, width), bf16),
        V((2, nt, rows, width), bf16),
        V((2, rows, width), bf16),
        V((2, rows, width), bf16),
        V((2, nb, HD, brows), bf16),
        V((2, brows, width), f32),
        V((2, brows, 1), f32),
        V((2, brows, width), f32),
        V((2, brows, 1), f32),
        V((brows, hidden), f32),
        V((brows, hidden), f32),
        V((2, length, length), bf16),
        V((2, z.prefix_pad, length), f32),
        V((2, nb, 1, brows), f32),
        V((length, length), bf16),
        V((z.prefix_pad, length), bf16),
        V((length, HD), bf16),
        V((length, HD), bf16),
        V((length, HD), bf16),
        V((2, nb, HD, brows), f32),
        V((2, length, HD), bf16),
        V((brows, width), bf16),
        V((brows, width), bf16),
        V((brows, width), f32),
        V((brows, width), f32),
        V((brows, width), f32),
        V((rows, width), bf16),
        V((brows, width), bf16),
        V((rows, width), f32),
        V((2, 2, z.prefix_pad, HD), f32),
        V((2, z.prefix_pad, HD), f32),
        V((2, z.prefix_pad, HD), f32),
        V((nb, 2, z.prefix_pad, HD), f32),
        V((z.prefix_pad, width), f32),
        V((width, z.inner), bf16),
        V((z.inner, 2, z.local_width), bf16),
        V((z.inner, 2 * z.local_width), bf16),
        V((z.prefix_pad, z.inner), f32),
        V((z.prefix_pad, z.inner), f32),
        V((rows, width), bf16),
        V((nt, z.prefix_pad, z.inner), f32),
        pltpu.SemaphoreType.DMA((z.sends,)),
        pltpu.SemaphoreType.DMA((109,)),
        pltpu.SemaphoreType.DMA((13,)),
    ]
    return pl.pallas_call(
        partial(both_layers, z),
        out_shape=(
            jax.ShapeDtypeStruct((3, 1, 2, rows, width), bf16),
        ),
        in_specs=[pl.BlockSpec(memory_space=pltpu.SMEM)]
        + [pl.BlockSpec(memory_space=pltpu.VMEM)] * (len(small) - 1)
        + [any_space] * len(large),
        out_specs=(any_space,),
        scratch_shapes=scratch,
        compiler_params=pltpu.CompilerParams(
            collective_id=0, has_side_effects=True, vmem_limit_bytes=60 * 2**20
        ),
        cost_estimate=pl.CostEstimate(
            flops=7 * 10**9, bytes_accessed=16 * 2**20, transcendentals=4 * 10**6
        ),
    )(*small, *large)


def prefix_end(
    z, rows_in, table_in, inner_in,
    lo_out, ig_out, states_out, table_out, inner_out, inner_bias_out, outer_out, outer_bias_out,
    table_pad, parts, inner_full, outer_full, sems,
):
    copies = []

    def start(src, dst):
        copies.append(pltpu.make_async_copy(src, dst, sems.at[len(copies)]))
        copies[-1].start()

    start(rows_in.at[2, 0, 0], parts)
    start(rows_in.at[0], lo_out)
    start(rows_in.at[1], ig_out)
    count, width = z.prefix_rows, z.local_width
    table_pad[...] = jnp.zeros_like(table_pad)
    table_pad[0:count, :] = table_in[...].astype(f32)
    table_turned = table_pad[...].T.astype(bf16)
    copies[0].wait()

    def halves(index):
        at, columns = index // 2 * z.prefix_pad, slice(index % 2 * z.inner, (index % 2 + 1) * z.inner)
        high = parts[at : at + z.prefix_pad, columns]
        at += 2 * z.prefix_pad
        return high, parts[at : at + z.prefix_pad, columns]

    act = halves(0)[0].astype(f32) + halves(0)[1].astype(f32)
    hidden = halves(3)[0].astype(f32) + halves(3)[1].astype(f32)
    inner_grad = hidden * (1.0 - act * act)
    high = inner_grad.astype(bf16)
    low = (inner_grad - high.astype(f32)).astype(bf16)
    some = z.width // 2
    for i in range(2):
        at = slice(i * some, (i + 1) * some)
        inner_full[at] = dot_nn(table_turned[at], high) + dot_nn(table_turned[at], low)
        start(inner_full.at[at], inner_out.at[at])
    act_turned = act.T.astype(bf16)
    total = halves(2)
    for c in range(2):
        at = slice(c * width, (c + 1) * width)
        outer_full[:, c, :] = dot_nn(act_turned, total[0][:, at]) + dot_nn(act_turned, total[1][:, at])
    start(outer_full, outer_out)
    whole = total[0].astype(f32) + total[1].astype(f32)
    for c in range(2):
        at = slice(c * width, (c + 1) * width)
        states_out[:, c, :] = halves(1)[0][0:count, at]
        outer_bias_out[0, c : c + 1, :] = jnp.sum(whole[:, at], axis=0, keepdims=True)
    inner_bias_out[...] = jnp.sum(inner_grad, axis=0, keepdims=True)
    table_out[...] = (dot_nt(high, inner_in[...]) + dot_nt(low, inner_in[...]))[0:count]
    for copy in copies[1:]:
        copy.wait()


def finish(z, both_rows, table, inner_weight):
    any_space = pl.BlockSpec(memory_space=pl.ANY)
    whole = pl.BlockSpec(memory_space=pltpu.VMEM)
    rows = jax.ShapeDtypeStruct(both_rows.shape[1:], bf16)
    return pl.pallas_call(
        partial(prefix_end, z),
        out_shape=(
            rows,
            rows,
            jax.ShapeDtypeStruct((z.prefix_rows, 2, z.local_width), bf16),
            jax.ShapeDtypeStruct((z.prefix_rows, z.width), f32),
            jax.ShapeDtypeStruct((z.width, z.inner), f32),
            jax.ShapeDtypeStruct((1, z.inner), f32),
            jax.ShapeDtypeStruct((z.inner, 2, z.local_width), f32),
            jax.ShapeDtypeStruct((1, 2, z.local_width), f32),
        ),
        in_specs=[any_space] + [whole] * 2,
        out_specs=(any_space,) * 2 + (whole,) * 2 + (any_space, whole, any_space, whole),
        scratch_shapes=[
            pltpu.VMEM((z.prefix_pad, z.width), f32),
            pltpu.VMEM(both_rows.shape[3:], bf16),
            pltpu.VMEM((z.width, z.inner), f32),
            pltpu.VMEM((z.inner, 2, z.local_width), f32),
            pltpu.SemaphoreType.DMA((6,)),
        ],
        compiler_params=pltpu.CompilerParams(vmem_limit_bytes=32 * 2**20),
    )(both_rows, table, inner_weight)


def head_a_device(
    block_input,
    output_grad,
    valid_len,
    first_gain,
    first_bias,
    triple_weight,
    triple_bias,
    mixer_weight,
    mixer_bias,
    second_gain,
    second_bias,
    expand_weight,
    expand_bias,
    reduce_weight,
    reduce_bias,
    prefix_table,
    inner_weight,
    inner_bias,
    outer_weight,
    outer_bias,
):
    planes, blocks = lax.axis_size("tensor"), lax.axis_size("dp")
    local_width = triple_weight.shape[3]
    prefix_rows = prefix_table.shape[0]
    z = Sizes(
        planes,
        blocks,
        block_input.shape[1],
        block_input.shape[2],
        local_width,
        expand_weight.shape[2],
        prefix_rows,
    )
    z.prefix_pad = -(-prefix_rows // 16) * 16
    z.inner = inner_weight.shape[1]
    small = (
        valid_len,
        first_gain,
        first_bias,
        triple_bias,
        mixer_bias,
        second_gain,
        second_bias,
        expand_bias,
        reduce_bias,
        prefix_table,
        inner_bias,
        outer_bias,
    )
    large = (
        block_input,
        output_grad,
        triple_weight[0].transpose(1, 0, 2),
        mixer_weight[0],
        expand_weight[0],
        reduce_weight[0],
        inner_weight,
        outer_weight[:, 0],
    )
    results = finish(z, *run_layers(z, small, large), prefix_table, inner_weight)
    (
        layer_outputs,
        input_grads,
        prefix_states,
        table_grad,
        inner_weight_grad,
        inner_bias_grad,
        outer_weight_grad,
        outer_bias_grad,
    ) = results
    return (
        layer_outputs,
        input_grads,
        prefix_states.transpose(1, 0, 2)[None],
        table_grad,
        inner_weight_grad,
        inner_bias_grad.reshape(-1),
        outer_weight_grad.reshape(-1, 1, 2, local_width),
        outer_bias_grad,
    )


def prefix_back(
    prefix_total,
    prefix_full,
    inner_act,
    inner_low,
    outer_local,
    prefix_table,
    inner_weight,
    local_width,
):
    inner_float = inner_low.astype(f32)
    outer_float = outer_local.astype(f32)
    outer_weight_grad = jnp.dot(inner_float.T, prefix_total, precision=highest).reshape(
        -1, 1, 2, local_width
    )
    outer_bias_grad = jnp.sum(prefix_total, axis=0).reshape(1, 2, local_width)
    hidden_grad = lax.psum(
        jnp.dot(prefix_total, outer_float.T, precision=highest), ("section", "tensor")
    )
    inner_grad = hidden_grad * (1.0 - inner_act * inner_act)
    inner_weight_grad = jnp.dot(prefix_table.astype(f32).T, inner_grad, precision=highest)
    inner_bias_grad = jnp.sum(inner_grad, axis=0)
    table_grad = jnp.dot(inner_grad, inner_weight.astype(f32).T, precision=highest)
    prefix_states = prefix_full.reshape(-1, 2, local_width).transpose(1, 0, 2)[None]
    return (
        prefix_states,
        table_grad,
        inner_weight_grad,
        inner_bias_grad,
        outer_weight_grad,
        outer_bias_grad,
    )


def solution(mesh):
    def step(*args):
        triple_weight = args[5]
        micro_count, share_rows, width = args[0].shape
        fits = (
            lax.axis_size("section") == 2
            and micro_count == 2
            and triple_weight.shape[3] == HD * lax.axis_size("dp")
            and share_rows * lax.axis_size("tensor") == 256
            and triple_weight.shape[3] % 256 == 0
            and width % 256 == 0
            and args[11].shape[2] == width
            and args[16].shape[1] * 2 == width
            and args[15].shape[0] <= 16
            and share_rows == 64
        )
        return head_a_device(*args) if fits else shards(*args)

    return jax.shard_map(
        step,
        mesh=mesh,
        in_specs=(
            P(None, ("dp", "tensor"), None),
            P(None, ("dp", "tensor"), None),
            P(),
            P("section", None),
            P("section", None),
            P("section", None, None, "tensor"),
            P("section", None, "tensor"),
            P("section", "tensor", None),
            P("section", None),
            P("section", None),
            P("section", None),
            P("section", None, "tensor"),
            P("section", "tensor"),
            P("section", "tensor", None),
            P("section", None),
            P(),
            P(),
            P(),
            P(None, "section", None, "tensor"),
            P("section", None, "tensor"),
        ),
        out_specs=(
            P("section", None, ("dp", "tensor"), None),
            P("section", None, ("dp", "tensor"), None),
            P("section", None, None, "tensor"),
            P(),
            P(),
            P(),
            P(None, "section", None, "tensor"),
            P("section", None, "tensor"),
        ),
        check_vma=False,
    )
```
